128 devices in a mesh: dp: 8 (over y_lo, x), mp: 16 (over z, y_hi, core).
Axes of the slice: x: 4, y: 4 (y_hi: 2, y_lo: 2; y = y_hi * 2 + y_lo), z: 4, core: 2. Of those that a mesh axis runs over, the one named last changes fastest.
Arguments:
- residual_input: float32 [16384, 1024], P(('dp', 'mp')), may hold values from -6 to 6
- cotangent: float32 [16384, 1024], P(('dp', 'mp')), may hold values from -6 to 6
- lengths: int32 [8, 4], P('dp'), may hold values from 1 to 1024, 2048 in all within a row
- layernorm_gain: float32 [2, 2, 1024], replicated, may hold values from 0.5 to 1.5
- layernorm_bias: float32 [2, 2, 1024], replicated, may hold values from -1.25 to 1.25
- query_key_value_weight: bfloat16 [2, 1024, 3, 1024], P(None, None, None, 'mp'), may hold values from -0.1875 to 0.1875
- query_key_value_bias: float32 [2, 3, 1024], P(None, None, 'mp'), may hold values from -1.25 to 1.25
- query_key_value_lower_factor: float32 [2, 3, 1024, 128], replicated, may hold values from -0.1875 to 0.1875
- query_key_value_upper_factor: float32 [2, 3, 128, 1024], P(None, None, None, 'mp'), may hold values from -0.5 to 0.5
- attention_out_weight: bfloat16 [2, 1024, 1024], P(None, 'mp'), may hold values from -0.375 to 0.375
- attention_out_bias: float32 [2, 1024], replicated, may hold values from -1.25 to 1.25
- attention_out_lower_factor: float32 [2, 1024, 128], P(None, 'mp'), may hold values from -0.375 to 0.375
- attention_out_upper_factor: float32 [2, 128, 1024], replicated, may hold values from -0.5 to 0.5
- feedforward_in_weight: bfloat16 [2, 1024, 4096], P(None, None, 'mp'), may hold values from -0.1875 to 0.1875
- feedforward_in_bias: float32 [2, 4096], P(None, 'mp'), may hold values from -1.25 to 1.25
- feedforward_in_lower_factor: float32 [2, 1024, 128], replicated, may hold values from -0.1875 to 0.1875
- feedforward_in_upper_factor: float32 [2, 128, 4096], P(None, None, 'mp'), may hold values from -0.5 to 0.5
- feedforward_out_weight: bfloat16 [2, 4096, 1024], P(None, 'mp'), may hold values from -0.09375 to 0.09375
- feedforward_out_bias: float32 [2, 1024], replicated, may hold values from -1.25 to 1.25
- feedforward_out_lower_factor: float32 [2, 4096, 128], P(None, 'mp'), may hold values from -0.09375 to 0.09375
- feedforward_out_upper_factor: float32 [2, 128, 1024], replicated, may hold values from -0.5 to 0.5
Outputs:
- hidden_out: float32 [16384, 1024], P(('dp', 'mp'))
- grad_hidden_in: float32 [16384, 1024], P(('dp', 'mp'))
- grad_ln_gain: float32 [2, 2, 1024], replicated
- grad_ln_bias: float32 [2, 2, 1024], replicated
- grad_b_qkv: float32 [2, 3, 1024], P(None, None, 'mp')
- grad_lora_a_qkv: float32 [2, 3, 1024, 128], replicated
- grad_lora_b_qkv: float32 [2, 3, 128, 1024], P(None, None, None, 'mp')
- grad_b_out: float32 [2, 1024], replicated
- grad_lora_a_out: float32 [2, 1024, 128], P(None, 'mp')
- grad_lora_b_out: float32 [2, 128, 1024], replicated
- grad_b_in: float32 [2, 4096], P(None, 'mp')
- grad_lora_a_in: float32 [2, 1024, 128], replicated
- grad_lora_b_in: float32 [2, 128, 4096], P(None, None, 'mp')
- grad_b_down: float32 [2, 1024], replicated
- grad_lora_a_down: float32 [2, 4096, 128], P(None, 'mp')
- grad_lora_b_down: float32 [2, 128, 1024], replicated
The draws below stay inside these ranges and needn't reach their ends.
Inputs may be any that keep to these rules, and one draw needn't show every extreme that they name: Each row holds the lengths of the sequences of one data group in order and sums to 2048; the longest is reached in every draw.
All inputs are finite; a program needn't handle non-finite values.
Results may differ from the reference program's by a relative error of at most 0.02.
The reference program's roundings to bfloat16 on the way count: a program that leaves them out, or rounds other values in their place, can miss the bound.
Values may be sent and summed in bfloat16 or wider, within the bound.
A program may use at most 192 MiB of HBM per device.

```python
import math
import jax
import jax.numpy as jnp
import numpy as np
from jax import lax

MODEL_WIDTH = 1024
HEADS = 16
HD = 64
FEEDFORWARD_UNITS = 4096
ROT = 16
ADAPTER_RANK = 128
LAYER_COUNT = 2
SEQ_MAX = 1024
TOKENS_GROUP = 2048
TOKENS = 16384
SLOTS = 4
N_DP = 8


def steps_of(key, dims, split, least, largest):
    loudness = 1.0
    for position, parts in split:
        steps = jax.random.uniform(jax.random.fold_in(jax.random.fold_in(key, 6), position), (parts,), jnp.float32, least / len(split), largest / len(split))
        loudness = loudness * jnp.repeat(jnp.exp(steps), dims[position] // parts).reshape((-1,) + (1,) * (len(dims) - 1 - position))
    return loudness


def split_up(count, total, reach, lean):
    weights = [(1 << 20) // math.isqrt(standing ** lean) + 1 for standing in range(2, count + 1)]
    surplus, holding = total - reach - (count - 1), [1] * (count - 1)
    while surplus > 0:
        movable = [i for i in range(count - 1) if holding[i] < reach]
        pool, left = sum([weights[i] for i in movable]), surplus
        for i in movable:
            addition = min(reach - holding[i], max(1, left * weights[i] // pool), surplus)
            holding[i] = holding[i] + addition
            surplus = surplus - addition
    return np.array([reach] + holding)


def uneven(stream_key, number_of, total, limit, lean):
    if number_of == 2:
        one = jax.random.randint(stream_key, (), max(1, total - limit), min(limit, total - 1) + 1)
        return jnp.stack([one, total - one])
    sizes = jnp.asarray(split_up(number_of, total, limit, lean), jnp.int32)
    twos = (number_of - 1) // 2
    source_of, receiver = sizes[1:1 + 2 * twos:2], sizes[2:2 + 2 * twos:2]
    room = jnp.minimum(source_of - 1, limit - receiver)
    passed = jax.random.randint(jax.random.fold_in(stream_key, 1), (twos,), 0, 1 << 20) % (room + 1)
    sizes = sizes.at[1:1 + 2 * twos:2].set(source_of - passed).at[2:2 + 2 * twos:2].set(receiver + passed)
    return sizes[jax.random.permutation(jax.random.fold_in(stream_key, 2), number_of)]


def bell_draw(stream_key, dims, scale, most, cuts=(), held_as=jnp.bfloat16):
    factor_of = steps_of(stream_key, dims, cuts, -0.22, 0.18) if cuts else 1.0
    values = jax.random.normal(stream_key, dims, jnp.float32) * scale * factor_of
    return jnp.minimum(jnp.maximum(values, -most), most).astype(held_as)


def setup_inputs(seed: int = 0) -> dict:
    arg_keys = jax.random.split(jax.random.key(seed), 22)
    return {
        "residual_input": bell_draw(arg_keys[0], (TOKENS, MODEL_WIDTH), 1.0, 6.0, ((0, 128),), jnp.float32),
        "cotangent": bell_draw(arg_keys[1], (TOKENS, MODEL_WIDTH), 1.0, 6.0, ((0, 128),), jnp.float32),
        "lengths": jax.vmap(lambda own: uneven(own, SLOTS, TOKENS_GROUP, min(SEQ_MAX, TOKENS_GROUP // 2), 2))(jax.random.split(arg_keys[2], N_DP)).reshape((N_DP, SLOTS)).astype(jnp.int32),
        "layernorm_gain": jnp.clip(1.0 + 0.1 * jax.random.normal(arg_keys[3], (LAYER_COUNT, 2, MODEL_WIDTH), jnp.float32), 0.5, 1.5),
        "layernorm_bias": bell_draw(arg_keys[4], (LAYER_COUNT, 2, MODEL_WIDTH), 0.2, 1.25, (), jnp.float32),
        "query_key_value_weight": bell_draw(arg_keys[5], (LAYER_COUNT, MODEL_WIDTH, 3, MODEL_WIDTH), MODEL_WIDTH ** -0.5, 0.1875, ((3, 16),)),
        "query_key_value_bias": bell_draw(arg_keys[6], (LAYER_COUNT, 3, MODEL_WIDTH), 0.2, 1.25, ((2, 16),), jnp.float32),
        "query_key_value_lower_factor": bell_draw(arg_keys[7], (LAYER_COUNT, 3, MODEL_WIDTH, ADAPTER_RANK), MODEL_WIDTH ** -0.5, 0.1875, (), jnp.float32),
        "query_key_value_upper_factor": bell_draw(arg_keys[8], (LAYER_COUNT, 3, ADAPTER_RANK, MODEL_WIDTH), ADAPTER_RANK ** -0.5, 0.5, ((3, 16),), jnp.float32),
        "attention_out_weight": bell_draw(arg_keys[9], (LAYER_COUNT, MODEL_WIDTH, MODEL_WIDTH), (MODEL_WIDTH // 4) ** -0.5, 0.375, ((1, 16),)),
        "attention_out_bias": bell_draw(arg_keys[10], (LAYER_COUNT, MODEL_WIDTH), 0.2, 1.25, (), jnp.float32),
        "attention_out_lower_factor": bell_draw(arg_keys[11], (LAYER_COUNT, MODEL_WIDTH, ADAPTER_RANK), (MODEL_WIDTH // 4) ** -0.5, 0.375, ((1, 16),), jnp.float32),
        "attention_out_upper_factor": bell_draw(arg_keys[12], (LAYER_COUNT, ADAPTER_RANK, MODEL_WIDTH), ADAPTER_RANK ** -0.5, 0.5, (), jnp.float32),
        "feedforward_in_weight": bell_draw(arg_keys[13], (LAYER_COUNT, MODEL_WIDTH, FEEDFORWARD_UNITS), MODEL_WIDTH ** -0.5, 0.1875, ((2, 16),)),
        "feedforward_in_bias": bell_draw(arg_keys[14], (LAYER_COUNT, FEEDFORWARD_UNITS), 0.2, 1.25, ((1, 16),), jnp.float32),
        "feedforward_in_lower_factor": bell_draw(arg_keys[15], (LAYER_COUNT, MODEL_WIDTH, ADAPTER_RANK), MODEL_WIDTH ** -0.5, 0.1875, (), jnp.float32),
        "feedforward_in_upper_factor": bell_draw(arg_keys[16], (LAYER_COUNT, ADAPTER_RANK, FEEDFORWARD_UNITS), ADAPTER_RANK ** -0.5, 0.5, ((2, 16),), jnp.float32),
        "feedforward_out_weight": bell_draw(arg_keys[17], (LAYER_COUNT, FEEDFORWARD_UNITS, MODEL_WIDTH), FEEDFORWARD_UNITS ** -0.5, 0.09375, ((1, 16),)),
        "feedforward_out_bias": bell_draw(arg_keys[18], (LAYER_COUNT, MODEL_WIDTH), 0.2, 1.25, (), jnp.float32),
        "feedforward_out_lower_factor": bell_draw(arg_keys[19], (LAYER_COUNT, FEEDFORWARD_UNITS, ADAPTER_RANK), FEEDFORWARD_UNITS ** -0.5, 0.09375, ((1, 16),), jnp.float32),
        "feedforward_out_upper_factor": bell_draw(arg_keys[20], (LAYER_COUNT, ADAPTER_RANK, MODEL_WIDTH), ADAPTER_RANK ** -0.5, 0.5, (), jnp.float32),
    }


@jax.custom_vjp
def low(v):
    return lax.optimization_barrier(v.astype(jnp.bfloat16)).astype(jnp.float32)

@jax.custom_vjp
def low_back(v):
    return v

def low_keep(v):
    return (low(v), None)

def low_pass(kept, grad):
    return (grad,)

def back_keep(v):
    return (v, None)

def back_low(kept, grad):
    return (low(grad),)
low.defvjp(low_keep, low_pass)
low_back.defvjp(back_keep, back_low)
EPSILON = 1e-05
MASK_FILL = -1000000000.0
HIGHEST = lax.Precision.HIGHEST

def layout(length_row, token_count):
    ends = jnp.cumsum(length_row).astype(jnp.int32)
    starts = (ends - length_row).astype(jnp.int32)
    token_index = jnp.arange(token_count, dtype=jnp.int32)
    doc_ids = lax.optimization_barrier(jnp.sum((token_index[:, None] >= ends[None, :]).astype(jnp.int32), axis=1)).astype(jnp.int32)
    slot_ids = jnp.arange(length_row.shape[0], dtype=jnp.int32)
    first_token = lax.optimization_barrier(jnp.sum(jnp.where(doc_ids[:, None] == slot_ids[None, :], starts[None, :], 0), axis=1)).astype(jnp.int32)
    return (doc_ids, (token_index - first_token).astype(jnp.int32))

def tables(positions, rot_width):
    frequency = jnp.exp(jnp.arange(0, rot_width, 2, dtype=jnp.float32) * (-math.log(10000.0) / rot_width))
    angles = positions.astype(jnp.float32)[:, None] * frequency[None, :]
    angles = jnp.concatenate([angles, angles], axis=1)
    return (jnp.cos(angles), jnp.sin(angles))

def rotate(head_values, cosine, sine_table, rot_width):
    rotated_part = head_values[..., :rot_width]
    unrotated = head_values[..., rot_width:]
    half_rot = rot_width // 2
    turned = jnp.concatenate([-rotated_part[..., half_rot:], rotated_part[..., :half_rot]], axis=-1)
    result = rotated_part * cosine[:, None, :] + turned * sine_table[:, None, :]
    return jnp.concatenate([result, unrotated], axis=-1)

def normalize(stream, ln_gain_row, ln_shift):
    average = lax.optimization_barrier(jnp.mean(stream, axis=-1, keepdims=True))
    centered = stream - average
    variance = lax.optimization_barrier(jnp.mean(centered * centered, axis=-1, keepdims=True))
    return centered * lax.rsqrt(variance + EPSILON) * ln_gain_row + ln_shift

def ref_layer(stream, weights, frozen, cosine, sine_table, doc_ids, token_index):
    gains, shifts, bias_qkv, adapt_a_qkv, adapt_b_qkv, bias_out, adapt_a_out, adapt_b_out, bias_in, adapt_a_in, adapt_b_in, bias_down, adapt_a_down, adapt_b_down = weights
    frozen_qkv, frozen_out, frozen_in, frozen_down = frozen
    token_count = stream.shape[0]
    normed_one = low(normalize(stream, gains[0], shifts[0]))
    normed_two = low(normalize(stream, gains[1], shifts[1]))
    merged_qkv = low(frozen_qkv + jnp.einsum('jdr,jre->dje', adapt_a_qkv, adapt_b_qkv, precision=HIGHEST))
    projected = jnp.einsum('td,dje->tje', normed_one, merged_qkv, precision=HIGHEST) + bias_qkv[None]
    projected = low_back(projected)
    head_values = projected.reshape(token_count, 3, HEADS, HD)
    queries = low(rotate(head_values[:, 0], cosine, sine_table, ROT))
    keys_rot = low(rotate(head_values[:, 1], cosine, sine_table, ROT))
    values = low(head_values[:, 2])
    block_rows = min(512, token_count)
    blocks_count = token_count // block_rows
    scale = HD ** (-0.5)

    def attend(inputs):
        query_block, block_start = inputs
        row_index = block_start + jnp.arange(block_rows, dtype=jnp.int32)
        row_docs = lax.dynamic_slice_in_dim(doc_ids, block_start, block_rows)
        allowed = (row_docs[:, None] == doc_ids[None, :]) & (token_index[None, :] <= row_index[:, None])
        scores = jnp.einsum('qhe,khe->hqk', query_block, keys_rot, precision=HIGHEST) * scale
        scores = jnp.where(allowed[None], scores, MASK_FILL)
        weights_soft = low(jax.nn.softmax(scores, axis=-1))
        return jnp.einsum('hqk,khe->qhe', weights_soft, values, precision=HIGHEST)
    block_starts = jnp.arange(blocks_count, dtype=jnp.int32) * block_rows
    attention_out = lax.map(jax.checkpoint(attend), (queries.reshape(blocks_count, block_rows, HEADS, HD), block_starts))
    attended = low(low_back(attention_out.reshape(token_count, HEADS * HD)))
    merged_out = low(frozen_out + jnp.dot(adapt_a_out, adapt_b_out, precision=HIGHEST))
    merged_in = low(frozen_in + jnp.dot(adapt_a_in, adapt_b_in, precision=HIGHEST))
    merged_down = low(frozen_down + jnp.dot(adapt_a_down, adapt_b_down, precision=HIGHEST))
    hidden_pre = low_back(jnp.dot(normed_two, merged_in, precision=HIGHEST) + bias_in[None])
    activated = low(jax.nn.gelu(hidden_pre, approximate=False))
    branch = low_back(jnp.dot(attended, merged_out, precision=HIGHEST) + jnp.dot(activated, merged_down, precision=HIGHEST))
    return stream + branch + bias_out[None] + bias_down[None]

def reference(residual_input, cotangent, lengths, layernorm_gain, layernorm_bias, query_key_value_weight, query_key_value_bias, query_key_value_lower_factor, query_key_value_upper_factor, attention_out_weight, attention_out_bias, attention_out_lower_factor, attention_out_upper_factor, feedforward_in_weight, feedforward_in_bias, feedforward_in_lower_factor, feedforward_in_upper_factor, feedforward_out_weight, feedforward_out_bias, feedforward_out_lower_factor, feedforward_out_upper_factor):
    learned_params = (layernorm_gain, layernorm_bias, query_key_value_bias, query_key_value_lower_factor, query_key_value_upper_factor, attention_out_bias, attention_out_lower_factor, attention_out_upper_factor, feedforward_in_bias, feedforward_in_lower_factor, feedforward_in_upper_factor, feedforward_out_bias, feedforward_out_lower_factor, feedforward_out_upper_factor)
    frozen = tuple((matrix.astype(jnp.float32) for matrix in (query_key_value_weight, attention_out_weight, feedforward_in_weight, feedforward_out_weight)))
    groups_in = residual_input.reshape(N_DP, TOKENS_GROUP, MODEL_WIDTH)
    groups_grad = cotangent.reshape(N_DP, TOKENS_GROUP, MODEL_WIDTH)

    def one_group(totals, inputs):
        group_stream, grad_output, length_row = inputs
        doc_ids, positions = layout(length_row, TOKENS_GROUP)
        cosine, sine_table = tables(positions, ROT)
        token_index = jnp.arange(TOKENS_GROUP, dtype=jnp.int32)

        def forward(params, start_stream):
            current = start_stream
            for layer_index in range(LAYER_COUNT):
                layer_weights = tuple((param[layer_index] for param in params))
                layer_frozen = tuple((matrix[layer_index] for matrix in frozen))
                current = ref_layer(current, layer_weights, layer_frozen, cosine, sine_table, doc_ids, token_index)
            return current
        output, pullback = jax.vjp(forward, learned_params, group_stream)
        gradient, grad_stream = pullback(grad_output)
        totals = jax.tree.map(lambda acc_sum, new_sum: acc_sum + new_sum, totals, gradient)
        return (totals, (output, grad_stream))
    zero_grads = jax.tree.map(jnp.zeros_like, learned_params)
    totals, (outputs, grad_streams) = lax.scan(one_group, zero_grads, (groups_in, groups_grad, lengths))
    return (outputs.reshape(TOKENS, MODEL_WIDTH), grad_streams.reshape(TOKENS, MODEL_WIDTH), totals[0], totals[1], totals[2], totals[3], totals[4], totals[5], totals[6], totals[7], totals[8], totals[9], totals[10], totals[11], totals[12], totals[13])
```

```python
import functools
import math

import jax
import jax.numpy as jnp
from jax import lax
from jax.experimental import pallas as pl
from jax.experimental.pallas import tpu as pltpu
from jax.sharding import Mesh
from jax.sharding import PartitionSpec as P

HD = 64
ROT = 16
LAYERS = 2
EPS = 1e-05
FILL = -1000000000.0
MP = ("z", "yh", "c")
DP = ("yl", "x")
ALL = ("yl", "x", "z", "yh", "c")
MESH = pl.DeviceIdType.MESH

D = 1024
T = 2048
OWN = 128
BLK = 256
NB = T // BLK
WIN = 5 * BLK
NQ = 256
FF = 256
NIN = NQ + FF
NOUT = 128 + FF
R = 128
NCH = 2
F32 = jnp.float32
BF16 = jnp.bfloat16
HIGH = lax.Precision.HIGHEST

NN = (((1,), (0,)), ((), ()))
NT = (((1,), (1,)), ((), ()))
TN = (((0,), (0,)), ((), ()))


def mm(a, b, dims=NN, precision=None):
    return lax.dot_general(a, b, dims, precision=precision, preferred_element_type=F32)


def split_bf16(a):
    high = a.astype(BF16)
    return high, (a - high.astype(F32)).astype(BF16)


def mm3(a, b, dims=NN):
    ah, al = split_bf16(a)
    bh, bl = split_bf16(b)
    return mm(ah, bh, dims) + (mm(al, bh, dims) + mm(ah, bl, dims))


def rows_of(ref, start, count):
    return ref.at[pl.ds(start if isinstance(start, int) else pl.multiple_of(start, count), count)]


class Place:
    def __init__(self):
        self.z, self.h, self.c = (lax.axis_index(a) for a in MP)
        self.up = {"z": lax.rem(self.z + 1, 4)}
        self.dn = {"z": lax.rem(self.z + 3, 4)}
        self.yy = {"yh": 1 - self.h}
        self.sib = {"c": 1 - self.c}

    def block(self, dz, dh):
        return lax.rem(self.z + dz, 4) * 2 + (self.h if dh == 0 else 1 - self.h)

    def shard(self, dz, dh, dc):
        return self.block(dz, dh) * 2 + (self.c if dc == 0 else 1 - self.c)

    def meet(self):
        barrier = pltpu.get_barrier_semaphore()
        for peer in (self.up, self.dn, self.yy, self.sib):
            pl.semaphore_signal(barrier, inc=1, device_id=peer, device_id_type=MESH)
        pl.semaphore_wait(barrier, 4)


class Sender:
    def __init__(self, sems):
        self.sems = sems
        self.live = []

    def send(self, src, dst, peer, recv_sem):
        copy = pltpu.make_async_remote_copy(
            src_ref=src,
            dst_ref=dst,
            send_sem=self.sems.at[len(self.live)],
            recv_sem=recv_sem,
            device_id=peer,
            device_id_type=MESH,
        )
        copy.start()
        self.live.append(copy)

    def got(self, ref, sem, peer):
        pltpu.make_async_remote_copy(
            src_ref=ref,
            dst_ref=ref,
            send_sem=self.sems.at[0],
            recv_sem=sem,
            device_id=peer,
            device_id_type=MESH,
        ).wait_recv()

    def finish(self):
        for copy in self.live:
            copy.wait_send()


GATHER_SENDS = 16 * NCH
GATHER_SEMS = [pltpu.SemaphoreType.DMA((8 * NCH,)), pltpu.SemaphoreType.DMA((8 * NCH,))]


def gather(me, out, buf, direct, cross, compute):
    rows = OWN // NCH

    def part(dz, dh, dc, k):
        return rows_of(buf, me.shard(dz, dh, dc) * OWN + k * rows, rows)

    def sem(sems, dz, dh, k):
        return sems.at[(dz * 2 + dh) * NCH + k]

    def send(dz, dh, k, peer, there):
        sems, tz, th = there
        ref = part(dz, dh, 0, k)
        out.send(ref, ref, peer, sem(sems, tz, th, k))

    def got(dz, dh, k):
        out.got(part(dz, dh, 0, k), sem(direct, dz, dh, k), me.sib)

    def done(dz, dh):
        for k in range(NCH):
            out.got(part(dz, dh, 1, k), sem(cross, dz, dh, k), me.sib)
        compute(dz, dh)

    def pass_on(dz, dh, k):
        send(dz, dh, k, me.sib, (cross, dz, dh))

    for k in range(NCH):
        send(0, 0, k, me.yy, (direct, 0, 1))
        send(0, 0, k, me.up, (direct, 3, 0))
        send(0, 0, k, me.dn, (direct, 1, 0))
    for k in range(NCH):
        pass_on(0, 0, k)
    done(0, 0)
    for k in range(NCH):
        got(0, 1, k)
        send(0, 1, k, me.dn, (direct, 1, 1))
        got(3, 0, k)
        send(3, 0, k, me.up, (direct, 2, 0))
        send(0, 1, k, me.up, (direct, 3, 1))
        pass_on(0, 1, k)
        pass_on(3, 0, k)
        got(1, 0, k)
        pass_on(1, 0, k)
    done(0, 1)
    done(3, 0)
    done(1, 0)
    for k in range(NCH):
        got(1, 1, k)
        send(1, 1, k, me.dn, (direct, 2, 1))
        pass_on(1, 1, k)
    for k in range(NCH):
        got(3, 1, k)
        pass_on(3, 1, k)
        got(2, 0, k)
        pass_on(2, 0, k)
    done(1, 1)
    done(3, 1)
    done(2, 0)
    for k in range(NCH):
        got(2, 1, k)
        pass_on(2, 1, k)
    done(2, 1)


SCATTER_SENDS = 8 + 7 * NCH
SCATTER_SCRATCH = [
    pltpu.VMEM((8 * OWN, D), F32),
    pltpu.VMEM((8 * OWN, D), BF16),
    pltpu.VMEM((8 * OWN, D), BF16),
    pltpu.VMEM((8 * OWN, D), BF16),
    pltpu.VMEM((2 * OWN, D), BF16),
    pltpu.VMEM((4 * OWN, D), BF16),
    pltpu.VMEM((OWN, D), BF16),
    pltpu.SemaphoreType.DMA((8,)),
    pltpu.SemaphoreType.DMA((2 * NCH,)),
    pltpu.SemaphoreType.DMA((4 * NCH,)),
    pltpu.SemaphoreType.DMA((NCH,)),
]


def scatter(me, out, bufs, compute, between, finish):
    own, other, cross, sums, via, ring, last, s_cross, s_via, s_ring, s_last = bufs
    rows = OWN // NCH

    def give(dz, dh):
        i = dz * 2 + dh

        def put(dc, terms):
            if dc == 0:
                own[pl.ds(i * OWN, OWN), :] = terms
            else:
                other[pl.ds(i * OWN, OWN), :] = terms.astype(BF16)

        compute(dz, dh, put)
        out.send(
            rows_of(other, i * OWN, OWN),
            rows_of(cross, i * OWN, OWN),
            me.sib,
            s_cross.at[i],
        )

    def wait_cross(dz, dh):
        i = dz * 2 + dh
        out.got(rows_of(cross, i * OWN, OWN), s_cross.at[i], me.sib)

    def both(dz, dh, k):
        here = pl.ds((dz * 2 + dh) * OWN + k * rows, rows)
        return own[here, :] + cross[here, :].astype(F32)

    def arrived(buf, sems, i, k):
        ref = rows_of(buf, i * OWN + k * rows, rows)
        out.got(ref, sems.at[i * NCH + k], me.sib)
        return ref[...].astype(F32)

    def pass_to(dz, dh, k, value, buf, sems, i, peer):
        at = (dz * 2 + dh) * OWN + k * rows
        sums[pl.ds(at, rows), :] = value.astype(BF16)
        out.send(
            rows_of(sums, at, rows),
            rows_of(buf, i * OWN + k * rows, rows),
            peer,
            sems.at[i * NCH + k],
        )

    chunks = range(NCH)
    give(2, 0)
    give(2, 1)
    wait_cross(2, 0)
    for k in chunks:
        pass_to(2, 0, k, both(2, 0, k), via, s_via, 0, me.up)
    wait_cross(2, 1)
    for k in chunks:
        pass_to(2, 1, k, both(2, 1, k), via, s_via, 1, me.dn)
    give(1, 1)
    give(3, 0)
    wait_cross(1, 1)
    for k in chunks:
        pass_to(1, 1, k, both(1, 1, k), ring, s_ring, 1, me.up)
    wait_cross(3, 0)
    for k in chunks:
        pass_to(3, 0, k, both(3, 0, k), ring, s_ring, 2, me.dn)
    give(1, 0)
    give(3, 1)
    wait_cross(3, 1)
    wait_cross(1, 0)
    for k in chunks:
        pass_to(3, 1, k, both(3, 1, k) + arrived(via, s_via, 1, k), ring, s_ring, 3, me.dn)
        pass_to(1, 0, k, both(1, 0, k) + arrived(via, s_via, 0, k), ring, s_ring, 0, me.up)
    give(0, 1)
    give(0, 0)
    between()
    wait_cross(0, 1)
    for k in chunks:
        total = both(0, 1, k) + arrived(ring, s_ring, 1, k) + arrived(ring, s_ring, 3, k)
        pass_to(0, 1, k, total, last, s_last, 0, me.yy)
    wait_cross(0, 0)
    for k in chunks:
        total = both(0, 0, k) + arrived(ring, s_ring, 0, k) + arrived(ring, s_ring, 2, k)
        finish(k * rows, rows, total + arrived(last, s_last, 0, k))


def gelu_parts(h):
    cdf = 0.5 * (1.0 + lax.erf(h * (2.0**-0.5)))
    return cdf


def prep_kernel(wqkv, aqkv, bqkv, win_, ain, bin_, wout_, aout, bout, wdown, adown, bdown, gains, shifts, biases,
                o_win, o_wint, o_bias, o_wout):
    ratio = gains[1:2, :] / gains[0:1, :]
    ab = mm3(aqkv[0], bqkv[0:R]) + mm3(aqkv[1], bqkv[R:2 * R]) + mm3(aqkv[2], bqkv[2 * R:])
    low = (wqkv[...].astype(F32) + ab).astype(BF16)
    o_win[:, 0:NQ] = low
    o_wint[0:NQ, :] = low.T
    o_bias[:, 0:NQ] = biases[:, 0:NQ]
    merged = win_[...].astype(F32) + mm3(ain[...], bin_[...])
    low = merged.astype(BF16)
    b_high, b_low = split_bf16(jnp.broadcast_to(shifts[1:2, :] - shifts[0:1, :] * ratio, (8, D)))
    shift = (mm(b_high, low) + mm(b_low, low))[0:1]
    o_bias[:, NQ:NIN] = biases[:, NQ:NIN] + shift
    turned = (merged.T * ratio).astype(BF16)
    o_wint[NQ:NIN, :] = turned
    o_win[:, NQ:NIN] = turned.T
    o_wout[0:64, :] = (wout_[...].astype(F32) + mm3(aout[...], bout[...])).astype(BF16)
    o_wout[64:128, :] = jnp.zeros((64, D), BF16)
    o_wout[128:NOUT, :] = (wdown[...].astype(F32) + mm3(adown[...], bdown[...])).astype(BF16)


def prep(wqkv, aqkv, bqkv, win_, ain, bin_, wout_, aout, bout, wdown, adown, bdown, gains, shifts, biases):
    ins = (wqkv, aqkv, bqkv, win_, ain, bin_, wout_, aout, bout, wdown, adown, bdown, gains, shifts, biases)

    def spec(a):
        rank = a.ndim - 1
        return pl.BlockSpec((None, *a.shape[1:]), lambda l: (l,) + (0,) * rank)

    outs = [
        jax.ShapeDtypeStruct((LAYERS, D, NIN), BF16),
        jax.ShapeDtypeStruct((LAYERS, NIN, D), BF16),
        jax.ShapeDtypeStruct((LAYERS, 1, NIN), F32),
        jax.ShapeDtypeStruct((LAYERS, NOUT, D), BF16),
    ]
    return pl.pallas_call(
        prep_kernel,
        grid=(LAYERS,),
        out_shape=outs,
        in_specs=[spec(a) for a in ins],
        out_specs=[spec(a) for a in outs],
        compiler_params=pltpu.CompilerParams(vmem_limit_bytes=48 << 20),
        name="prep",
    )(*ins)


def lane_roll(a, shift):
    return pltpu.roll(a, shift % 128, 1)


def normalized(x):
    mean = jnp.mean(x, axis=1, keepdims=True)
    centered = x - mean
    scale = lax.rsqrt(jnp.mean(centered * centered, axis=1, keepdims=True) + EPS)
    return centered * scale, scale


class Loads:
    def __init__(self, sems):
        self.sems = sems
        self.count = 0

    def start(self, src, dst):
        copy = pltpu.make_async_copy(src, dst, self.sems.at[self.count])
        self.count += 1
        copy.start()
        return copy


def forward_kernel(layer, x_ref, gains, shifts, win_h, bias_h, wout_h, obias, tabs_h, first_h,
                   o_x, o_xh, o_qkv, o_ho, o_out, o_lse,
                   xh, qkv, ho, ou, out_t, scores, probs, win, bias, wout, tabs, first,
                   load_sems, send_sems, g_direct, g_cross, *scat):
    me = Place()
    loads = Loads(load_sems)
    ins = [
        loads.start(win_h.at[layer], win),
        loads.start(bias_h.at[layer], bias),
        loads.start(tabs_h, tabs),
        loads.start(first_h, first),
        loads.start(wout_h.at[layer], wout),
    ]
    out = Sender(send_sems)
    me.meet()
    x = x_ref[...]
    rows_of(xh, me.shard(0, 0, 0) * OWN, OWN)[...] = (
        normalized(x)[0] * gains[0:1, :] + shifts[0:1, :]
    ).astype(BF16)
    state = {"loaded": False}

    def project(dz, dh):
        if not state["loaded"]:
            for copy in ins:
                copy.wait()
            state["loaded"] = True
        at = pl.ds(pl.multiple_of(me.block(dz, dh) * BLK, BLK), BLK)
        rows = xh[at, :]
        pq = mm(rows, win[:, 0:NQ]) + bias[:, 0:NQ]
        qk = pq[:, 0:128]
        turned = qk * tabs[0, at, :] + lane_roll(qk, -8) * tabs[1, at, :] + lane_roll(qk, 8) * tabs[2, at, :]
        lane = lax.broadcasted_iota(jnp.int32, (BLK, 128), 1)
        qkv[at, 0:128] = jnp.where(lane < HD, turned, 0.0).astype(BF16)
        qkv[at, 128:256] = jnp.where(lane < HD, lane_roll(turned, HD), 0.0).astype(BF16)
        qkv[at, 256:384] = pq[:, 128:256].astype(BF16)
        h = mm(rows, win[:, NQ:NIN]) + bias[:, NQ:NIN]
        ho[at, 128:NOUT] = h
        ou[at, 128:NOUT] = (h * gelu_parts(h)).astype(BF16)

    gather(me, out, xh, g_direct, g_cross, project)
    outs = [loads.start(xh, o_xh), loads.start(qkv, o_qkv)]

    def attend(dz, dh, put):
        b = me.block(dz, dh)
        at = pl.ds(pl.multiple_of(b * BLK, BLK), BLK)
        key_at = jnp.maximum(b - 4, 0) * BLK
        q = qkv[at, 0:128]
        row = b * BLK + lax.broadcasted_iota(jnp.int32, (BLK, BLK), 0)
        start = jnp.concatenate([first[at, :], first[at, :]], axis=1)
        peak = None
        for j in range(5):
            keys = pl.ds(pl.multiple_of(key_at + j * BLK, BLK), BLK)
            s = mm(q, qkv[keys, 128:256], NT) * (HD**-0.5)
            col = key_at + j * BLK + lax.broadcasted_iota(jnp.int32, (BLK, BLK), 1)
            s = jnp.where((col >= start) & (col <= row), s, FILL)
            scores[:, j * BLK:(j + 1) * BLK] = s
            peak = s if peak is None else jnp.maximum(peak, s)
        peak = jnp.max(peak, axis=1, keepdims=True)
        summed = None
        for j in range(5):
            p = jnp.exp(scores[:, j * BLK:(j + 1) * BLK] - peak)
            scores[:, j * BLK:(j + 1) * BLK] = p
            summed = p if summed is None else summed + p
        summed = jnp.sum(summed, axis=1, keepdims=True)
        share = 1.0 / summed
        for j in range(5):
            here = slice(j * BLK, (j + 1) * BLK)
            probs[:, here] = (scores[:, here] * share).astype(BF16)
        o = mm(probs[...], qkv[pl.ds(pl.multiple_of(key_at, BLK), WIN), 256:384])
        ho[at, 0:128] = o
        ou[at, 0:128] = o.astype(BF16)
        lse = jnp.broadcast_to(peak + jnp.log(summed), (BLK, 128)).T
        o_lse[:, at] = lse[0:8, :]
        out_t[:, at] = ou[at, :].astype(F32).T.astype(BF16)
        for dc in range(2):
            put(dc, mm(rows_of(ou, me.shard(dz, dh, dc) * OWN, OWN)[...], wout[...]))

    def between():
        outs.append(loads.start(ho, o_ho))
        outs.append(loads.start(out_t, o_out))

    def finish(at, rows, total):
        here = pl.ds(at, rows)
        o_x[here, :] = x_ref[here, :] + total + obias[...]

    scatter(me, out, scat, attend, between, finish)
    for copy in outs:
        copy.wait()
    out.finish()


VM = pl.BlockSpec(memory_space=pltpu.VMEM)
HBM = pl.BlockSpec(memory_space=pl.ANY)


def forward(layer, x, gains, shifts, win, bias, wout, obias, tabs, first):
    shapes = [
        jax.ShapeDtypeStruct((OWN, D), F32),
        jax.ShapeDtypeStruct((T, D), BF16),
        jax.ShapeDtypeStruct((T, 384), BF16),
        jax.ShapeDtypeStruct((T, NOUT), F32),
        jax.ShapeDtypeStruct((NOUT, T), BF16),
        jax.ShapeDtypeStruct((8, T), F32),
    ]
    return pl.pallas_call(
        functools.partial(forward_kernel, layer),
        out_shape=shapes,
        in_specs=[VM, VM, VM, HBM, HBM, HBM, VM, HBM, HBM],
        out_specs=[VM, HBM, HBM, HBM, HBM, VM],
        scratch_shapes=[
            pltpu.VMEM((T, D), BF16),
            pltpu.VMEM((T, 384), BF16),
            pltpu.VMEM((T, NOUT), F32),
            pltpu.VMEM((T, NOUT), BF16),
            pltpu.VMEM((NOUT, T), BF16),
            pltpu.VMEM((BLK, WIN), F32),
            pltpu.VMEM((BLK, WIN), BF16),
            pltpu.VMEM((D, NIN), BF16),
            pltpu.VMEM((1, NIN), F32),
            pltpu.VMEM((NOUT, D), BF16),
            pltpu.VMEM((3, T, 128), F32),
            pltpu.VMEM((T, 128), jnp.int32),
            pltpu.SemaphoreType.DMA((16,)),
            pltpu.SemaphoreType.DMA((GATHER_SENDS + SCATTER_SENDS,)),
            *GATHER_SEMS,
            *SCATTER_SCRATCH,
        ],
        compiler_params=pltpu.CompilerParams(
            collective_id=layer, has_side_effects=True, vmem_limit_bytes=60 << 20
        ),
        name=f"forward_layer{layer}",
    )(x, gains[layer], shifts[layer], win, bias, wout, obias, tabs, first)


def backward_kernel(layer, dy_ref, x_ref, xh_h, qkv_h, ho_h, out_h, lse_ref, wint_h, wout_h, gains, shifts, tabs_h, first_ref,
                    aqkv_h, bqkv_h, ain_h, bin_h, aout_h, bout_h, adown_h, bdown_h,
                    o_dx, o_spread, o_norm, o_group, o_sums,
                    dy, xh, qkv, ho, out_t, dph, dph_t, acc, wint, wout, tabs, aqkv, bqkv, ain, bin_, aout, bout, adown, bdown,
                    load_sems, send_sems, g_direct, g_cross, *scat):
    me = Place()
    loads = Loads(load_sems)
    early = [
        loads.start(wout_h.at[layer], wout),
        loads.start(ho_h, ho),
        loads.start(qkv_h, qkv),
    ]
    late = [
        loads.start(tabs_h, tabs),
        loads.start(wint_h.at[layer], wint),
        loads.start(xh_h, xh),
        loads.start(out_h, out_t),
        loads.start(aqkv_h.at[layer], aqkv),
        loads.start(bqkv_h.at[layer], bqkv),
        loads.start(ain_h.at[layer], ain),
        loads.start(bin_h.at[layer], bin_),
        loads.start(aout_h.at[layer], aout),
        loads.start(bout_h.at[layer], bout),
        loads.start(adown_h.at[layer], adown),
        loads.start(bdown_h.at[layer], bdown),
    ]
    out = Sender(send_sems)
    me.meet()
    rows_of(dy, me.shard(0, 0, 0) * OWN, OWN)[...] = dy_ref[...].astype(BF16)
    acc[...] = jnp.zeros(acc.shape, F32)
    state = {"early": False}
    scale = HD**-0.5

    def pull(dz, dh):
        if not state["early"]:
            for copy in early:
                copy.wait()
            state["early"] = True
        b = me.block(dz, dh)
        at = pl.ds(pl.multiple_of(b * BLK, BLK), BLK)
        rows = dy[at, :]
        du = mm(rows, wout[128:NOUT, :], NT)
        h = ho[at, 128:NOUT]
        slope = gelu_parts(h) + h * (jnp.exp(-0.5 * h * h) * (2.0 * math.pi) ** -0.5)
        dph[at, NQ:NIN] = (slope * du).astype(BF16)
        do = mm(rows, wout[0:128, :], NT).astype(BF16)
        drop = jnp.sum((do.astype(F32) * ho[at, 0:128]).T, axis=0, keepdims=True)
        lse = lse_ref[0:1, at]
        start = first_ref[0:1, at]
        q = qkv[at, 0:128]
        key_at = jnp.maximum(b - 4, 0) * BLK
        col = b * BLK + lax.broadcasted_iota(jnp.int32, (BLK, BLK), 1)

        def step(j, dq):
            key = key_at + j * BLK
            keys = pl.ds(pl.multiple_of(key, BLK), BLK)
            k = qkv[keys, 128:256]
            s = mm(k, q, NT) * scale
            row = key + lax.broadcasted_iota(jnp.int32, (BLK, BLK), 0)
            p = jnp.where((row >= start) & (row <= col), jnp.exp(s - lse), 0.0)
            dp = mm(qkv[keys, 256:384], do, NT)
            ds = (p * (dp - drop)).astype(BF16)
            acc[keys, 256:384] += mm(p.astype(BF16), do)
            acc[keys, 128:256] += mm(ds, q)
            return dq + mm(ds, k, TN)

        acc[at, 0:128] = lax.fori_loop(0, 5, step, jnp.zeros((BLK, 128), F32))

    gather(me, out, dy, g_direct, g_cross, pull)
    for copy in late:
        copy.wait()

    def send_back(dz, dh, put):
        b = me.block(dz, dh)
        at = pl.ds(pl.multiple_of(b * BLK, BLK), BLK)
        g = (acc[at, 0:128] + lane_roll(acc[at, 128:256], HD)) * scale
        turned = g * tabs[0, at, :] + lane_roll(g * tabs[1, at, :], 8) + lane_roll(g * tabs[2, at, :], -8)
        dph[at, 0:128] = turned.astype(BF16)
        dph[at, 128:256] = acc[at, 256:384].astype(BF16)
        rows = dph[at, :]
        for dc in range(2):
            put(dc, mm(rows_of(dph, me.shard(dz, dh, dc) * OWN, OWN)[...], wint[...]))
        dph_t[:, at] = rows.astype(F32).T.astype(BF16)

    def factors():
        totals = jnp.sum(dph_t[...].astype(F32), axis=1, keepdims=True)
        o_sums[...] = jnp.broadcast_to(totals, (NIN, 128)).T[0:8, :]
        for row, at, width in ((0, 0, NQ), (1, NQ, FF)):
            here = pl.ds(at, width)
            grad = mm(dph_t[here, :], xh[...])
            weight = wint[here, :].astype(F32)
            total = totals[at:at + width]
            by_gain = jnp.sum(grad * weight, axis=0, keepdims=True)
            by_shift = jnp.sum(total * weight, axis=0, keepdims=True)
            g = gains[0:1, :]
            if row == 1:
                ratio = gains[1:2, :] / g
                by_gain, by_shift = by_gain / ratio, by_shift / ratio
                grad = grad * ratio + total * (shifts[1:2, :] - shifts[0:1, :] * ratio)
            o_norm[row:row + 1, :] = (by_gain - shifts[0:1, :] * by_shift) / g
            o_norm[2 + row:3 + row, :] = by_shift
            low = grad.astype(BF16)
            if row == 0:
                for j in range(3):
                    mine = low[j * HD:(j + 1) * HD]
                    o_spread[j * R:(j + 1) * R, :] = mm(bqkv[j * R:(j + 1) * R, :].astype(BF16), low)
                    o_group[j * HD:(j + 1) * HD, :] = mm(mine, aqkv[j].astype(BF16))
            else:
                o_spread[3 * R:4 * R, :] = mm(bin_[...].astype(BF16), low)
                o_group[256:512, :] = mm(low, ain[...].astype(BF16))
        low = mm(out_t[0:64, :], dy[...]).astype(BF16)
        o_spread[4 * R:5 * R, :] = mm(aout[...].astype(BF16), low, TN)
        o_group[192:256, :] = mm(low, bout[...].astype(BF16), NT)
        low = mm(out_t[128:NOUT, :], dy[...]).astype(BF16)
        o_spread[5 * R:6 * R, :] = mm(adown[...].astype(BF16), low, TN)
        o_group[512:768, :] = mm(low, bdown[...].astype(BF16), NT)
        o_norm[4:5, :] = jnp.sum(dy_ref[...], axis=0, keepdims=True)
        o_norm[5:8, :] = jnp.zeros((3, D), F32)

    def finish(at, rows, total):
        here = pl.ds(at, rows)
        hat, rstd = normalized(x_ref[here, :])
        total = total * gains[0:1, :]
        mean = jnp.mean(total, axis=1, keepdims=True)
        along = jnp.mean(total * hat, axis=1, keepdims=True)
        o_dx[here, :] = dy_ref[here, :] + rstd * (total - mean - hat * along)

    scatter(me, out, scat, send_back, factors, finish)
    out.finish()


def backward(layer, dy, x, saved, wint, wout, gains, shifts, tabs, first, factors):
    xh, qkv, ho, out_t, lse = saved
    shapes = [
        jax.ShapeDtypeStruct((OWN, D), F32),
        jax.ShapeDtypeStruct((6 * R, D), F32),
        jax.ShapeDtypeStruct((8, D), F32),
        jax.ShapeDtypeStruct((768, R), F32),
        jax.ShapeDtypeStruct((8, NIN), F32),
    ]
    return pl.pallas_call(
        functools.partial(backward_kernel, layer),
        out_shape=shapes,
        in_specs=[VM, VM, HBM, HBM, HBM, HBM, VM, HBM, HBM, VM, VM, HBM, VM] + [HBM] * 8,
        out_specs=[VM] * 5,
        scratch_shapes=[
            pltpu.VMEM((T, D), BF16),
            pltpu.VMEM((T, D), BF16),
            pltpu.VMEM((T, 384), BF16),
            pltpu.VMEM((T, NOUT), F32),
            pltpu.VMEM((NOUT, T), BF16),
            pltpu.VMEM((T, NIN), BF16),
            pltpu.VMEM((NIN, T), BF16),
            pltpu.VMEM((T, 384), F32),
            pltpu.VMEM((NIN, D), BF16),
            pltpu.VMEM((NOUT, D), BF16),
            pltpu.VMEM((3, T, 128), F32),
            pltpu.VMEM((3, D, R), F32),
            pltpu.VMEM((3 * R, NQ), F32),
            pltpu.VMEM((D, R), F32),
            pltpu.VMEM((R, FF), F32),
            pltpu.VMEM((64, R), F32),
            pltpu.VMEM((R, D), F32),
            pltpu.VMEM((FF, R), F32),
            pltpu.VMEM((R, D), F32),
            pltpu.SemaphoreType.DMA((16,)),
            pltpu.SemaphoreType.DMA((GATHER_SENDS + SCATTER_SENDS,)),
            *GATHER_SEMS,
            *SCATTER_SCRATCH,
        ],
        compiler_params=pltpu.CompilerParams(
            collective_id=LAYERS + layer, has_side_effects=True, vmem_limit_bytes=62 << 20
        ),
        name=f"backward_layer{layer}",
    )(dy, x, xh, qkv, ho, out_t, lse, wint, wout, gains[layer], shifts[layer], tabs, first, *factors)


def positions_of(lengths):
    ends = jnp.cumsum(lengths)
    starts = ends - lengths
    token = jnp.arange(T, dtype=jnp.int32)
    within = (token[:, None] >= starts[None, :]) & (token[:, None] < ends[None, :])
    first = jnp.sum(jnp.where(within, starts[None, :], 0), axis=1).astype(jnp.int32)
    return first, token - first


def rotary(pos):
    half = ROT // 2
    freq = jnp.exp(jnp.arange(0, ROT, 2, dtype=F32) * (-math.log(10000.0) / ROT))
    angle = pos.astype(F32)[:, None] * freq[None, :]
    cos, sin = jnp.cos(angle), jnp.sin(angle)
    none = jnp.zeros((T, HD - ROT), F32)
    zero = jnp.zeros_like(sin)
    tabs = [
        jnp.concatenate([cos, cos, none + 1.0], axis=1),
        jnp.concatenate([-sin, zero, none], axis=1),
        jnp.concatenate([zero, sin, none], axis=1),
    ]
    return jnp.stack([jnp.concatenate([t, t], axis=1) for t in tabs])


def body(x, dy, lengths, gain, shift, w_qkv, b_qkv, a_qkv, u_qkv, w_out, b_out, a_out, u_out,
         w_in, b_in, a_in, u_in, w_down, b_down, a_down, u_down):
    first, pos = positions_of(lengths[0])
    tabs = rotary(pos)
    first_wide = jnp.broadcast_to(first[:, None], (T, 128))
    first_row = jnp.broadcast_to(first[None, :], (8, T))
    wq = jnp.pad(w_qkv.reshape(LAYERS, D, 192), ((0, 0), (0, 0), (0, 64)))
    uq = jnp.zeros((LAYERS, 3, R, 4, HD), F32)
    for j in range(3):
        uq = uq.at[:, j, :, j].set(u_qkv[:, j])
    uq = uq.reshape(LAYERS, 3 * R, NQ)
    biases = jnp.concatenate([b_qkv.reshape(LAYERS, 192), jnp.zeros((LAYERS, 64), F32), b_in], axis=1)[:, None, :]
    win, wint, bias, wout = prep(wq, a_qkv, uq, w_in, a_in, u_in, w_out, a_out, u_out, w_down, a_down, u_down,
                                 gain, shift, biases)
    obias = (b_out + b_down)[:, None, :]
    kept = []
    stream = x
    for layer in range(LAYERS):
        nxt, *saved = forward(layer, stream, gain, shift, win, bias, wout, obias[layer], tabs, first_wide)
        kept.append((stream, saved))
        stream = nxt
    grad = dy
    spread, norm, group, sums = ([None] * LAYERS for _ in range(4))
    for layer in reversed(range(LAYERS)):
        layer_in, saved = kept[layer]
        grad, spread[layer], norm[layer], group[layer], sums[layer] = backward(
            layer, grad, layer_in, saved, wint, wout, gain, shift, tabs, first_row,
            (a_qkv, uq, a_in, u_in, a_out, u_out, a_down, u_down),
        )
    spread, norm = lax.psum((jnp.stack(spread).astype(BF16), jnp.stack(norm)), ALL)
    group, sums = lax.psum((jnp.stack(group), jnp.stack(sums)), DP)
    spread = spread.astype(F32).reshape(LAYERS, 6, R, D)
    g_aqkv = spread[:, 0:3].swapaxes(2, 3)
    g_ain = spread[:, 3].swapaxes(1, 2)
    g_bqkv = group[:, 0:192].reshape(LAYERS, 3, HD, R).swapaxes(2, 3)
    return (
        stream,
        grad,
        norm[:, 0:2],
        norm[:, 2:4],
        sums[:, 0, 0:192].reshape(LAYERS, 3, HD),
        g_aqkv,
        g_bqkv,
        norm[:, 4],
        group[:, 192:256],
        spread[:, 4],
        sums[:, 0, NQ:NIN],
        g_ain,
        group[:, 256:512].swapaxes(1, 2),
        norm[:, 4],
        group[:, 512:768],
        spread[:, 5],
    )


def solution(mesh):
    torus = Mesh(mesh.devices.reshape(2, 4, 4, 2, 2), ALL)
    return jax.shard_map(
        body,
        mesh=torus,
        in_specs=(
            P(ALL, None),
            P(ALL, None),
            P(DP, None),
            P(),
            P(),
            P(None, None, None, MP),
            P(None, None, MP),
            P(),
            P(None, None, None, MP),
            P(None, MP, None),
            P(),
            P(None, MP, None),
            P(),
            P(None, None, MP),
            P(None, MP),
            P(),
            P(None, None, MP),
            P(None, MP, None),
            P(),
            P(None, MP, None),
            P(),
        ),
        out_specs=(
            P(ALL, None),
            P(ALL, None),
            P(),
            P(),
            P(None, None, MP),
            P(),
            P(None, None, None, MP),
            P(),
            P(None, MP, None),
            P(),
            P(None, MP),
            P(),
            P(None, None, MP),
            P(),
            P(None, MP, None),
            P(),
        ),
        check_vma=False,
    )
```

```python
import functools
import math

import jax
import jax.numpy as jnp
from jax import lax
from jax.experimental import pallas as pl
from jax.experimental.pallas import tpu as pltpu
from jax.sharding import Mesh
from jax.sharding import PartitionSpec as P

HD = 64
ROT = 16
LAYERS = 2
EPS = 1e-05
FILL = -1000000000.0
MP = ("z", "yh", "c")
DP = ("yl", "x")
ALL = ("yl", "x", "z", "yh", "c")
MESH = pl.DeviceIdType.MESH

D = 1024
T = 2048
OWN = 128
BLK = 256
NB = T // BLK
WIN = 5 * BLK
NQ = 256
FF = 256
NIN = NQ + FF
NOUT = 128 + FF
R = 128
NCH = 2
F32 = jnp.float32
BF16 = jnp.bfloat16
HIGH = lax.Precision.HIGHEST

NN = (((1,), (0,)), ((), ()))
NT = (((1,), (1,)), ((), ()))
TN = (((0,), (0,)), ((), ()))


def mm(a, b, dims=NN, precision=None):
    return lax.dot_general(a, b, dims, precision=precision, preferred_element_type=F32)


def split_bf16(a):
    high = a.astype(BF16)
    return high, (a - high.astype(F32)).astype(BF16)


def mm3(a, b, dims=NN):
    ah, al = split_bf16(a)
    bh, bl = split_bf16(b)
    return mm(ah, bh, dims) + (mm(al, bh, dims) + mm(ah, bl, dims))


def rows_of(ref, start, count):
    return ref.at[pl.ds(start if isinstance(start, int) else pl.multiple_of(start, count), count)]


class Place:
    def __init__(self):
        self.z, self.h, self.c = (lax.axis_index(a) for a in MP)
        self.up = {"z": lax.rem(self.z + 1, 4)}
        self.dn = {"z": lax.rem(self.z + 3, 4)}
        self.yy = {"yh": 1 - self.h}
        self.sib = {"c": 1 - self.c}

    def block(self, dz, dh):
        return lax.rem(self.z + dz, 4) * 2 + (self.h if dh == 0 else 1 - self.h)

    def shard(self, dz, dh, dc):
        return self.block(dz, dh) * 2 + (self.c if dc == 0 else 1 - self.c)

    def meet(self):
        barrier = pltpu.get_barrier_semaphore()
        for peer in (self.up, self.dn, self.yy, self.sib):
            pl.semaphore_signal(barrier, inc=1, device_id=peer, device_id_type=MESH)
        pl.semaphore_wait(barrier, 4)


class Sender:
    def __init__(self, sems):
        self.sems = sems
        self.live = []

    def send(self, src, dst, peer, recv_sem):
        copy = pltpu.make_async_remote_copy(
            src_ref=src,
            dst_ref=dst,
            send_sem=self.sems.at[len(self.live)],
            recv_sem=recv_sem,
            device_id=peer,
            device_id_type=MESH,
        )
        copy.start()
        self.live.append(copy)

    def got(self, ref, sem, peer):
        pltpu.make_async_remote_copy(
            src_ref=ref,
            dst_ref=ref,
            send_sem=self.sems.at[0],
            recv_sem=sem,
            device_id=peer,
            device_id_type=MESH,
        ).wait_recv()

    def finish(self):
        for copy in self.live:
            copy.wait_send()


GATHER_SENDS = 16 * NCH
GATHER_SEMS = [pltpu.SemaphoreType.DMA((8 * NCH,)), pltpu.SemaphoreType.DMA((8 * NCH,))]


def gather(me, out, buf, direct, cross, compute):
    rows = OWN // NCH

    def part(dz, dh, dc, k):
        return rows_of(buf, me.shard(dz, dh, dc) * OWN + k * rows, rows)

    def sem(sems, dz, dh, k):
        return sems.at[(dz * 2 + dh) * NCH + k]

    def send(dz, dh, k, peer, there):
        sems, tz, th = there
        ref = part(dz, dh, 0, k)
        out.send(ref, ref, peer, sem(sems, tz, th, k))

    def got(dz, dh, k):
        out.got(part(dz, dh, 0, k), sem(direct, dz, dh, k), me.sib)

    def done(dz, dh):
        for k in range(NCH):
            out.got(part(dz, dh, 1, k), sem(cross, dz, dh, k), me.sib)
        compute(dz, dh)

    def pass_on(dz, dh, k):
        send(dz, dh, k, me.sib, (cross, dz, dh))

    for k in range(NCH):
        send(0, 0, k, me.yy, (direct, 0, 1))
        send(0, 0, k, me.up, (direct, 3, 0))
        send(0, 0, k, me.dn, (direct, 1, 0))
    for k in range(NCH):
        pass_on(0, 0, k)
    done(0, 0)
    for k in range(NCH):
        got(0, 1, k)
        send(0, 1, k, me.dn, (direct, 1, 1))
        got(3, 0, k)
        send(3, 0, k, me.up, (direct, 2, 0))
        send(0, 1, k, me.up, (direct, 3, 1))
        pass_on(0, 1, k)
        pass_on(3, 0, k)
        got(1, 0, k)
        pass_on(1, 0, k)
    done(0, 1)
    done(3, 0)
    done(1, 0)
    for k in range(NCH):
        got(1, 1, k)
        send(1, 1, k, me.dn, (direct, 2, 1))
        pass_on(1, 1, k)
    for k in range(NCH):
        got(3, 1, k)
        pass_on(3, 1, k)
        got(2, 0, k)
        pass_on(2, 0, k)
    done(1, 1)
    done(3, 1)
    done(2, 0)
    for k in range(NCH):
        got(2, 1, k)
        pass_on(2, 1, k)
    done(2, 1)


SCATTER_SENDS = 8 + 7 * NCH
SCATTER_SCRATCH = [
    pltpu.VMEM((8 * OWN, D), F32),
    pltpu.VMEM((8 * OWN, D), BF16),
    pltpu.VMEM((8 * OWN, D), BF16),
    pltpu.VMEM((8 * OWN, D), BF16),
    pltpu.VMEM((2 * OWN, D), BF16),
    pltpu.VMEM((4 * OWN, D), BF16),
    pltpu.VMEM((OWN, D), BF16),
    pltpu.SemaphoreType.DMA((8,)),
    pltpu.SemaphoreType.DMA((2 * NCH,)),
    pltpu.SemaphoreType.DMA((4 * NCH,)),
    pltpu.SemaphoreType.DMA((NCH,)),
]


def scatter(me, out, bufs, compute, between, finish):
    own, other, cross, sums, via, ring, last, s_cross, s_via, s_ring, s_last = bufs
    rows = OWN // NCH

    def give(dz, dh):
        i = dz * 2 + dh

        def put(dc, terms):
            if dc == 0:
                own[pl.ds(i * OWN, OWN), :] = terms
            else:
                other[pl.ds(i * OWN, OWN), :] = terms.astype(BF16)

        compute(dz, dh, put)
        out.send(
            rows_of(other, i * OWN, OWN),
            rows_of(cross, i * OWN, OWN),
            me.sib,
            s_cross.at[i],
        )

    def wait_cross(dz, dh):
        i = dz * 2 + dh
        out.got(rows_of(cross, i * OWN, OWN), s_cross.at[i], me.sib)

    def both(dz, dh, k):
        here = pl.ds((dz * 2 + dh) * OWN + k * rows, rows)
        return own[here, :] + cross[here, :].astype(F32)

    def arrived(buf, sems, i, k):
        ref = rows_of(buf, i * OWN + k * rows, rows)
        out.got(ref, sems.at[i * NCH + k], me.sib)
        return ref[...].astype(F32)

    def pass_to(dz, dh, k, value, buf, sems, i, peer):
        at = (dz * 2 + dh) * OWN + k * rows
        sums[pl.ds(at, rows), :] = value.astype(BF16)
        out.send(
            rows_of(sums, at, rows),
            rows_of(buf, i * OWN + k * rows, rows),
            peer,
            sems.at[i * NCH + k],
        )

    chunks = range(NCH)
    give(2, 0)
    give(2, 1)
    wait_cross(2, 0)
    for k in chunks:
        pass_to(2, 0, k, both(2, 0, k), via, s_via, 0, me.up)
    wait_cross(2, 1)
    for k in chunks:
        pass_to(2, 1, k, both(2, 1, k), via, s_via, 1, me.dn)
    give(1, 1)
    give(3, 0)
    wait_cross(1, 1)
    for k in chunks:
        pass_to(1, 1, k, both(1, 1, k), ring, s_ring, 1, me.up)
    wait_cross(3, 0)
    for k in chunks:
        pass_to(3, 0, k, both(3, 0, k), ring, s_ring, 2, me.dn)
    give(1, 0)
    give(3, 1)
    wait_cross(3, 1)
    wait_cross(1, 0)
    for k in chunks:
        pass_to(3, 1, k, both(3, 1, k) + arrived(via, s_via, 1, k), ring, s_ring, 3, me.dn)
        pass_to(1, 0, k, both(1, 0, k) + arrived(via, s_via, 0, k), ring, s_ring, 0, me.up)
    give(0, 1)
    give(0, 0)
    between()
    wait_cross(0, 1)
    for k in chunks:
        total = both(0, 1, k) + arrived(ring, s_ring, 1, k) + arrived(ring, s_ring, 3, k)
        pass_to(0, 1, k, total, last, s_last, 0, me.yy)
    wait_cross(0, 0)
    for k in chunks:
        total = both(0, 0, k) + arrived(ring, s_ring, 0, k) + arrived(ring, s_ring, 2, k)
        finish(k * rows, rows, total + arrived(last, s_last, 0, k))


def gelu_parts(h):
    cdf = 0.5 * (1.0 + lax.erf(h * (2.0**-0.5)))
    return cdf


def prep_kernel(wqkv, aqkv, bqkv, win_, ain, bin_, wout_, aout, bout, wdown, adown, bdown, gains, shifts, biases,
                o_win, o_wint, o_bias, o_wout):
    ratio = gains[1:2, :] / gains[0:1, :]
    ab = mm3(aqkv[0], bqkv[0:R]) + mm3(aqkv[1], bqkv[R:2 * R]) + mm3(aqkv[2], bqkv[2 * R:])
    low = (wqkv[...].astype(F32) + ab).astype(BF16)
    o_win[:, 0:NQ] = low
    o_wint[0:NQ, :] = low.T
    o_bias[:, 0:NQ] = biases[:, 0:NQ]
    merged = win_[...].astype(F32) + mm3(ain[...], bin_[...])
    low = merged.astype(BF16)
    b_high, b_low = split_bf16(jnp.broadcast_to(shifts[1:2, :] - shifts[0:1, :] * ratio, (8, D)))
    shift = (mm(b_high, low) + mm(b_low, low))[0:1]
    o_bias[:, NQ:NIN] = biases[:, NQ:NIN] + shift
    turned = (merged.T * ratio).astype(BF16)
    o_wint[NQ:NIN, :] = turned
    o_win[:, NQ:NIN] = turned.T
    o_wout[0:64, :] = (wout_[...].astype(F32) + mm3(aout[...], bout[...])).astype(BF16)
    o_wout[64:128, :] = jnp.zeros((64, D), BF16)
    o_wout[128:NOUT, :] = (wdown[...].astype(F32) + mm3(adown[...], bdown[...])).astype(BF16)


def prep(wqkv, aqkv, bqkv, win_, ain, bin_, wout_, aout, bout, wdown, adown, bdown, gains, shifts, biases):
    ins = (wqkv, aqkv, bqkv, win_, ain, bin_, wout_, aout, bout, wdown, adown, bdown, gains, shifts, biases)

    def spec(a):
        rank = a.ndim - 1
        return pl.BlockSpec((None, *a.shape[1:]), lambda l: (l,) + (0,) * rank)

    outs = [
        jax.ShapeDtypeStruct((LAYERS, D, NIN), BF16),
        jax.ShapeDtypeStruct((LAYERS, NIN, D), BF16),
        jax.ShapeDtypeStruct((LAYERS, 1, NIN), F32),
        jax.ShapeDtypeStruct((LAYERS, NOUT, D), BF16),
    ]
    return pl.pallas_call(
        prep_kernel,
        grid=(LAYERS,),
        out_shape=outs,
        in_specs=[spec(a) for a in ins],
        out_specs=[spec(a) for a in outs],
        compiler_params=pltpu.CompilerParams(vmem_limit_bytes=48 << 20),
        name="prep",
    )(*ins)


def lane_roll(a, shift):
    return pltpu.roll(a, shift % 128, 1)


def normalized(x):
    mean = jnp.mean(x, axis=1, keepdims=True)
    centered = x - mean
    scale = lax.rsqrt(jnp.mean(centered * centered, axis=1, keepdims=True) + EPS)
    return centered * scale, scale


class Loads:
    def __init__(self, sems):
        self.sems = sems
        self.count = 0

    def start(self, src, dst):
        copy = pltpu.make_async_copy(src, dst, self.sems.at[self.count])
        self.count += 1
        copy.start()
        return copy


def forward_kernel(layer, x_ref, gains, shifts, win_h, bias_h, wout_h, obias, tabs_h, first_h,
                   o_x, o_xh, o_qkv, o_ho, o_out, o_lse,
                   xh, qkv, ho, ou, out_t, scores, probs, win, bias, wout, tabs, first,
                   load_sems, send_sems, g_direct, g_cross, *scat):
    me = Place()
    loads = Loads(load_sems)
    ins = [
        loads.start(win_h.at[layer], win),
        loads.start(bias_h.at[layer], bias),
        loads.start(tabs_h, tabs),
        loads.start(first_h, first),
        loads.start(wout_h.at[layer], wout),
    ]
    out = Sender(send_sems)
    me.meet()
    x = x_ref[...]
    rows_of(xh, me.shard(0, 0, 0) * OWN, OWN)[...] = (
        normalized(x)[0] * gains[0:1, :] + shifts[0:1, :]
    ).astype(BF16)
    state = {"loaded": False}

    def project(dz, dh):
        if not state["loaded"]:
            for copy in ins:
                copy.wait()
            state["loaded"] = True
        at = pl.ds(pl.multiple_of(me.block(dz, dh) * BLK, BLK), BLK)
        rows = xh[at, :]
        pq = mm(rows, win[:, 0:NQ]) + bias[:, 0:NQ]
        qk = pq[:, 0:128]
        turned = qk * tabs[0, at, :] + lane_roll(qk, -8) * tabs[1, at, :] + lane_roll(qk, 8) * tabs[2, at, :]
        lane = lax.broadcasted_iota(jnp.int32, (BLK, 128), 1)
        qkv[at, 0:128] = jnp.where(lane < HD, turned, 0.0).astype(BF16)
        qkv[at, 128:256] = jnp.where(lane < HD, lane_roll(turned, HD), 0.0).astype(BF16)
        qkv[at, 256:384] = pq[:, 128:256].astype(BF16)
        h = mm(rows, win[:, NQ:NIN]) + bias[:, NQ:NIN]
        ho[at, 128:NOUT] = h
        ou[at, 128:NOUT] = (h * gelu_parts(h)).astype(BF16)

    gather(me, out, xh, g_direct, g_cross, project)
    outs = [loads.start(xh, o_xh), loads.start(qkv, o_qkv)]

    def attend(dz, dh, put):
        b = me.block(dz, dh)
        at = pl.ds(pl.multiple_of(b * BLK, BLK), BLK)
        key_at = jnp.maximum(b - 4, 0) * BLK
        q = qkv[at, 0:128]
        row = b * BLK + lax.broadcasted_iota(jnp.int32, (BLK, BLK), 0)
        start = jnp.concatenate([first[at, :], first[at, :]], axis=1)
        peak = None
        for j in range(5):
            keys = pl.ds(pl.multiple_of(key_at + j * BLK, BLK), BLK)
            s = mm(q, qkv[keys, 128:256], NT) * (HD**-0.5)
            col = key_at + j * BLK + lax.broadcasted_iota(jnp.int32, (BLK, BLK), 1)
            s = jnp.where((col >= start) & (col <= row), s, FILL)
            scores[:, j * BLK:(j + 1) * BLK] = s
            peak = s if peak is None else jnp.maximum(peak, s)
        peak = jnp.max(peak, axis=1, keepdims=True)
        summed = None
        for j in range(5):
            p = jnp.exp(scores[:, j * BLK:(j + 1) * BLK] - peak)
            scores[:, j * BLK:(j + 1) * BLK] = p
            summed = p if summed is None else summed + p
        summed = jnp.sum(summed, axis=1, keepdims=True)
        share = 1.0 / summed
        for j in range(5):
            here = slice(j * BLK, (j + 1) * BLK)
            probs[:, here] = (scores[:, here] * share).astype(BF16)
        o = mm(probs[...], qkv[pl.ds(pl.multiple_of(key_at, BLK), WIN), 256:384])
        ho[at, 0:128] = o
        ou[at, 0:128] = o.astype(BF16)
        lse = jnp.broadcast_to(peak + jnp.log(summed), (BLK, 128)).T
        o_lse[:, at] = lse[0:8, :]
        out_t[:, at] = ou[at, :].astype(F32).T.astype(BF16)
        for dc in range(2):
            put(dc, mm(rows_of(ou, me.shard(dz, dh, dc) * OWN, OWN)[...], wout[...]))

    def between():
        outs.append(loads.start(ho, o_ho))
        outs.append(loads.start(out_t, o_out))

    def finish(at, rows, total):
        here = pl.ds(at, rows)
        o_x[here, :] = x_ref[here, :] + total + obias[...]

    scatter(me, out, scat, attend, between, finish)
    for copy in outs:
        copy.wait()
    out.finish()


VM = pl.BlockSpec(memory_space=pltpu.VMEM)
HBM = pl.BlockSpec(memory_space=pl.ANY)


def forward(layer, x, gains, shifts, win, bias, wout, obias, tabs, first):
    shapes = [
        jax.ShapeDtypeStruct((OWN, D), F32),
        jax.ShapeDtypeStruct((T, D), BF16),
        jax.ShapeDtypeStruct((T, 384), BF16),
        jax.ShapeDtypeStruct((T, NOUT), F32),
        jax.ShapeDtypeStruct((NOUT, T), BF16),
        jax.ShapeDtypeStruct((8, T), F32),
    ]
    return pl.pallas_call(
        functools.partial(forward_kernel, layer),
        out_shape=shapes,
        in_specs=[VM, VM, VM, HBM, HBM, HBM, VM, HBM, HBM],
        out_specs=[VM, HBM, HBM, HBM, HBM, VM],
        scratch_shapes=[
            pltpu.VMEM((T, D), BF16),
            pltpu.VMEM((T, 384), BF16),
            pltpu.VMEM((T, NOUT), F32),
            pltpu.VMEM((T, NOUT), BF16),
            pltpu.VMEM((NOUT, T), BF16),
            pltpu.VMEM((BLK, WIN), F32),
            pltpu.VMEM((BLK, WIN), BF16),
            pltpu.VMEM((D, NIN), BF16),
            pltpu.VMEM((1, NIN), F32),
            pltpu.VMEM((NOUT, D), BF16),
            pltpu.VMEM((3, T, 128), F32),
            pltpu.VMEM((T, 128), jnp.int32),
            pltpu.SemaphoreType.DMA((16,)),
            pltpu.SemaphoreType.DMA((GATHER_SENDS + SCATTER_SENDS,)),
            *GATHER_SEMS,
            *SCATTER_SCRATCH,
        ],
        compiler_params=pltpu.CompilerParams(
            collective_id=layer, has_side_effects=True, vmem_limit_bytes=60 << 20
        ),
        name=f"forward_layer{layer}",
    )(x, gains[layer], shifts[layer], win, bias, wout, obias, tabs, first)


def backward_kernel(layer, dy_ref, x_ref, xh_h, qkv_h, ho_h, out_h, lse_ref, wint_h, wout_h, gains, shifts, tabs_h, first_ref,
                    aqkv_h, bqkv_h, ain_h, bin_h, aout_h, bout_h, adown_h, bdown_h,
                    o_dx, o_spread, o_norm, o_group, o_sums,
                    dy, xh, qkv, ho, out_t, dph, dph_t, acc, wint, wout, tabs, aqkv, bqkv, ain, bin_, aout, bout, adown, bdown,
                    load_sems, send_sems, g_direct, g_cross, *scat):
    me = Place()
    loads = Loads(load_sems)
    early = [
        loads.start(wout_h.at[layer], wout),
        loads.start(ho_h, ho),
        loads.start(qkv_h, qkv),
    ]
    late = [
        loads.start(tabs_h, tabs),
        loads.start(wint_h.at[layer], wint),
        loads.start(xh_h, xh),
        loads.start(out_h, out_t),
        loads.start(aqkv_h.at[layer], aqkv),
        loads.start(bqkv_h.at[layer], bqkv),
        loads.start(ain_h.at[layer], ain),
        loads.start(bin_h.at[layer], bin_),
        loads.start(aout_h.at[layer], aout),
        loads.start(bout_h.at[layer], bout),
        loads.start(adown_h.at[layer], adown),
        loads.start(bdown_h.at[layer], bdown),
    ]
    out = Sender(send_sems)
    me.meet()
    rows_of(dy, me.shard(0, 0, 0) * OWN, OWN)[...] = dy_ref[...].astype(BF16)
    acc[...] = jnp.zeros(acc.shape, F32)
    state = {"early": False}
    scale = HD**-0.5

    def pull(dz, dh):
        if not state["early"]:
            for copy in early:
                copy.wait()
            state["early"] = True
        b = me.block(dz, dh)
        at = pl.ds(pl.multiple_of(b * BLK, BLK), BLK)
        rows = dy[at, :]
        du = mm(rows, wout[128:NOUT, :], NT)
        h = ho[at, 128:NOUT]
        slope = gelu_parts(h) + h * (jnp.exp(-0.5 * h * h) * (2.0 * math.pi) ** -0.5)
        dph[at, NQ:NIN] = (slope * du).astype(BF16)
        do = mm(rows, wout[0:128, :], NT).astype(BF16)
        drop = jnp.sum((do.astype(F32) * ho[at, 0:128]).T, axis=0, keepdims=True)
        lse = lse_ref[0:1, at]
        start = first_ref[0:1, at]
        q = qkv[at, 0:128]
        key_at = jnp.maximum(b - 4, 0) * BLK
        col = b * BLK + lax.broadcasted_iota(jnp.int32, (BLK, BLK), 1)

        def step(j, dq):
            key = key_at + j * BLK
            keys = pl.ds(pl.multiple_of(key, BLK), BLK)
            k = qkv[keys, 128:256]
            s = mm(k, q, NT) * scale
            row = key + lax.broadcasted_iota(jnp.int32, (BLK, BLK), 0)
            p = jnp.where((row >= start) & (row <= col), jnp.exp(s - lse), 0.0)
            dp = mm(qkv[keys, 256:384], do, NT)
            ds = (p * (dp - drop)).astype(BF16)
            acc[keys, 256:384] += mm(p.astype(BF16), do)
            acc[keys, 128:256] += mm(ds, q)
            return dq + mm(ds, k, TN)

        acc[at, 0:128] = lax.fori_loop(0, 5, step, jnp.zeros((BLK, 128), F32))

    gather(me, out, dy, g_direct, g_cross, pull)
    for copy in late:
        copy.wait()

    def send_back(dz, dh, put):
        b = me.block(dz, dh)
        at = pl.ds(pl.multiple_of(b * BLK, BLK), BLK)
        g = (acc[at, 0:128] + lane_roll(acc[at, 128:256], HD)) * scale
        turned = g * tabs[0, at, :] + lane_roll(g * tabs[1, at, :], 8) + lane_roll(g * tabs[2, at, :], -8)
        dph[at, 0:128] = turned.astype(BF16)
        dph[at, 128:256] = acc[at, 256:384].astype(BF16)
        rows = dph[at, :]
        for dc in range(2):
            put(dc, mm(rows_of(dph, me.shard(dz, dh, dc) * OWN, OWN)[...], wint[...]))
        dph_t[:, at] = rows.astype(F32).T.astype(BF16)

    def factors():
        totals = jnp.sum(dph_t[...].astype(F32), axis=1, keepdims=True)
        o_sums[...] = jnp.broadcast_to(totals, (NIN, 128)).T[0:8, :]
        for row, at, width in ((0, 0, NQ), (1, NQ, FF)):
            here = pl.ds(at, width)
            grad = mm(dph_t[here, :], xh[...])
            weight = wint[here, :].astype(F32)
            total = totals[at:at + width]
            by_gain = jnp.sum(grad * weight, axis=0, keepdims=True)
            by_shift = jnp.sum(total * weight, axis=0, keepdims=True)
            g = gains[0:1, :]
            if row == 1:
                ratio = gains[1:2, :] / g
                by_gain, by_shift = by_gain / ratio, by_shift / ratio
                grad = grad * ratio + total * (shifts[1:2, :] - shifts[0:1, :] * ratio)
            o_norm[row:row + 1, :] = (by_gain - shifts[0:1, :] * by_shift) / g
            o_norm[2 + row:3 + row, :] = by_shift
            low = grad.astype(BF16)
            if row == 0:
                for j in range(3):
                    mine = low[j * HD:(j + 1) * HD]
                    o_spread[j * R:(j + 1) * R, :] = mm(bqkv[j * R:(j + 1) * R, :].astype(BF16), low)
                    o_group[j * HD:(j + 1) * HD, :] = mm(mine, aqkv[j].astype(BF16))
            else:
                o_spread[3 * R:4 * R, :] = mm(bin_[...].astype(BF16), low)
                o_group[256:512, :] = mm(low, ain[...].astype(BF16))
        low = mm(out_t[0:64, :], dy[...]).astype(BF16)
        o_spread[4 * R:5 * R, :] = mm(aout[...].astype(BF16), low, TN)
        o_group[192:256, :] = mm(low, bout[...].astype(BF16), NT)
        low = mm(out_t[128:NOUT, :], dy[...]).astype(BF16)
        o_spread[5 * R:6 * R, :] = mm(adown[...].astype(BF16), low, TN)
        o_group[512:768, :] = mm(low, bdown[...].astype(BF16), NT)
        o_norm[4:5, :] = jnp.sum(dy_ref[...], axis=0, keepdims=True)
        o_norm[5:8, :] = jnp.zeros((3, D), F32)

    def finish(at, rows, total):
        here = pl.ds(at, rows)
        hat, rstd = normalized(x_ref[here, :])
        total = total * gains[0:1, :]
        mean = jnp.mean(total, axis=1, keepdims=True)
        along = jnp.mean(total * hat, axis=1, keepdims=True)
        o_dx[here, :] = dy_ref[here, :] + rstd * (total - mean - hat * along)

    scatter(me, out, scat, send_back, factors, finish)
    out.finish()


def backward(layer, dy, x, saved, wint, wout, gains, shifts, tabs, first, factors):
    xh, qkv, ho, out_t, lse = saved
    shapes = [
        jax.ShapeDtypeStruct((OWN, D), F32),
        jax.ShapeDtypeStruct((6 * R, D), F32),
        jax.ShapeDtypeStruct((8, D), F32),
        jax.ShapeDtypeStruct((768, R), F32),
        jax.ShapeDtypeStruct((8, NIN), F32),
    ]
    return pl.pallas_call(
        functools.partial(backward_kernel, layer),
        out_shape=shapes,
        in_specs=[VM, VM, HBM, HBM, HBM, HBM, VM, HBM, HBM, VM, VM, HBM, VM] + [HBM] * 8,
        out_specs=[VM] * 5,
        scratch_shapes=[
            pltpu.VMEM((T, D), BF16),
            pltpu.VMEM((T, D), BF16),
            pltpu.VMEM((T, 384), BF16),
            pltpu.VMEM((T, NOUT), F32),
            pltpu.VMEM((NOUT, T), BF16),
            pltpu.VMEM((T, NIN), BF16),
            pltpu.VMEM((NIN, T), BF16),
            pltpu.VMEM((T, 384), F32),
            pltpu.VMEM((NIN, D), BF16),
            pltpu.VMEM((NOUT, D), BF16),
            pltpu.VMEM((3, T, 128), F32),
            pltpu.VMEM((3, D, R), F32),
            pltpu.VMEM((3 * R, NQ), F32),
            pltpu.VMEM((D, R), F32),
            pltpu.VMEM((R, FF), F32),
            pltpu.VMEM((64, R), F32),
            pltpu.VMEM((R, D), F32),
            pltpu.VMEM((FF, R), F32),
            pltpu.VMEM((R, D), F32),
            pltpu.SemaphoreType.DMA((16,)),
            pltpu.SemaphoreType.DMA((GATHER_SENDS + SCATTER_SENDS,)),
            *GATHER_SEMS,
            *SCATTER_SCRATCH,
        ],
        compiler_params=pltpu.CompilerParams(
            collective_id=LAYERS + layer, has_side_effects=True, vmem_limit_bytes=62 << 20
        ),
        name=f"backward_layer{layer}",
    )(dy, x, xh, qkv, ho, out_t, lse, wint, wout, gains[layer], shifts[layer], tabs, first, *factors)


QUARTER = 768 // 4
GROUP = 400


def total_kernel(spread_a, spread_b, norm_a, norm_b, group_a, group_b, sums_a, sums_b, o_spread, o_norm, o_group,
                 other, cross, low, slots1, acc1, low2, slots2, acc2, low3, slots3, g3, g2,
                 n_first, n_slots, g_own, g_low, g_slots, g_pair,
                 send_sems, s_cross, s_one, s_two, s_three, s_back3, s_back2, s_back1, s_backc,
                 s_norm, s_group):
    yl, x, z, yh, c = (lax.axis_index(a) for a in ALL)
    y = yh * 2 + yl
    sib = {"c": 1 - c}

    def along(axis, d):
        return {axis: lax.rem((x if axis == "x" else z) + d, 4)}

    def y_peer(d):
        there = lax.rem(y + d, 4)
        return {"yh": there // 2, "yl": lax.rem(there, 2)}

    barrier = pltpu.get_barrier_semaphore()
    peers = [sib] + [along(a, d) for a in ("x", "z") for d in (1, 2, 3)] + [y_peer(1), y_peer(2), y_peer(3)]
    for peer in peers:
        pl.semaphore_signal(barrier, inc=1, device_id=peer, device_id_type=MESH)
    pl.semaphore_wait(barrier, len(peers))

    out = Sender(send_sems)
    mine = pl.ds(pl.multiple_of(c * 512, 512), 512)
    theirs = pl.ds(pl.multiple_of((1 - c) * 512, 512), 512)
    paths = ((0, spread_a, "x", "z"), (1, spread_b, "z", "x"))
    here = {"x": x, "z": z}

    def quarter(axis, d, size):
        return pl.multiple_of(lax.rem(here[axis] + d, 4) * size, size)

    def rows(ref, start, size):
        return ref.at[pl.ds(start, size)]

    for d in (2, 1, 3, 0):
        for p, ref, axis, _ in paths:
            at = quarter(axis, d, QUARTER)
            to = pl.multiple_of(p * 768 + at, 64)
            other[pl.ds(to, QUARTER), :] = ref[pl.ds(at, QUARTER), theirs].astype(BF16)
            out.send(rows(other, to, QUARTER), rows(cross, to, QUARTER), sib, s_cross.at[p * 4 + d])
    n_first[0, 0:8, :] = norm_a[:, theirs]
    n_first[0, 8:16, :] = norm_b[:, theirs]
    out.send(n_first.at[0], n_first.at[1], sib, s_norm.at[0])
    for i in range(4):
        ref, sums = (group_a, sums_a) if i < 2 else (group_b, sums_b)
        g_own[i * GROUP:i * GROUP + 384, :] = ref[(i % 2) * 384:(i % 2) * 384 + 384, :]
        g_own[i * GROUP + 384:i * GROUP + 392, :] = sums[:, (i % 2) * 256:(i % 2) * 256 + 128]
        g_own[i * GROUP + 392:i * GROUP + 400, :] = sums[:, (i % 2) * 256 + 128:(i % 2) * 256 + 256]
    g_low[...] = g_own[...].astype(BF16)
    for d in (2, 1, 3):
        at = quarter("x", d, GROUP)
        out.send(rows(g_low, at, GROUP), g_slots.at[d - 1], along("x", d), s_group.at[d - 1])
    for d in (2, 1, 3, 0):
        for p, ref, axis, _ in paths:
            at = quarter(axis, d, QUARTER)
            to = pl.multiple_of(p * 768 + at, 64)
            out.got(rows(cross, to, QUARTER), s_cross.at[p * 4 + d], sib)
            both = ref[pl.ds(at, QUARTER), mine] + cross[pl.ds(to, QUARTER), :].astype(F32)
            if d == 0:
                acc1[p] = both
            else:
                low[pl.ds(to, QUARTER), :] = both.astype(BF16)
                out.send(rows(low, to, QUARTER), slots1.at[p * 3 + d - 1], along(axis, d), s_one.at[p * 3 + d - 1])
    out.got(n_first.at[1], s_norm.at[0], sib)

    def n_stage(stage, value, index, peer_of, base):
        own = n_slots.at[stage * 4 + index]
        own[...] = value
        for d in (1, 2, 3):
            out.send(own, own, peer_of(d), s_norm.at[base + d - 1])

    def n_sum(stage, index, base):
        for d in (1, 2, 3):
            out.got(n_slots.at[stage * 4 + lax.rem(index + 4 - d, 4)], s_norm.at[base + d - 1], sib)
        return (n_slots[stage * 4] + n_slots[stage * 4 + 1]) + (n_slots[stage * 4 + 2] + n_slots[stage * 4 + 3])

    first = jnp.concatenate([norm_a[:, mine], norm_b[:, mine]], axis=0) + n_first[1]
    n_stage(0, first, x, lambda d: along("x", d), 1)
    total = g_own[pl.ds(quarter("x", 0, GROUP), GROUP), :]
    for d in (1, 2, 3):
        out.got(g_slots.at[d - 1], s_group.at[d - 1], sib)
        total = total + g_slots[d - 1].astype(F32)
    g_pair[0] = total.astype(BF16)
    out.send(g_pair.at[0], g_pair.at[1], {"yl": 1 - yl}, s_group.at[3])
    for p, _, axis, second in paths:
        for d in (1, 2, 3):
            out.got(slots1.at[p * 3 + d - 1], s_one.at[p * 3 + d - 1], sib)
            acc1[p] += slots1[p * 3 + d - 1].astype(F32)
        low2[p] = acc1[p].astype(BF16)
        for d in (2, 1, 3):
            at = quarter(second, d, 48)
            out.send(
                low2.at[p, pl.ds(at, 48)], slots2.at[p * 3 + d - 1], along(second, d), s_two.at[p * 3 + d - 1]
            )
    n_stage(1, n_sum(0, x, 1), z, lambda d: along("z", d), 4)
    out.got(g_pair.at[1], s_group.at[3], sib)
    at = quarter("x", 0, GROUP)
    o_group[pl.ds(at, GROUP), :] = (g_pair[0].astype(F32) + g_pair[1].astype(F32)).astype(BF16)
    for d in (1, 2, 3):
        out.send(rows(o_group, at, GROUP), rows(o_group, at, GROUP), along("x", d), s_group.at[3 + d])
    for p, _, axis, second in paths:
        total = acc1[p, pl.ds(quarter(second, 0, 48), 48), :]
        for d in (1, 2, 3):
            out.got(slots2.at[p * 3 + d - 1], s_two.at[p * 3 + d - 1], sib)
            total = total + slots2[p * 3 + d - 1].astype(F32)
        acc2[p * 48:p * 48 + 48, :] = total
    low3[...] = acc2[...].astype(BF16)

    def y_lanes(d):
        return pl.ds(pl.multiple_of(lax.rem(y + d, 4) * 128, 128), 128)

    for d in (2, 1, 3):
        out.send(low3.at[:, y_lanes(d)], slots3.at[d - 1], y_peer(d), s_three.at[d - 1])
    n_stage(2, n_sum(1, z, 4), y, y_peer, 7)
    total = acc2[:, y_lanes(0)]
    for d in (1, 2, 3):
        out.got(slots3.at[d - 1], s_three.at[d - 1], sib)
        total = total + slots3[d - 1].astype(F32)
    g3[:, y_lanes(0)] = total.astype(BF16)
    for d in (2, 1, 3):
        out.send(g3.at[:, y_lanes(0)], g3.at[:, y_lanes(0)], y_peer(d), s_back3.at[d - 1])
    o_norm[:, mine] = n_sum(2, y, 7)
    out.send(o_norm.at[:, mine], o_norm.at[:, mine], sib, s_norm.at[10])
    for d in (1, 2, 3):
        out.got(g3.at[:, y_lanes(4 - d)], s_back3.at[d - 1], sib)
    for p, _, axis, second in paths:
        at = quarter(second, 0, 48)
        g2[p, pl.ds(at, 48), :] = g3[p * 48:p * 48 + 48, :]
        for d in (2, 1, 3):
            ref = g2.at[p, pl.ds(at, 48)]
            out.send(ref, ref, along(second, d), s_back2.at[p * 3 + d - 1])
    for p, _, axis, second in paths:
        for d in (1, 2, 3):
            out.got(g2.at[p, pl.ds(quarter(second, 4 - d, 48), 48)], s_back2.at[p * 3 + d - 1], sib)
        to = pl.multiple_of(p * 768 + quarter(axis, 0, QUARTER), 64)
        o_spread[pl.ds(to, QUARTER), mine] = g2[p]
        ref = o_spread.at[pl.ds(to, QUARTER), mine]
        for d in (2, 1, 3):
            out.send(ref, ref, along(axis, d), s_back1.at[p * 3 + d - 1])
        out.send(ref, ref, sib, s_backc.at[p * 4])
    for d in (1, 3, 2):
        for p, _, axis, second in paths:
            to = pl.multiple_of(p * 768 + quarter(axis, 4 - d, QUARTER), 64)
            ref = o_spread.at[pl.ds(to, QUARTER), mine]
            out.got(ref, s_back1.at[p * 3 + d - 1], sib)
            out.send(ref, ref, sib, s_backc.at[p * 4 + d])
    for d in (1, 2, 3):
        out.got(rows(o_group, quarter("x", 4 - d, GROUP), GROUP), s_group.at[3 + d], sib)
    out.got(o_norm.at[:, theirs], s_norm.at[10], sib)
    for d in (0, 1, 3, 2):
        for p, _, axis, second in paths:
            to = pl.multiple_of(p * 768 + quarter(axis, 4 - d, QUARTER), 64)
            out.got(o_spread.at[pl.ds(to, QUARTER), theirs], s_backc.at[p * 4 + d], sib)
    out.finish()


TOTAL_SENDS = 8 + 1 + 3 + 6 + 3 + 1 + 6 + 3 + 3 + 3 + 3 + 3 + 1 + 6 + 8 + 6


def total_over_devices(spread, norm, group, sums):
    dma = pltpu.SemaphoreType.DMA
    return pl.pallas_call(
        total_kernel,
        out_shape=[
            jax.ShapeDtypeStruct((1536, D), BF16),
            jax.ShapeDtypeStruct((16, D), F32),
            jax.ShapeDtypeStruct((4 * GROUP, R), BF16),
        ],
        in_specs=[VM] * 8,
        out_specs=[VM] * 3,
        scratch_shapes=[
            pltpu.VMEM((1536, 512), BF16),
            pltpu.VMEM((1536, 512), BF16),
            pltpu.VMEM((1536, 512), BF16),
            pltpu.VMEM((6, QUARTER, 512), BF16),
            pltpu.VMEM((2, QUARTER, 512), F32),
            pltpu.VMEM((2, QUARTER, 512), BF16),
            pltpu.VMEM((6, 48, 512), BF16),
            pltpu.VMEM((96, 512), F32),
            pltpu.VMEM((96, 512), BF16),
            pltpu.VMEM((3, 96, 128), BF16),
            pltpu.VMEM((96, 512), BF16),
            pltpu.VMEM((2, QUARTER, 512), BF16),
            pltpu.VMEM((2, 16, 512), F32),
            pltpu.VMEM((12, 16, 512), F32),
            pltpu.VMEM((4 * GROUP, R), F32),
            pltpu.VMEM((4 * GROUP, R), BF16),
            pltpu.VMEM((3, GROUP, R), BF16),
            pltpu.VMEM((2, GROUP, R), BF16),
            dma((TOTAL_SENDS,)),
            dma((8,)),
            dma((6,)),
            dma((6,)),
            dma((3,)),
            dma((3,)),
            dma((6,)),
            dma((6,)),
            dma((8,)),
            dma((11,)),
            dma((7,)),
        ],
        compiler_params=pltpu.CompilerParams(
            collective_id=2 * LAYERS, has_side_effects=True, vmem_limit_bytes=48 << 20
        ),
        name="total_over_devices",
    )(*spread, *norm, *group, *sums)


def unpack_kernel(spread, norm, group, o_gain, o_shift, o_bqkv, o_aqkv, o_uqkv, o_bout, o_aout, o_uout, o_bin, o_ain, o_uin,
                  o_bdown, o_adown, o_udown):
    layer = pl.program_id(0)
    for j in range(3):
        o_aqkv[j] = spread[j * R:(j + 1) * R, :].astype(F32).T
    o_ain[...] = spread[3 * R:4 * R, :].astype(F32).T
    o_uout[...] = spread[4 * R:5 * R, :].astype(F32)
    o_udown[...] = spread[5 * R:6 * R, :].astype(F32)
    o_gain[...] = norm[0:2, :]
    o_shift[...] = norm[2:4, :]
    o_bout[...] = norm[4:5, :]
    o_bdown[...] = norm[4:5, :]
    for j in range(3):
        o_uqkv[j] = group[j * HD:(j + 1) * HD, :].astype(F32).T
    o_aout[...] = group[192:256, :].astype(F32)
    o_uin[:, 0:128] = group[256:384, :].astype(F32).T
    o_uin[:, 128:256] = group[GROUP:GROUP + 128, :].astype(F32).T
    o_adown[...] = group[GROUP + 128:GROUP + 384, :].astype(F32)
    o_bqkv[...] = jnp.concatenate(
        [group[384:385, 0:64], group[384:385, 64:128], group[392:393, 0:64]], axis=0
    ).astype(F32)
    o_bin[...] = jnp.concatenate([group[GROUP + 384:GROUP + 385, :], group[GROUP + 392:GROUP + 393, :]], axis=1).astype(F32)


def unpack(spread, norm, group):
    shapes = [
        (2, D), (2, D), (3, HD), (3, D, R), (3, R, HD), (1, D), (64, R), (R, D), (1, FF), (D, R), (R, FF),
        (1, D), (FF, R), (R, D),
    ]

    def spec(shape):
        rank = len(shape)
        return pl.BlockSpec((None, *shape), lambda l: (l,) + (0,) * rank)

    def pair(rows, cols):
        return pl.BlockSpec((rows, cols), lambda l: (l, 0))

    return pl.pallas_call(
        unpack_kernel,
        grid=(LAYERS,),
        out_shape=[jax.ShapeDtypeStruct((LAYERS, *shape), F32) for shape in shapes],
        in_specs=[pair(768, D), pair(8, D), pair(2 * GROUP, R)],
        out_specs=[spec(shape) for shape in shapes],
        compiler_params=pltpu.CompilerParams(vmem_limit_bytes=48 << 20),
        name="unpack",
    )(spread, norm, group)


def positions_of(lengths):
    ends = jnp.cumsum(lengths)
    starts = ends - lengths
    token = jnp.arange(T, dtype=jnp.int32)
    within = (token[:, None] >= starts[None, :]) & (token[:, None] < ends[None, :])
    first = jnp.sum(jnp.where(within, starts[None, :], 0), axis=1).astype(jnp.int32)
    return first, token - first


def rotary(pos):
    half = ROT // 2
    freq = jnp.exp(jnp.arange(0, ROT, 2, dtype=F32) * (-math.log(10000.0) / ROT))
    angle = pos.astype(F32)[:, None] * freq[None, :]
    cos, sin = jnp.cos(angle), jnp.sin(angle)
    none = jnp.zeros((T, HD - ROT), F32)
    zero = jnp.zeros_like(sin)
    tabs = [
        jnp.concatenate([cos, cos, none + 1.0], axis=1),
        jnp.concatenate([-sin, zero, none], axis=1),
        jnp.concatenate([zero, sin, none], axis=1),
    ]
    return jnp.stack([jnp.concatenate([t, t], axis=1) for t in tabs])


def body(x, dy, lengths, gain, shift, w_qkv, b_qkv, a_qkv, u_qkv, w_out, b_out, a_out, u_out,
         w_in, b_in, a_in, u_in, w_down, b_down, a_down, u_down):
    first, pos = positions_of(lengths[0])
    tabs = rotary(pos)
    first_wide = jnp.broadcast_to(first[:, None], (T, 128))
    first_row = jnp.broadcast_to(first[None, :], (8, T))
    wq = jnp.pad(w_qkv.reshape(LAYERS, D, 192), ((0, 0), (0, 0), (0, 64)))
    uq = jnp.zeros((LAYERS, 3, R, 4, HD), F32)
    for j in range(3):
        uq = uq.at[:, j, :, j].set(u_qkv[:, j])
    uq = uq.reshape(LAYERS, 3 * R, NQ)
    biases = jnp.concatenate([b_qkv.reshape(LAYERS, 192), jnp.zeros((LAYERS, 64), F32), b_in], axis=1)[:, None, :]
    win, wint, bias, wout = prep(wq, a_qkv, uq, w_in, a_in, u_in, w_out, a_out, u_out, w_down, a_down, u_down,
                                 gain, shift, biases)
    obias = (b_out + b_down)[:, None, :]
    kept = []
    stream = x
    for layer in range(LAYERS):
        nxt, *saved = forward(layer, stream, gain, shift, win, bias, wout, obias[layer], tabs, first_wide)
        kept.append((stream, saved))
        stream = nxt
    grad = dy
    spread, norm, group, sums = ([None] * LAYERS for _ in range(4))
    for layer in reversed(range(LAYERS)):
        layer_in, saved = kept[layer]
        grad, spread[layer], norm[layer], group[layer], sums[layer] = backward(
            layer, grad, layer_in, saved, wint, wout, gain, shift, tabs, first_row,
            (a_qkv, uq, a_in, u_in, a_out, u_out, a_down, u_down),
        )
    (g_gain, g_shift, g_bqkv, g_aqkv, g_uqkv, g_bout, g_aout, g_uout, g_bin, g_ain, g_uin, g_bdown, g_adown, g_udown) = unpack(
        *total_over_devices(spread, norm, group, sums)
    )
    return (
        stream,
        grad,
        g_gain,
        g_shift,
        g_bqkv,
        g_aqkv,
        g_uqkv,
        g_bout[:, 0],
        g_aout,
        g_uout,
        g_bin[:, 0],
        g_ain,
        g_uin,
        g_bdown[:, 0],
        g_adown,
        g_udown,
    )


def solution(mesh):
    torus = Mesh(mesh.devices.reshape(2, 4, 4, 2, 2), ALL)
    return jax.shard_map(
        body,
        mesh=torus,
        in_specs=(
            P(ALL, None),
            P(ALL, None),
            P(DP, None),
            P(),
            P(),
            P(None, None, None, MP),
            P(None, None, MP),
            P(),
            P(None, None, None, MP),
            P(None, MP, None),
            P(),
            P(None, MP, None),
            P(),
            P(None, None, MP),
            P(None, MP),
            P(),
            P(None, None, MP),
            P(None, MP, None),
            P(),
            P(None, MP, None),
            P(),
        ),
        out_specs=(
            P(ALL, None),
            P(ALL, None),
            P(),
            P(),
            P(None, None, MP),
            P(),
            P(None, None, None, MP),
            P(),
            P(None, MP, None),
            P(),
            P(None, MP),
            P(),
            P(None, None, MP),
            P(),
            P(None, MP, None),
            P(),
        ),
        check_vma=False,
    )
```

```python
import functools
import math

import jax
import jax.numpy as jnp
from jax import lax
from jax.experimental import pallas as pl
from jax.experimental.pallas import tpu as pltpu
from jax.sharding import Mesh
from jax.sharding import PartitionSpec as P

HD = 64
ROT = 16
LAYERS = 2
EPS = 1e-05
FILL = -1000000000.0
MP = ("z", "yh", "c")
DP = ("yl", "x")
ALL = ("yl", "x", "z", "yh", "c")
MESH = pl.DeviceIdType.MESH

D = 1024
T = 2048
OWN = 128
BLK = 256
NB = T // BLK
WIN = 5 * BLK
NQ = 256
FF = 256
NIN = NQ + FF
NOUT = 128 + FF
R = 128
F32 = jnp.float32
BF16 = jnp.bfloat16
HIGH = lax.Precision.HIGHEST

NN = (((1,), (0,)), ((), ()))
NT = (((1,), (1,)), ((), ()))
TN = (((0,), (0,)), ((), ()))


def mm(a, b, dims=NN, precision=None):
    return lax.dot_general(a, b, dims, precision=precision, preferred_element_type=F32)


def split_bf16(a):
    high = a.astype(BF16)
    return high, (a - high.astype(F32)).astype(BF16)


def mm3(a, b, dims=NN):
    ah, al = split_bf16(a)
    bh, bl = split_bf16(b)
    return mm(ah, bh, dims) + (mm(al, bh, dims) + mm(ah, bl, dims))


def rows_of(ref, start, count):
    return ref.at[pl.ds(start if isinstance(start, int) else pl.multiple_of(start, count), count)]


class Place:
    def __init__(self):
        self.z, self.h, self.c = (lax.axis_index(a) for a in MP)
        self.up = {"z": lax.rem(self.z + 1, 4)}
        self.dn = {"z": lax.rem(self.z + 3, 4)}
        self.yy = {"yh": 1 - self.h}
        self.sib = {"c": 1 - self.c}

    def block(self, dz, dh):
        return lax.rem(self.z + dz, 4) * 2 + (self.h if dh == 0 else 1 - self.h)

    def shard(self, dz, dh, dc):
        return self.block(dz, dh) * 2 + (self.c if dc == 0 else 1 - self.c)

    def meet(self):
        barrier = pltpu.get_barrier_semaphore()
        for peer in (self.up, self.dn, self.yy, self.sib):
            pl.semaphore_signal(barrier, inc=1, device_id=peer, device_id_type=MESH)
        pl.semaphore_wait(barrier, 4)


class Sender:
    def __init__(self, sems):
        self.sems = sems
        self.live = []

    def send(self, src, dst, peer, recv_sem):
        copy = pltpu.make_async_remote_copy(
            src_ref=src,
            dst_ref=dst,
            send_sem=self.sems.at[len(self.live)],
            recv_sem=recv_sem,
            device_id=peer,
            device_id_type=MESH,
        )
        copy.start()
        self.live.append(copy)

    def got(self, ref, sem, peer):
        pltpu.make_async_remote_copy(
            src_ref=ref,
            dst_ref=ref,
            send_sem=self.sems.at[0],
            recv_sem=sem,
            device_id=peer,
            device_id_type=MESH,
        ).wait_recv()

    def finish(self):
        for copy in self.live:
            copy.wait_send()


HALF = OWN // 2
QUART = OWN // 4
GATHER_SENDS = 32
GATHER_SEMS = [pltpu.SemaphoreType.DMA((17,)), pltpu.SemaphoreType.DMA((16,))]


def gather(me, out, buf, direct, cross, compute, before, amid):
    def part(dz, dh, dc, k):
        return rows_of(buf, me.shard(dz, dh, dc) * OWN + k * HALF, HALF)

    def sem(sems, dz, dh, k):
        return sems.at[(dz * 2 + dh) * 2 + k]

    def send(dz, dh, k, peer, tz, th):
        ref = part(dz, dh, 0, k)
        out.send(ref, ref, peer, sem(direct, tz, th, k))

    def over(dz, dh, k):
        ref = part(dz, dh, 0, k)
        out.send(ref, ref, me.sib, sem(cross, dz, dh, k))

    def got(dz, dh, k):
        out.got(part(dz, dh, 0, k), sem(direct, dz, dh, k), me.sib)

    def quarter(dz, k):
        return rows_of(buf, me.shard(dz, 0, 0) * OWN + HALF + k * QUART, QUART)

    def done(dz, dh):
        for k in range(2):
            out.got(part(dz, dh, 1, k), sem(cross, dz, dh, k), me.sib)
        compute(dz, dh)

    send(0, 0, 1, me.up, 3, 0)
    send(0, 0, 1, me.dn, 1, 0)
    send(0, 0, 0, me.yy, 0, 1)
    send(0, 0, 0, me.up, 3, 0)
    send(0, 0, 0, me.dn, 1, 0)
    send(0, 0, 1, me.yy, 0, 1)
    over(0, 0, 0)
    over(0, 0, 1)
    before()
    got(3, 0, 1)
    out.send(quarter(3, 0), quarter(3, 0), me.up, sem(direct, 2, 0, 1))
    got(1, 0, 1)
    out.send(quarter(1, 1), quarter(1, 1), me.dn, direct.at[16])
    got(0, 1, 0)
    send(0, 1, 0, me.dn, 1, 1)
    send(0, 1, 0, me.up, 3, 1)
    send(3, 0, 1, me.yy, 3, 1)
    send(1, 0, 1, me.yy, 1, 1)
    over(3, 0, 1)
    over(1, 0, 1)
    over(0, 1, 0)
    got(3, 0, 0)
    send(3, 0, 0, me.up, 2, 0)
    over(3, 0, 0)
    got(1, 0, 0)
    over(1, 0, 0)
    out.got(quarter(2, 0), sem(direct, 2, 0, 1), me.sib)
    out.got(quarter(2, 1), direct.at[16], me.sib)
    send(2, 0, 1, me.yy, 2, 1)
    over(2, 0, 1)
    got(0, 1, 1)
    over(0, 1, 1)
    amid()
    done(0, 0)
    got(1, 1, 0)
    send(1, 1, 0, me.dn, 2, 1)
    over(1, 1, 0)
    done(3, 0)
    done(1, 0)
    got(3, 1, 0)
    over(3, 1, 0)
    got(2, 0, 0)
    over(2, 0, 0)
    done(0, 1)
    got(3, 1, 1)
    over(3, 1, 1)
    got(1, 1, 1)
    over(1, 1, 1)
    done(2, 0)
    done(3, 1)
    done(1, 1)
    got(2, 1, 0)
    over(2, 1, 0)
    got(2, 1, 1)
    over(2, 1, 1)
    done(2, 1)


SCATTER_SENDS = 24
SCATTER_SCRATCH = [
    pltpu.VMEM((8 * OWN, D), F32),
    pltpu.VMEM((8 * OWN, D), BF16),
    pltpu.VMEM((8 * OWN, D), BF16),
    pltpu.VMEM((8 * OWN, D), BF16),
    pltpu.VMEM((2 * HALF, D), BF16),
    pltpu.VMEM((4 * HALF, D), BF16),
    pltpu.VMEM((HALF, D), BF16),
    pltpu.VMEM((4 * HALF, D), BF16),
    pltpu.VMEM((2 * QUART, D), BF16),
    pltpu.VMEM((2 * HALF, D), BF16),
    pltpu.SemaphoreType.DMA((8,)),
    pltpu.SemaphoreType.DMA((2,)),
    pltpu.SemaphoreType.DMA((4,)),
    pltpu.SemaphoreType.DMA((1,)),
    pltpu.SemaphoreType.DMA((4,)),
    pltpu.SemaphoreType.DMA((2,)),
    pltpu.SemaphoreType.DMA((2,)),
]


def scatter(me, out, bufs, compute, between, finish):
    (own, other, cross, sums, via, ring, last, pair, via2, ring2,
     s_cross, s_via, s_ring, s_last, s_pair, s_via2, s_ring2) = bufs

    def give(dz, dh):
        i = dz * 2 + dh

        def put(dc, terms):
            if dc == 0:
                own[pl.ds(i * OWN, OWN), :] = terms
            else:
                other[pl.ds(i * OWN, OWN), :] = terms.astype(BF16)

        compute(dz, dh, put)
        out.send(rows_of(other, i * OWN, OWN), rows_of(cross, i * OWN, OWN), me.sib, s_cross.at[i])

    def wait_cross(dz, dh):
        i = dz * 2 + dh
        out.got(rows_of(cross, i * OWN, OWN), s_cross.at[i], me.sib)

    def both(dz, dh, start, rows):
        here = pl.ds((dz * 2 + dh) * OWN + start, rows)
        return own[here, :] + cross[here, :].astype(F32)

    def arrived(buf, sems, i, rows):
        ref = rows_of(buf, i * rows, rows)
        out.got(ref, sems.at[i], me.sib)
        return ref[...].astype(F32)

    def pass_to(dz, dh, start, rows, value, buf, sems, i, peer):
        at = (dz * 2 + dh) * OWN + start
        sums[pl.ds(at, rows), :] = value.astype(BF16)
        out.send(rows_of(sums, at, rows), rows_of(buf, i * rows, rows), peer, sems.at[i])

    def first(dz, dh):
        return both(dz, dh, 0, HALF)

    def to_partner(dz):
        pass_to(dz, 1, HALF, HALF, both(dz, 1, HALF, HALF), pair, s_pair, dz, me.yy)

    def second(dz):
        return both(dz, 0, HALF, HALF) + arrived(pair, s_pair, dz, HALF)

    give(2, 1)
    give(2, 0)
    wait_cross(2, 1)
    pass_to(2, 1, 0, HALF, first(2, 1), via, s_via, 1, me.dn)
    to_partner(2)
    wait_cross(2, 0)
    pass_to(2, 0, 0, HALF, first(2, 0), via, s_via, 0, me.up)
    give(1, 1)
    give(3, 0)
    wait_cross(1, 1)
    pass_to(1, 1, 0, HALF, first(1, 1), ring, s_ring, 1, me.up)
    to_partner(1)
    wait_cross(3, 0)
    pass_to(3, 0, 0, HALF, first(3, 0), ring, s_ring, 2, me.dn)
    give(3, 1)
    wait_cross(3, 1)
    to_partner(3)
    give(1, 0)
    wait_cross(1, 0)
    own[pl.ds(4 * OWN + HALF, HALF), :] = second(2)
    for k, peer in ((0, me.up), (1, me.dn)):
        value = own[pl.ds(4 * OWN + HALF + k * QUART, QUART), :]
        pass_to(2, 0, HALF + k * QUART, QUART, value, via2, s_via2, k, peer)
    give(0, 1)
    wait_cross(0, 1)
    to_partner(0)
    pass_to(3, 1, 0, HALF, first(3, 1) + arrived(via, s_via, 1, HALF), ring, s_ring, 3, me.dn)
    pass_to(1, 0, 0, HALF, first(1, 0) + arrived(via, s_via, 0, HALF), ring, s_ring, 0, me.up)
    give(0, 0)
    between[0]()
    for dz, k, peer in ((1, 0, me.up), (3, 1, me.dn)):
        mine = pl.ds(dz * 2 * OWN + HALF, HALF)
        own[mine, :] = second(dz)
        own[pl.ds(dz * 2 * OWN + HALF + k * QUART, QUART), :] += arrived(via2, s_via2, k, QUART)
        pass_to(dz, 0, HALF, HALF, own[mine, :], ring2, s_ring2, k, peer)
    between[1]()
    total = first(0, 1) + arrived(ring, s_ring, 1, HALF) + arrived(ring, s_ring, 3, HALF)
    pass_to(0, 1, 0, HALF, total, last, s_last, 0, me.yy)
    wait_cross(0, 0)
    between[2]()
    finish(HALF, HALF, second(0) + arrived(ring2, s_ring2, 0, HALF) + arrived(ring2, s_ring2, 1, HALF))
    total = first(0, 0) + arrived(ring, s_ring, 0, HALF) + arrived(ring, s_ring, 2, HALF)
    finish(0, HALF, total + arrived(last, s_last, 0, HALF))


def gelu_parts(h):
    cdf = 0.5 * (1.0 + lax.erf(h * (2.0**-0.5)))
    return cdf


def lane_roll(a, shift):
    return pltpu.roll(a, shift % 128, 1)


def normalized(x):
    mean = jnp.mean(x, axis=1, keepdims=True)
    centered = x - mean
    scale = lax.rsqrt(jnp.mean(centered * centered, axis=1, keepdims=True) + EPS)
    return centered * scale, scale


class Loads:
    def __init__(self, sems):
        self.sems = sems
        self.count = 0

    def start(self, src, dst):
        copy = pltpu.make_async_copy(src, dst, self.sems.at[self.count])
        self.count += 1
        copy.start()
        return copy


def rotary_tables(lens, tabs, first_row, first, angles):
    token = lax.broadcasted_iota(jnp.int32, (8, T), 1)
    begin = jnp.zeros((8, T), jnp.int32)
    end = 0
    for i in range(3):
        end = end + lens[0, i]
        begin = jnp.where(token >= end, end, begin)
    first_row[...] = begin
    step = lax.broadcasted_iota(jnp.int32, (8, T), 0).astype(F32)
    angle = (token - begin).astype(F32) * jnp.exp(step * (-2.0 * math.log(10000.0) / ROT))
    angles[0:8, :] = jnp.cos(angle)
    angles[8:16, :] = jnp.sin(angle)

    def turn(i, _):
        at = pl.ds(pl.multiple_of(i * BLK, BLK), BLK)
        cos, sin = angles[0:8, at], angles[8:16, at]
        zero, none = jnp.zeros((8, BLK), F32), jnp.zeros((HD - ROT, BLK), F32)
        for k, head in enumerate(((cos, cos, none + 1.0), (-sin, zero, none), (zero, sin, none))):
            tabs[k, at, :] = jnp.concatenate(head + head, axis=0).T
        first[at, :] = jnp.broadcast_to(first_row[0:1, at].astype(F32), (128, BLK)).T.astype(jnp.int32)
        return 0

    lax.fori_loop(0, NB, turn, 0)


def forward_kernel(layer, lens, x_ref, gains, shifts, biases, obias,
                   wqkv_h, aqkv_h, uqkv_h, win_h, ain_h, uin_h, wout_h, aout_h, uout_h, wdown_h, adown_h, udown_h, *refs):
    (o_x, o_xh, o_qkv, o_ho, o_out, o_lse, o_kt, o_wint, o_wout, o_bqkv, o_tabs, o_first,
     xh, qkv, ho, ou, out_t, kt, scores, probs, win, wint, bias, wout, bqkv, tabs, first, angles,
     wqkv, aqkv, uqkv, w_in, ain, uin, w_out, aout, uout, wdown, adown, udown,
     load_sems, send_sems, g_direct, g_cross, *scat) = refs
    me = Place()
    loads = Loads(load_sems)
    ins = [
        loads.start(src.at[layer], dst)
        for src, dst in (
            (wqkv_h, wqkv), (aqkv_h, aqkv), (uqkv_h, uqkv), (win_h, w_in), (ain_h, ain), (uin_h, uin),
            (wout_h, w_out), (aout_h, aout), (uout_h, uout), (wdown_h, wdown), (adown_h, adown), (udown_h, udown),
        )
    ]
    out = Sender(send_sems)
    me.meet()
    rows_of(xh, me.shard(0, 0, 0) * OWN, OWN)[...] = (
        normalized(x_ref[...])[0] * gains[0:1, :] + shifts[0:1, :]
    ).astype(BF16)
    outs = []

    def before():
        rotary_tables(lens, tabs, o_first, first, angles)
        for copy in ins[:3]:
            copy.wait()
        bqkv[...] = jnp.zeros(bqkv.shape, F32)
        for j in range(3):
            bqkv[j * R:(j + 1) * R, j * HD:(j + 1) * HD] = uqkv[j]
        ab = None
        for j in range(3):
            term = mm3(aqkv[j], bqkv[j * R:(j + 1) * R, :])
            ab = term if ab is None else ab + term
        win[:, 0:NQ] = ab.astype(BF16)
        win[:, 0:128] = (wqkv[:, 0:128].astype(F32) + ab[:, 0:128]).astype(BF16)
        win[:, 128:192] = (wqkv[:, 128:192].astype(F32) + ab[:, 128:192]).astype(BF16)
        wint[0:NQ, :] = win[:, 0:NQ].astype(F32).T.astype(BF16)

    def amid():
        for copy in ins[3:]:
            copy.wait()
        ratio = gains[1:2, :] / gains[0:1, :]
        merged = w_in[...].astype(F32) + mm3(ain[...], uin[...])
        low = merged.astype(BF16)
        b_high, b_low = split_bf16(jnp.broadcast_to(shifts[1:2, :] - shifts[0:1, :] * ratio, (8, D)))
        bias[...] = biases[...]
        bias[:, NQ:NIN] += (mm(b_high, low) + mm(b_low, low))[0:1]
        turned = merged.T * ratio
        wint[NQ:NIN, :] = turned.astype(BF16)
        win[:, NQ:NIN] = turned.T.astype(BF16)
        wout[0:64, :] = (w_out[...].astype(F32) + mm3(aout[...], uout[...])).astype(BF16)
        wout[64:128, :] = jnp.zeros((64, D), BF16)
        wout[128:NOUT, :] = (wdown[...].astype(F32) + mm3(adown[...], udown[...])).astype(BF16)
        outs.append(loads.start(wint, o_wint))
        outs.append(loads.start(wout, o_wout))
        outs.append(loads.start(bqkv, o_bqkv))
        if layer == 0:
            outs.append(loads.start(tabs, o_tabs))

    def project(dz, dh):
        at = pl.ds(pl.multiple_of(me.block(dz, dh) * BLK, BLK), BLK)
        rows = xh[at, :]
        pq = mm(rows, win[:, 0:NQ]) + bias[:, 0:NQ]
        qk = pq[:, 0:128]
        turned = qk * tabs[0, at, :] + lane_roll(qk, -8) * tabs[1, at, :] + lane_roll(qk, 8) * tabs[2, at, :]
        lane = lax.broadcasted_iota(jnp.int32, (BLK, 128), 1)
        qkv[at, 0:128] = jnp.where(lane < HD, turned * HD**-0.5, 0.0).astype(BF16)
        keys = jnp.where(lane < HD, lane_roll(turned, HD), 0.0)
        qkv[at, 128:256] = keys.astype(BF16)
        kt[:, at] = keys.T.astype(BF16)
        qkv[at, 256:384] = pq[:, 128:256].astype(BF16)
        h = mm(rows, win[:, NQ:NIN]) + bias[:, NQ:NIN]
        ho[at, 128:NOUT] = h
        ou[at, 128:NOUT] = (h * gelu_parts(h)).astype(BF16)

    gather(me, out, xh, g_direct, g_cross, project, before, amid)
    outs.extend([loads.start(xh, o_xh), loads.start(qkv, o_qkv), loads.start(kt, o_kt)])

    def attend(dz, dh, put):
        b = me.block(dz, dh)
        at = pl.ds(pl.multiple_of(b * BLK, BLK), BLK)
        key_at = jnp.maximum(b - 4, 0) * BLK
        q = qkv[at, 0:128]
        row = b * BLK + lax.broadcasted_iota(jnp.int32, (BLK, BLK), 0)
        start = jnp.concatenate([first[at, :], first[at, :]], axis=1)
        peak = None
        for j in range(5):
            keys = pl.ds(pl.multiple_of(key_at + j * BLK, BLK), BLK)
            s = mm(q, qkv[keys, 128:256], NT)
            col = key_at + j * BLK + lax.broadcasted_iota(jnp.int32, (BLK, BLK), 1)
            s = jnp.where((col >= start) & (col <= row), s, FILL)
            scores[:, j * BLK:(j + 1) * BLK] = s
            peak = s if peak is None else jnp.maximum(peak, s)
        peak = jnp.max(peak, axis=1, keepdims=True)
        summed = None
        for j in range(5):
            p = jnp.exp(scores[:, j * BLK:(j + 1) * BLK] - peak)
            scores[:, j * BLK:(j + 1) * BLK] = p
            summed = p if summed is None else summed + p
        summed = jnp.sum(summed, axis=1, keepdims=True)
        share = 1.0 / summed
        for j in range(5):
            here = slice(j * BLK, (j + 1) * BLK)
            probs[:, here] = (scores[:, here] * share).astype(BF16)
        o = mm(probs[...], qkv[pl.ds(pl.multiple_of(key_at, BLK), WIN), 256:384])
        ho[at, 0:128] = o
        ou[at, 0:128] = o.astype(BF16)
        lse = jnp.broadcast_to(peak + jnp.log(summed), (BLK, 128)).T
        o_lse[:, at] = lse[0:8, :]
        out_t[:, at] = ou[at, :].astype(F32).T.astype(BF16)
        for dc in range(2):
            put(dc, mm(rows_of(ou, me.shard(dz, dh, dc) * OWN, OWN)[...], wout[...]))

    def store():
        outs.append(loads.start(ho, o_ho))
        outs.append(loads.start(out_t, o_out))

    def nothing():
        pass

    def finish(at, rows, total):
        here = pl.ds(at, rows)
        o_x[here, :] = x_ref[here, :] + total + obias[...]

    scatter(me, out, scat, attend, (store, nothing, nothing), finish)
    for copy in outs:
        copy.wait()
    out.finish()


VM = pl.BlockSpec(memory_space=pltpu.VMEM)
HBM = pl.BlockSpec(memory_space=pl.ANY)


SMEM = pl.BlockSpec(memory_space=pltpu.SMEM)


def forward(layer, lens, x, gains, shifts, biases, obias, weights):
    vmem = pltpu.VMEM
    shapes = [
        jax.ShapeDtypeStruct((OWN, D), F32),
        jax.ShapeDtypeStruct((T, D), BF16),
        jax.ShapeDtypeStruct((T, 384), BF16),
        jax.ShapeDtypeStruct((T, NOUT), F32),
        jax.ShapeDtypeStruct((NOUT, T), BF16),
        jax.ShapeDtypeStruct((8, T), F32),
        jax.ShapeDtypeStruct((128, T), BF16),
        jax.ShapeDtypeStruct((NIN, D), BF16),
        jax.ShapeDtypeStruct((NOUT, D), BF16),
        jax.ShapeDtypeStruct((3 * R, NQ), F32),
        jax.ShapeDtypeStruct((3, T, 128), F32),
        jax.ShapeDtypeStruct((8, T), jnp.int32),
    ]
    return pl.pallas_call(
        functools.partial(forward_kernel, layer),
        out_shape=shapes,
        in_specs=[SMEM] + [VM] * 5 + [HBM] * 12,
        out_specs=[VM, HBM, HBM, HBM, HBM, VM, HBM, HBM, HBM, HBM, HBM, VM],
        scratch_shapes=[
            vmem((T, D), BF16),
            vmem((T, 384), BF16),
            vmem((T, NOUT), F32),
            vmem((T, NOUT), BF16),
            vmem((NOUT, T), BF16),
            vmem((128, T), BF16),
            vmem((BLK, WIN), F32),
            vmem((BLK, WIN), BF16),
            vmem((D, NIN), BF16),
            vmem((NIN, D), BF16),
            vmem((1, NIN), F32),
            vmem((NOUT, D), BF16),
            vmem((3 * R, NQ), F32),
            vmem((3, T, 128), F32),
            vmem((T, 128), jnp.int32),
            vmem((16, T), F32),
            vmem((D, 192), BF16),
            vmem((3, D, R), F32),
            vmem((3, R, HD), F32),
            vmem((D, FF), BF16),
            vmem((D, R), F32),
            vmem((R, FF), F32),
            vmem((64, D), BF16),
            vmem((64, R), F32),
            vmem((R, D), F32),
            vmem((FF, D), BF16),
            vmem((FF, R), F32),
            vmem((R, D), F32),
            pltpu.SemaphoreType.DMA((24,)),
            pltpu.SemaphoreType.DMA((GATHER_SENDS + SCATTER_SENDS,)),
            *GATHER_SEMS,
            *SCATTER_SCRATCH,
        ],
        compiler_params=pltpu.CompilerParams(
            collective_id=layer, has_side_effects=True, vmem_limit_bytes=60 << 20
        ),
        name=f"forward_layer{layer}",
    )(lens, x, gains[layer], shifts[layer], biases[layer], obias[layer], *weights)


def backward_kernel(layer, dy_ref, x_ref, xh_h, qkv_h, ho_h, out_h, lse_ref, kt_h, wint_h, wout_h, bqkv_h, gains, shifts, tabs_h, first_ref,
                    aqkv_h, ain_h, bin_h, aout_h, bout_h, adown_h, bdown_h,
                    o_dx, o_spread, o_norm, o_group, o_sums,
                    dy, xh, qkv, ho, out_t, kt, dph, dph_t, acc, wint, wout, tabs, aqkv, bqkv, ain, bin_, aout, bout, adown, bdown,
                    load_sems, send_sems, g_direct, g_cross, *scat):
    me = Place()
    loads = Loads(load_sems)
    early = [
        loads.start(wout_h, wout),
        loads.start(ho_h, ho),
        loads.start(qkv_h, qkv),
        loads.start(kt_h, kt),
    ]
    late = [
        loads.start(tabs_h, tabs),
        loads.start(wint_h, wint),
        loads.start(xh_h, xh),
        loads.start(out_h, out_t),
        loads.start(aqkv_h.at[layer], aqkv),
        loads.start(bqkv_h, bqkv),
        loads.start(ain_h.at[layer], ain),
        loads.start(bin_h.at[layer], bin_),
        loads.start(aout_h.at[layer], aout),
        loads.start(bout_h.at[layer], bout),
        loads.start(adown_h.at[layer], adown),
        loads.start(bdown_h.at[layer], bdown),
    ]
    out = Sender(send_sems)
    me.meet()
    rows_of(dy, me.shard(0, 0, 0) * OWN, OWN)[...] = dy_ref[...].astype(BF16)

    def before():
        acc[...] = jnp.zeros(acc.shape, F32)

    def amid():
        for copy in early:
            copy.wait()

    def pull(dz, dh):
        b = me.block(dz, dh)
        at = pl.ds(pl.multiple_of(b * BLK, BLK), BLK)
        rows = dy[at, :]
        du = mm(rows, wout[128:NOUT, :], NT)
        h = ho[at, 128:NOUT]
        slope = gelu_parts(h) + h * (jnp.exp(-0.5 * h * h) * (2.0 * math.pi) ** -0.5)
        dph[at, NQ:NIN] = (slope * du).astype(BF16)
        do = mm(rows, wout[0:128, :], NT).astype(BF16)
        drop = jnp.sum((do.astype(F32) * ho[at, 0:128]).T, axis=0, keepdims=True)
        lse = lse_ref[0:1, at]
        start = first_ref[0:1, at]
        q = qkv[at, 0:128]
        key_at = jnp.maximum(b - 5, 0)
        wide = 3 * BLK
        col = b * BLK + lax.broadcasted_iota(jnp.int32, (wide, BLK), 1)

        def step(j, dq):
            key = (key_at + 3 * j) * BLK
            keys = pl.ds(pl.multiple_of(key, BLK), wide)
            s = mm(qkv[keys, 128:256], q, NT)
            row = key + lax.broadcasted_iota(jnp.int32, (wide, BLK), 0)
            p = jnp.where((row >= start) & (row <= col), jnp.exp(s - lse), 0.0)
            dp = mm(qkv[keys, 256:384], do, NT)
            ds = (p * (dp - drop)).astype(BF16)
            acc[keys, 256:384] += mm(p.astype(BF16), do)
            acc[keys, 128:256] += mm(ds, q)
            return dq + mm(kt[:, keys], ds)

        dq = lax.fori_loop(0, (jnp.minimum(b, 5) + 3) // 3, step, jnp.zeros((128, BLK), F32))
        acc[at, 0:128] = dq.T * HD**-0.5

    gather(me, out, dy, g_direct, g_cross, pull, before, amid)
    for copy in late:
        copy.wait()

    def send_back(dz, dh, put):
        b = me.block(dz, dh)
        at = pl.ds(pl.multiple_of(b * BLK, BLK), BLK)
        g = acc[at, 0:128] + lane_roll(acc[at, 128:256], HD)
        turned = g * tabs[0, at, :] + lane_roll(g * tabs[1, at, :], 8) + lane_roll(g * tabs[2, at, :], -8)
        dph[at, 0:128] = turned.astype(BF16)
        dph[at, 128:256] = acc[at, 256:384].astype(BF16)
        rows = dph[at, :]
        for dc in range(2):
            put(dc, mm(rows_of(dph, me.shard(dz, dh, dc) * OWN, OWN)[...], wint[...]))
        dph_t[:, at] = rows.astype(F32).T.astype(BF16)

    def weight_grad(row, at, width):
        here = pl.ds(at, width)
        grad = mm(dph_t[here, :], xh[...])
        weight = wint[here, :].astype(F32)
        total = jnp.sum(dph_t[here, :].astype(F32), axis=1, keepdims=True)
        o_sums[:, here] = jnp.broadcast_to(total, (width, 128)).T[0:8, :]
        by_gain = jnp.sum(grad * weight, axis=0, keepdims=True)
        by_shift = jnp.sum(total * weight, axis=0, keepdims=True)
        g = gains[0:1, :]
        if row == 1:
            ratio = gains[1:2, :] / g
            by_gain, by_shift = by_gain / ratio, by_shift / ratio
            grad = grad * ratio + total * (shifts[1:2, :] - shifts[0:1, :] * ratio)
        o_norm[row:row + 1, :] = (by_gain - shifts[0:1, :] * by_shift) / g
        o_norm[2 + row:3 + row, :] = by_shift
        return grad.astype(BF16)

    def factors_qkv():
        low = weight_grad(0, 0, NQ)
        for j in range(3):
            o_spread[j * R:(j + 1) * R, :] = mm(bqkv[j * R:(j + 1) * R, :].astype(BF16), low)
            o_group[j * HD:(j + 1) * HD, :] = mm(low[j * HD:(j + 1) * HD], aqkv[j].astype(BF16))

    def factors_in():
        low = weight_grad(1, NQ, FF)
        o_spread[3 * R:4 * R, :] = mm(bin_[...].astype(BF16), low)
        o_group[256:512, :] = mm(low, ain[...].astype(BF16))

    def factors_out():
        low = mm(out_t[0:64, :], dy[...]).astype(BF16)
        o_spread[4 * R:5 * R, :] = mm(aout[...].astype(BF16), low, TN)
        o_group[192:256, :] = mm(low, bout[...].astype(BF16), NT)
        low = mm(out_t[128:NOUT, :], dy[...]).astype(BF16)
        o_spread[5 * R:6 * R, :] = mm(adown[...].astype(BF16), low, TN)
        o_group[512:768, :] = mm(low, bdown[...].astype(BF16), NT)
        o_norm[4:5, :] = jnp.sum(dy_ref[...], axis=0, keepdims=True)
        o_norm[5:8, :] = jnp.zeros((3, D), F32)

    def finish(at, rows, total):
        here = pl.ds(at, rows)
        hat, rstd = normalized(x_ref[here, :])
        total = total * gains[0:1, :]
        mean = jnp.mean(total, axis=1, keepdims=True)
        along = jnp.mean(total * hat, axis=1, keepdims=True)
        o_dx[here, :] = dy_ref[here, :] + rstd * (total - mean - hat * along)

    scatter(me, out, scat, send_back, (factors_qkv, factors_in, factors_out), finish)
    out.finish()


def backward(layer, dy, x, saved, gains, shifts, tabs, first, factors):
    shapes = [
        jax.ShapeDtypeStruct((OWN, D), F32),
        jax.ShapeDtypeStruct((6 * R, D), F32),
        jax.ShapeDtypeStruct((8, D), F32),
        jax.ShapeDtypeStruct((768, R), F32),
        jax.ShapeDtypeStruct((8, NIN), F32),
    ]
    return pl.pallas_call(
        functools.partial(backward_kernel, layer),
        out_shape=shapes,
        in_specs=[VM, VM, HBM, HBM, HBM, HBM, VM, HBM, HBM, HBM, HBM, VM, VM, HBM, VM] + [HBM] * 7,
        out_specs=[VM] * 5,
        scratch_shapes=[
            pltpu.VMEM((T, D), BF16),
            pltpu.VMEM((T, D), BF16),
            pltpu.VMEM((T, 384), BF16),
            pltpu.VMEM((T, NOUT), F32),
            pltpu.VMEM((NOUT, T), BF16),
            pltpu.VMEM((128, T), BF16),
            pltpu.VMEM((T, NIN), BF16),
            pltpu.VMEM((NIN, T), BF16),
            pltpu.VMEM((T, 384), F32),
            pltpu.VMEM((NIN, D), BF16),
            pltpu.VMEM((NOUT, D), BF16),
            pltpu.VMEM((3, T, 128), F32),
            pltpu.VMEM((3, D, R), F32),
            pltpu.VMEM((3 * R, NQ), F32),
            pltpu.VMEM((D, R), F32),
            pltpu.VMEM((R, FF), F32),
            pltpu.VMEM((64, R), F32),
            pltpu.VMEM((R, D), F32),
            pltpu.VMEM((FF, R), F32),
            pltpu.VMEM((R, D), F32),
            pltpu.SemaphoreType.DMA((16,)),
            pltpu.SemaphoreType.DMA((GATHER_SENDS + SCATTER_SENDS,)),
            *GATHER_SEMS,
            *SCATTER_SCRATCH,
        ],
        compiler_params=pltpu.CompilerParams(
            collective_id=LAYERS + layer, has_side_effects=True, vmem_limit_bytes=62 << 20
        ),
        name=f"backward_layer{layer}",
    )(dy, x, *saved, gains[layer], shifts[layer], tabs, first, *factors)


QUARTER = 768 // 4
GROUP = 400


def total_kernel(spread_a, spread_b, norm_a, norm_b, group_a, group_b, sums_a, sums_b, o_spread, o_norm, o_group,
                 other, cross, low, slots1, acc1, low2, slots2, acc2, low3, slots3, g3, g2,
                 n_first, n_slots, g_own, g_low, g_slots, g_pair,
                 send_sems, s_cross, s_one, s_two, s_three, s_back3, s_back2, s_back1, s_backc,
                 s_norm, s_group):
    yl, x, z, yh, c = (lax.axis_index(a) for a in ALL)
    y = yh * 2 + yl
    sib = {"c": 1 - c}

    def along(axis, d):
        return {axis: lax.rem((x if axis == "x" else z) + d, 4)}

    def y_peer(d):
        there = lax.rem(y + d, 4)
        return {"yh": there // 2, "yl": lax.rem(there, 2)}

    barrier = pltpu.get_barrier_semaphore()
    peers = [sib] + [along(a, d) for a in ("x", "z") for d in (1, 2, 3)] + [y_peer(1), y_peer(2), y_peer(3)]
    for peer in peers:
        pl.semaphore_signal(barrier, inc=1, device_id=peer, device_id_type=MESH)
    pl.semaphore_wait(barrier, len(peers))

    out = Sender(send_sems)
    mine = pl.ds(pl.multiple_of(c * 512, 512), 512)
    theirs = pl.ds(pl.multiple_of((1 - c) * 512, 512), 512)
    paths = ((0, spread_a, "x", "z"), (1, spread_b, "z", "x"))
    here = {"x": x, "z": z}

    def quarter(axis, d, size):
        return pl.multiple_of(lax.rem(here[axis] + d, 4) * size, size)

    def rows(ref, start, size):
        return ref.at[pl.ds(start, size)]

    for d in (2, 1, 3, 0):
        for p, ref, axis, _ in paths:
            at = quarter(axis, d, QUARTER)
            to = pl.multiple_of(p * 768 + at, 64)
            other[pl.ds(to, QUARTER), :] = ref[pl.ds(at, QUARTER), theirs].astype(BF16)
            out.send(rows(other, to, QUARTER), rows(cross, to, QUARTER), sib, s_cross.at[p * 4 + d])
    n_first[0, 0:8, :] = norm_a[:, theirs]
    n_first[0, 8:16, :] = norm_b[:, theirs]
    out.send(n_first.at[0], n_first.at[1], sib, s_norm.at[0])
    for i in range(4):
        ref, sums = (group_a, sums_a) if i < 2 else (group_b, sums_b)
        g_own[i * GROUP:i * GROUP + 384, :] = ref[(i % 2) * 384:(i % 2) * 384 + 384, :]
        g_own[i * GROUP + 384:i * GROUP + 392, :] = sums[:, (i % 2) * 256:(i % 2) * 256 + 128]
        g_own[i * GROUP + 392:i * GROUP + 400, :] = sums[:, (i % 2) * 256 + 128:(i % 2) * 256 + 256]
    g_low[...] = g_own[...].astype(BF16)
    for d in (2, 1, 3):
        at = quarter("x", d, GROUP)
        out.send(rows(g_low, at, GROUP), g_slots.at[d - 1], along("x", d), s_group.at[d - 1])
    for d in (2, 1, 3, 0):
        for p, ref, axis, _ in paths:
            at = quarter(axis, d, QUARTER)
            to = pl.multiple_of(p * 768 + at, 64)
            out.got(rows(cross, to, QUARTER), s_cross.at[p * 4 + d], sib)
            both = ref[pl.ds(at, QUARTER), mine] + cross[pl.ds(to, QUARTER), :].astype(F32)
            if d == 0:
                acc1[p] = both
            else:
                low[pl.ds(to, QUARTER), :] = both.astype(BF16)
                out.send(rows(low, to, QUARTER), slots1.at[p * 3 + d - 1], along(axis, d), s_one.at[p * 3 + d - 1])
    out.got(n_first.at[1], s_norm.at[0], sib)

    def n_stage(stage, value, index, peer_of, base):
        own = n_slots.at[stage * 4 + index]
        own[...] = value
        for d in (1, 2, 3):
            out.send(own, own, peer_of(d), s_norm.at[base + d - 1])

    def n_sum(stage, index, base):
        for d in (1, 2, 3):
            out.got(n_slots.at[stage * 4 + lax.rem(index + 4 - d, 4)], s_norm.at[base + d - 1], sib)
        return (n_slots[stage * 4] + n_slots[stage * 4 + 1]) + (n_slots[stage * 4 + 2] + n_slots[stage * 4 + 3])

    first = jnp.concatenate([norm_a[:, mine], norm_b[:, mine]], axis=0) + n_first[1]
    n_stage(0, first, x, lambda d: along("x", d), 1)
    total = g_own[pl.ds(quarter("x", 0, GROUP), GROUP), :]
    for d in (1, 2, 3):
        out.got(g_slots.at[d - 1], s_group.at[d - 1], sib)
        total = total + g_slots[d - 1].astype(F32)
    g_pair[0] = total.astype(BF16)
    out.send(g_pair.at[0], g_pair.at[1], {"yl": 1 - yl}, s_group.at[3])
    for p, _, axis, second in paths:
        for d in (1, 2, 3):
            out.got(slots1.at[p * 3 + d - 1], s_one.at[p * 3 + d - 1], sib)
            acc1[p] += slots1[p * 3 + d - 1].astype(F32)
        low2[p] = acc1[p].astype(BF16)
        for d in (2, 1, 3):
            at = quarter(second, d, 48)
            out.send(
                low2.at[p, pl.ds(at, 48)], slots2.at[p * 3 + d - 1], along(second, d), s_two.at[p * 3 + d - 1]
            )
    n_stage(1, n_sum(0, x, 1), z, lambda d: along("z", d), 4)
    out.got(g_pair.at[1], s_group.at[3], sib)
    at = quarter("x", 0, GROUP)
    o_group[pl.ds(at, GROUP), :] = (g_pair[0].astype(F32) + g_pair[1].astype(F32)).astype(BF16)
    for d in (1, 2, 3):
        out.send(rows(o_group, at, GROUP), rows(o_group, at, GROUP), along("x", d), s_group.at[3 + d])
    for p, _, axis, second in paths:
        total = acc1[p, pl.ds(quarter(second, 0, 48), 48), :]
        for d in (1, 2, 3):
            out.got(slots2.at[p * 3 + d - 1], s_two.at[p * 3 + d - 1], sib)
            total = total + slots2[p * 3 + d - 1].astype(F32)
        acc2[p * 48:p * 48 + 48, :] = total
    low3[...] = acc2[...].astype(BF16)

    def y_lanes(d):
        return pl.ds(pl.multiple_of(lax.rem(y + d, 4) * 128, 128), 128)

    for d in (2, 1, 3):
        out.send(low3.at[:, y_lanes(d)], slots3.at[d - 1], y_peer(d), s_three.at[d - 1])
    n_stage(2, n_sum(1, z, 4), y, y_peer, 7)
    total = acc2[:, y_lanes(0)]
    for d in (1, 2, 3):
        out.got(slots3.at[d - 1], s_three.at[d - 1], sib)
        total = total + slots3[d - 1].astype(F32)
    g3[:, y_lanes(0)] = total.astype(BF16)
    for d in (2, 1, 3):
        out.send(g3.at[:, y_lanes(0)], g3.at[:, y_lanes(0)], y_peer(d), s_back3.at[d - 1])
    o_norm[:, mine] = n_sum(2, y, 7)
    out.send(o_norm.at[:, mine], o_norm.at[:, mine], sib, s_norm.at[10])
    for d in (1, 2, 3):
        out.got(g3.at[:, y_lanes(4 - d)], s_back3.at[d - 1], sib)
    for p, _, axis, second in paths:
        at = quarter(second, 0, 48)
        g2[p, pl.ds(at, 48), :] = g3[p * 48:p * 48 + 48, :]
        for d in (2, 1, 3):
            ref = g2.at[p, pl.ds(at, 48)]
            out.send(ref, ref, along(second, d), s_back2.at[p * 3 + d - 1])
    for p, _, axis, second in paths:
        for d in (1, 2, 3):
            out.got(g2.at[p, pl.ds(quarter(second, 4 - d, 48), 48)], s_back2.at[p * 3 + d - 1], sib)
        to = pl.multiple_of(p * 768 + quarter(axis, 0, QUARTER), 64)
        o_spread[pl.ds(to, QUARTER), mine] = g2[p]
        ref = o_spread.at[pl.ds(to, QUARTER), mine]
        for d in (2, 1, 3):
            out.send(ref, ref, along(axis, d), s_back1.at[p * 3 + d - 1])
        out.send(ref, ref, sib, s_backc.at[p * 4])
    for d in (1, 3, 2):
        for p, _, axis, second in paths:
            to = pl.multiple_of(p * 768 + quarter(axis, 4 - d, QUARTER), 64)
            ref = o_spread.at[pl.ds(to, QUARTER), mine]
            out.got(ref, s_back1.at[p * 3 + d - 1], sib)
            out.send(ref, ref, sib, s_backc.at[p * 4 + d])
    for d in (1, 2, 3):
        out.got(rows(o_group, quarter("x", 4 - d, GROUP), GROUP), s_group.at[3 + d], sib)
    out.got(o_norm.at[:, theirs], s_norm.at[10], sib)
    for d in (0, 1, 3, 2):
        for p, _, axis, second in paths:
            to = pl.multiple_of(p * 768 + quarter(axis, 4 - d, QUARTER), 64)
            out.got(o_spread.at[pl.ds(to, QUARTER), theirs], s_backc.at[p * 4 + d], sib)
    out.finish()


TOTAL_SENDS = 8 + 1 + 3 + 6 + 3 + 1 + 6 + 3 + 3 + 3 + 3 + 3 + 1 + 6 + 8 + 6


def total_over_devices(spread, norm, group, sums):
    dma = pltpu.SemaphoreType.DMA
    return pl.pallas_call(
        total_kernel,
        out_shape=[
            jax.ShapeDtypeStruct((1536, D), BF16),
            jax.ShapeDtypeStruct((16, D), F32),
            jax.ShapeDtypeStruct((4 * GROUP, R), BF16),
        ],
        in_specs=[VM] * 8,
        out_specs=[VM] * 3,
        scratch_shapes=[
            pltpu.VMEM((1536, 512), BF16),
            pltpu.VMEM((1536, 512), BF16),
            pltpu.VMEM((1536, 512), BF16),
            pltpu.VMEM((6, QUARTER, 512), BF16),
            pltpu.VMEM((2, QUARTER, 512), F32),
            pltpu.VMEM((2, QUARTER, 512), BF16),
            pltpu.VMEM((6, 48, 512), BF16),
            pltpu.VMEM((96, 512), F32),
            pltpu.VMEM((96, 512), BF16),
            pltpu.VMEM((3, 96, 128), BF16),
            pltpu.VMEM((96, 512), BF16),
            pltpu.VMEM((2, QUARTER, 512), BF16),
            pltpu.VMEM((2, 16, 512), F32),
            pltpu.VMEM((12, 16, 512), F32),
            pltpu.VMEM((4 * GROUP, R), F32),
            pltpu.VMEM((4 * GROUP, R), BF16),
            pltpu.VMEM((3, GROUP, R), BF16),
            pltpu.VMEM((2, GROUP, R), BF16),
            dma((TOTAL_SENDS,)),
            dma((8,)),
            dma((6,)),
            dma((6,)),
            dma((3,)),
            dma((3,)),
            dma((6,)),
            dma((6,)),
            dma((8,)),
            dma((11,)),
            dma((7,)),
        ],
        compiler_params=pltpu.CompilerParams(
            collective_id=2 * LAYERS, has_side_effects=True, vmem_limit_bytes=48 << 20
        ),
        name="total_over_devices",
    )(*spread, *norm, *group, *sums)


def unpack_kernel(spread, norm, group, o_gain, o_shift, o_bqkv, o_aqkv, o_uqkv, o_bout, o_aout, o_uout, o_bin, o_ain, o_uin,
                  o_bdown, o_adown, o_udown):
    layer = pl.program_id(0)
    for j in range(3):
        o_aqkv[j] = spread[j * R:(j + 1) * R, :].astype(F32).T
    o_ain[...] = spread[3 * R:4 * R, :].astype(F32).T
    o_uout[...] = spread[4 * R:5 * R, :].astype(F32)
    o_udown[...] = spread[5 * R:6 * R, :].astype(F32)
    o_gain[...] = norm[0:2, :]
    o_shift[...] = norm[2:4, :]
    o_bout[...] = norm[4:5, :]
    o_bdown[...] = norm[4:5, :]
    for j in range(3):
        o_uqkv[j] = group[j * HD:(j + 1) * HD, :].astype(F32).T
    o_aout[...] = group[192:256, :].astype(F32)
    o_uin[:, 0:128] = group[256:384, :].astype(F32).T
    o_uin[:, 128:256] = group[GROUP:GROUP + 128, :].astype(F32).T
    o_adown[...] = group[GROUP + 128:GROUP + 384, :].astype(F32)
    o_bqkv[...] = jnp.concatenate(
        [group[384:385, 0:64], group[384:385, 64:128], group[392:393, 0:64]], axis=0
    ).astype(F32)
    o_bin[...] = jnp.concatenate([group[GROUP + 384:GROUP + 385, :], group[GROUP + 392:GROUP + 393, :]], axis=1).astype(F32)


def unpack(spread, norm, group):
    shapes = [
        (2, D), (2, D), (3, HD), (3, D, R), (3, R, HD), (1, D), (64, R), (R, D), (1, FF), (D, R), (R, FF),
        (1, D), (FF, R), (R, D),
    ]

    def spec(shape):
        rank = len(shape)
        return pl.BlockSpec((None, *shape), lambda l: (l,) + (0,) * rank)

    def pair(rows, cols):
        return pl.BlockSpec((rows, cols), lambda l: (l, 0))

    return pl.pallas_call(
        unpack_kernel,
        grid=(LAYERS,),
        out_shape=[jax.ShapeDtypeStruct((LAYERS, *shape), F32) for shape in shapes],
        in_specs=[pair(768, D), pair(8, D), pair(2 * GROUP, R)],
        out_specs=[spec(shape) for shape in shapes],
        compiler_params=pltpu.CompilerParams(vmem_limit_bytes=48 << 20),
        name="unpack",
    )(spread, norm, group)


def body(x, dy, lengths, gain, shift, w_qkv, b_qkv, a_qkv, u_qkv, w_out, b_out, a_out, u_out,
         w_in, b_in, a_in, u_in, w_down, b_down, a_down, u_down):
    weights = (w_qkv.reshape(LAYERS, D, 192), a_qkv, u_qkv, w_in, a_in, u_in, w_out, a_out, u_out, w_down, a_down, u_down)
    biases = jnp.concatenate([b_qkv.reshape(LAYERS, 192), jnp.zeros((LAYERS, 64), F32), b_in], axis=1)[:, None, :]
    obias = (b_out + b_down)[:, None, :]
    kept = []
    stream = x
    for layer in range(LAYERS):
        nxt, *saved = forward(layer, lengths, stream, gain, shift, biases, obias, weights)
        if layer == 0:
            tabs, first = saved[-2:]
        kept.append((stream, saved[:-2]))
        stream = nxt
    grad = dy
    spread, norm, group, sums = ([None] * LAYERS for _ in range(4))
    for layer in reversed(range(LAYERS)):
        layer_in, saved = kept[layer]
        grad, spread[layer], norm[layer], group[layer], sums[layer] = backward(
            layer, grad, layer_in, saved, gain, shift, tabs, first, (a_qkv, a_in, u_in, a_out, u_out, a_down, u_down)
        )
    (g_gain, g_shift, g_bqkv, g_aqkv, g_uqkv, g_bout, g_aout, g_uout, g_bin, g_ain, g_uin, g_bdown, g_adown, g_udown) = unpack(
        *total_over_devices(spread, norm, group, sums)
    )
    return (
        stream,
        grad,
        g_gain,
        g_shift,
        g_bqkv,
        g_aqkv,
        g_uqkv,
        g_bout[:, 0],
        g_aout,
        g_uout,
        g_bin[:, 0],
        g_ain,
        g_uin,
        g_bdown[:, 0],
        g_adown,
        g_udown,
    )


def solution(mesh):
    torus = Mesh(mesh.devices.reshape(2, 4, 4, 2, 2), ALL)
    return jax.shard_map(
        body,
        mesh=torus,
        in_specs=(
            P(ALL, None),
            P(ALL, None),
            P(DP, None),
            P(),
            P(),
            P(None, None, None, MP),
            P(None, None, MP),
            P(),
            P(None, None, None, MP),
            P(None, MP, None),
            P(),
            P(None, MP, None),
            P(),
            P(None, None, MP),
            P(None, MP),
            P(),
            P(None, None, MP),
            P(None, MP, None),
            P(),
            P(None, MP, None),
            P(),
        ),
        out_specs=(
            P(ALL, None),
            P(ALL, None),
            P(),
            P(),
            P(None, None, MP),
            P(),
            P(None, None, None, MP),
            P(),
            P(None, MP, None),
            P(),
            P(None, MP),
            P(),
            P(None, None, MP),
            P(),
            P(None, MP, None),
            P(),
        ),
        check_vma=False,
    )
```

```python
import functools
import math

import jax
import jax.numpy as jnp
from jax import lax
from jax.experimental import pallas as pl
from jax.experimental.pallas import tpu as pltpu
from jax.sharding import Mesh
from jax.sharding import PartitionSpec as P

HD = 64
ROT = 16
LAYERS = 2
EPS = 1e-05
FILL = -1000000000.0
MP = ("z", "yh", "c")
DP = ("yl", "x")
ALL = ("yl", "x", "z", "yh", "c")
MESH = pl.DeviceIdType.MESH

D = 1024
T = 2048
OWN = 128
BLK = 256
NB = T // BLK
WIN = 5 * BLK
NQ = 256
FF = 256
NIN = NQ + FF
NOUT = 128 + FF
R = 128
F32 = jnp.float32
BF16 = jnp.bfloat16
HIGH = lax.Precision.HIGHEST

NN = (((1,), (0,)), ((), ()))
NT = (((1,), (1,)), ((), ()))
TN = (((0,), (0,)), ((), ()))


def mm(a, b, dims=NN, precision=None):
    return lax.dot_general(a, b, dims, precision=precision, preferred_element_type=F32)


def split_bf16(a):
    high = a.astype(BF16)
    return high, (a - high.astype(F32)).astype(BF16)


def mm3(a, b, dims=NN):
    ah, al = split_bf16(a)
    bh, bl = split_bf16(b)
    return mm(ah, bh, dims) + (mm(al, bh, dims) + mm(ah, bl, dims))


def rows_of(ref, start, count):
    return ref.at[pl.ds(start if isinstance(start, int) else pl.multiple_of(start, count), count)]


class Place:
    def __init__(self):
        self.z, self.h, self.c = (lax.axis_index(a) for a in MP)
        self.up = {"z": lax.rem(self.z + 1, 4)}
        self.dn = {"z": lax.rem(self.z + 3, 4)}
        self.yy = {"yh": 1 - self.h}
        self.sib = {"c": 1 - self.c}

    def block(self, dz, dh):
        return lax.rem(self.z + dz, 4) * 2 + lax.rem(self.h + dh, 2)

    def shard(self, dz, dh, dc):
        return self.block(dz, dh) * 2 + lax.rem(self.c + dc, 2)

    def meet(self, wide=False):
        peers = [self.up, self.dn, self.yy, self.sib]
        if wide:
            at = Chips()
            peers = [at.sib] + [at.along(a, d) for a in ("x", "z") for d in (1, 2, 3)] + [at.y_peer(d) for d in (1, 2, 3)]
        barrier = pltpu.get_barrier_semaphore()
        for peer in peers:
            pl.semaphore_signal(barrier, inc=1, device_id=peer, device_id_type=MESH)
        pl.semaphore_wait(barrier, len(peers))


def entry(values, i):
    total = values[0]
    for k in range(1, len(values)):
        if values[k] != values[k - 1]:
            total = total + (values[k] - values[k - 1]) * lax.div(i + (len(values) - k), len(values))
    return total


class Sender:
    def __init__(self, sems, partner):
        self.sems = sems
        self.partner = partner
        self.live = []

    def copy(self, src, dst, send_sem, recv_sem, peer):
        return pltpu.make_async_remote_copy(
            src_ref=src, dst_ref=dst, send_sem=send_sem, recv_sem=recv_sem, device_id=peer, device_id_type=MESH
        )

    def send(self, src, dst, peer, recv_sem, like=None):
        self.copy(src, dst, self.sems.at[len(self.live)], recv_sem, peer).start()
        self.live.append(src if like is None else like)

    def got(self, ref, sem):
        self.copy(ref, ref, self.sems.at[0], sem, self.partner).wait_recv()

    def finish(self):
        for k, like in enumerate(self.live):
            self.copy(like, like, self.sems.at[k], self.sems.at[k], self.partner).wait_send()


HALF = OWN // 2
QUART = OWN // 4
GATHER_SENDS = 32
GATHER_SEMS = [pltpu.SemaphoreType.DMA((17,)), pltpu.SemaphoreType.DMA((16,))]


def gather(me, out, buf, direct, cross, compute, before, amid, extra=None):
    def part(dz, dh, dc, k):
        return rows_of(buf, me.shard(dz, dh, dc) * OWN + k * HALF, HALF)

    def sem(sems, dz, dh, k):
        return sems.at[(dz * 2 + dh) * 2 + k]

    half, fourth = rows_of(buf, 0, HALF), rows_of(buf, 0, QUART)

    def send(dz, dh, k, peer, tz, th):
        ref = part(dz, dh, 0, k)
        out.send(ref, ref, peer, sem(direct, tz, th, k), half)

    def over(dz, dh, k):
        ref = part(dz, dh, 0, k)
        out.send(ref, ref, me.sib, sem(cross, dz, dh, k), half)

    def got(dz, dh, k):
        out.got(part(dz, dh, 0, k), sem(direct, dz, dh, k))

    def quarter(dz, k):
        return rows_of(buf, me.shard(dz, 0, 0) * OWN + HALF + k * QUART, QUART)

    send(0, 0, 1, me.up, 3, 0)
    send(0, 0, 1, me.dn, 1, 0)
    send(0, 0, 0, me.yy, 0, 1)
    send(0, 0, 0, me.up, 3, 0)
    send(0, 0, 0, me.dn, 1, 0)
    send(0, 0, 1, me.yy, 0, 1)
    over(0, 0, 0)
    over(0, 0, 1)
    before()
    got(3, 0, 1)
    out.send(quarter(3, 0), quarter(3, 0), me.up, sem(direct, 2, 0, 1), fourth)
    got(1, 0, 1)
    out.send(quarter(1, 1), quarter(1, 1), me.dn, direct.at[16], fourth)
    got(0, 1, 0)
    send(0, 1, 0, me.dn, 1, 1)
    send(0, 1, 0, me.up, 3, 1)
    send(3, 0, 1, me.yy, 3, 1)
    send(1, 0, 1, me.yy, 1, 1)
    over(3, 0, 1)
    over(1, 0, 1)
    over(0, 1, 0)
    got(3, 0, 0)
    send(3, 0, 0, me.up, 2, 0)
    over(3, 0, 0)
    got(1, 0, 0)
    over(1, 0, 0)
    out.got(quarter(2, 0), sem(direct, 2, 0, 1))
    out.got(quarter(2, 1), direct.at[16])
    send(2, 0, 1, me.yy, 2, 1)
    over(2, 0, 1)
    got(0, 1, 1)
    over(0, 1, 1)
    amid()

    def onward():
        got(1, 1, 0)
        send(1, 1, 0, me.dn, 2, 1)
        over(1, 1, 0)

    def late(pairs):
        for dz, dh, k in pairs:
            got(dz, dh, k)
            over(dz, dh, k)

    order = ((0, 0), (3, 0), (1, 0), (0, 1), (2, 0), (3, 1), (1, 1), (2, 1))
    steps = {
        1: onward,
        3: lambda: late(((3, 1, 0), (2, 0, 0))),
        4: lambda: late(((3, 1, 1), (1, 1, 1))),
        7: lambda: late(((2, 1, 0), (2, 1, 1))),
    }

    def visit(i, _):
        for at, step in [*steps.items(), *(extra or {}).items()]:
            pl.when(i == at)(step)
        dz, dh = (entry([pair[j] for pair in order], i) for j in range(2))
        for k in range(2):
            out.got(part(dz, dh, 1, k), sem(cross, dz, dh, k))
        compute(dz, dh)
        return 0

    lax.fori_loop(0, 8, visit, 0)


SCATTER_SENDS = 16
SCATTER_SCRATCH = [
    pltpu.VMEM((8 * OWN, D), F32),
    pltpu.VMEM((8 * OWN, D), BF16),
    pltpu.VMEM((8 * OWN, D), BF16),
    pltpu.VMEM((8 * OWN, D), BF16),
    pltpu.VMEM((2 * HALF, D), BF16),
    pltpu.VMEM((4 * HALF, D), BF16),
    pltpu.VMEM((HALF, D), BF16),
    pltpu.VMEM((4 * HALF, D), BF16),
    pltpu.VMEM((2 * QUART, D), BF16),
    pltpu.VMEM((2 * HALF, D), BF16),
    pltpu.SemaphoreType.DMA((8,)),
    pltpu.SemaphoreType.DMA((8,)),
    pltpu.SemaphoreType.DMA((2,)),
    pltpu.SemaphoreType.DMA((4,)),
    pltpu.SemaphoreType.DMA((1,)),
    pltpu.SemaphoreType.DMA((4,)),
    pltpu.SemaphoreType.DMA((2,)),
    pltpu.SemaphoreType.DMA((2,)),
]


def scatter(me, out, bufs, compute, between, finish, extra=None):
    (own, other, cross, sums, via, ring, last, pair, via2, ring2,
     s_over, s_cross, s_via, s_ring, s_last, s_pair, s_via2, s_ring2) = bufs

    def give(dz, dh):
        i = dz * 2 + dh

        at = pl.ds(pl.multiple_of(i * OWN, OWN), OWN)

        def put(dc, terms):
            if dc == 0:
                own[at, :] = terms
            else:
                other[at, :] = terms.astype(BF16)

        compute(dz, dh, put)
        rows = rows_of(other, i * OWN, OWN)
        out.copy(rows, rows_of(cross, i * OWN, OWN), s_over.at[i], s_cross.at[i], me.sib).start()

    def wait_cross(dz, dh):
        i = dz * 2 + dh
        out.got(rows_of(cross, i * OWN, OWN), s_cross.at[i])

    def both(dz, dh, start, rows):
        here = pl.ds((dz * 2 + dh) * OWN + start, rows)
        return own[here, :] + cross[here, :].astype(F32)

    def arrived(buf, sems, i, rows):
        ref = rows_of(buf, i * rows, rows)
        out.got(ref, sems.at[i])
        return ref[...].astype(F32)

    def pass_to(dz, dh, start, rows, value, buf, sems, i, peer):
        at = (dz * 2 + dh) * OWN + start
        sums[pl.ds(at, rows), :] = value.astype(BF16)
        out.send(rows_of(sums, at, rows), rows_of(buf, i * rows, rows), peer, sems.at[i], rows_of(sums, 0, rows))

    def first(dz, dh):
        return both(dz, dh, 0, HALF)

    def to_partner(dz):
        pass_to(dz, 1, HALF, HALF, both(dz, 1, HALF, HALF), pair, s_pair, dz, me.yy)

    def second(dz):
        return both(dz, 0, HALF, HALF) + arrived(pair, s_pair, dz, HALF)

    def start_far():
        wait_cross(2, 1)
        pass_to(2, 1, 0, HALF, first(2, 1), via, s_via, 1, me.dn)
        to_partner(2)
        wait_cross(2, 0)
        pass_to(2, 0, 0, HALF, first(2, 0), via, s_via, 0, me.up)

    def start_near():
        wait_cross(1, 1)
        pass_to(1, 1, 0, HALF, first(1, 1), ring, s_ring, 1, me.up)
        to_partner(1)
        wait_cross(3, 0)
        pass_to(3, 0, 0, HALF, first(3, 0), ring, s_ring, 2, me.dn)

    def partner_three():
        wait_cross(3, 1)
        to_partner(3)

    def far_seconds():
        wait_cross(1, 0)
        own[pl.ds(4 * OWN + HALF, HALF), :] = second(2)
        for k, peer in ((0, me.up), (1, me.dn)):
            value = own[pl.ds(4 * OWN + HALF + k * QUART, QUART), :]
            pass_to(2, 0, HALF + k * QUART, QUART, value, via2, s_via2, k, peer)

    def onward():
        wait_cross(0, 1)
        to_partner(0)
        pass_to(3, 1, 0, HALF, first(3, 1) + arrived(via, s_via, 1, HALF), ring, s_ring, 3, me.dn)
        pass_to(1, 0, 0, HALF, first(1, 0) + arrived(via, s_via, 0, HALF), ring, s_ring, 0, me.up)

    order = ((2, 1), (2, 0), (1, 1), (3, 0), (3, 1), (1, 0), (0, 1), (0, 0))
    steps = {1: start_far, 3: start_near, 4: partner_three, 5: far_seconds, 6: onward}

    def visit(i, _):
        give(*(entry([pair[j] for pair in order], i) for j in range(2)))
        for at, step in [*steps.items(), *(extra or {}).items()]:
            pl.when(i == at)(step)
        return 0

    lax.fori_loop(0, 8, visit, 0)
    between[0]()
    for dz, k, peer in ((1, 0, me.up), (3, 1, me.dn)):
        mine = pl.ds(dz * 2 * OWN + HALF, HALF)
        own[mine, :] = second(dz)
        own[pl.ds(dz * 2 * OWN + HALF + k * QUART, QUART), :] += arrived(via2, s_via2, k, QUART)
        pass_to(dz, 0, HALF, HALF, own[mine, :], ring2, s_ring2, k, peer)
    between[1]()
    total = first(0, 1) + arrived(ring, s_ring, 1, HALF) + arrived(ring, s_ring, 3, HALF)
    pass_to(0, 1, 0, HALF, total, last, s_last, 0, me.yy)
    wait_cross(0, 0)
    between[2]()
    finish(HALF, HALF, second(0) + arrived(ring2, s_ring2, 0, HALF) + arrived(ring2, s_ring2, 1, HALF))
    total = first(0, 0) + arrived(ring, s_ring, 0, HALF) + arrived(ring, s_ring, 2, HALF)
    finish(0, HALF, total + arrived(last, s_last, 0, HALF))
    for i in range(8):
        rows = rows_of(other, i * OWN, OWN)
        out.copy(rows, rows, s_over.at[i], s_cross.at[i], me.sib).wait_send()


def gelu_parts(h):
    cdf = 0.5 * (1.0 + lax.erf(h * (2.0**-0.5)))
    return cdf


def lane_roll(a, shift):
    return pltpu.roll(a, shift % 128, 1)


def normalized(x):
    mean = jnp.mean(x, axis=1, keepdims=True)
    centered = x - mean
    scale = lax.rsqrt(jnp.mean(centered * centered, axis=1, keepdims=True) + EPS)
    return centered * scale, scale


class Loads:
    def __init__(self, sems):
        self.sems = sems
        self.count = 0

    def start(self, src, dst):
        copy = pltpu.make_async_copy(src, dst, self.sems.at[self.count])
        self.count += 1
        copy.start()
        return copy


def rotary_tables(lens, tabs, first_row, first, angles):
    token = lax.broadcasted_iota(jnp.int32, (8, T), 1)
    begin = jnp.zeros((8, T), jnp.int32)
    end = 0
    for i in range(3):
        end = end + lens[0, i]
        begin = jnp.where(token >= end, end, begin)
    first_row[...] = begin
    step = lax.broadcasted_iota(jnp.int32, (8, T), 0).astype(F32)
    angle = (token - begin).astype(F32) * jnp.exp(step * (-2.0 * math.log(10000.0) / ROT))
    angles[0:8, :] = jnp.cos(angle)
    angles[8:16, :] = jnp.sin(angle)

    def turn(i, _):
        at = pl.ds(pl.multiple_of(i * BLK, BLK), BLK)
        cos, sin = angles[0:8, at], angles[8:16, at]
        none = jnp.zeros((HD - ROT, BLK), F32)
        for k, head in enumerate(((cos, cos, none + 1.0), (-sin, sin, none))):
            tabs[k, at, :] = jnp.concatenate(head + head, axis=0).T
        first[at, :] = jnp.broadcast_to(first_row[0:1, at].astype(F32), (128, BLK)).T.astype(jnp.int32)
        return 0

    lax.fori_loop(0, NB, turn, 0)


def forward_kernel(layer, lens, x_ref, gains_ref, shifts_ref, b_qkv, b_in, b_out, b_down,
                   wqkv_h, aqkv_h, uqkv_h, win_h, ain_h, uin_h, wout_h, aout_h, uout_h, wdown_h, adown_h, udown_h, *refs):
    (o_x, o_xh, o_qkv, o_ho, o_out, o_lse, o_kt, o_wint, o_wout, o_tabs, o_first,
     xh, qkv, ho, ou, out_t, kt, scores, probs, win, wint, bias, wout, tabs, first, angles,
     wqkv, aqkv, uqkv, w_in, ain, uin, w_out, aout, uout, wdown, adown, udown,
     load_sems, send_sems, g_direct, g_cross, *scat) = refs
    gains, shifts = gains_ref.at[layer], shifts_ref.at[layer]
    me = Place()
    loads = Loads(load_sems)
    ins = [
        loads.start(src.at[layer], dst)
        for src, dst in (
            (wqkv_h, wqkv), (aqkv_h, aqkv), (uqkv_h, uqkv), (win_h, w_in), (ain_h, ain), (uin_h, uin),
            (wout_h, w_out), (aout_h, aout), (uout_h, uout), (wdown_h, wdown), (adown_h, adown), (udown_h, udown),
        )
    ]
    out = Sender(send_sems, me.sib)
    me.meet()
    rows_of(xh, me.shard(0, 0, 0) * OWN, OWN)[...] = (
        normalized(x_ref[...])[0] * gains[0:1, :] + shifts[0:1, :]
    ).astype(BF16)
    outs = []

    def before():
        rotary_tables(lens, tabs, o_first, first, angles)
        for copy in ins[:3]:
            copy.wait()
        for j in range(3):
            here = pl.ds(j * HD, HD)
            wint[here, :] = (wqkv[here, :].astype(F32) + mm3(uqkv[j], aqkv[j], NT)).astype(BF16)
            bias[:, here] = b_qkv[j, layer:layer + 1, :]
        wint[3 * HD:NQ, :] = jnp.zeros((NQ - 3 * HD, D), BF16)
        bias[:, 3 * HD:NQ] = jnp.zeros((1, NQ - 3 * HD), F32)
        win[:, 0:NQ] = wint[0:NQ, :].astype(F32).T.astype(BF16)

    def amid():
        for copy in ins[3:]:
            copy.wait()
        ratio = gains[1:2, :] / gains[0:1, :]
        merged = w_in[...].astype(F32) + mm3(ain[...], uin[...])
        low = merged.astype(BF16)
        b_high, b_low = split_bf16(jnp.broadcast_to(shifts[1:2, :] - shifts[0:1, :] * ratio, (8, D)))
        bias[:, NQ:NIN] = b_in[layer:layer + 1, :] + (mm(b_high, low) + mm(b_low, low))[0:1]
        turned = merged.T * ratio
        wint[NQ:NIN, :] = turned.astype(BF16)
        win[:, NQ:NIN] = turned.T.astype(BF16)
        wout[0:64, :] = (w_out[...].astype(F32) + mm3(aout[...], uout[...])).astype(BF16)
        wout[64:128, :] = jnp.zeros((64, D), BF16)
        wout[128:NOUT, :] = (wdown[...].astype(F32) + mm3(adown[...], udown[...])).astype(BF16)
        outs.append(loads.start(wint, o_wint))
        outs.append(loads.start(wout, o_wout))
        if layer == 0:
            outs.append(loads.start(tabs, o_tabs))

    def project(dz, dh):
        at = pl.ds(pl.multiple_of(me.block(dz, dh) * BLK, BLK), BLK)
        rows = xh[at, :]
        pq = mm(rows, win[:, 0:NQ]) + bias[:, 0:NQ]
        qk = pq[:, 0:128]
        lane = lax.broadcasted_iota(jnp.int32, (BLK, 128), 1)
        other = jnp.where(lax.rem(lane, HD) < ROT // 2, lane_roll(qk, -8), lane_roll(qk, 8))
        turned = qk * tabs[0, at, :] + other * tabs[1, at, :]
        qkv[at, 0:128] = jnp.where(lane < HD, turned * HD**-0.5, 0.0).astype(BF16)
        keys = jnp.where(lane < HD, lane_roll(turned, HD), 0.0)
        qkv[at, 128:256] = keys.astype(BF16)
        kt[:, at] = keys.T.astype(BF16)
        qkv[at, 256:384] = pq[:, 128:256].astype(BF16)
        h = mm(rows, win[:, NQ:NIN]) + bias[:, NQ:NIN]
        ho[at, 128:NOUT] = h
        ou[at, 128:NOUT] = (h * gelu_parts(h)).astype(BF16)

    gather(me, out, xh, g_direct, g_cross, project, before, amid)
    outs.extend([loads.start(xh, o_xh), loads.start(qkv, o_qkv), loads.start(kt, o_kt)])

    def attend(dz, dh, put):
        b = me.block(dz, dh)
        at = pl.ds(pl.multiple_of(b * BLK, BLK), BLK)
        key_at = jnp.maximum(b - 4, 0) * BLK
        q = qkv[at, 0:128]
        row = b * BLK + lax.broadcasted_iota(jnp.int32, (BLK, BLK), 0)
        start = jnp.concatenate([first[at, :], first[at, :]], axis=1)
        peak = None
        for j in range(5):
            keys = pl.ds(pl.multiple_of(key_at + j * BLK, BLK), BLK)
            s = mm(q, qkv[keys, 128:256], NT)
            col = key_at + j * BLK + lax.broadcasted_iota(jnp.int32, (BLK, BLK), 1)
            s = jnp.where((col >= start) & (col <= row), s, FILL)
            scores[:, j * BLK:(j + 1) * BLK] = s
            peak = s if peak is None else jnp.maximum(peak, s)
        peak = jnp.max(peak, axis=1, keepdims=True)
        summed = None
        for j in range(5):
            p = jnp.exp(scores[:, j * BLK:(j + 1) * BLK] - peak)
            scores[:, j * BLK:(j + 1) * BLK] = p
            summed = p if summed is None else summed + p
        summed = jnp.sum(summed, axis=1, keepdims=True)
        share = 1.0 / summed
        for j in range(5):
            here = slice(j * BLK, (j + 1) * BLK)
            probs[:, here] = (scores[:, here] * share).astype(BF16)
        o = mm(probs[...], qkv[pl.ds(pl.multiple_of(key_at, BLK), WIN), 256:384])
        ho[at, 0:128] = o
        ou[at, 0:128] = o.astype(BF16)
        lse = jnp.broadcast_to(peak + jnp.log(summed), (BLK, 128)).T
        o_lse[:, at] = lse[0:8, :]
        out_t[:, at] = ou[at, :].astype(F32).T.astype(BF16)
        for dc in range(2):
            put(dc, mm(rows_of(ou, me.shard(dz, dh, dc) * OWN, OWN)[...], wout[...]))

    def store():
        outs.append(loads.start(ho, o_ho))
        outs.append(loads.start(out_t, o_out))

    def nothing():
        pass

    def finish(at, rows, total):
        here = pl.ds(at, rows)
        o_x[here, :] = x_ref[here, :] + total + (b_out[layer:layer + 1, :] + b_down[layer:layer + 1, :])

    scatter(me, out, scat, attend, (store, nothing, nothing), finish)
    for copy in outs:
        copy.wait()
    out.finish()


VM = pl.BlockSpec(memory_space=pltpu.VMEM)
HBM = pl.BlockSpec(memory_space=pl.ANY)


SMEM = pl.BlockSpec(memory_space=pltpu.SMEM)


def forward(layer, lens, x, gains, shifts, biases, weights):
    vmem = pltpu.VMEM
    shapes = [
        jax.ShapeDtypeStruct((OWN, D), F32),
        jax.ShapeDtypeStruct((T, D), BF16),
        jax.ShapeDtypeStruct((T, 384), BF16),
        jax.ShapeDtypeStruct((T, NOUT), F32),
        jax.ShapeDtypeStruct((NOUT, T), BF16),
        jax.ShapeDtypeStruct((8, T), F32),
        jax.ShapeDtypeStruct((128, T), BF16),
        jax.ShapeDtypeStruct((NIN, D), BF16),
        jax.ShapeDtypeStruct((NOUT, D), BF16),
        jax.ShapeDtypeStruct((2, T, 128), F32),
        jax.ShapeDtypeStruct((8, T), jnp.int32),
    ]
    return pl.pallas_call(
        functools.partial(forward_kernel, layer),
        out_shape=shapes,
        in_specs=[SMEM] + [VM] * 7 + [HBM] * 12,
        out_specs=[VM, HBM, HBM, HBM, HBM, VM, HBM, HBM, HBM, HBM, VM],
        scratch_shapes=[
            vmem((T, D), BF16),
            vmem((T, 384), BF16),
            vmem((T, NOUT), F32),
            vmem((T, NOUT), BF16),
            vmem((NOUT, T), BF16),
            vmem((128, T), BF16),
            vmem((BLK, WIN), F32),
            vmem((BLK, WIN), BF16),
            vmem((D, NIN), BF16),
            vmem((NIN, D), BF16),
            vmem((1, NIN), F32),
            vmem((NOUT, D), BF16),
            vmem((2, T, 128), F32),
            vmem((T, 128), jnp.int32),
            vmem((16, T), F32),
            vmem((192, D), BF16),
            vmem((3, D, R), F32),
            vmem((3, HD, R), F32),
            vmem((D, FF), BF16),
            vmem((D, R), F32),
            vmem((R, FF), F32),
            vmem((64, D), BF16),
            vmem((64, R), F32),
            vmem((R, D), F32),
            vmem((FF, D), BF16),
            vmem((FF, R), F32),
            vmem((R, D), F32),
            pltpu.SemaphoreType.DMA((24,)),
            pltpu.SemaphoreType.DMA((GATHER_SENDS + SCATTER_SENDS,)),
            *GATHER_SEMS,
            *SCATTER_SCRATCH,
        ],
        compiler_params=pltpu.CompilerParams(
            collective_id=layer, has_side_effects=True, vmem_limit_bytes=60 << 20
        ),
        name=f"forward_layer{layer}",
    )(lens, x, gains, shifts, *biases, *weights)


def backward_kernel(layer, last, dy_ref, x_ref, xh_h, qkv_h, ho_h, out_h, lse_ref, kt_h, wint_h, wout_h, gains_ref, shifts_ref,
                    tabs_h, first_ref, aqkv_h, uqkv_h, ain_h, bin_h, aout_h, bout_h, adown_h, bdown_h, *refs):
    refs = list(refs)
    take = lambda count: [refs.pop(0) for _ in range(count)]
    if last:
        earlier_h, earlier_norm, earlier_group, earlier_sums = take(4)
        o_dx, o_total, o_norm_total, o_group_total = take(4)
    else:
        o_dx, o_spread, o_norm, o_group, o_sums = take(5)
    (dy, xh, qkv, ho, out_t, kt, dph, low, dph_t, acc, wint, wout, tabs, aqkv, uqkv, ain, bin_, aout, bout, adown, bdown,
     load_sems, send_sems, g_direct, g_cross) = take(25)
    scat = take(len(SCATTER_SCRATCH))
    if last:
        o_spread, o_norm, o_group, o_sums, earlier, total = take(6)
    gains, shifts = gains_ref.at[layer], shifts_ref.at[layer]
    me = Place()
    loads = Loads(load_sems)
    early = [
        loads.start(wout_h, wout),
        loads.start(ho_h, ho),
        loads.start(qkv_h, qkv),
        loads.start(kt_h, kt),
    ]
    late = [
        loads.start(tabs_h, tabs),
        loads.start(wint_h, wint),
        loads.start(xh_h, xh),
        loads.start(out_h, out_t),
        loads.start(aqkv_h.at[layer], aqkv),
        loads.start(uqkv_h.at[layer], uqkv),
        loads.start(ain_h.at[layer], ain),
        loads.start(bin_h.at[layer], bin_),
        loads.start(aout_h.at[layer], aout),
        loads.start(bout_h.at[layer], bout),
        loads.start(adown_h.at[layer], adown),
        loads.start(bdown_h.at[layer], bdown),
    ]
    out = Sender(send_sems, me.sib)
    me.meet(last)
    rows_of(dy, me.shard(0, 0, 0) * OWN, OWN)[...] = dy_ref[...].astype(BF16)

    stages, ends = [], []
    if last:
        at_chip = Chips()
        half = pl.ds(pl.multiple_of(at_chip.c * (D // 2), D // 2), D // 2)
        copy_in = loads.start(earlier_h.at[:, half], earlier)
        n = len(path_scratch(128))
        stages = spread_stages(
            at_chip, out, earlier_h, total.at[pl.ds(768, 768)], (0, 512), "x", "z", take(n), earlier
        )
        for begin, axes in ((0, ("x", "z")), (256, ("z", "x"))):
            ends.append(spread_stages(at_chip, out, o_spread, total.at[pl.ds(0, 768)], (begin, 256), *axes, take(n)))
        ends.append(norm_group_stages(
            at_chip, out, (o_norm, earlier_norm), (o_group, earlier_group), (o_sums, earlier_sums),
            o_norm_total, o_group_total, refs,
        ))

    def stage(i):
        if stages:
            stages[i]()

    def end(i):
        for kind in ends:
            kind[i]()

    def extra(at, i):
        return {at: lambda: stage(i)} if last else None

    def before():
        if last:
            copy_in.wait()
        stage(0)
        acc[...] = jnp.zeros(acc.shape, F32)

    def amid():
        stage(1)
        for copy in early:
            copy.wait()

    def pull(dz, dh):
        b = me.block(dz, dh)
        at = pl.ds(pl.multiple_of(b * BLK, BLK), BLK)
        rows = dy[at, :]
        du = mm(rows, wout[128:NOUT, :], NT)
        h = ho[at, 128:NOUT]
        slope = gelu_parts(h) + h * (jnp.exp(-0.5 * h * h) * (2.0 * math.pi) ** -0.5)
        ho[at, 128:NOUT] = slope * du
        do = mm(rows, wout[0:128, :], NT).astype(BF16)
        drop = jnp.sum((do.astype(F32) * ho[at, 0:128]).T, axis=0, keepdims=True)
        lse = lse_ref[0:1, at]
        start = first_ref[0:1, at]
        q = qkv[at, 0:128]
        key_at = jnp.maximum(b - 5, 0)
        wide = 3 * BLK
        col = b * BLK + lax.broadcasted_iota(jnp.int32, (wide, BLK), 1)

        def step(j, dq):
            key = (key_at + 3 * j) * BLK
            keys = pl.ds(pl.multiple_of(key, BLK), wide)
            s = mm(qkv[keys, 128:256], q, NT)
            row = key + lax.broadcasted_iota(jnp.int32, (wide, BLK), 0)
            p = jnp.where((row >= start) & (row <= col), jnp.exp(s - lse), 0.0)
            dp = mm(qkv[keys, 256:384], do, NT)
            ds = (p * (dp - drop)).astype(BF16)
            acc[keys, 128:256] += mm(p.astype(BF16), do)
            acc[keys, 0:128] += mm(ds, q)
            return dq + mm(kt[:, keys], ds)

        dq = lax.fori_loop(0, (jnp.minimum(b, 5) + 3) // 3, step, jnp.zeros((128, BLK), F32))
        ho[at, 0:128] = dq.T * HD**-0.5

    gather(me, out, dy, g_direct, g_cross, pull, before, amid, extra(4, 2))
    stage(3)
    for copy in late:
        copy.wait()

    def send_back(dz, dh, put):
        b = me.block(dz, dh)
        at = pl.ds(pl.multiple_of(b * BLK, BLK), BLK)
        g = ho[at, 0:128] + lane_roll(acc[at, 0:128], HD)
        side = g * tabs[1, at, :]
        lane = lax.rem(lax.broadcasted_iota(jnp.int32, (BLK, 128), 1), HD)
        side = jnp.where(lane < ROT // 2, lane_roll(side, -8), jnp.where(lane < ROT, lane_roll(side, 8), 0.0))
        turned = g * tabs[0, at, :] + side
        dph[:, 0:128] = turned.astype(BF16)
        dph[:, 128:256] = acc[at, 128:256].astype(BF16)
        dph[:, NQ:NIN] = ho[at, 128:NOUT].astype(BF16)
        rows = dph[...]
        for dc in range(2):
            put(dc, mm(rows_of(dph, lax.rem(me.c + dc, 2) * OWN, OWN)[...], wint[...]))
        dph_t[:, at] = rows.astype(F32).T.astype(BF16)

    def by_columns(piece):
        def visit(i, _):
            piece(pl.ds(pl.multiple_of(i * 256, 256), 256))
            return 0

        lax.fori_loop(0, D // 256, visit, 0)

    def weight_grad(row, at, width):
        here = pl.ds(at, width)
        total = jnp.sum(dph_t[here, :].astype(F32), axis=1, keepdims=True)
        o_sums[:, here] = jnp.broadcast_to(total, (width, 128)).T[0:8, :]

        def piece(cols):
            grad = mm(dph_t[here, :], xh[:, cols])
            weight = wint[here, cols].astype(F32)
            by_gain = jnp.sum(grad * weight, axis=0, keepdims=True)
            by_shift = jnp.sum(total * weight, axis=0, keepdims=True)
            g, b = gains[0:1, cols], shifts[0:1, cols]
            if row == 1:
                ratio = gains[1:2, cols] / g
                by_gain, by_shift = by_gain / ratio, by_shift / ratio
                grad = grad * ratio + total * (shifts[1:2, cols] - b * ratio)
            o_norm[row:row + 1, cols] = (by_gain - b * by_shift) / g
            o_norm[2 + row:3 + row, cols] = by_shift
            low[here, cols] = grad.astype(BF16)

        by_columns(piece)

    def factors_qkv():
        stage(5)
        weight_grad(0, 0, NQ)
        for j in range(3):
            o_spread[j * R:(j + 1) * R, :] = mm(uqkv[j].astype(BF16), low[j * HD:(j + 1) * HD, :], TN).astype(BF16)
            o_group[j * HD:(j + 1) * HD, :] = mm(low[j * HD:(j + 1) * HD, :], aqkv[j].astype(BF16))

    def factors_in():
        weight_grad(1, NQ, FF)
        o_spread[3 * R:4 * R, :] = mm(bin_[...].astype(BF16), low[NQ:NIN, :]).astype(BF16)
        o_group[256:512, :] = mm(low[NQ:NIN, :], ain[...].astype(BF16))

    def factors_out():
        def piece(cols):
            low[0:64, cols] = mm(out_t[0:64, :], dy[:, cols]).astype(BF16)
            low[NQ:NIN, cols] = mm(out_t[128:NOUT, :], dy[:, cols]).astype(BF16)

        by_columns(piece)
        o_spread[4 * R:5 * R, :] = mm(aout[...].astype(BF16), low[0:64, :], TN).astype(BF16)
        o_group[192:256, :] = mm(low[0:64, :], bout[...].astype(BF16), NT)
        o_spread[5 * R:6 * R, :] = mm(adown[...].astype(BF16), low[NQ:NIN, :], TN).astype(BF16)
        o_group[512:768, :] = mm(low[NQ:NIN, :], bdown[...].astype(BF16), NT)
        o_norm[4:5, :] = jnp.sum(dy_ref[...], axis=0, keepdims=True)
        o_norm[5:8, :] = jnp.zeros((3, D), F32)
        stage(6)
        end(0)
        end(1)

    def finish(at, rows, total):
        here = pl.ds(at, rows)
        hat, rstd = normalized(x_ref[here, :])
        total = total * gains[0:1, :]
        mean = jnp.mean(total, axis=1, keepdims=True)
        along = jnp.mean(total * hat, axis=1, keepdims=True)
        o_dx[here, :] = dy_ref[here, :] + rstd * (total - mean - hat * along)

    scatter(me, out, scat, send_back, (factors_qkv, factors_in, factors_out), finish, extra(4, 4))
    if last:
        stage(7)
        for i in range(2, 8):
            end(i)
        store = loads.start(total, o_total)
        out.finish()
        store.wait()
    else:
        out.finish()


def backward(layer, dy, x, saved, gains, shifts, tabs, first, factors, earlier=None):
    last = earlier is not None
    grads = [((6 * R, D), BF16), ((8, D), F32), ((768, R), F32), ((8, NIN), F32)]
    totals = [((LAYERS * 6 * R, D), BF16), ((8 * LAYERS, D), F32), ((4 * GROUP, R), BF16)]
    shapes = [jax.ShapeDtypeStruct(*kind) for kind in [((OWN, D), F32), *(totals if last else grads)]]
    sums = [pltpu.VMEM(*kind) for kind in grads] + [pltpu.VMEM((6 * R, D // 2), BF16), pltpu.VMEM(*totals[0])]
    sums += path_scratch(512) + path_scratch(256) * 2 + NORM_GROUP_SCRATCH
    sends = GATHER_SENDS + SCATTER_SENDS + (3 * PATH_SENDS + NORM_GROUP_SENDS if last else 0)
    return pl.pallas_call(
        functools.partial(backward_kernel, layer, last),
        out_shape=shapes,
        in_specs=[VM, VM, HBM, HBM, HBM, HBM, VM, HBM, HBM, HBM, VM, VM, HBM, VM] + [HBM] * 8 + ([HBM, VM, VM, VM] if last else []),
        out_specs=[VM, HBM, VM, VM] if last else [VM] * 5,
        scratch_shapes=[
            pltpu.VMEM((T, D), BF16),
            pltpu.VMEM((T, D), BF16),
            pltpu.VMEM((T, 384), BF16),
            pltpu.VMEM((T, NOUT), F32),
            pltpu.VMEM((NOUT, T), BF16),
            pltpu.VMEM((128, T), BF16),
            pltpu.VMEM((BLK, NIN), BF16),
            pltpu.VMEM((NIN, D), BF16),
            pltpu.VMEM((NIN, T), BF16),
            pltpu.VMEM((T, 256), F32),
            pltpu.VMEM((NIN, D), BF16),
            pltpu.VMEM((NOUT, D), BF16),
            pltpu.VMEM((2, T, 128), F32),
            pltpu.VMEM((3, D, R), F32),
            pltpu.VMEM((3, HD, R), F32),
            pltpu.VMEM((D, R), F32),
            pltpu.VMEM((R, FF), F32),
            pltpu.VMEM((64, R), F32),
            pltpu.VMEM((R, D), F32),
            pltpu.VMEM((FF, R), F32),
            pltpu.VMEM((R, D), F32),
            pltpu.SemaphoreType.DMA((24,)),
            pltpu.SemaphoreType.DMA((sends,)),
            *GATHER_SEMS,
            *SCATTER_SCRATCH,
            *(sums if last else []),
        ],
        compiler_params=pltpu.CompilerParams(
            collective_id=LAYERS + layer, has_side_effects=True, vmem_limit_bytes=60 << 20
        ),
        name=f"backward_layer{layer}",
    )(dy, x, *saved, gains, shifts, tabs, first, *factors, *(earlier or ()))


QUARTER = 768 // 4
PATH_SENDS = 23


def path_scratch(width):
    dma = pltpu.SemaphoreType.DMA
    return [
        pltpu.VMEM((768, width), BF16),
        pltpu.VMEM((768, width), BF16),
        pltpu.VMEM((3, QUARTER, width), BF16),
        pltpu.VMEM((QUARTER, width), F32),
        pltpu.VMEM((QUARTER, width), BF16),
        pltpu.VMEM((3, 48, width), BF16),
        pltpu.VMEM((4, 48, width), BF16),
        pltpu.VMEM((QUARTER, width), BF16),
        dma((4,)),
        dma((3,)),
        dma((3,)),
        dma((3,)),
        dma((3,)),
        dma((3,)),
        dma((4,)),
    ]


class Chips:
    def __init__(self):
        self.yl, self.x, self.z, self.yh, self.c = (lax.axis_index(a) for a in ALL)
        self.y = self.yh * 2 + self.yl
        self.sib = {"c": 1 - self.c}

    def here(self, axis):
        return {"x": self.x, "z": self.z}[axis]

    def along(self, axis, d):
        return {axis: lax.rem(self.here(axis) + d, 4)}

    def y_peer(self, d):
        there = lax.rem(self.y + d, 4)
        return {"yh": lax.div(there, 2), "yl": lax.rem(there, 2)}

    def quarter(self, axis, d, size):
        return pl.multiple_of(lax.rem(self.here(axis) + d, 4) * size, size)


def spread_stages(at, out, src, dst, lanes, first, second, bufs, own_half=None):
    cross, low, slots1, acc, low2, slots2, along_y, totals, s_cross, s_one, s_two, s_y, s_back2, s_back1, s_backc = bufs
    begin, width = lanes
    mine = pl.ds(pl.multiple_of(at.c * 512 + begin, 128), width)
    theirs = pl.ds(pl.multiple_of((1 - at.c) * 512 + begin, 128), width)

    def rows(d):
        return pl.ds(at.quarter(first, d, QUARTER), QUARTER)

    def part(d):
        return pl.ds(at.quarter(second, d, 48), 48)

    big = dst.at[pl.ds(0, QUARTER), pl.ds(0, width)]
    small = low2.at[pl.ds(0, 48)]

    def over_core():
        for d in (2, 1, 3, 0):
            out.send(src.at[rows(d), theirs], cross.at[rows(d)], at.sib, s_cross.at[d], big)

    def along_first():
        for d in (2, 1, 3, 0):
            out.got(cross.at[rows(d)], s_cross.at[d])
            both = (src[rows(d), mine] if own_half is None else own_half[rows(d), :]).astype(F32)
            both = both + cross[rows(d), :].astype(F32)
            if d == 0:
                acc[...] = both
            else:
                low[rows(d), :] = both.astype(BF16)
                out.send(low.at[rows(d)], slots1.at[d - 1], at.along(first, d), s_one.at[d - 1], low.at[pl.ds(0, QUARTER)])

    def along_second():
        total = acc[...]
        for d in (1, 2, 3):
            out.got(slots1.at[d - 1], s_one.at[d - 1])
            total = total + slots1[d - 1].astype(F32)
        acc[...] = total
        low2[...] = total.astype(BF16)
        for d in (2, 1, 3):
            out.send(low2.at[part(d)], slots2.at[d - 1], at.along(second, d), s_two.at[d - 1], small)

    def along_third():
        total = acc[part(0), :]
        for d in (1, 2, 3):
            out.got(slots2.at[d - 1], s_two.at[d - 1])
            total = total + slots2[d - 1].astype(F32)
        own = along_y.at[at.y]
        own[...] = total.astype(BF16)
        for d in (2, 1, 3):
            out.send(own, own, at.y_peer(d), s_y.at[d - 1], along_y.at[0])

    def back_second():
        for d in (1, 2, 3):
            out.got(along_y.at[lax.rem(at.y + 4 - d, 4)], s_y.at[d - 1])
        term = [along_y[i].astype(F32) for i in range(4)]
        own = totals.at[part(0)]
        own[...] = ((term[0] + term[1]) + (term[2] + term[3])).astype(BF16)
        for d in (2, 1, 3):
            out.send(own, own, at.along(second, d), s_back2.at[d - 1], small)

    def back_first():
        for d in (1, 2, 3):
            out.got(totals.at[part(4 - d)], s_back2.at[d - 1])
        own = dst.at[rows(0), mine]
        own[...] = totals[...]
        for d in (2, 1, 3):
            out.send(own, own, at.along(first, d), s_back1.at[d - 1], big)
        out.send(own, own, at.sib, s_backc.at[0], big)

    def back_core():
        for d in (1, 3, 2):
            own = dst.at[rows(4 - d), mine]
            out.got(own, s_back1.at[d - 1])
            out.send(own, own, at.sib, s_backc.at[d], big)

    def arrive():
        for d in range(4):
            out.got(dst.at[rows(4 - d), theirs], s_backc.at[d])

    return [over_core, along_first, along_second, along_third, back_second, back_first, back_core, arrive]


GROUP = 400


NORM_GROUP_SENDS = 1 + 3 + 3 + 3 + 1 + 3 + 3 + 1
NORM_GROUP_SCRATCH = [
    pltpu.VMEM((2, 16, 512), F32),
    pltpu.VMEM((12, 16, 512), F32),
    pltpu.VMEM((4 * GROUP, R), F32),
    pltpu.VMEM((4 * GROUP, R), BF16),
    pltpu.VMEM((3, GROUP, R), BF16),
    pltpu.VMEM((2, GROUP, R), BF16),
    pltpu.SemaphoreType.DMA((11,)),
    pltpu.SemaphoreType.DMA((7,)),
]


def norm_group_stages(at, out, norms, groups, sums, o_norm, o_group, bufs):
    n_first, n_slots, g_own, g_low, g_slots, g_pair, s_norm, s_group = bufs
    mine = pl.ds(pl.multiple_of(at.c * 512, 512), 512)
    theirs = pl.ds(pl.multiple_of((1 - at.c) * 512, 512), 512)

    def n_stage(stage, value, index, peer_of, base):
        own = n_slots.at[stage * 4 + index]
        own[...] = value
        for d in (1, 2, 3):
            out.send(own, own, peer_of(d), s_norm.at[base + d - 1])

    def n_sum(stage, index, base):
        for d in (1, 2, 3):
            out.got(n_slots.at[stage * 4 + lax.rem(index + 4 - d, 4)], s_norm.at[base + d - 1])
        return (n_slots[stage * 4] + n_slots[stage * 4 + 1]) + (n_slots[stage * 4 + 2] + n_slots[stage * 4 + 3])

    def g_rows(d):
        return pl.ds(at.quarter("x", d, GROUP), GROUP)

    def begin():
        for i, norm in enumerate(norms):
            n_first[0, i * 8:i * 8 + 8, :] = norm[:, theirs]
        out.send(n_first.at[0], n_first.at[1], at.sib, s_norm.at[0])
        for i in range(4):
            group, total, half = groups[i // 2], sums[i // 2], i % 2
            g_own[i * GROUP:i * GROUP + 384, :] = group[half * 384:half * 384 + 384, :]
            for k in range(2):
                rows = pl.ds(i * GROUP + 384 + 8 * k, 8)
                g_own[rows, :] = total[:, half * 256 + 128 * k:half * 256 + 128 * k + 128]
        g_low[...] = g_own[...].astype(BF16)
        for d in (2, 1, 3):
            out.send(g_low.at[g_rows(d)], g_slots.at[d - 1], at.along("x", d), s_group.at[d - 1])

    def along_x():
        out.got(n_first.at[1], s_norm.at[0])
        first = jnp.concatenate([norm[:, mine] for norm in norms], axis=0) + n_first[1]
        n_stage(0, first, at.x, lambda d: at.along("x", d), 1)

    def along_z():
        total = g_own[g_rows(0), :]
        for d in (1, 2, 3):
            out.got(g_slots.at[d - 1], s_group.at[d - 1])
            total = total + g_slots[d - 1].astype(F32)
        g_pair[0] = total.astype(BF16)
        out.send(g_pair.at[0], g_pair.at[1], {"yl": 1 - at.yl}, s_group.at[3])
        n_stage(1, n_sum(0, at.x, 1), at.z, lambda d: at.along("z", d), 4)

    def along_third():
        out.got(g_pair.at[1], s_group.at[3])
        own = o_group.at[g_rows(0)]
        own[...] = (g_pair[0].astype(F32) + g_pair[1].astype(F32)).astype(BF16)
        for d in (1, 2, 3):
            out.send(own, own, at.along("x", d), s_group.at[3 + d])
        n_stage(2, n_sum(1, at.z, 4), at.y, at.y_peer, 7)

    def back_core():
        o_norm[:, mine] = n_sum(2, at.y, 7)
        out.send(o_norm.at[:, mine], o_norm.at[:, mine], at.sib, s_norm.at[10])

    def nothing():
        pass

    def arrive():
        for d in (1, 2, 3):
            out.got(o_group.at[g_rows(4 - d)], s_group.at[3 + d])
        out.got(o_norm.at[:, theirs], s_norm.at[10])

    return [begin, along_x, along_z, along_third, back_core, nothing, nothing, arrive]


def unpack_kernel(spread, norm, group, o_gain, o_shift, o_bqkv, o_aqkv, o_uqkv, o_bout, o_aout, o_uout, o_bin, o_ain, o_uin,
                  o_bdown, o_adown, o_udown):
    layer = pl.program_id(0)
    for j in range(3):
        o_aqkv[j] = spread[j * R:(j + 1) * R, :].astype(F32).T
    o_ain[...] = spread[3 * R:4 * R, :].astype(F32).T
    o_uout[...] = spread[4 * R:5 * R, :].astype(F32)
    o_udown[...] = spread[5 * R:6 * R, :].astype(F32)
    o_gain[...] = norm[0:2, :]
    o_shift[...] = norm[2:4, :]
    o_bout[...] = norm[4:5, :]
    o_bdown[...] = norm[4:5, :]
    for j in range(3):
        o_uqkv[j] = group[j * HD:(j + 1) * HD, :].astype(F32)
    o_aout[...] = group[192:256, :].astype(F32)
    o_uin[:, 0:128] = group[256:384, :].astype(F32).T
    o_uin[:, 128:256] = group[GROUP:GROUP + 128, :].astype(F32).T
    o_adown[...] = group[GROUP + 128:GROUP + 384, :].astype(F32)
    o_bqkv[...] = jnp.concatenate(
        [group[384:385, 0:64], group[384:385, 64:128], group[392:393, 0:64]], axis=0
    ).astype(F32)
    o_bin[...] = jnp.concatenate([group[GROUP + 384:GROUP + 385, :], group[GROUP + 392:GROUP + 393, :]], axis=1).astype(F32)


def unpack(spread, norm, group):
    shapes = [
        (2, D), (2, D), (3, HD), (3, D, R), (3, HD, R), (1, D), (64, R), (R, D), (1, FF), (D, R), (R, FF),
        (1, D), (FF, R), (R, D),
    ]

    def spec(shape):
        rank = len(shape)
        return pl.BlockSpec((None, *shape), lambda l: (l,) + (0,) * rank)

    def pair(rows, cols):
        return pl.BlockSpec((rows, cols), lambda l: (l, 0))

    return pl.pallas_call(
        unpack_kernel,
        grid=(LAYERS,),
        out_shape=[jax.ShapeDtypeStruct((LAYERS, *shape), F32) for shape in shapes],
        in_specs=[pair(768, D), pair(8, D), pair(2 * GROUP, R)],
        out_specs=[spec(shape) for shape in shapes],
        compiler_params=pltpu.CompilerParams(vmem_limit_bytes=48 << 20),
        name="unpack",
    )(spread, norm, group)


def body(x, dy, lengths, gain, shift, w_qkv, b_qkv, a_qkv, u_qkv, w_out, b_out, a_out, u_out,
         w_in, b_in, a_in, u_in, w_down, b_down, a_down, u_down):
    w_qkv = w_qkv.transpose(0, 2, 3, 1).reshape(LAYERS, 3 * HD, D)
    u_qkv = u_qkv.swapaxes(2, 3)
    weights = (w_qkv, a_qkv, u_qkv, w_in, a_in, u_in, w_out, a_out, u_out, w_down, a_down, u_down)
    biases = (b_qkv.swapaxes(0, 1), b_in, b_out, b_down)
    kept = []
    stream = x
    for layer in range(LAYERS):
        nxt, *saved = forward(layer, lengths, stream, gain, shift, biases, weights)
        if layer == 0:
            tabs, first = saved[-2:]
        kept.append((stream, saved[:-2]))
        stream = nxt
    factors = (a_qkv, u_qkv, a_in, u_in, a_out, u_out, a_down, u_down)
    grad, *earlier = backward(1, dy, *kept[1], gain, shift, tabs, first, factors)
    grad, *totals = backward(0, grad, *kept[0], gain, shift, tabs, first, factors, earlier)
    (g_gain, g_shift, g_bqkv, g_aqkv, g_uqkv, g_bout, g_aout, g_uout, g_bin, g_ain, g_uin, g_bdown, g_adown, g_udown) = unpack(
        *totals
    )
    return (
        stream,
        grad,
        g_gain,
        g_shift,
        g_bqkv,
        g_aqkv,
        g_uqkv.swapaxes(2, 3),
        g_bout[:, 0],
        g_aout,
        g_uout,
        g_bin[:, 0],
        g_ain,
        g_uin,
        g_bdown[:, 0],
        g_adown,
        g_udown,
    )


def solution(mesh):
    torus = Mesh(mesh.devices.reshape(2, 4, 4, 2, 2), ALL)
    return jax.shard_map(
        body,
        mesh=torus,
        in_specs=(
            P(ALL, None),
            P(ALL, None),
            P(DP, None),
            P(),
            P(),
            P(None, None, None, MP),
            P(None, None, MP),
            P(),
            P(None, None, None, MP),
            P(None, MP, None),
            P(),
            P(None, MP, None),
            P(),
            P(None, None, MP),
            P(None, MP),
            P(),
            P(None, None, MP),
            P(None, MP, None),
            P(),
            P(None, MP, None),
            P(),
        ),
        out_specs=(
            P(ALL, None),
            P(ALL, None),
            P(),
            P(),
            P(None, None, MP),
            P(),
            P(None, None, None, MP),
            P(),
            P(None, MP, None),
            P(),
            P(None, MP),
            P(),
            P(None, None, MP),
            P(),
            P(None, MP, None),
            P(),
        ),
        check_vma=False,
    )
```

```python
import functools
import math

import jax
import jax.numpy as jnp
from jax import lax
from jax.experimental import pallas as pl
from jax.experimental.pallas import tpu as pltpu
from jax.sharding import Mesh
from jax.sharding import PartitionSpec as P

HD = 64
ROT = 16
LAYERS = 2
EPS = 1e-05
FILL = -1000000000.0
MP = ("z", "yh", "c")
DP = ("yl", "x")
ALL = ("yl", "x", "z", "yh", "c")
MESH = pl.DeviceIdType.MESH

D = 1024
T = 2048
OWN = 128
BLK = 256
NB = T // BLK
WIN = 5 * BLK
NQ = 256
FF = 256
NIN = NQ + FF
NOUT = 128 + FF
R = 128
F32 = jnp.float32
BF16 = jnp.bfloat16
HIGH = lax.Precision.HIGHEST

NN = (((1,), (0,)), ((), ()))
NT = (((1,), (1,)), ((), ()))
TN = (((0,), (0,)), ((), ()))


def mm(a, b, dims=NN, precision=None):
    return lax.dot_general(a, b, dims, precision=precision, preferred_element_type=F32)


def split_bf16(a):
    high = a.astype(BF16)
    return high, (a - high.astype(F32)).astype(BF16)


def mm3(a, b, dims=NN):
    ah, al = split_bf16(a)
    bh, bl = split_bf16(b)
    return mm(ah, bh, dims) + (mm(al, bh, dims) + mm(ah, bl, dims))


def rows_of(ref, start, count):
    return ref.at[pl.ds(start if isinstance(start, int) else pl.multiple_of(start, count), count)]


class Place:
    def __init__(self):
        self.z, self.h, self.c = (lax.axis_index(a) for a in MP)
        self.up = {"z": lax.rem(self.z + 1, 4)}
        self.dn = {"z": lax.rem(self.z + 3, 4)}
        self.yy = {"yh": 1 - self.h}
        self.sib = {"c": 1 - self.c}

    def block(self, dz, dh):
        return lax.rem(self.z + dz, 4) * 2 + lax.rem(self.h + dh, 2)

    def shard(self, dz, dh, dc):
        return self.block(dz, dh) * 2 + lax.rem(self.c + dc, 2)

    def meet(self, wide=False):
        peers = [self.up, self.dn, self.yy, self.sib]
        if wide:
            at = Chips()
            peers = [at.sib] + [at.along(a, d) for a in ("x", "z") for d in (1, 2, 3)] + [at.y_peer(d) for d in (1, 2, 3)]
        barrier = pltpu.get_barrier_semaphore()
        for peer in peers:
            pl.semaphore_signal(barrier, inc=1, device_id=peer, device_id_type=MESH)
        pl.semaphore_wait(barrier, len(peers))


def entry(values, i):
    total = values[0]
    for k in range(1, len(values)):
        if values[k] != values[k - 1]:
            total = total + (values[k] - values[k - 1]) * lax.div(i + (len(values) - k), len(values))
    return total


class Sender:
    def __init__(self, sems, partner):
        self.sems = sems
        self.partner = partner
        self.live = []

    def copy(self, src, dst, send_sem, recv_sem, peer):
        return pltpu.make_async_remote_copy(
            src_ref=src, dst_ref=dst, send_sem=send_sem, recv_sem=recv_sem, device_id=peer, device_id_type=MESH
        )

    def send(self, src, dst, peer, recv_sem, like=None):
        self.copy(src, dst, self.sems.at[len(self.live)], recv_sem, peer).start()
        self.live.append(src if like is None else like)

    def got(self, ref, sem):
        self.copy(ref, ref, self.sems.at[0], sem, self.partner).wait_recv()

    def finish(self):
        for k, like in enumerate(self.live):
            self.copy(like, like, self.sems.at[k], self.sems.at[k], self.partner).wait_send()


HALF = OWN // 2
QUART = OWN // 4
GATHER_SENDS = 32
GATHER_SEMS = [pltpu.SemaphoreType.DMA((17,)), pltpu.SemaphoreType.DMA((16,))]


def gather(me, out, buf, direct, cross, compute, before, amid, extra=None):
    def part(dz, dh, dc, k):
        return rows_of(buf, me.shard(dz, dh, dc) * OWN + k * HALF, HALF)

    def sem(sems, dz, dh, k):
        return sems.at[(dz * 2 + dh) * 2 + k]

    half, fourth = rows_of(buf, 0, HALF), rows_of(buf, 0, QUART)

    def send(dz, dh, k, peer, tz, th):
        ref = part(dz, dh, 0, k)
        out.send(ref, ref, peer, sem(direct, tz, th, k), half)

    def over(dz, dh, k):
        ref = part(dz, dh, 0, k)
        out.send(ref, ref, me.sib, sem(cross, dz, dh, k), half)

    def got(dz, dh, k):
        out.got(part(dz, dh, 0, k), sem(direct, dz, dh, k))

    def quarter(dz, k):
        return rows_of(buf, me.shard(dz, 0, 0) * OWN + HALF + k * QUART, QUART)

    send(0, 0, 1, me.up, 3, 0)
    send(0, 0, 1, me.dn, 1, 0)
    send(0, 0, 0, me.yy, 0, 1)
    send(0, 0, 0, me.up, 3, 0)
    send(0, 0, 0, me.dn, 1, 0)
    send(0, 0, 1, me.yy, 0, 1)
    over(0, 0, 0)
    over(0, 0, 1)
    before()
    got(3, 0, 1)
    out.send(quarter(3, 0), quarter(3, 0), me.up, sem(direct, 2, 0, 1), fourth)
    got(1, 0, 1)
    out.send(quarter(1, 1), quarter(1, 1), me.dn, direct.at[16], fourth)
    got(0, 1, 0)
    send(0, 1, 0, me.dn, 1, 1)
    send(0, 1, 0, me.up, 3, 1)
    send(3, 0, 1, me.yy, 3, 1)
    send(1, 0, 1, me.yy, 1, 1)
    over(3, 0, 1)
    over(1, 0, 1)
    over(0, 1, 0)
    got(3, 0, 0)
    send(3, 0, 0, me.up, 2, 0)
    over(3, 0, 0)
    got(1, 0, 0)
    over(1, 0, 0)
    out.got(quarter(2, 0), sem(direct, 2, 0, 1))
    out.got(quarter(2, 1), direct.at[16])
    send(2, 0, 1, me.yy, 2, 1)
    over(2, 0, 1)
    got(0, 1, 1)
    over(0, 1, 1)
    amid()

    def onward():
        got(1, 1, 0)
        send(1, 1, 0, me.dn, 2, 1)
        over(1, 1, 0)

    def late(pairs):
        for dz, dh, k in pairs:
            got(dz, dh, k)
            over(dz, dh, k)

    order = ((0, 0), (3, 0), (1, 0), (0, 1), (2, 0), (3, 1), (1, 1), (2, 1))
    steps = {
        1: onward,
        3: lambda: late(((3, 1, 0), (2, 0, 0))),
        4: lambda: late(((3, 1, 1), (1, 1, 1))),
        7: lambda: late(((2, 1, 0), (2, 1, 1))),
    }

    def visit(i, _):
        for at, step in [*steps.items(), *(extra or {}).items()]:
            pl.when(i == at)(step)
        dz, dh = (entry([pair[j] for pair in order], i) for j in range(2))
        for k in range(2):
            out.got(part(dz, dh, 1, k), sem(cross, dz, dh, k))
        compute(dz, dh)
        return 0

    lax.fori_loop(0, 8, visit, 0)


SCATTER_SENDS = 16
SCATTER_SCRATCH = [
    pltpu.VMEM((8 * OWN, D), F32),
    pltpu.VMEM((8 * OWN, D), BF16),
    pltpu.VMEM((8 * OWN, D), BF16),
    pltpu.VMEM((8 * OWN, D), BF16),
    pltpu.VMEM((2 * HALF, D), BF16),
    pltpu.VMEM((4 * HALF, D), BF16),
    pltpu.VMEM((HALF, D), BF16),
    pltpu.VMEM((4 * HALF, D), BF16),
    pltpu.VMEM((2 * QUART, D), BF16),
    pltpu.VMEM((2 * HALF, D), BF16),
    pltpu.SemaphoreType.DMA((8,)),
    pltpu.SemaphoreType.DMA((8,)),
    pltpu.SemaphoreType.DMA((2,)),
    pltpu.SemaphoreType.DMA((4,)),
    pltpu.SemaphoreType.DMA((1,)),
    pltpu.SemaphoreType.DMA((4,)),
    pltpu.SemaphoreType.DMA((2,)),
    pltpu.SemaphoreType.DMA((2,)),
]


def scatter(me, out, bufs, compute, between, finish, extra=None, quick=False, tail=None):
    (own, other, cross, sums, via, ring, last, pair, via2, ring2,
     s_over, s_cross, s_via, s_ring, s_last, s_pair, s_via2, s_ring2) = bufs

    def give(dz, dh):
        i = dz * 2 + dh

        at = pl.ds(pl.multiple_of(i * OWN, OWN), OWN)

        def put(dc, terms):
            if dc == 0:
                own[at, :] = terms
            else:
                other[at, :] = terms.astype(BF16)

        compute(dz, dh, put)
        rows = rows_of(other, i * OWN, OWN)
        out.copy(rows, rows_of(cross, i * OWN, OWN), s_over.at[i], s_cross.at[i], me.sib).start()

    def wait_cross(dz, dh):
        i = dz * 2 + dh
        out.got(rows_of(cross, i * OWN, OWN), s_cross.at[i])

    def both(dz, dh, start, rows):
        here = pl.ds((dz * 2 + dh) * OWN + start, rows)
        return own[here, :] + cross[here, :].astype(F32)

    def arrived(buf, sems, i, rows):
        ref = rows_of(buf, i * rows, rows)
        out.got(ref, sems.at[i])
        return ref[...].astype(F32)

    def pass_to(dz, dh, start, rows, value, buf, sems, i, peer):
        at = (dz * 2 + dh) * OWN + start
        sums[pl.ds(at, rows), :] = value.astype(BF16)
        out.send(rows_of(sums, at, rows), rows_of(buf, i * rows, rows), peer, sems.at[i], rows_of(sums, 0, rows))

    def first(dz, dh):
        return both(dz, dh, 0, HALF)

    def to_partner(dz):
        pass_to(dz, 1, HALF, HALF, both(dz, 1, HALF, HALF), pair, s_pair, dz, me.yy)

    def second(dz):
        return both(dz, 0, HALF, HALF) + arrived(pair, s_pair, dz, HALF)

    def start_far():
        wait_cross(2, 1)
        pass_to(2, 1, 0, HALF, first(2, 1), via, s_via, 1, me.dn)
        to_partner(2)
        wait_cross(2, 0)
        pass_to(2, 0, 0, HALF, first(2, 0), via, s_via, 0, me.up)

    def near_others():
        wait_cross(1, 1)
        pass_to(1, 1, 0, HALF, first(1, 1), ring, s_ring, 1, me.up)
        to_partner(1)

    def partner_three():
        wait_cross(3, 1)
        to_partner(3)

    def near_own():
        wait_cross(3, 0)
        pass_to(3, 0, 0, HALF, first(3, 0), ring, s_ring, 2, me.dn)

    def far_seconds():
        own[pl.ds(4 * OWN + HALF, HALF), :] = second(2)
        for k, peer in ((0, me.up), (1, me.dn)):
            value = own[pl.ds(4 * OWN + HALF + k * QUART, QUART), :]
            pass_to(2, 0, HALF + k * QUART, QUART, value, via2, s_via2, k, peer)

    def onward():
        wait_cross(1, 0)
        pass_to(3, 1, 0, HALF, first(3, 1) + arrived(via, s_via, 1, HALF), ring, s_ring, 3, me.dn)
        pass_to(1, 0, 0, HALF, first(1, 0) + arrived(via, s_via, 0, HALF), ring, s_ring, 0, me.up)

    def partner_own():
        wait_cross(0, 1)
        to_partner(0)

    if quick:
        order = ((2, 1), (2, 0), (1, 1), (3, 0), (3, 1), (1, 0), (0, 1), (0, 0))
        steps = [(1, start_far), (3, near_others), (3, near_own), (4, partner_three), (5, far_seconds), (6, partner_own), (6, onward)]
    else:
        order = ((2, 1), (2, 0), (1, 1), (3, 1), (1, 0), (3, 0), (0, 1), (0, 0))
        steps = [(1, start_far), (2, near_others), (3, partner_three), (4, onward), (4, far_seconds), (5, near_own), (6, partner_own)]

    def visit(i, _):
        give(*(entry([pair[j] for pair in order], i) for j in range(2)))
        for at, step in [*steps, *(extra or {}).items()]:
            pl.when(i == at)(step)
        return 0

    lax.fori_loop(0, 8, visit, 0)
    if tail is not None:
        for work in between:
            work()
        between = [lambda: None, lambda: None, tail]
    between[0]()
    for dz, k, peer in ((1, 0, me.up), (3, 1, me.dn)):
        mine = pl.ds(dz * 2 * OWN + HALF, HALF)
        own[mine, :] = second(dz)
        own[pl.ds(dz * 2 * OWN + HALF + k * QUART, QUART), :] += arrived(via2, s_via2, k, QUART)
        pass_to(dz, 0, HALF, HALF, own[mine, :], ring2, s_ring2, k, peer)
    between[1]()
    total = first(0, 1) + arrived(ring, s_ring, 1, HALF) + arrived(ring, s_ring, 3, HALF)
    pass_to(0, 1, 0, HALF, total, last, s_last, 0, me.yy)
    wait_cross(0, 0)
    between[2]()
    finish(HALF, HALF, second(0) + arrived(ring2, s_ring2, 0, HALF) + arrived(ring2, s_ring2, 1, HALF))
    total = first(0, 0) + arrived(ring, s_ring, 0, HALF) + arrived(ring, s_ring, 2, HALF)
    finish(0, HALF, total + arrived(last, s_last, 0, HALF))
    for i in range(8):
        rows = rows_of(other, i * OWN, OWN)
        out.copy(rows, rows, s_over.at[i], s_cross.at[i], me.sib).wait_send()


def gelu_parts(h):
    cdf = 0.5 * (1.0 + lax.erf(h * (2.0**-0.5)))
    return cdf


def lane_roll(a, shift):
    return pltpu.roll(a, shift % 128, 1)


def normalized(x):
    mean = jnp.mean(x, axis=1, keepdims=True)
    centered = x - mean
    scale = lax.rsqrt(jnp.mean(centered * centered, axis=1, keepdims=True) + EPS)
    return centered * scale, scale


class Loads:
    def __init__(self, sems):
        self.sems = sems
        self.count = 0

    def start(self, src, dst):
        copy = pltpu.make_async_copy(src, dst, self.sems.at[self.count])
        self.count += 1
        copy.start()
        return copy


def rotary_tables(lens, tabs, first_row, first, angles):
    token = lax.broadcasted_iota(jnp.int32, (8, T), 1)
    begin = jnp.zeros((8, T), jnp.int32)
    end = 0
    for i in range(3):
        end = end + lens[0, i]
        begin = jnp.where(token >= end, end, begin)
    first_row[...] = begin
    step = lax.broadcasted_iota(jnp.int32, (8, T), 0).astype(F32)
    angle = (token - begin).astype(F32) * jnp.exp(step * (-2.0 * math.log(10000.0) / ROT))
    angles[0:8, :] = jnp.cos(angle)
    angles[8:16, :] = jnp.sin(angle)

    def turn(i, _):
        at = pl.ds(pl.multiple_of(i * BLK, BLK), BLK)
        cos, sin = angles[0:8, at], angles[8:16, at]
        none = jnp.zeros((HD - ROT, BLK), F32)
        for k, head in enumerate(((cos, cos, none + 1.0), (-sin, sin, none))):
            tabs[k, at, :] = jnp.concatenate(head + head, axis=0).T
        first[at, :] = jnp.broadcast_to(first_row[0:1, at].astype(F32), (128, BLK)).T.astype(jnp.int32)
        return 0

    lax.fori_loop(0, NB, turn, 0)


def forward_kernel(layer, lens, x_ref, gains_ref, shifts_ref, b_qkv, b_in, b_out, b_down,
                   wqkv_h, aqkv_h, uqkv_h, win_h, ain_h, uin_h, wout_h, aout_h, uout_h, wdown_h, adown_h, udown_h, *refs):
    (o_x, o_xh, o_qkv, o_ho, o_out, o_lse, o_kt, o_wint, o_wout, o_tabs, o_first,
     xh, qkv, ho, ou, out_t, kt, scores, probs, win, wint, bias, wout, tabs, first, angles,
     wqkv, aqkv, uqkv, w_in, ain, uin, w_out, aout, uout, wdown, adown, udown,
     load_sems, send_sems, g_direct, g_cross, *scat) = refs
    gains, shifts = gains_ref.at[layer], shifts_ref.at[layer]
    me = Place()
    loads = Loads(load_sems)
    ins = [
        loads.start(src.at[layer], dst)
        for src, dst in (
            (wqkv_h, wqkv), (aqkv_h, aqkv), (uqkv_h, uqkv), (win_h, w_in), (ain_h, ain), (uin_h, uin),
            (wout_h, w_out), (aout_h, aout), (uout_h, uout), (wdown_h, wdown), (adown_h, adown), (udown_h, udown),
        )
    ]
    out = Sender(send_sems, me.sib)
    me.meet()
    rows_of(xh, me.shard(0, 0, 0) * OWN, OWN)[...] = (
        normalized(x_ref[...])[0] * gains[0:1, :] + shifts[0:1, :]
    ).astype(BF16)
    outs = []

    def before():
        rotary_tables(lens, tabs, o_first, first, angles)
        for copy in ins[:3]:
            copy.wait()
        for j in range(3):
            here = pl.ds(j * HD, HD)
            wint[here, :] = (wqkv[here, :].astype(F32) + mm3(uqkv[j], aqkv[j], NT)).astype(BF16)
            bias[:, here] = b_qkv[j, layer:layer + 1, :]
        wint[3 * HD:NQ, :] = jnp.zeros((NQ - 3 * HD, D), BF16)
        bias[:, 3 * HD:NQ] = jnp.zeros((1, NQ - 3 * HD), F32)
        win[:, 0:NQ] = wint[0:NQ, :].astype(F32).T.astype(BF16)

    def amid():
        for copy in ins[3:]:
            copy.wait()
        ratio = gains[1:2, :] / gains[0:1, :]
        merged = w_in[...].astype(F32) + mm3(ain[...], uin[...])
        low = merged.astype(BF16)
        b_high, b_low = split_bf16(jnp.broadcast_to(shifts[1:2, :] - shifts[0:1, :] * ratio, (8, D)))
        bias[:, NQ:NIN] = b_in[layer:layer + 1, :] + (mm(b_high, low) + mm(b_low, low))[0:1]
        turned = merged.T * ratio
        wint[NQ:NIN, :] = turned.astype(BF16)
        win[:, NQ:NIN] = turned.T.astype(BF16)
        wout[0:64, :] = (w_out[...].astype(F32) + mm3(aout[...], uout[...])).astype(BF16)
        wout[64:128, :] = jnp.zeros((64, D), BF16)
        wout[128:NOUT, :] = (wdown[...].astype(F32) + mm3(adown[...], udown[...])).astype(BF16)
        outs.append(loads.start(wint, o_wint))
        outs.append(loads.start(wout, o_wout))
        if layer == 0:
            outs.append(loads.start(tabs, o_tabs))

    def project(dz, dh):
        at = pl.ds(pl.multiple_of(me.block(dz, dh) * BLK, BLK), BLK)
        rows = xh[at, :]
        pq = mm(rows, win[:, 0:NQ]) + bias[:, 0:NQ]
        qk = pq[:, 0:128]
        lane = lax.broadcasted_iota(jnp.int32, (BLK, 128), 1)
        other = jnp.where(lax.rem(lane, HD) < ROT // 2, lane_roll(qk, -8), lane_roll(qk, 8))
        turned = qk * tabs[0, at, :] + other * tabs[1, at, :]
        qkv[at, 0:128] = jnp.where(lane < HD, turned * HD**-0.5, 0.0).astype(BF16)
        keys = jnp.where(lane < HD, lane_roll(turned, HD), 0.0)
        qkv[at, 128:256] = keys.astype(BF16)
        kt[:, at] = keys.T.astype(BF16)
        qkv[at, 256:384] = pq[:, 128:256].astype(BF16)
        h = mm(rows, win[:, NQ:NIN]) + bias[:, NQ:NIN]
        ho[at, 128:NOUT] = h
        ou[at, 128:NOUT] = (h * gelu_parts(h)).astype(BF16)

    gather(me, out, xh, g_direct, g_cross, project, before, amid)
    outs.extend([loads.start(xh, o_xh), loads.start(qkv, o_qkv), loads.start(kt, o_kt)])

    def attend(dz, dh, put):
        b = me.block(dz, dh)
        at = pl.ds(pl.multiple_of(b * BLK, BLK), BLK)
        key_at = jnp.maximum(b - 4, 0) * BLK
        q = qkv[at, 0:128]
        row = b * BLK + lax.broadcasted_iota(jnp.int32, (BLK, BLK), 0)
        start = jnp.concatenate([first[at, :], first[at, :]], axis=1)
        peak = None
        for j in range(5):
            keys = pl.ds(pl.multiple_of(key_at + j * BLK, BLK), BLK)
            s = mm(q, qkv[keys, 128:256], NT)
            col = key_at + j * BLK + lax.broadcasted_iota(jnp.int32, (BLK, BLK), 1)
            s = jnp.where((col >= start) & (col <= row), s, FILL)
            scores[:, j * BLK:(j + 1) * BLK] = s
            peak = s if peak is None else jnp.maximum(peak, s)
        peak = jnp.max(peak, axis=1, keepdims=True)
        summed = None
        for j in range(5):
            p = jnp.exp(scores[:, j * BLK:(j + 1) * BLK] - peak)
            probs[:, j * BLK:(j + 1) * BLK] = p.astype(BF16)
            summed = p if summed is None else summed + p
        summed = jnp.sum(summed, axis=1, keepdims=True)
        o = mm(probs[...], qkv[pl.ds(pl.multiple_of(key_at, BLK), WIN), 256:384]) * (1.0 / summed)
        ho[at, 0:128] = o
        ou[at, 0:128] = o.astype(BF16)
        lse = jnp.broadcast_to(peak + jnp.log(summed), (BLK, 128)).T
        o_lse[:, at] = lse[0:8, :]
        out_t[:, at] = ou[at, :].astype(F32).T.astype(BF16)
        for dc in range(2):
            put(dc, mm(rows_of(ou, me.shard(dz, dh, dc) * OWN, OWN)[...], wout[...]))

    def store():
        outs.append(loads.start(ho, o_ho))
        outs.append(loads.start(out_t, o_out))

    def nothing():
        pass

    def finish(at, rows, total):
        here = pl.ds(at, rows)
        o_x[here, :] = x_ref[here, :] + total + (b_out[layer:layer + 1, :] + b_down[layer:layer + 1, :])

    scatter(me, out, scat, attend, (store, nothing, nothing), finish)
    for copy in outs:
        copy.wait()
    out.finish()


VM = pl.BlockSpec(memory_space=pltpu.VMEM)
HBM = pl.BlockSpec(memory_space=pl.ANY)


SMEM = pl.BlockSpec(memory_space=pltpu.SMEM)


def forward(layer, lens, x, gains, shifts, biases, weights):
    vmem = pltpu.VMEM
    shapes = [
        jax.ShapeDtypeStruct((OWN, D), F32),
        jax.ShapeDtypeStruct((T, D), BF16),
        jax.ShapeDtypeStruct((T, 384), BF16),
        jax.ShapeDtypeStruct((T, NOUT), F32),
        jax.ShapeDtypeStruct((NOUT, T), BF16),
        jax.ShapeDtypeStruct((8, T), F32),
        jax.ShapeDtypeStruct((128, T), BF16),
        jax.ShapeDtypeStruct((NIN, D), BF16),
        jax.ShapeDtypeStruct((NOUT, D), BF16),
        jax.ShapeDtypeStruct((2, T, 128), F32),
        jax.ShapeDtypeStruct((8, T), jnp.int32),
    ]
    return pl.pallas_call(
        functools.partial(forward_kernel, layer),
        out_shape=shapes,
        in_specs=[SMEM] + [VM] * 7 + [HBM] * 12,
        out_specs=[VM, HBM, HBM, HBM, HBM, VM, HBM, HBM, HBM, HBM, VM],
        scratch_shapes=[
            vmem((T, D), BF16),
            vmem((T, 384), BF16),
            vmem((T, NOUT), F32),
            vmem((T, NOUT), BF16),
            vmem((NOUT, T), BF16),
            vmem((128, T), BF16),
            vmem((BLK, WIN), F32),
            vmem((BLK, WIN), BF16),
            vmem((D, NIN), BF16),
            vmem((NIN, D), BF16),
            vmem((1, NIN), F32),
            vmem((NOUT, D), BF16),
            vmem((2, T, 128), F32),
            vmem((T, 128), jnp.int32),
            vmem((16, T), F32),
            vmem((192, D), BF16),
            vmem((3, D, R), F32),
            vmem((3, HD, R), F32),
            vmem((D, FF), BF16),
            vmem((D, R), F32),
            vmem((R, FF), F32),
            vmem((64, D), BF16),
            vmem((64, R), F32),
            vmem((R, D), F32),
            vmem((FF, D), BF16),
            vmem((FF, R), F32),
            vmem((R, D), F32),
            pltpu.SemaphoreType.DMA((24,)),
            pltpu.SemaphoreType.DMA((GATHER_SENDS + SCATTER_SENDS,)),
            *GATHER_SEMS,
            *SCATTER_SCRATCH,
        ],
        compiler_params=pltpu.CompilerParams(
            collective_id=layer, has_side_effects=True, vmem_limit_bytes=60 << 20
        ),
        name=f"forward_layer{layer}",
    )(lens, x, gains, shifts, *biases, *weights)


def backward_kernel(layer, last, dy_ref, x_ref, xh_h, qkv_h, ho_h, out_h, lse_ref, kt_h, wint_h, wout_h, gains_ref, shifts_ref,
                    tabs_h, first_ref, aqkv_h, uqkv_h, ain_h, bin_h, aout_h, bout_h, adown_h, bdown_h, *refs):
    refs = list(refs)
    take = lambda count: [refs.pop(0) for _ in range(count)]
    if last:
        earlier_h, earlier_norm, earlier_group, earlier_sums = take(4)
        o_dx, o_total, o_norm_total, o_group_total = take(4)
    else:
        o_dx, o_spread, o_norm, o_group, o_sums = take(5)
    (dy, xh, qkv, ho, out_t, kt, dph, low, dph_t, acc, wint, wout, tabs, aqkv, uqkv, ain, bin_, aout, bout, adown, bdown,
     load_sems, send_sems, g_direct, g_cross) = take(25)
    scat = take(len(SCATTER_SCRATCH))
    if last:
        o_spread, o_norm, o_group, o_sums, earlier, total = take(6)
    gains, shifts = gains_ref.at[layer], shifts_ref.at[layer]
    me = Place()
    loads = Loads(load_sems)
    early = [
        loads.start(wout_h, wout),
        loads.start(ho_h, ho),
        loads.start(qkv_h, qkv),
        loads.start(kt_h, kt),
    ]
    late = [
        loads.start(tabs_h, tabs),
        loads.start(wint_h, wint),
        loads.start(xh_h, xh),
        loads.start(out_h, out_t),
        loads.start(aqkv_h.at[layer], aqkv),
        loads.start(uqkv_h.at[layer], uqkv),
        loads.start(ain_h.at[layer], ain),
        loads.start(bin_h.at[layer], bin_),
        loads.start(aout_h.at[layer], aout),
        loads.start(bout_h.at[layer], bout),
        loads.start(adown_h.at[layer], adown),
        loads.start(bdown_h.at[layer], bdown),
    ]
    out = Sender(send_sems, me.sib)
    me.meet(last)
    rows_of(dy, me.shard(0, 0, 0) * OWN, OWN)[...] = dy_ref[...].astype(BF16)

    stages, ends = [], []
    if last:
        at_chip = Chips()
        half = pl.ds(pl.multiple_of(at_chip.c * (D // 2), D // 2), D // 2)
        copy_in = loads.start(earlier_h.at[:, half], earlier)
        n = len(path_scratch(128))
        stages = spread_stages(
            at_chip, out, earlier_h, total.at[pl.ds(768, 768)], (0, 512), "x", "z", take(n), earlier
        )
        for begin, axes in ((0, ("x", "z")), (256, ("z", "x"))):
            ends.append(spread_stages(at_chip, out, o_spread, total.at[pl.ds(0, 768)], (begin, 256), *axes, take(n)))
        ends.append(norm_group_stages(
            at_chip, out, (o_norm, earlier_norm), (o_group, earlier_group), (o_sums, earlier_sums),
            o_norm_total, o_group_total, refs,
        ))

    def stage(i):
        if stages:
            stages[i]()

    def end(i):
        for kind in ends:
            kind[i]()

    def extra(at, i):
        return {at: lambda: stage(i)} if last else None

    def before():
        if last:
            copy_in.wait()
        stage(0)
        acc[...] = jnp.zeros(acc.shape, F32)

    def amid():
        stage(1)
        for copy in early:
            copy.wait()

    def pull(dz, dh):
        b = me.block(dz, dh)
        at = pl.ds(pl.multiple_of(b * BLK, BLK), BLK)
        rows = dy[at, :]
        du = mm(rows, wout[128:NOUT, :], NT)
        h = ho[at, 128:NOUT]
        slope = gelu_parts(h) + h * (jnp.exp(-0.5 * h * h) * (2.0 * math.pi) ** -0.5)
        ho[at, 128:NOUT] = slope * du
        do = mm(rows, wout[0:128, :], NT).astype(BF16)
        drop = jnp.sum((do.astype(F32) * ho[at, 0:128]).T, axis=0, keepdims=True)
        lse = lse_ref[0:1, at]
        start = first_ref[0:1, at]
        q = qkv[at, 0:128]
        key_at = jnp.maximum(b - 5, 0)
        wide = 3 * BLK
        col = b * BLK + lax.broadcasted_iota(jnp.int32, (wide, BLK), 1)

        def step(j, dq):
            key = (key_at + 3 * j) * BLK
            keys = pl.ds(pl.multiple_of(key, BLK), wide)
            s = mm(qkv[keys, 128:256], q, NT)
            row = key + lax.broadcasted_iota(jnp.int32, (wide, BLK), 0)
            p = jnp.where((row >= start) & (row <= col), jnp.exp(s - lse), 0.0)
            dp = mm(qkv[keys, 256:384], do, NT)
            ds = (p * (dp - drop)).astype(BF16)
            acc[keys, 128:256] += mm(p.astype(BF16), do)
            acc[keys, 0:128] += mm(ds, q)
            return dq + mm(kt[:, keys], ds)

        dq = lax.fori_loop(0, (jnp.minimum(b, 5) + 3) // 3, step, jnp.zeros((128, BLK), F32))
        ho[at, 0:128] = dq.T * HD**-0.5

    gather(me, out, dy, g_direct, g_cross, pull, before, amid, extra(4, 2))
    stage(3)
    for copy in late:
        copy.wait()

    def send_back(dz, dh, put):
        b = me.block(dz, dh)
        at = pl.ds(pl.multiple_of(b * BLK, BLK), BLK)
        g = ho[at, 0:128] + lane_roll(acc[at, 0:128], HD)
        side = g * tabs[1, at, :]
        lane = lax.rem(lax.broadcasted_iota(jnp.int32, (BLK, 128), 1), HD)
        side = jnp.where(lane < ROT // 2, lane_roll(side, -8), jnp.where(lane < ROT, lane_roll(side, 8), 0.0))
        turned = g * tabs[0, at, :] + side
        dph[:, 0:128] = turned.astype(BF16)
        dph[:, 128:256] = acc[at, 128:256].astype(BF16)
        dph[:, NQ:NIN] = ho[at, 128:NOUT].astype(BF16)
        rows = dph[...]
        for dc in range(2):
            put(dc, mm(rows_of(dph, lax.rem(me.c + dc, 2) * OWN, OWN)[...], wint[...]))
        dph_t[:, at] = rows.astype(F32).T.astype(BF16)

    def by_columns(piece):
        def visit(i, _):
            piece(pl.ds(pl.multiple_of(i * 256, 256), 256))
            return 0

        lax.fori_loop(0, D // 256, visit, 0)

    def weight_grad(row, at, width):
        here = pl.ds(at, width)
        total = jnp.sum(dph_t[here, :].astype(F32), axis=1, keepdims=True)
        o_sums[:, here] = jnp.broadcast_to(total, (width, 128)).T[0:8, :]

        def piece(cols):
            grad = mm(dph_t[here, :], xh[:, cols])
            weight = wint[here, cols].astype(F32)
            by_gain = jnp.sum(grad * weight, axis=0, keepdims=True)
            by_shift = jnp.sum(total * weight, axis=0, keepdims=True)
            g, b = gains[0:1, cols], shifts[0:1, cols]
            if row == 1:
                ratio = gains[1:2, cols] / g
                by_gain, by_shift = by_gain / ratio, by_shift / ratio
                grad = grad * ratio + total * (shifts[1:2, cols] - b * ratio)
            o_norm[row:row + 1, cols] = (by_gain - b * by_shift) / g
            o_norm[2 + row:3 + row, cols] = by_shift
            low[here, cols] = grad.astype(BF16)

        by_columns(piece)

    def factors_qkv():
        stage(5)
        weight_grad(0, 0, NQ)
        for j in range(3):
            o_spread[j * R:(j + 1) * R, :] = mm(uqkv[j].astype(BF16), low[j * HD:(j + 1) * HD, :], TN).astype(BF16)
            o_group[j * HD:(j + 1) * HD, :] = mm(low[j * HD:(j + 1) * HD, :], aqkv[j].astype(BF16))

    def factors_in():
        weight_grad(1, NQ, FF)
        o_spread[3 * R:4 * R, :] = mm(bin_[...].astype(BF16), low[NQ:NIN, :]).astype(BF16)
        o_group[256:512, :] = mm(low[NQ:NIN, :], ain[...].astype(BF16))

    def factors_out():
        def piece(cols):
            low[0:64, cols] = mm(out_t[0:64, :], dy[:, cols]).astype(BF16)
            low[NQ:NIN, cols] = mm(out_t[128:NOUT, :], dy[:, cols]).astype(BF16)

        by_columns(piece)
        o_spread[4 * R:5 * R, :] = mm(aout[...].astype(BF16), low[0:64, :], TN).astype(BF16)
        o_group[192:256, :] = mm(low[0:64, :], bout[...].astype(BF16), NT)
        o_spread[5 * R:6 * R, :] = mm(adown[...].astype(BF16), low[NQ:NIN, :], TN).astype(BF16)
        o_group[512:768, :] = mm(low[NQ:NIN, :], bdown[...].astype(BF16), NT)
        o_norm[4:5, :] = jnp.sum(dy_ref[...], axis=0, keepdims=True)
        o_norm[5:8, :] = jnp.zeros((3, D), F32)
        stage(6)
        end(0)
        end(1)

    def finish(at, rows, total):
        here = pl.ds(at, rows)
        hat, rstd = normalized(x_ref[here, :])
        total = total * gains[0:1, :]
        mean = jnp.mean(total, axis=1, keepdims=True)
        along = jnp.mean(total * hat, axis=1, keepdims=True)
        o_dx[here, :] = dy_ref[here, :] + rstd * (total - mean - hat * along)

    scatter(me, out, scat, send_back, (factors_qkv, factors_in, factors_out), finish, extra(4, 4), True, (lambda: end(2)) if last else None)
    if last:
        stage(7)
        for i in range(3, 8):
            end(i)
        store = loads.start(total, o_total)
        out.finish()
        store.wait()
    else:
        out.finish()


def backward(layer, dy, x, saved, gains, shifts, tabs, first, factors, earlier=None):
    last = earlier is not None
    grads = [((6 * R, D), BF16), ((8, D), F32), ((768, R), F32), ((8, NIN), F32)]
    totals = [((LAYERS * 6 * R, D), BF16), ((8 * LAYERS, D), F32), ((4 * GROUP, R), BF16)]
    shapes = [jax.ShapeDtypeStruct(*kind) for kind in [((OWN, D), F32), *(totals if last else grads)]]
    sums = [pltpu.VMEM(*kind) for kind in grads] + [pltpu.VMEM((6 * R, D // 2), BF16), pltpu.VMEM(*totals[0])]
    sums += path_scratch(512) + path_scratch(256) * 2 + NORM_GROUP_SCRATCH
    sends = GATHER_SENDS + SCATTER_SENDS + (3 * PATH_SENDS + NORM_GROUP_SENDS if last else 0)
    return pl.pallas_call(
        functools.partial(backward_kernel, layer, last),
        out_shape=shapes,
        in_specs=[VM, VM, HBM, HBM, HBM, HBM, VM, HBM, HBM, HBM, VM, VM, HBM, VM] + [HBM] * 8 + ([HBM, VM, VM, VM] if last else []),
        out_specs=[VM, HBM, VM, VM] if last else [VM] * 5,
        scratch_shapes=[
            pltpu.VMEM((T, D), BF16),
            pltpu.VMEM((T, D), BF16),
            pltpu.VMEM((T, 384), BF16),
            pltpu.VMEM((T, NOUT), F32),
            pltpu.VMEM((NOUT, T), BF16),
            pltpu.VMEM((128, T), BF16),
            pltpu.VMEM((BLK, NIN), BF16),
            pltpu.VMEM((NIN, D), BF16),
            pltpu.VMEM((NIN, T), BF16),
            pltpu.VMEM((T, 256), F32),
            pltpu.VMEM((NIN, D), BF16),
            pltpu.VMEM((NOUT, D), BF16),
            pltpu.VMEM((2, T, 128), F32),
            pltpu.VMEM((3, D, R), F32),
            pltpu.VMEM((3, HD, R), F32),
            pltpu.VMEM((D, R), F32),
            pltpu.VMEM((R, FF), F32),
            pltpu.VMEM((64, R), F32),
            pltpu.VMEM((R, D), F32),
            pltpu.VMEM((FF, R), F32),
            pltpu.VMEM((R, D), F32),
            pltpu.SemaphoreType.DMA((24,)),
            pltpu.SemaphoreType.DMA((sends,)),
            *GATHER_SEMS,
            *SCATTER_SCRATCH,
            *(sums if last else []),
        ],
        compiler_params=pltpu.CompilerParams(
            collective_id=LAYERS + layer, has_side_effects=True, vmem_limit_bytes=60 << 20
        ),
        name=f"backward_layer{layer}",
    )(dy, x, *saved, gains, shifts, tabs, first, *factors, *(earlier or ()))


QUARTER = 768 // 4
PATH_SENDS = 23


def path_scratch(width):
    dma = pltpu.SemaphoreType.DMA
    return [
        pltpu.VMEM((768, width), BF16),
        pltpu.VMEM((768, width), BF16),
        pltpu.VMEM((3, QUARTER, width), BF16),
        pltpu.VMEM((QUARTER, width), F32),
        pltpu.VMEM((QUARTER, width), BF16),
        pltpu.VMEM((3, 48, width), BF16),
        pltpu.VMEM((4, 48, width), BF16),
        pltpu.VMEM((QUARTER, width), BF16),
        dma((4,)),
        dma((3,)),
        dma((3,)),
        dma((3,)),
        dma((3,)),
        dma((3,)),
        dma((4,)),
    ]


class Chips:
    def __init__(self):
        self.yl, self.x, self.z, self.yh, self.c = (lax.axis_index(a) for a in ALL)
        self.y = self.yh * 2 + self.yl
        self.sib = {"c": 1 - self.c}

    def here(self, axis):
        return {"x": self.x, "z": self.z}[axis]

    def along(self, axis, d):
        return {axis: lax.rem(self.here(axis) + d, 4)}

    def y_peer(self, d):
        there = lax.rem(self.y + d, 4)
        return {"yh": lax.div(there, 2), "yl": lax.rem(there, 2)}

    def quarter(self, axis, d, size):
        return pl.multiple_of(lax.rem(self.here(axis) + d, 4) * size, size)


def spread_stages(at, out, src, dst, lanes, first, second, bufs, own_half=None):
    cross, low, slots1, acc, low2, slots2, along_y, totals, s_cross, s_one, s_two, s_y, s_back2, s_back1, s_backc = bufs
    begin, width = lanes
    mine = pl.ds(pl.multiple_of(at.c * 512 + begin, 128), width)
    theirs = pl.ds(pl.multiple_of((1 - at.c) * 512 + begin, 128), width)

    def rows(d):
        return pl.ds(at.quarter(first, d, QUARTER), QUARTER)

    def part(d):
        return pl.ds(at.quarter(second, d, 48), 48)

    big = dst.at[pl.ds(0, QUARTER), pl.ds(0, width)]
    small = low2.at[pl.ds(0, 48)]

    def over_core():
        for d in (2, 1, 3, 0):
            out.send(src.at[rows(d), theirs], cross.at[rows(d)], at.sib, s_cross.at[d], big)

    def along_first():
        for d in (2, 1, 3, 0):
            out.got(cross.at[rows(d)], s_cross.at[d])
            both = (src[rows(d), mine] if own_half is None else own_half[rows(d), :]).astype(F32)
            both = both + cross[rows(d), :].astype(F32)
            if d == 0:
                acc[...] = both
            else:
                low[rows(d), :] = both.astype(BF16)
                out.send(low.at[rows(d)], slots1.at[d - 1], at.along(first, d), s_one.at[d - 1], low.at[pl.ds(0, QUARTER)])

    def along_second():
        total = acc[...]
        for d in (1, 2, 3):
            out.got(slots1.at[d - 1], s_one.at[d - 1])
            total = total + slots1[d - 1].astype(F32)
        acc[...] = total
        low2[...] = total.astype(BF16)
        for d in (2, 1, 3):
            out.send(low2.at[part(d)], slots2.at[d - 1], at.along(second, d), s_two.at[d - 1], small)

    def along_third():
        total = acc[part(0), :]
        for d in (1, 2, 3):
            out.got(slots2.at[d - 1], s_two.at[d - 1])
            total = total + slots2[d - 1].astype(F32)
        own = along_y.at[at.y]
        own[...] = total.astype(BF16)
        for d in (2, 1, 3):
            out.send(own, own, at.y_peer(d), s_y.at[d - 1], along_y.at[0])

    def back_second():
        for d in (1, 2, 3):
            out.got(along_y.at[lax.rem(at.y + 4 - d, 4)], s_y.at[d - 1])
        term = [along_y[i].astype(F32) for i in range(4)]
        own = totals.at[part(0)]
        own[...] = ((term[0] + term[1]) + (term[2] + term[3])).astype(BF16)
        for d in (2, 1, 3):
            out.send(own, own, at.along(second, d), s_back2.at[d - 1], small)

    def back_first():
        for d in (1, 2, 3):
            out.got(totals.at[part(4 - d)], s_back2.at[d - 1])
        own = dst.at[rows(0), mine]
        own[...] = totals[...]
        for d in (2, 1, 3):
            out.send(own, own, at.along(first, d), s_back1.at[d - 1], big)
        out.send(own, own, at.sib, s_backc.at[0], big)

    def back_core():
        for d in (1, 3, 2):
            own = dst.at[rows(4 - d), mine]
            out.got(own, s_back1.at[d - 1])
            out.send(own, own, at.sib, s_backc.at[d], big)

    def arrive():
        for d in range(4):
            out.got(dst.at[rows(4 - d), theirs], s_backc.at[d])

    return [over_core, along_first, along_second, along_third, back_second, back_first, back_core, arrive]


GROUP = 400


NORM_GROUP_SENDS = 1 + 3 + 3 + 3 + 1 + 3 + 3 + 1
NORM_GROUP_SCRATCH = [
    pltpu.VMEM((2, 16, 512), F32),
    pltpu.VMEM((12, 16, 512), F32),
    pltpu.VMEM((4 * GROUP, R), F32),
    pltpu.VMEM((4 * GROUP, R), BF16),
    pltpu.VMEM((3, GROUP, R), BF16),
    pltpu.VMEM((2, GROUP, R), BF16),
    pltpu.SemaphoreType.DMA((11,)),
    pltpu.SemaphoreType.DMA((7,)),
]


def norm_group_stages(at, out, norms, groups, sums, o_norm, o_group, bufs):
    n_first, n_slots, g_own, g_low, g_slots, g_pair, s_norm, s_group = bufs
    mine = pl.ds(pl.multiple_of(at.c * 512, 512), 512)
    theirs = pl.ds(pl.multiple_of((1 - at.c) * 512, 512), 512)

    def n_stage(stage, value, index, peer_of, base):
        own = n_slots.at[stage * 4 + index]
        own[...] = value
        for d in (1, 2, 3):
            out.send(own, own, peer_of(d), s_norm.at[base + d - 1])

    def n_sum(stage, index, base):
        for d in (1, 2, 3):
            out.got(n_slots.at[stage * 4 + lax.rem(index + 4 - d, 4)], s_norm.at[base + d - 1])
        return (n_slots[stage * 4] + n_slots[stage * 4 + 1]) + (n_slots[stage * 4 + 2] + n_slots[stage * 4 + 3])

    def g_rows(d):
        return pl.ds(at.quarter("x", d, GROUP), GROUP)

    def begin():
        for i, norm in enumerate(norms):
            n_first[0, i * 8:i * 8 + 8, :] = norm[:, theirs]
        out.send(n_first.at[0], n_first.at[1], at.sib, s_norm.at[0])
        for i in range(4):
            group, total, half = groups[i // 2], sums[i // 2], i % 2
            g_own[i * GROUP:i * GROUP + 384, :] = group[half * 384:half * 384 + 384, :]
            for k in range(2):
                rows = pl.ds(i * GROUP + 384 + 8 * k, 8)
                g_own[rows, :] = total[:, half * 256 + 128 * k:half * 256 + 128 * k + 128]
        g_low[...] = g_own[...].astype(BF16)
        for d in (2, 1, 3):
            out.send(g_low.at[g_rows(d)], g_slots.at[d - 1], at.along("x", d), s_group.at[d - 1])

    def along_x():
        out.got(n_first.at[1], s_norm.at[0])
        first = jnp.concatenate([norm[:, mine] for norm in norms], axis=0) + n_first[1]
        n_stage(0, first, at.x, lambda d: at.along("x", d), 1)

    def along_z():
        total = g_own[g_rows(0), :]
        for d in (1, 2, 3):
            out.got(g_slots.at[d - 1], s_group.at[d - 1])
            total = total + g_slots[d - 1].astype(F32)
        g_pair[0] = total.astype(BF16)
        out.send(g_pair.at[0], g_pair.at[1], {"yl": 1 - at.yl}, s_group.at[3])
        n_stage(1, n_sum(0, at.x, 1), at.z, lambda d: at.along("z", d), 4)

    def along_third():
        out.got(g_pair.at[1], s_group.at[3])
        own = o_group.at[g_rows(0)]
        own[...] = (g_pair[0].astype(F32) + g_pair[1].astype(F32)).astype(BF16)
        for d in (1, 2, 3):
            out.send(own, own, at.along("x", d), s_group.at[3 + d])
        n_stage(2, n_sum(1, at.z, 4), at.y, at.y_peer, 7)

    def back_core():
        o_norm[:, mine] = n_sum(2, at.y, 7)
        out.send(o_norm.at[:, mine], o_norm.at[:, mine], at.sib, s_norm.at[10])

    def nothing():
        pass

    def arrive():
        for d in (1, 2, 3):
            out.got(o_group.at[g_rows(4 - d)], s_group.at[3 + d])
        out.got(o_norm.at[:, theirs], s_norm.at[10])

    return [begin, along_x, along_z, along_third, back_core, nothing, nothing, arrive]


def unpack_kernel(spread, norm, group, stream, grad, o_stream, o_grad, o_gain, o_shift, o_bqkv, o_aqkv, o_uqkv, o_bout, o_aout, o_uout, o_bin, o_ain, o_uin,
                  o_bdown, o_adown, o_udown):
    o_stream[...] = stream[...]
    o_grad[...] = grad[...]
    for j in range(3):
        o_aqkv[j] = spread[j * R:(j + 1) * R, :].astype(F32).T
    o_ain[...] = spread[3 * R:4 * R, :].astype(F32).T
    o_uout[...] = spread[4 * R:5 * R, :].astype(F32)
    o_udown[...] = spread[5 * R:6 * R, :].astype(F32)
    o_gain[...] = norm[0:2, :]
    o_shift[...] = norm[2:4, :]
    for j in range(3):
        o_uqkv[j] = group[j * HD:(j + 1) * HD, :].astype(F32)
    o_aout[...] = group[192:256, :].astype(F32)
    o_uin[:, 0:128] = group[256:384, :].astype(F32).T
    o_uin[:, 128:256] = group[GROUP:GROUP + 128, :].astype(F32).T
    o_adown[...] = group[GROUP + 128:GROUP + 384, :].astype(F32)
    query_key, value = group[384:385, :].astype(F32), group[392:393, :].astype(F32)
    hidden = [group[GROUP + 384 + 8 * k:GROUP + 385 + 8 * k, :].astype(F32) for k in range(2)]

    def small(layer):
        row = slice(layer, layer + 1)
        o_bout[row, :] = norm[4:5, :]
        o_bdown[row, :] = norm[4:5, :]
        o_bqkv[0, row, :] = query_key[:, 0:HD]
        o_bqkv[1, row, :] = query_key[:, HD:2 * HD]
        o_bqkv[2, row, :] = value[:, 0:HD]
        o_bin[row, 0:128] = hidden[0]
        o_bin[row, 128:256] = hidden[1]

    for layer in range(LAYERS):
        pl.when(pl.program_id(0) == layer)(functools.partial(small, layer))


def unpack(spread, norm, group, stream, grad):
    by_layer = {
        "gain": (2, D), "shift": (2, D), "aqkv": (3, D, R), "uqkv": (3, HD, R), "aout": (64, R), "uout": (R, D),
        "ain": (D, R), "uin": (R, FF), "adown": (FF, R), "udown": (R, D),
    }
    whole = {"bqkv": (3, LAYERS, HD), "bout": (LAYERS, D), "bin": (LAYERS, FF), "bdown": (LAYERS, D)}
    names = ["gain", "shift", "bqkv", "aqkv", "uqkv", "bout", "aout", "uout", "bin", "ain", "uin", "bdown", "adown", "udown"]

    def pair(rows, cols):
        return pl.BlockSpec((rows, cols), lambda l: (l, 0))

    shapes, specs = [(OWN, D)] * 2, [pair(OWN // 2, D)] * 2
    for name in names:
        if name in whole:
            shape, rank = whole[name], len(whole[name])
            shapes.append(shape)
            specs.append(pl.BlockSpec(shape, lambda l, rank=rank: (0,) * rank))
        else:
            shape, rank = by_layer[name], len(by_layer[name])
            shapes.append((LAYERS, *shape))
            specs.append(pl.BlockSpec((None, *shape), lambda l, rank=rank: (l,) + (0,) * rank))
    return pl.pallas_call(
        unpack_kernel,
        grid=(LAYERS,),
        out_shape=[jax.ShapeDtypeStruct(shape, F32) for shape in shapes],
        in_specs=[pair(768, D), pair(8, D), pair(2 * GROUP, R), pair(OWN // 2, D), pair(OWN // 2, D)],
        out_specs=specs,
        compiler_params=pltpu.CompilerParams(vmem_limit_bytes=60 << 20),
        name="unpack",
    )(spread, norm, group, stream, grad)


def body(x, dy, lengths, gain, shift, w_qkv, b_qkv, a_qkv, u_qkv, w_out, b_out, a_out, u_out,
         w_in, b_in, a_in, u_in, w_down, b_down, a_down, u_down):
    w_qkv = w_qkv.transpose(0, 2, 3, 1).reshape(LAYERS, 3 * HD, D)
    u_qkv = u_qkv.swapaxes(2, 3)
    weights = (w_qkv, a_qkv, u_qkv, w_in, a_in, u_in, w_out, a_out, u_out, w_down, a_down, u_down)
    biases = (b_qkv.swapaxes(0, 1), b_in, b_out, b_down)
    kept = []
    stream = x
    for layer in range(LAYERS):
        nxt, *saved = forward(layer, lengths, stream, gain, shift, biases, weights)
        if layer == 0:
            tabs, first = saved[-2:]
        kept.append((stream, saved[:-2]))
        stream = nxt
    factors = (a_qkv, u_qkv, a_in, u_in, a_out, u_out, a_down, u_down)
    grad, *earlier = backward(1, dy, *kept[1], gain, shift, tabs, first, factors)
    grad, *totals = backward(0, grad, *kept[0], gain, shift, tabs, first, factors, earlier)
    (stream, grad, g_gain, g_shift, g_bqkv, g_aqkv, g_uqkv, g_bout, g_aout, g_uout, g_bin, g_ain, g_uin, g_bdown, g_adown, g_udown) = unpack(
        *totals, stream, grad
    )
    return (
        stream,
        grad,
        g_gain,
        g_shift,
        g_bqkv.swapaxes(0, 1),
        g_aqkv,
        g_uqkv.swapaxes(2, 3),
        g_bout,
        g_aout,
        g_uout,
        g_bin,
        g_ain,
        g_uin,
        g_bdown,
        g_adown,
        g_udown,
    )


def solution(mesh):
    torus = Mesh(mesh.devices.reshape(2, 4, 4, 2, 2), ALL)
    return jax.shard_map(
        body,
        mesh=torus,
        in_specs=(
            P(ALL, None),
            P(ALL, None),
            P(DP, None),
            P(),
            P(),
            P(None, None, None, MP),
            P(None, None, MP),
            P(),
            P(None, None, None, MP),
            P(None, MP, None),
            P(),
            P(None, MP, None),
            P(),
            P(None, None, MP),
            P(None, MP),
            P(),
            P(None, None, MP),
            P(None, MP, None),
            P(),
            P(None, MP, None),
            P(),
        ),
        out_specs=(
            P(ALL, None),
            P(ALL, None),
            P(),
            P(),
            P(None, None, MP),
            P(),
            P(None, None, None, MP),
            P(),
            P(None, MP, None),
            P(),
            P(None, MP),
            P(),
            P(None, None, MP),
            P(),
            P(None, MP, None),
            P(),
        ),
        check_vma=False,
    )
```

```python
import functools
import math

import jax
import jax.numpy as jnp
from jax import lax
from jax.experimental import pallas as pl
from jax.experimental.pallas import tpu as pltpu
from jax.sharding import Mesh
from jax.sharding import PartitionSpec as P

HD = 64
ROT = 16
LAYERS = 2
EPS = 1e-05
FILL = -1000000000.0
MP = ("z", "yh", "c")
DP = ("yl", "x")
ALL = ("yl", "x", "z", "yh", "c")
MESH = pl.DeviceIdType.MESH

D = 1024
T = 2048
OWN = 128
BLK = 256
NB = T // BLK
WIN = 5 * BLK
NQ = 256
FF = 256
NIN = NQ + FF
NOUT = 128 + FF
R = 128
F32 = jnp.float32
BF16 = jnp.bfloat16
HIGH = lax.Precision.HIGHEST

NN = (((1,), (0,)), ((), ()))
NT = (((1,), (1,)), ((), ()))
TN = (((0,), (0,)), ((), ()))


def mm(a, b, dims=NN, precision=None):
    return lax.dot_general(a, b, dims, precision=precision, preferred_element_type=F32)


def split_bf16(a):
    high = a.astype(BF16)
    return high, (a - high.astype(F32)).astype(BF16)


def mm3(a, b, dims=NN):
    ah, al = split_bf16(a)
    bh, bl = split_bf16(b)
    return mm(ah, bh, dims) + (mm(al, bh, dims) + mm(ah, bl, dims))


def rows_of(ref, start, count):
    return ref.at[pl.ds(start if isinstance(start, int) else pl.multiple_of(start, count), count)]


class Place:
    def __init__(self):
        self.z, self.h, self.c = (lax.axis_index(a) for a in MP)
        self.up = {"z": lax.rem(self.z + 1, 4)}
        self.dn = {"z": lax.rem(self.z + 3, 4)}
        self.yy = {"yh": 1 - self.h}
        self.sib = {"c": 1 - self.c}

    def block(self, dz, dh):
        return lax.rem(self.z + dz, 4) * 2 + lax.rem(self.h + dh, 2)

    def shard(self, dz, dh, dc):
        return self.block(dz, dh) * 2 + lax.rem(self.c + dc, 2)

    def arrive(self, wide=False):
        peers = [self.up, self.dn, self.yy, self.sib]
        if wide:
            at = Chips()
            peers = [at.sib] + [at.along(a, d) for a in ("x", "z") for d in (1, 2, 3)] + [at.y_peer(d) for d in (1, 2, 3)]
        barrier = pltpu.get_barrier_semaphore()
        for peer in peers:
            pl.semaphore_signal(barrier, inc=1, device_id=peer, device_id_type=MESH)
        return lambda: pl.semaphore_wait(barrier, len(peers))


def entry(values, i):
    total = values[0]
    for k in range(1, len(values)):
        if values[k] != values[k - 1]:
            total = total + (values[k] - values[k - 1]) * lax.div(i + (len(values) - k), len(values))
    return total


class Sender:
    def __init__(self, sems, partner):
        self.sems = sems
        self.partner = partner
        self.live = []

    def copy(self, src, dst, send_sem, recv_sem, peer):
        return pltpu.make_async_remote_copy(
            src_ref=src, dst_ref=dst, send_sem=send_sem, recv_sem=recv_sem, device_id=peer, device_id_type=MESH
        )

    def send(self, src, dst, peer, recv_sem, like=None):
        self.copy(src, dst, self.sems.at[len(self.live)], recv_sem, peer).start()
        self.live.append(src if like is None else like)

    def got(self, ref, sem):
        self.copy(ref, ref, self.sems.at[0], sem, self.partner).wait_recv()

    def finish(self):
        for k, like in enumerate(self.live):
            self.copy(like, like, self.sems.at[k], self.sems.at[k], self.partner).wait_send()


HALF = OWN // 2
QUART = OWN // 4
GATHER_SENDS = 32
GATHER_SEMS = [pltpu.SemaphoreType.DMA((17,)), pltpu.SemaphoreType.DMA((16,))]


def gather(me, out, buf, direct, cross, compute, before, amid, extra=None):
    def part(dz, dh, dc, k):
        return rows_of(buf, me.shard(dz, dh, dc) * OWN + k * HALF, HALF)

    def sem(sems, dz, dh, k):
        return sems.at[(dz * 2 + dh) * 2 + k]

    half, fourth = rows_of(buf, 0, HALF), rows_of(buf, 0, QUART)

    def send(dz, dh, k, peer, tz, th):
        ref = part(dz, dh, 0, k)
        out.send(ref, ref, peer, sem(direct, tz, th, k), half)

    def over(dz, dh, k):
        ref = part(dz, dh, 0, k)
        out.send(ref, ref, me.sib, sem(cross, dz, dh, k), half)

    def got(dz, dh, k):
        out.got(part(dz, dh, 0, k), sem(direct, dz, dh, k))

    def quarter(dz, k):
        return rows_of(buf, me.shard(dz, 0, 0) * OWN + HALF + k * QUART, QUART)

    send(0, 0, 0, me.yy, 0, 1)
    send(0, 0, 1, me.up, 3, 0)
    send(0, 0, 1, me.dn, 1, 0)
    send(0, 0, 0, me.up, 3, 0)
    send(0, 0, 0, me.dn, 1, 0)
    send(0, 0, 1, me.yy, 0, 1)
    over(0, 0, 0)
    over(0, 0, 1)
    before()
    got(3, 0, 1)
    out.send(quarter(3, 0), quarter(3, 0), me.up, sem(direct, 2, 0, 1), fourth)
    got(1, 0, 1)
    out.send(quarter(1, 1), quarter(1, 1), me.dn, direct.at[16], fourth)
    got(0, 1, 0)
    send(0, 1, 0, me.dn, 1, 1)
    send(0, 1, 0, me.up, 3, 1)
    send(3, 0, 1, me.yy, 3, 1)
    send(1, 0, 1, me.yy, 1, 1)
    over(3, 0, 1)
    over(1, 0, 1)
    over(0, 1, 0)
    got(3, 0, 0)
    send(3, 0, 0, me.up, 2, 0)
    over(3, 0, 0)
    got(1, 0, 0)
    over(1, 0, 0)
    out.got(quarter(2, 0), sem(direct, 2, 0, 1))
    out.got(quarter(2, 1), direct.at[16])
    send(2, 0, 1, me.yy, 2, 1)
    over(2, 0, 1)
    got(0, 1, 1)
    over(0, 1, 1)
    amid()

    def onward():
        got(1, 1, 0)
        send(1, 1, 0, me.dn, 2, 1)
        over(1, 1, 0)

    def late(pairs):
        for dz, dh, k in pairs:
            got(dz, dh, k)
            over(dz, dh, k)

    order = ((0, 0), (3, 0), (1, 0), (0, 1), (2, 0), (3, 1), (1, 1), (2, 1))
    steps = {
        1: onward,
        3: lambda: late(((3, 1, 0), (2, 0, 0))),
        4: lambda: late(((3, 1, 1), (1, 1, 1))),
        7: lambda: late(((2, 1, 0), (2, 1, 1))),
    }

    def visit(i, _):
        for at, step in [*steps.items(), *(extra or {}).items()]:
            pl.when(i == at)(step)
        dz, dh = (entry([pair[j] for pair in order], i) for j in range(2))
        for k in range(2):
            out.got(part(dz, dh, 1, k), sem(cross, dz, dh, k))
        compute(dz, dh)
        return 0

    lax.fori_loop(0, 8, visit, 0)


SCATTER_SENDS = 16
SCATTER_SCRATCH = [
    pltpu.VMEM((8 * OWN, D), F32),
    pltpu.VMEM((8 * OWN, D), BF16),
    pltpu.VMEM((8 * OWN, D), BF16),
    pltpu.VMEM((8 * OWN, D), BF16),
    pltpu.VMEM((2 * HALF, D), BF16),
    pltpu.VMEM((4 * HALF, D), BF16),
    pltpu.VMEM((HALF, D), BF16),
    pltpu.VMEM((4 * HALF, D), BF16),
    pltpu.VMEM((2 * QUART, D), BF16),
    pltpu.VMEM((2 * HALF, D), BF16),
    pltpu.SemaphoreType.DMA((8,)),
    pltpu.SemaphoreType.DMA((8,)),
    pltpu.SemaphoreType.DMA((2,)),
    pltpu.SemaphoreType.DMA((4,)),
    pltpu.SemaphoreType.DMA((1,)),
    pltpu.SemaphoreType.DMA((4,)),
    pltpu.SemaphoreType.DMA((2,)),
    pltpu.SemaphoreType.DMA((2,)),
]


def scatter(me, out, bufs, compute, between, finish, extra=None, quick=False, tail=None):
    (own, other, cross, sums, via, ring, last, pair, via2, ring2,
     s_over, s_cross, s_via, s_ring, s_last, s_pair, s_via2, s_ring2) = bufs

    def give(dz, dh):
        i = dz * 2 + dh

        at = pl.ds(pl.multiple_of(i * OWN, OWN), OWN)

        def put(dc, terms):
            if dc == 0:
                own[at, :] = terms
            else:
                other[at, :] = terms.astype(BF16)

        compute(dz, dh, put)
        rows = rows_of(other, i * OWN, OWN)
        out.copy(rows, rows_of(cross, i * OWN, OWN), s_over.at[i], s_cross.at[i], me.sib).start()

    def wait_cross(dz, dh):
        i = dz * 2 + dh
        out.got(rows_of(cross, i * OWN, OWN), s_cross.at[i])

    def both(dz, dh, start, rows):
        here = pl.ds((dz * 2 + dh) * OWN + start, rows)
        return own[here, :] + cross[here, :].astype(F32)

    def arrived(buf, sems, i, rows):
        ref = rows_of(buf, i * rows, rows)
        out.got(ref, sems.at[i])
        return ref[...].astype(F32)

    def pass_to(dz, dh, start, rows, value, buf, sems, i, peer):
        at = (dz * 2 + dh) * OWN + start
        sums[pl.ds(at, rows), :] = value.astype(BF16)
        out.send(rows_of(sums, at, rows), rows_of(buf, i * rows, rows), peer, sems.at[i], rows_of(sums, 0, rows))

    def first(dz, dh):
        return both(dz, dh, 0, HALF)

    def to_partner(dz):
        pass_to(dz, 1, HALF, HALF, both(dz, 1, HALF, HALF), pair, s_pair, dz, me.yy)

    def second(dz):
        return both(dz, 0, HALF, HALF) + arrived(pair, s_pair, dz, HALF)

    def start_far():
        wait_cross(2, 1)
        pass_to(2, 1, 0, HALF, first(2, 1), via, s_via, 1, me.dn)
        to_partner(2)
        wait_cross(2, 0)
        pass_to(2, 0, 0, HALF, first(2, 0), via, s_via, 0, me.up)

    def near_others():
        wait_cross(1, 1)
        pass_to(1, 1, 0, HALF, first(1, 1), ring, s_ring, 1, me.up)
        to_partner(1)

    def partner_three():
        wait_cross(3, 1)
        to_partner(3)

    def near_own():
        wait_cross(3, 0)
        pass_to(3, 0, 0, HALF, first(3, 0), ring, s_ring, 2, me.dn)

    def far_seconds():
        own[pl.ds(4 * OWN + HALF, HALF), :] = second(2)
        for k, peer in ((0, me.up), (1, me.dn)):
            value = own[pl.ds(4 * OWN + HALF + k * QUART, QUART), :]
            pass_to(2, 0, HALF + k * QUART, QUART, value, via2, s_via2, k, peer)

    def onward():
        wait_cross(1, 0)
        pass_to(3, 1, 0, HALF, first(3, 1) + arrived(via, s_via, 1, HALF), ring, s_ring, 3, me.dn)
        pass_to(1, 0, 0, HALF, first(1, 0) + arrived(via, s_via, 0, HALF), ring, s_ring, 0, me.up)

    def partner_own():
        wait_cross(0, 1)
        to_partner(0)

    if quick:
        order = ((2, 1), (2, 0), (1, 1), (3, 0), (3, 1), (1, 0), (0, 1), (0, 0))
        steps = [(1, start_far), (3, near_others), (3, near_own), (4, partner_three), (5, far_seconds), (6, partner_own), (6, onward)]
    else:
        order = ((2, 1), (2, 0), (1, 1), (3, 1), (1, 0), (3, 0), (0, 1), (0, 0))
        steps = [(1, start_far), (2, near_others), (3, partner_three), (4, onward), (4, far_seconds), (5, near_own), (6, partner_own)]

    def visit(i, _):
        give(*(entry([pair[j] for pair in order], i) for j in range(2)))
        for at, step in [*steps, *(extra or {}).items()]:
            pl.when(i == at)(step)
        return 0

    lax.fori_loop(0, 8, visit, 0)
    if tail is not None:
        for work in between:
            work()
        between = tail
    between[0]()
    for dz, k, peer in ((1, 0, me.up), (3, 1, me.dn)):
        mine = pl.ds(dz * 2 * OWN + HALF, HALF)
        own[mine, :] = second(dz)
        own[pl.ds(dz * 2 * OWN + HALF + k * QUART, QUART), :] += arrived(via2, s_via2, k, QUART)
        pass_to(dz, 0, HALF, HALF, own[mine, :], ring2, s_ring2, k, peer)
    between[1]()
    total = first(0, 1) + arrived(ring, s_ring, 1, HALF) + arrived(ring, s_ring, 3, HALF)
    pass_to(0, 1, 0, HALF, total, last, s_last, 0, me.yy)
    wait_cross(0, 0)
    between[2]()
    finish(HALF, HALF, second(0) + arrived(ring2, s_ring2, 0, HALF) + arrived(ring2, s_ring2, 1, HALF))
    total = first(0, 0) + arrived(ring, s_ring, 0, HALF) + arrived(ring, s_ring, 2, HALF)
    finish(0, HALF, total + arrived(last, s_last, 0, HALF))
    for i in range(8):
        rows = rows_of(other, i * OWN, OWN)
        out.copy(rows, rows, s_over.at[i], s_cross.at[i], me.sib).wait_send()


def gelu_parts(h):
    cdf = 0.5 * (1.0 + lax.erf(h * (2.0**-0.5)))
    return cdf


def lane_roll(a, shift):
    return pltpu.roll(a, shift % 128, 1)


def normalized(x):
    mean = jnp.mean(x, axis=1, keepdims=True)
    centered = x - mean
    scale = lax.rsqrt(jnp.mean(centered * centered, axis=1, keepdims=True) + EPS)
    return centered * scale, scale


class Loads:
    def __init__(self, sems):
        self.sems = sems
        self.count = 0

    def start(self, src, dst):
        copy = pltpu.make_async_copy(src, dst, self.sems.at[self.count])
        self.count += 1
        copy.start()
        return copy


def rotary_tables(lens, tabs, first_row, first, angles):
    token = lax.broadcasted_iota(jnp.int32, (8, T), 1)
    begin = jnp.zeros((8, T), jnp.int32)
    end = 0
    for i in range(3):
        end = end + lens[0, i]
        begin = jnp.where(token >= end, end, begin)
    first_row[...] = begin
    step = lax.broadcasted_iota(jnp.int32, (8, T), 0).astype(F32)
    angle = (token - begin).astype(F32) * jnp.exp(step * (-2.0 * math.log(10000.0) / ROT))
    angles[0:8, :] = jnp.cos(angle)
    angles[8:16, :] = jnp.sin(angle)

    def turn(i, _):
        at = pl.ds(pl.multiple_of(i * BLK, BLK), BLK)
        cos, sin = angles[0:8, at], angles[8:16, at]
        none = jnp.zeros((HD - ROT, BLK), F32)
        for k, head in enumerate(((cos, cos, none + 1.0), (-sin, sin, none))):
            tabs[k, at, :] = jnp.concatenate(head + head, axis=0).T
        first[at, :] = jnp.broadcast_to(first_row[0:1, at].astype(F32), (128, BLK)).T.astype(jnp.int32)
        return 0

    lax.fori_loop(0, NB, turn, 0)


def forward_kernel(layer, lens, x_ref, gains_ref, shifts_ref, b_qkv, b_in, b_out, b_down,
                   wqkv_h, aqkv_h, uqkv_h, win_h, ain_h, uin_h, wout_h, aout_h, uout_h, wdown_h, adown_h, udown_h, *refs):
    (o_x, o_xh, o_qkv, o_ho, o_out, o_lse, o_kt, o_wint, o_wout, o_tabs, o_first,
     xh, qkv, ho, ou, out_t, kt, scores, probs, win, wint, bias, wout, tabs, first, angles,
     wqkv, aqkv, uqkv, w_in, ain, uin, w_out, aout, uout, wdown, adown, udown,
     load_sems, send_sems, g_direct, g_cross, *scat) = refs
    gains, shifts = gains_ref.at[layer], shifts_ref.at[layer]
    me = Place()
    meet = me.arrive()
    loads = Loads(load_sems)
    ins = [
        loads.start(src.at[layer], dst)
        for src, dst in (
            (wqkv_h, wqkv), (aqkv_h, aqkv), (uqkv_h, uqkv), (win_h, w_in), (ain_h, ain), (uin_h, uin),
            (wout_h, w_out), (aout_h, aout), (uout_h, uout), (wdown_h, wdown), (adown_h, adown), (udown_h, udown),
        )
    ]
    out = Sender(send_sems, me.sib)
    rows_of(xh, me.shard(0, 0, 0) * OWN, OWN)[...] = (
        normalized(x_ref[...])[0] * gains[0:1, :] + shifts[0:1, :]
    ).astype(BF16)
    meet()
    outs = []

    def before():
        rotary_tables(lens, tabs, o_first, first, angles)
        for copy in ins[:3]:
            copy.wait()
        for j in range(3):
            here = pl.ds(j * HD, HD)
            wint[here, :] = (wqkv[here, :].astype(F32) + mm3(uqkv[j], aqkv[j], NT)).astype(BF16)
            bias[:, here] = b_qkv[j, layer:layer + 1, :]
        wint[3 * HD:NQ, :] = jnp.zeros((NQ - 3 * HD, D), BF16)
        bias[:, 3 * HD:NQ] = jnp.zeros((1, NQ - 3 * HD), F32)
        win[:, 0:NQ] = wint[0:NQ, :].astype(F32).T.astype(BF16)

    def amid():
        for copy in ins[3:]:
            copy.wait()
        ratio = gains[1:2, :] / gains[0:1, :]
        merged = w_in[...].astype(F32) + mm3(ain[...], uin[...])
        low = merged.astype(BF16)
        b_high, b_low = split_bf16(jnp.broadcast_to(shifts[1:2, :] - shifts[0:1, :] * ratio, (8, D)))
        bias[:, NQ:NIN] = b_in[layer:layer + 1, :] + (mm(b_high, low) + mm(b_low, low))[0:1]
        turned = merged.T * ratio
        wint[NQ:NIN, :] = turned.astype(BF16)
        win[:, NQ:NIN] = turned.T.astype(BF16)
        wout[0:64, :] = (w_out[...].astype(F32) + mm3(aout[...], uout[...])).astype(BF16)
        wout[64:128, :] = jnp.zeros((64, D), BF16)
        wout[128:NOUT, :] = (wdown[...].astype(F32) + mm3(adown[...], udown[...])).astype(BF16)
        outs.append(loads.start(wint, o_wint))
        outs.append(loads.start(wout, o_wout))
        if layer == 0:
            outs.append(loads.start(tabs, o_tabs))

    def project(dz, dh):
        at = pl.ds(pl.multiple_of(me.block(dz, dh) * BLK, BLK), BLK)
        rows = xh[at, :]
        pq = mm(rows, win[:, 0:NQ]) + bias[:, 0:NQ]
        qk = pq[:, 0:128]
        lane = lax.broadcasted_iota(jnp.int32, (BLK, 128), 1)
        other = jnp.where(lax.rem(lane, HD) < ROT // 2, lane_roll(qk, -8), lane_roll(qk, 8))
        turned = qk * tabs[0, at, :] + other * tabs[1, at, :]
        qkv[at, 0:128] = jnp.where(lane < HD, turned * HD**-0.5, 0.0).astype(BF16)
        keys = jnp.where(lane < HD, lane_roll(turned, HD), 0.0)
        qkv[at, 128:256] = keys.astype(BF16)
        kt[:, at] = keys.T.astype(BF16)
        qkv[at, 256:384] = pq[:, 128:256].astype(BF16)
        h = mm(rows, win[:, NQ:NIN]) + bias[:, NQ:NIN]
        ho[at, 128:NOUT] = h
        ou[at, 128:NOUT] = (h * gelu_parts(h)).astype(BF16)

    gather(me, out, xh, g_direct, g_cross, project, before, amid)
    outs.extend([loads.start(xh, o_xh), loads.start(qkv, o_qkv), loads.start(kt, o_kt)])

    def attend(dz, dh, put):
        b = me.block(dz, dh)
        at = pl.ds(pl.multiple_of(b * BLK, BLK), BLK)
        key_at = jnp.maximum(b - 4, 0) * BLK
        q = qkv[at, 0:128]
        row = b * BLK + lax.broadcasted_iota(jnp.int32, (BLK, BLK), 0)
        start = jnp.concatenate([first[at, :], first[at, :]], axis=1)
        peak = None
        for j in range(5):
            keys = pl.ds(pl.multiple_of(key_at + j * BLK, BLK), BLK)
            s = mm(q, qkv[keys, 128:256], NT)
            col = key_at + j * BLK + lax.broadcasted_iota(jnp.int32, (BLK, BLK), 1)
            s = jnp.where((col >= start) & (col <= row), s, FILL)
            scores[:, j * BLK:(j + 1) * BLK] = s
            peak = s if peak is None else jnp.maximum(peak, s)
        peak = jnp.max(peak, axis=1, keepdims=True)
        summed = None
        for j in range(5):
            p = jnp.exp(scores[:, j * BLK:(j + 1) * BLK] - peak)
            probs[:, j * BLK:(j + 1) * BLK] = p.astype(BF16)
            summed = p if summed is None else summed + p
        summed = jnp.sum(summed, axis=1, keepdims=True)
        o = mm(probs[...], qkv[pl.ds(pl.multiple_of(key_at, BLK), WIN), 256:384]) * (1.0 / summed)
        ho[at, 0:128] = o
        ou[at, 0:128] = o.astype(BF16)
        lse = jnp.broadcast_to(peak + jnp.log(summed), (BLK, 128)).T
        o_lse[:, at] = lse[0:8, :]
        out_t[:, at] = ou[at, :].astype(F32).T.astype(BF16)
        for dc in range(2):
            put(dc, mm(rows_of(ou, me.shard(dz, dh, dc) * OWN, OWN)[...], wout[...]))

    def store():
        outs.append(loads.start(ho, o_ho))
        outs.append(loads.start(out_t, o_out))

    def nothing():
        pass

    def finish(at, rows, total):
        here = pl.ds(at, rows)
        o_x[here, :] = x_ref[here, :] + total + (b_out[layer:layer + 1, :] + b_down[layer:layer + 1, :])

    scatter(me, out, scat, attend, (store, nothing, nothing), finish)
    for copy in outs:
        copy.wait()
    out.finish()


VM = pl.BlockSpec(memory_space=pltpu.VMEM)
HBM = pl.BlockSpec(memory_space=pl.ANY)


SMEM = pl.BlockSpec(memory_space=pltpu.SMEM)


def forward(layer, lens, x, gains, shifts, biases, weights):
    vmem = pltpu.VMEM
    shapes = [
        jax.ShapeDtypeStruct((OWN, D), F32),
        jax.ShapeDtypeStruct((T, D), BF16),
        jax.ShapeDtypeStruct((T, 384), BF16),
        jax.ShapeDtypeStruct((T, NOUT), F32),
        jax.ShapeDtypeStruct((NOUT, T), BF16),
        jax.ShapeDtypeStruct((8, T), F32),
        jax.ShapeDtypeStruct((128, T), BF16),
        jax.ShapeDtypeStruct((NIN, D), BF16),
        jax.ShapeDtypeStruct((NOUT, D), BF16),
        jax.ShapeDtypeStruct((2, T, 128), F32),
        jax.ShapeDtypeStruct((8, T), jnp.int32),
    ]
    return pl.pallas_call(
        functools.partial(forward_kernel, layer),
        out_shape=shapes,
        in_specs=[SMEM] + [VM] * 7 + [HBM] * 12,
        out_specs=[VM, HBM, HBM, HBM, HBM, VM, HBM, HBM, HBM, HBM, VM],
        scratch_shapes=[
            vmem((T, D), BF16),
            vmem((T, 384), BF16),
            vmem((T, NOUT), F32),
            vmem((T, NOUT), BF16),
            vmem((NOUT, T), BF16),
            vmem((128, T), BF16),
            vmem((BLK, WIN), F32),
            vmem((BLK, WIN), BF16),
            vmem((D, NIN), BF16),
            vmem((NIN, D), BF16),
            vmem((1, NIN), F32),
            vmem((NOUT, D), BF16),
            vmem((2, T, 128), F32),
            vmem((T, 128), jnp.int32),
            vmem((16, T), F32),
            vmem((192, D), BF16),
            vmem((3, D, R), F32),
            vmem((3, HD, R), F32),
            vmem((D, FF), BF16),
            vmem((D, R), F32),
            vmem((R, FF), F32),
            vmem((64, D), BF16),
            vmem((64, R), F32),
            vmem((R, D), F32),
            vmem((FF, D), BF16),
            vmem((FF, R), F32),
            vmem((R, D), F32),
            pltpu.SemaphoreType.DMA((24,)),
            pltpu.SemaphoreType.DMA((GATHER_SENDS + SCATTER_SENDS,)),
            *GATHER_SEMS,
            *SCATTER_SCRATCH,
        ],
        compiler_params=pltpu.CompilerParams(
            collective_id=layer, has_side_effects=True, vmem_limit_bytes=60 << 20
        ),
        name=f"forward_layer{layer}",
    )(lens, x, gains, shifts, *biases, *weights)


def backward_kernel(layer, last, dy_ref, x_ref, xh_h, qkv_h, ho_h, out_h, lse_ref, kt_h, wint_h, wout_h, gains_ref, shifts_ref,
                    tabs_h, first_ref, aqkv_h, uqkv_h, ain_h, bin_h, aout_h, bout_h, adown_h, bdown_h, *refs):
    refs = list(refs)
    take = lambda count: [refs.pop(0) for _ in range(count)]
    if last:
        earlier_h, earlier_norm, earlier_group, earlier_sums = take(4)
        o_dx, o_total, o_norm_total, o_group_total = take(4)
    else:
        o_dx, o_spread, o_norm, o_group, o_sums = take(5)
    (dy, xh, qkv, ho, out_t, kt, dph, low, dph_t, acc, wint, wout, tabs, aqkv, uqkv, ain, bin_, aout, bout, adown, bdown,
     load_sems, send_sems, g_direct, g_cross) = take(25)
    scat = take(len(SCATTER_SCRATCH))
    if last:
        o_spread, o_norm, o_group, o_sums, earlier, total = take(6)
    gains, shifts = gains_ref.at[layer], shifts_ref.at[layer]
    me = Place()
    meet = me.arrive(last)
    loads = Loads(load_sems)
    early = [
        loads.start(wout_h, wout),
        loads.start(ho_h, ho),
        loads.start(qkv_h, qkv),
        loads.start(kt_h, kt),
    ]
    late = [
        loads.start(tabs_h, tabs),
        loads.start(wint_h, wint),
        loads.start(xh_h, xh),
        loads.start(out_h, out_t),
        loads.start(aqkv_h.at[layer], aqkv),
        loads.start(uqkv_h.at[layer], uqkv),
        loads.start(ain_h.at[layer], ain),
        loads.start(bin_h.at[layer], bin_),
        loads.start(aout_h.at[layer], aout),
        loads.start(bout_h.at[layer], bout),
        loads.start(adown_h.at[layer], adown),
        loads.start(bdown_h.at[layer], bdown),
    ]
    out = Sender(send_sems, me.sib)
    rows_of(dy, me.shard(0, 0, 0) * OWN, OWN)[...] = dy_ref[...].astype(BF16)
    meet()

    stages, ends = [], []
    if last:
        at_chip = Chips()
        half = pl.ds(pl.multiple_of(at_chip.c * (D // 2), D // 2), D // 2)
        copy_in = loads.start(earlier_h.at[:, half], earlier)
        n = len(path_scratch(128))
        stages = spread_stages(
            at_chip, out, earlier_h, total.at[pl.ds(768, 768)], (0, 512), "x", "z", take(n), earlier
        )
        for begin, axes in ((0, ("x", "z")), (256, ("z", "x"))):
            ends.append(spread_stages(at_chip, out, o_spread, total.at[pl.ds(0, 768)], (begin, 256), *axes, take(n)))
        ends.append(norm_group_stages(
            at_chip, out, (o_norm, earlier_norm), (o_group, earlier_group), (o_sums, earlier_sums),
            o_norm_total, o_group_total, refs,
        ))

    def stage(i):
        if stages:
            stages[i]()

    def end(i):
        for kind in ends:
            kind[i]()

    def extra(at, i):
        return {at: lambda: stage(i)} if last else None

    def before():
        if last:
            copy_in.wait()
        stage(0)
        acc[...] = jnp.zeros(acc.shape, F32)
        stage(1)

    def amid():
        for copy in early:
            copy.wait()

    def pull(dz, dh):
        b = me.block(dz, dh)
        at = pl.ds(pl.multiple_of(b * BLK, BLK), BLK)
        rows = dy[at, :]
        du = mm(rows, wout[128:NOUT, :], NT)
        h = ho[at, 128:NOUT]
        slope = gelu_parts(h) + h * (jnp.exp(-0.5 * h * h) * (2.0 * math.pi) ** -0.5)
        ho[at, 128:NOUT] = slope * du
        do = mm(rows, wout[0:128, :], NT).astype(BF16)
        drop = jnp.sum((do.astype(F32) * ho[at, 0:128]).T, axis=0, keepdims=True)
        lse = lse_ref[0:1, at]
        start = first_ref[0:1, at]
        q = qkv[at, 0:128]
        key_at = jnp.maximum(b - 5, 0)
        wide = 3 * BLK
        col = b * BLK + lax.broadcasted_iota(jnp.int32, (wide, BLK), 1)

        def step(j, dq):
            key = (key_at + 3 * j) * BLK
            keys = pl.ds(pl.multiple_of(key, BLK), wide)
            s = mm(qkv[keys, 128:256], q, NT)
            row = key + lax.broadcasted_iota(jnp.int32, (wide, BLK), 0)
            p = jnp.where((row >= start) & (row <= col), jnp.exp(s - lse), 0.0)
            dp = mm(qkv[keys, 256:384], do, NT)
            ds = (p * (dp - drop)).astype(BF16)
            acc[keys, 128:256] += mm(p.astype(BF16), do)
            acc[keys, 0:128] += mm(ds, q)
            return dq + mm(kt[:, keys], ds)

        dq = lax.fori_loop(0, (jnp.minimum(b, 5) + 3) // 3, step, jnp.zeros((128, BLK), F32))
        ho[at, 0:128] = dq.T * HD**-0.5

    gather(me, out, dy, g_direct, g_cross, pull, before, amid, extra(4, 2))
    stage(3)
    for copy in late:
        copy.wait()

    def send_back(dz, dh, put):
        b = me.block(dz, dh)
        at = pl.ds(pl.multiple_of(b * BLK, BLK), BLK)
        g = ho[at, 0:128] + lane_roll(acc[at, 0:128], HD)
        side = g * tabs[1, at, :]
        lane = lax.rem(lax.broadcasted_iota(jnp.int32, (BLK, 128), 1), HD)
        side = jnp.where(lane < ROT // 2, lane_roll(side, -8), jnp.where(lane < ROT, lane_roll(side, 8), 0.0))
        turned = g * tabs[0, at, :] + side
        dph[:, 0:128] = turned.astype(BF16)
        dph[:, 128:256] = acc[at, 128:256].astype(BF16)
        dph[:, NQ:NIN] = ho[at, 128:NOUT].astype(BF16)
        rows = dph[...]
        for dc in range(2):
            put(dc, mm(rows_of(dph, lax.rem(me.c + dc, 2) * OWN, OWN)[...], wint[...]))
        dph_t[:, at] = rows.astype(F32).T.astype(BF16)

    def by_columns(piece):
        def visit(i, _):
            piece(pl.ds(pl.multiple_of(i * 256, 256), 256))
            return 0

        lax.fori_loop(0, D // 256, visit, 0)

    def weight_grad(row, at, width):
        here = pl.ds(at, width)
        total = jnp.sum(dph_t[here, :].astype(F32), axis=1, keepdims=True)
        o_sums[:, here] = jnp.broadcast_to(total, (width, 128)).T[0:8, :]

        def piece(cols):
            grad = mm(dph_t[here, :], xh[:, cols])
            weight = wint[here, cols].astype(F32)
            by_gain = jnp.sum(grad * weight, axis=0, keepdims=True)
            by_shift = jnp.sum(total * weight, axis=0, keepdims=True)
            g, b = gains[0:1, cols], shifts[0:1, cols]
            if row == 1:
                ratio = gains[1:2, cols] / g
                by_gain, by_shift = by_gain / ratio, by_shift / ratio
                grad = grad * ratio + total * (shifts[1:2, cols] - b * ratio)
            o_norm[row:row + 1, cols] = (by_gain - b * by_shift) / g
            o_norm[2 + row:3 + row, cols] = by_shift
            low[here, cols] = grad.astype(BF16)

        by_columns(piece)

    def factors_qkv():
        stage(5)
        weight_grad(0, 0, NQ)
        for j in range(3):
            o_spread[j * R:(j + 1) * R, :] = mm(uqkv[j].astype(BF16), low[j * HD:(j + 1) * HD, :], TN).astype(BF16)
            o_group[j * HD:(j + 1) * HD, :] = mm(low[j * HD:(j + 1) * HD, :], aqkv[j].astype(BF16))

    def factors_in():
        weight_grad(1, NQ, FF)
        o_spread[3 * R:4 * R, :] = mm(bin_[...].astype(BF16), low[NQ:NIN, :]).astype(BF16)
        o_group[256:512, :] = mm(low[NQ:NIN, :], ain[...].astype(BF16))

    def factors_out():
        def piece(cols):
            low[0:64, cols] = mm(out_t[0:64, :], dy[:, cols]).astype(BF16)
            low[NQ:NIN, cols] = mm(out_t[128:NOUT, :], dy[:, cols]).astype(BF16)

        by_columns(piece)
        o_spread[4 * R:5 * R, :] = mm(aout[...].astype(BF16), low[0:64, :], TN).astype(BF16)
        o_group[192:256, :] = mm(low[0:64, :], bout[...].astype(BF16), NT)
        o_spread[5 * R:6 * R, :] = mm(adown[...].astype(BF16), low[NQ:NIN, :], TN).astype(BF16)
        o_group[512:768, :] = mm(low[NQ:NIN, :], bdown[...].astype(BF16), NT)
        o_norm[4:5, :] = jnp.sum(dy_ref[...], axis=0, keepdims=True)
        o_norm[5:8, :] = jnp.zeros((3, D), F32)
        stage(6)
        end(0)
        end(1)

    def finish(at, rows, total):
        here = pl.ds(at, rows)
        hat, rstd = normalized(x_ref[here, :])
        total = total * gains[0:1, :]
        mean = jnp.mean(total, axis=1, keepdims=True)
        along = jnp.mean(total * hat, axis=1, keepdims=True)
        o_dx[here, :] = dy_ref[here, :] + rstd * (total - mean - hat * along)

    ends_between = [lambda: None, lambda: None, lambda: end(2)]
    scatter(me, out, scat, send_back, (factors_qkv, factors_in, factors_out), finish, extra(4, 4), True, ends_between if last else None)
    if last:
        stage(7)
        for i in range(3, 8):
            end(i)
        store = loads.start(total, o_total)
        out.finish()
        store.wait()
    else:
        out.finish()


def backward(layer, dy, x, saved, gains, shifts, tabs, first, factors, earlier=None):
    last = earlier is not None
    grads = [((6 * R, D), BF16), ((8, D), F32), ((768, R), F32), ((8, NIN), F32)]
    totals = [((LAYERS * 6 * R, D), BF16), ((8 * LAYERS, D), F32), ((4 * GROUP, R), BF16)]
    shapes = [jax.ShapeDtypeStruct(*kind) for kind in [((OWN, D), F32), *(totals if last else grads)]]
    sums = [pltpu.VMEM(*kind) for kind in grads] + [pltpu.VMEM((6 * R, D // 2), BF16), pltpu.VMEM(*totals[0])]
    sums += path_scratch(512) + path_scratch(256) * 2 + NORM_GROUP_SCRATCH
    sends = GATHER_SENDS + SCATTER_SENDS + (3 * PATH_SENDS + NORM_GROUP_SENDS if last else 0)
    return pl.pallas_call(
        functools.partial(backward_kernel, layer, last),
        out_shape=shapes,
        in_specs=[VM, VM, HBM, HBM, HBM, HBM, VM, HBM, HBM, HBM, VM, VM, HBM, VM] + [HBM] * 8 + ([HBM, VM, VM, VM] if last else []),
        out_specs=[VM, HBM, VM, VM] if last else [VM] * 5,
        scratch_shapes=[
            pltpu.VMEM((T, D), BF16),
            pltpu.VMEM((T, D), BF16),
            pltpu.VMEM((T, 384), BF16),
            pltpu.VMEM((T, NOUT), F32),
            pltpu.VMEM((NOUT, T), BF16),
            pltpu.VMEM((128, T), BF16),
            pltpu.VMEM((BLK, NIN), BF16),
            pltpu.VMEM((NIN, D), BF16),
            pltpu.VMEM((NIN, T), BF16),
            pltpu.VMEM((T, 256), F32),
            pltpu.VMEM((NIN, D), BF16),
            pltpu.VMEM((NOUT, D), BF16),
            pltpu.VMEM((2, T, 128), F32),
            pltpu.VMEM((3, D, R), F32),
            pltpu.VMEM((3, HD, R), F32),
            pltpu.VMEM((D, R), F32),
            pltpu.VMEM((R, FF), F32),
            pltpu.VMEM((64, R), F32),
            pltpu.VMEM((R, D), F32),
            pltpu.VMEM((FF, R), F32),
            pltpu.VMEM((R, D), F32),
            pltpu.SemaphoreType.DMA((24,)),
            pltpu.SemaphoreType.DMA((sends,)),
            *GATHER_SEMS,
            *SCATTER_SCRATCH,
            *(sums if last else []),
        ],
        compiler_params=pltpu.CompilerParams(
            collective_id=LAYERS + layer, has_side_effects=True, vmem_limit_bytes=60 << 20
        ),
        name=f"backward_layer{layer}",
    )(dy, x, *saved, gains, shifts, tabs, first, *factors, *(earlier or ()))


QUARTER = 768 // 4
PATH_SENDS = 23


def path_scratch(width):
    dma = pltpu.SemaphoreType.DMA
    return [
        pltpu.VMEM((768, width), BF16),
        pltpu.VMEM((768, width), BF16),
        pltpu.VMEM((3, QUARTER, width), BF16),
        pltpu.VMEM((QUARTER, width), F32),
        pltpu.VMEM((QUARTER, width), BF16),
        pltpu.VMEM((3, 48, width), BF16),
        pltpu.VMEM((4, 48, width), BF16),
        pltpu.VMEM((QUARTER, width), BF16),
        dma((4,)),
        dma((3,)),
        dma((3,)),
        dma((3,)),
        dma((3,)),
        dma((3,)),
        dma((4,)),
    ]


class Chips:
    def __init__(self):
        self.yl, self.x, self.z, self.yh, self.c = (lax.axis_index(a) for a in ALL)
        self.y = self.yh * 2 + self.yl
        self.sib = {"c": 1 - self.c}

    def here(self, axis):
        return {"x": self.x, "z": self.z}[axis]

    def along(self, axis, d):
        return {axis: lax.rem(self.here(axis) + d, 4)}

    def y_peer(self, d):
        there = lax.rem(self.y + d, 4)
        return {"yh": lax.div(there, 2), "yl": lax.rem(there, 2)}

    def quarter(self, axis, d, size):
        return pl.multiple_of(lax.rem(self.here(axis) + d, 4) * size, size)


def spread_stages(at, out, src, dst, lanes, first, second, bufs, own_half=None):
    cross, low, slots1, acc, low2, slots2, along_y, totals, s_cross, s_one, s_two, s_y, s_back2, s_back1, s_backc = bufs
    begin, width = lanes
    mine = pl.ds(pl.multiple_of(at.c * 512 + begin, 128), width)
    theirs = pl.ds(pl.multiple_of((1 - at.c) * 512 + begin, 128), width)

    def rows(d):
        return pl.ds(at.quarter(first, d, QUARTER), QUARTER)

    def part(d):
        return pl.ds(at.quarter(second, d, 48), 48)

    big = dst.at[pl.ds(0, QUARTER), pl.ds(0, width)]
    small = low2.at[pl.ds(0, 48)]

    def over_core():
        for d in (2, 1, 3, 0):
            out.send(src.at[rows(d), theirs], cross.at[rows(d)], at.sib, s_cross.at[d], big)

    def along_first():
        for d in (2, 1, 3, 0):
            out.got(cross.at[rows(d)], s_cross.at[d])
            both = (src[rows(d), mine] if own_half is None else own_half[rows(d), :]).astype(F32)
            both = both + cross[rows(d), :].astype(F32)
            if d == 0:
                acc[...] = both
            else:
                low[rows(d), :] = both.astype(BF16)
                out.send(low.at[rows(d)], slots1.at[d - 1], at.along(first, d), s_one.at[d - 1], low.at[pl.ds(0, QUARTER)])

    def along_second():
        total = acc[...]
        for d in (1, 2, 3):
            out.got(slots1.at[d - 1], s_one.at[d - 1])
            total = total + slots1[d - 1].astype(F32)
        acc[...] = total
        low2[...] = total.astype(BF16)
        for d in (2, 1, 3):
            out.send(low2.at[part(d)], slots2.at[d - 1], at.along(second, d), s_two.at[d - 1], small)

    def along_third():
        total = acc[part(0), :]
        for d in (1, 2, 3):
            out.got(slots2.at[d - 1], s_two.at[d - 1])
            total = total + slots2[d - 1].astype(F32)
        own = along_y.at[at.y]
        own[...] = total.astype(BF16)
        for d in (2, 1, 3):
            out.send(own, own, at.y_peer(d), s_y.at[d - 1], along_y.at[0])

    def back_second():
        for d in (1, 2, 3):
            out.got(along_y.at[lax.rem(at.y + 4 - d, 4)], s_y.at[d - 1])
        term = [along_y[i].astype(F32) for i in range(4)]
        own = totals.at[part(0)]
        own[...] = ((term[0] + term[1]) + (term[2] + term[3])).astype(BF16)
        for d in (2, 1, 3):
            out.send(own, own, at.along(second, d), s_back2.at[d - 1], small)

    def back_first():
        for d in (1, 2, 3):
            out.got(totals.at[part(4 - d)], s_back2.at[d - 1])
        own = dst.at[rows(0), mine]
        own[...] = totals[...]
        for d in (2, 1, 3):
            out.send(own, own, at.along(first, d), s_back1.at[d - 1], big)
        out.send(own, own, at.sib, s_backc.at[0], big)

    def back_core():
        for d in (1, 3, 2):
            own = dst.at[rows(4 - d), mine]
            out.got(own, s_back1.at[d - 1])
            out.send(own, own, at.sib, s_backc.at[d], big)

    def arrive():
        for d in range(4):
            out.got(dst.at[rows(4 - d), theirs], s_backc.at[d])

    return [over_core, along_first, along_second, along_third, back_second, back_first, back_core, arrive]


GROUP = 400


NORM_GROUP_SENDS = 1 + 3 + 3 + 3 + 1 + 3 + 3 + 1
NORM_GROUP_SCRATCH = [
    pltpu.VMEM((2, 16, 512), F32),
    pltpu.VMEM((12, 16, 512), F32),
    pltpu.VMEM((4 * GROUP, R), F32),
    pltpu.VMEM((4 * GROUP, R), BF16),
    pltpu.VMEM((3, GROUP, R), BF16),
    pltpu.VMEM((2, GROUP, R), BF16),
    pltpu.SemaphoreType.DMA((11,)),
    pltpu.SemaphoreType.DMA((7,)),
]


def norm_group_stages(at, out, norms, groups, sums, o_norm, o_group, bufs):
    n_first, n_slots, g_own, g_low, g_slots, g_pair, s_norm, s_group = bufs
    mine = pl.ds(pl.multiple_of(at.c * 512, 512), 512)
    theirs = pl.ds(pl.multiple_of((1 - at.c) * 512, 512), 512)

    def n_stage(stage, value, index, peer_of, base):
        own = n_slots.at[stage * 4 + index]
        own[...] = value
        for d in (1, 2, 3):
            out.send(own, own, peer_of(d), s_norm.at[base + d - 1])

    def n_sum(stage, index, base):
        for d in (1, 2, 3):
            out.got(n_slots.at[stage * 4 + lax.rem(index + 4 - d, 4)], s_norm.at[base + d - 1])
        return (n_slots[stage * 4] + n_slots[stage * 4 + 1]) + (n_slots[stage * 4 + 2] + n_slots[stage * 4 + 3])

    def g_rows(d):
        return pl.ds(at.quarter("x", d, GROUP), GROUP)

    def begin():
        for i, norm in enumerate(norms):
            n_first[0, i * 8:i * 8 + 8, :] = norm[:, theirs]
        out.send(n_first.at[0], n_first.at[1], at.sib, s_norm.at[0])
        for i in range(4):
            group, total, half = groups[i // 2], sums[i // 2], i % 2
            g_own[i * GROUP:i * GROUP + 384, :] = group[half * 384:half * 384 + 384, :]
            for k in range(2):
                rows = pl.ds(i * GROUP + 384 + 8 * k, 8)
                g_own[rows, :] = total[:, half * 256 + 128 * k:half * 256 + 128 * k + 128]
        g_low[...] = g_own[...].astype(BF16)
        for d in (2, 1, 3):
            out.send(g_low.at[g_rows(d)], g_slots.at[d - 1], at.along("x", d), s_group.at[d - 1])

    def along_x():
        out.got(n_first.at[1], s_norm.at[0])
        first = jnp.concatenate([norm[:, mine] for norm in norms], axis=0) + n_first[1]
        n_stage(0, first, at.x, lambda d: at.along("x", d), 1)

    def along_z():
        total = g_own[g_rows(0), :]
        for d in (1, 2, 3):
            out.got(g_slots.at[d - 1], s_group.at[d - 1])
            total = total + g_slots[d - 1].astype(F32)
        g_pair[0] = total.astype(BF16)
        out.send(g_pair.at[0], g_pair.at[1], {"yl": 1 - at.yl}, s_group.at[3])
        n_stage(1, n_sum(0, at.x, 1), at.z, lambda d: at.along("z", d), 4)

    def along_third():
        out.got(g_pair.at[1], s_group.at[3])
        own = o_group.at[g_rows(0)]
        own[...] = (g_pair[0].astype(F32) + g_pair[1].astype(F32)).astype(BF16)
        for d in (1, 2, 3):
            out.send(own, own, at.along("x", d), s_group.at[3 + d])
        n_stage(2, n_sum(1, at.z, 4), at.y, at.y_peer, 7)

    def back_core():
        o_norm[:, mine] = n_sum(2, at.y, 7)
        out.send(o_norm.at[:, mine], o_norm.at[:, mine], at.sib, s_norm.at[10])

    def nothing():
        pass

    def arrive():
        for d in (1, 2, 3):
            out.got(o_group.at[g_rows(4 - d)], s_group.at[3 + d])
        out.got(o_norm.at[:, theirs], s_norm.at[10])

    return [begin, along_x, along_z, along_third, back_core, nothing, nothing, arrive]


def unpack_kernel(spread, norm, group, stream, grad, o_stream, o_grad, o_gain, o_shift, o_bqkv, o_aqkv, o_uqkv, o_bout, o_aout, o_uout, o_bin, o_ain, o_uin,
                  o_bdown, o_adown, o_udown):
    o_stream[...] = stream[...]
    o_grad[...] = grad[...]
    for j in range(3):
        o_aqkv[j] = spread[j * R:(j + 1) * R, :].astype(F32).T
    o_ain[...] = spread[3 * R:4 * R, :].astype(F32).T
    o_uout[...] = spread[4 * R:5 * R, :].astype(F32)
    o_udown[...] = spread[5 * R:6 * R, :].astype(F32)
    o_gain[...] = norm[0:2, :]
    o_shift[...] = norm[2:4, :]
    for j in range(3):
        o_uqkv[j] = group[j * HD:(j + 1) * HD, :].astype(F32)
    o_aout[...] = group[192:256, :].astype(F32)
    o_uin[:, 0:128] = group[256:384, :].astype(F32).T
    o_uin[:, 128:256] = group[GROUP:GROUP + 128, :].astype(F32).T
    o_adown[...] = group[GROUP + 128:GROUP + 384, :].astype(F32)
    query_key, value = group[384:385, :].astype(F32), group[392:393, :].astype(F32)
    hidden = [group[GROUP + 384 + 8 * k:GROUP + 385 + 8 * k, :].astype(F32) for k in range(2)]

    def small(layer):
        row = slice(layer, layer + 1)
        o_bout[row, :] = norm[4:5, :]
        o_bdown[row, :] = norm[4:5, :]
        o_bqkv[0, row, :] = query_key[:, 0:HD]
        o_bqkv[1, row, :] = query_key[:, HD:2 * HD]
        o_bqkv[2, row, :] = value[:, 0:HD]
        o_bin[row, 0:128] = hidden[0]
        o_bin[row, 128:256] = hidden[1]

    for layer in range(LAYERS):
        pl.when(pl.program_id(0) == layer)(functools.partial(small, layer))


def unpack(spread, norm, group, stream, grad):
    by_layer = {
        "gain": (2, D), "shift": (2, D), "aqkv": (3, D, R), "uqkv": (3, HD, R), "aout": (64, R), "uout": (R, D),
        "ain": (D, R), "uin": (R, FF), "adown": (FF, R), "udown": (R, D),
    }
    whole = {"bqkv": (3, LAYERS, HD), "bout": (LAYERS, D), "bin": (LAYERS, FF), "bdown": (LAYERS, D)}
    names = ["gain", "shift", "bqkv", "aqkv", "uqkv", "bout", "aout", "uout", "bin", "ain", "uin", "bdown", "adown", "udown"]

    def pair(rows, cols):
        return pl.BlockSpec((rows, cols), lambda l: (l, 0))

    shapes, specs = [(OWN, D)] * 2, [pair(OWN // 2, D)] * 2
    for name in names:
        if name in whole:
            shape, rank = whole[name], len(whole[name])
            shapes.append(shape)
            specs.append(pl.BlockSpec(shape, lambda l, rank=rank: (0,) * rank))
        else:
            shape, rank = by_layer[name], len(by_layer[name])
            shapes.append((LAYERS, *shape))
            specs.append(pl.BlockSpec((None, *shape), lambda l, rank=rank: (l,) + (0,) * rank))
    return pl.pallas_call(
        unpack_kernel,
        grid=(LAYERS,),
        out_shape=[jax.ShapeDtypeStruct(shape, F32) for shape in shapes],
        in_specs=[pair(768, D), pair(8, D), pair(2 * GROUP, R), pair(OWN // 2, D), pair(OWN // 2, D)],
        out_specs=specs,
        compiler_params=pltpu.CompilerParams(vmem_limit_bytes=60 << 20),
        name="unpack",
    )(spread, norm, group, stream, grad)


def body(x, dy, lengths, gain, shift, w_qkv, b_qkv, a_qkv, u_qkv, w_out, b_out, a_out, u_out,
         w_in, b_in, a_in, u_in, w_down, b_down, a_down, u_down):
    w_qkv = w_qkv.transpose(0, 2, 3, 1).reshape(LAYERS, 3 * HD, D)
    u_qkv = u_qkv.swapaxes(2, 3)
    weights = (w_qkv, a_qkv, u_qkv, w_in, a_in, u_in, w_out, a_out, u_out, w_down, a_down, u_down)
    biases = (b_qkv.swapaxes(0, 1), b_in, b_out, b_down)
    kept = []
    stream = x
    for layer in range(LAYERS):
        nxt, *saved = forward(layer, lengths, stream, gain, shift, biases, weights)
        if layer == 0:
            tabs, first = saved[-2:]
        kept.append((stream, saved[:-2]))
        stream = nxt
    factors = (a_qkv, u_qkv, a_in, u_in, a_out, u_out, a_down, u_down)
    grad, *earlier = backward(1, dy, *kept[1], gain, shift, tabs, first, factors)
    grad, *totals = backward(0, grad, *kept[0], gain, shift, tabs, first, factors, earlier)
    (stream, grad, g_gain, g_shift, g_bqkv, g_aqkv, g_uqkv, g_bout, g_aout, g_uout, g_bin, g_ain, g_uin, g_bdown, g_adown, g_udown) = unpack(
        *totals, stream, grad
    )
    return (
        stream,
        grad,
        g_gain,
        g_shift,
        g_bqkv.swapaxes(0, 1),
        g_aqkv,
        g_uqkv.swapaxes(2, 3),
        g_bout,
        g_aout,
        g_uout,
        g_bin,
        g_ain,
        g_uin,
        g_bdown,
        g_adown,
        g_udown,
    )


def solution(mesh):
    torus = Mesh(mesh.devices.reshape(2, 4, 4, 2, 2), ALL)
    return jax.shard_map(
        body,
        mesh=torus,
        in_specs=(
            P(ALL, None),
            P(ALL, None),
            P(DP, None),
            P(),
            P(),
            P(None, None, None, MP),
            P(None, None, MP),
            P(),
            P(None, None, None, MP),
            P(None, MP, None),
            P(),
            P(None, MP, None),
            P(),
            P(None, None, MP),
            P(None, MP),
            P(),
            P(None, None, MP),
            P(None, MP, None),
            P(),
            P(None, MP, None),
            P(),
        ),
        out_specs=(
            P(ALL, None),
            P(ALL, None),
            P(),
            P(),
            P(None, None, MP),
            P(),
            P(None, None, None, MP),
            P(),
            P(None, MP, None),
            P(),
            P(None, MP),
            P(),
            P(None, None, MP),
            P(),
            P(None, MP, None),
            P(),
        ),
        check_vma=False,
    )
```

```python
import functools
import math

import jax
import jax.numpy as jnp
from jax import lax
from jax.experimental import pallas as pl
from jax.experimental.pallas import tpu as pltpu
from jax.sharding import Mesh
from jax.sharding import PartitionSpec as P

HD = 64
ROT = 16
LAYERS = 2
EPS = 1e-05
FILL = -1000000000.0
MP = ("z", "yh", "c")
DP = ("yl", "x")
ALL = ("yl", "x", "z", "yh", "c")
MESH = pl.DeviceIdType.MESH

D = 1024
T = 2048
OWN = 128
BLK = 256
NB = T // BLK
WIN = 5 * BLK
NQ = 256
FF = 256
NIN = NQ + FF
NOUT = 128 + FF
R = 128
F32 = jnp.float32
BF16 = jnp.bfloat16
HIGH = lax.Precision.HIGHEST

NN = (((1,), (0,)), ((), ()))
NT = (((1,), (1,)), ((), ()))
TN = (((0,), (0,)), ((), ()))


def mm(a, b, dims=NN, precision=None):
    return lax.dot_general(a, b, dims, precision=precision, preferred_element_type=F32)


def split_bf16(a):
    high = a.astype(BF16)
    return high, (a - high.astype(F32)).astype(BF16)


def mm3(a, b, dims=NN):
    ah, al = split_bf16(a)
    bh, bl = split_bf16(b)
    return mm(ah, bh, dims) + (mm(al, bh, dims) + mm(ah, bl, dims))


def rows_of(ref, start, count):
    return ref.at[pl.ds(start if isinstance(start, int) else pl.multiple_of(start, count), count)]


class Place:
    def __init__(self):
        self.z, self.h, self.c = (lax.axis_index(a) for a in MP)
        self.up = {"z": lax.rem(self.z + 1, 4)}
        self.dn = {"z": lax.rem(self.z + 3, 4)}
        self.yy = {"yh": 1 - self.h}
        self.sib = {"c": 1 - self.c}

    def block(self, dz, dh):
        return lax.rem(self.z + dz, 4) * 2 + lax.rem(self.h + dh, 2)

    def shard(self, dz, dh, dc):
        return self.block(dz, dh) * 2 + lax.rem(self.c + dc, 2)

    def arrive(self, wide=False):
        peers = [self.up, self.dn, self.yy, self.sib]
        if wide:
            at = Chips()
            peers = [at.sib] + [at.along(a, d) for a in ("x", "z") for d in (1, 2, 3)] + [at.y_peer(d) for d in (1, 2, 3)]
        barrier = pltpu.get_barrier_semaphore()
        for peer in peers:
            pl.semaphore_signal(barrier, inc=1, device_id=peer, device_id_type=MESH)
        return lambda: pl.semaphore_wait(barrier, len(peers))


def entry(values, i):
    total = values[0]
    for k in range(1, len(values)):
        if values[k] != values[k - 1]:
            total = total + (values[k] - values[k - 1]) * lax.div(i + (len(values) - k), len(values))
    return total


class Sender:
    def __init__(self, sems, partner):
        self.sems = sems
        self.partner = partner
        self.live = []

    def copy(self, src, dst, send_sem, recv_sem, peer):
        return pltpu.make_async_remote_copy(
            src_ref=src, dst_ref=dst, send_sem=send_sem, recv_sem=recv_sem, device_id=peer, device_id_type=MESH
        )

    def send(self, src, dst, peer, recv_sem, like=None):
        self.copy(src, dst, self.sems.at[len(self.live)], recv_sem, peer).start()
        self.live.append(src if like is None else like)

    def got(self, ref, sem):
        self.copy(ref, ref, self.sems.at[0], sem, self.partner).wait_recv()

    def finish(self):
        for k, like in enumerate(self.live):
            self.copy(like, like, self.sems.at[k], self.sems.at[k], self.partner).wait_send()


HALF = OWN // 2
QUART = OWN // 4
GATHER_SENDS = 32
GATHER_SEMS = [pltpu.SemaphoreType.DMA((17,)), pltpu.SemaphoreType.DMA((16,))]


def gather(me, out, buf, direct, cross, compute, before, amid, extra=None):
    def part(dz, dh, dc, k):
        return rows_of(buf, me.shard(dz, dh, dc) * OWN + k * HALF, HALF)

    def sem(sems, dz, dh, k):
        return sems.at[(dz * 2 + dh) * 2 + k]

    half, fourth = rows_of(buf, 0, HALF), rows_of(buf, 0, QUART)

    def send(dz, dh, k, peer, tz, th):
        ref = part(dz, dh, 0, k)
        out.send(ref, ref, peer, sem(direct, tz, th, k), half)

    def over(dz, dh, k):
        ref = part(dz, dh, 0, k)
        out.send(ref, ref, me.sib, sem(cross, dz, dh, k), half)

    def got(dz, dh, k):
        out.got(part(dz, dh, 0, k), sem(direct, dz, dh, k))

    def quarter(dz, k):
        return rows_of(buf, me.shard(dz, 0, 0) * OWN + HALF + k * QUART, QUART)

    send(0, 0, 0, me.yy, 0, 1)
    send(0, 0, 1, me.up, 3, 0)
    send(0, 0, 1, me.dn, 1, 0)
    send(0, 0, 0, me.up, 3, 0)
    send(0, 0, 0, me.dn, 1, 0)
    send(0, 0, 1, me.yy, 0, 1)
    over(0, 0, 0)
    over(0, 0, 1)
    before()
    got(3, 0, 1)
    out.send(quarter(3, 0), quarter(3, 0), me.up, sem(direct, 2, 0, 1), fourth)
    got(1, 0, 1)
    out.send(quarter(1, 1), quarter(1, 1), me.dn, direct.at[16], fourth)
    got(0, 1, 0)
    send(0, 1, 0, me.dn, 1, 1)
    send(0, 1, 0, me.up, 3, 1)
    send(3, 0, 1, me.yy, 3, 1)
    send(1, 0, 1, me.yy, 1, 1)
    over(3, 0, 1)
    over(1, 0, 1)
    over(0, 1, 0)
    got(3, 0, 0)
    send(3, 0, 0, me.up, 2, 0)
    over(3, 0, 0)
    got(1, 0, 0)
    over(1, 0, 0)
    out.got(quarter(2, 0), sem(direct, 2, 0, 1))
    out.got(quarter(2, 1), direct.at[16])
    send(2, 0, 1, me.yy, 2, 1)
    over(2, 0, 1)
    got(0, 1, 1)
    over(0, 1, 1)
    amid()

    def onward():
        got(1, 1, 0)
        send(1, 1, 0, me.dn, 2, 1)
        over(1, 1, 0)

    def late(pairs):
        for dz, dh, k in pairs:
            got(dz, dh, k)
            over(dz, dh, k)

    order = ((0, 0), (3, 0), (1, 0), (0, 1), (2, 0), (3, 1), (1, 1), (2, 1))
    steps = {
        1: onward,
        3: lambda: late(((3, 1, 0), (2, 0, 0))),
        4: lambda: late(((3, 1, 1), (1, 1, 1))),
        7: lambda: late(((2, 1, 0), (2, 1, 1))),
    }

    def visit(i, _):
        for at, step in [*steps.items(), *(extra or {}).items()]:
            pl.when(i == at)(step)
        dz, dh = (entry([pair[j] for pair in order], i) for j in range(2))
        for k in range(2):
            out.got(part(dz, dh, 1, k), sem(cross, dz, dh, k))
        compute(dz, dh)
        return 0

    lax.fori_loop(0, 8, visit, 0)


SCATTER_SENDS = 16
SCATTER_SCRATCH = [
    pltpu.VMEM((8 * OWN, D), F32),
    pltpu.VMEM((8 * OWN, D), BF16),
    pltpu.VMEM((8 * OWN, D), BF16),
    pltpu.VMEM((8 * OWN, D), BF16),
    pltpu.VMEM((2 * HALF, D), BF16),
    pltpu.VMEM((4 * HALF, D), BF16),
    pltpu.VMEM((HALF, D), BF16),
    pltpu.VMEM((4 * HALF, D), BF16),
    pltpu.VMEM((2 * QUART, D), BF16),
    pltpu.VMEM((2 * HALF, D), BF16),
    pltpu.SemaphoreType.DMA((8,)),
    pltpu.SemaphoreType.DMA((8,)),
    pltpu.SemaphoreType.DMA((2,)),
    pltpu.SemaphoreType.DMA((4,)),
    pltpu.SemaphoreType.DMA((1,)),
    pltpu.SemaphoreType.DMA((4,)),
    pltpu.SemaphoreType.DMA((2,)),
    pltpu.SemaphoreType.DMA((2,)),
]


def scatter(me, out, bufs, compute, between, finish, extra=None, quick=False, tail=None):
    (own, other, cross, sums, via, ring, last, pair, via2, ring2,
     s_over, s_cross, s_via, s_ring, s_last, s_pair, s_via2, s_ring2) = bufs

    def give(dz, dh):
        i = dz * 2 + dh

        at = pl.ds(pl.multiple_of(i * OWN, OWN), OWN)

        def put(dc, terms):
            if dc == 0:
                own[at, :] = terms
            else:
                other[at, :] = terms.astype(BF16)

        compute(dz, dh, put)
        rows = rows_of(other, i * OWN, OWN)
        out.copy(rows, rows_of(cross, i * OWN, OWN), s_over.at[i], s_cross.at[i], me.sib).start()

    def wait_cross(dz, dh):
        i = dz * 2 + dh
        out.got(rows_of(cross, i * OWN, OWN), s_cross.at[i])

    def both(dz, dh, start, rows):
        here = pl.ds((dz * 2 + dh) * OWN + start, rows)
        return own[here, :] + cross[here, :].astype(F32)

    def arrived(buf, sems, i, rows):
        ref = rows_of(buf, i * rows, rows)
        out.got(ref, sems.at[i])
        return ref[...].astype(F32)

    def pass_to(dz, dh, start, rows, value, buf, sems, i, peer):
        at = (dz * 2 + dh) * OWN + start
        sums[pl.ds(at, rows), :] = value.astype(BF16)
        out.send(rows_of(sums, at, rows), rows_of(buf, i * rows, rows), peer, sems.at[i], rows_of(sums, 0, rows))

    def first(dz, dh):
        return both(dz, dh, 0, HALF)

    def to_partner(dz):
        pass_to(dz, 1, HALF, HALF, both(dz, 1, HALF, HALF), pair, s_pair, dz, me.yy)

    def second(dz):
        return both(dz, 0, HALF, HALF) + arrived(pair, s_pair, dz, HALF)

    def start_far():
        wait_cross(2, 1)
        pass_to(2, 1, 0, HALF, first(2, 1), via, s_via, 1, me.dn)
        to_partner(2)
        wait_cross(2, 0)
        pass_to(2, 0, 0, HALF, first(2, 0), via, s_via, 0, me.up)

    def near_others():
        wait_cross(1, 1)
        pass_to(1, 1, 0, HALF, first(1, 1), ring, s_ring, 1, me.up)
        to_partner(1)

    def partner_three():
        wait_cross(3, 1)
        to_partner(3)

    def near_own():
        wait_cross(3, 0)
        pass_to(3, 0, 0, HALF, first(3, 0), ring, s_ring, 2, me.dn)

    def far_seconds():
        own[pl.ds(4 * OWN + HALF, HALF), :] = second(2)
        for k, peer in ((0, me.up), (1, me.dn)):
            value = own[pl.ds(4 * OWN + HALF + k * QUART, QUART), :]
            pass_to(2, 0, HALF + k * QUART, QUART, value, via2, s_via2, k, peer)

    def onward():
        wait_cross(1, 0)
        pass_to(3, 1, 0, HALF, first(3, 1) + arrived(via, s_via, 1, HALF), ring, s_ring, 3, me.dn)
        pass_to(1, 0, 0, HALF, first(1, 0) + arrived(via, s_via, 0, HALF), ring, s_ring, 0, me.up)

    def partner_own():
        wait_cross(0, 1)
        to_partner(0)

    if quick:
        order = ((2, 1), (2, 0), (1, 1), (3, 0), (3, 1), (1, 0), (0, 1), (0, 0))
        steps = [(1, start_far), (3, near_others), (3, near_own), (4, partner_three), (5, far_seconds), (6, partner_own), (6, onward)]
    else:
        order = ((2, 1), (2, 0), (1, 1), (3, 1), (1, 0), (3, 0), (0, 1), (0, 0))
        steps = [(1, start_far), (2, near_others), (3, partner_three), (4, onward), (4, far_seconds), (5, near_own), (6, partner_own)]

    def visit(i, _):
        give(*(entry([pair[j] for pair in order], i) for j in range(2)))
        for at, step in [*steps, *(extra or {}).items()]:
            pl.when(i == at)(step)
        return 0

    lax.fori_loop(0, 8, visit, 0)
    if tail is not None:
        for work in between:
            work()
        between = tail
    between[0]()
    for dz, k, peer in ((1, 0, me.up), (3, 1, me.dn)):
        mine = pl.ds(dz * 2 * OWN + HALF, HALF)
        own[mine, :] = second(dz)
        own[pl.ds(dz * 2 * OWN + HALF + k * QUART, QUART), :] += arrived(via2, s_via2, k, QUART)
        pass_to(dz, 0, HALF, HALF, own[mine, :], ring2, s_ring2, k, peer)
    between[1]()
    total = first(0, 1) + arrived(ring, s_ring, 1, HALF) + arrived(ring, s_ring, 3, HALF)
    pass_to(0, 1, 0, HALF, total, last, s_last, 0, me.yy)
    wait_cross(0, 0)
    between[2]()
    finish(HALF, HALF, second(0) + arrived(ring2, s_ring2, 0, HALF) + arrived(ring2, s_ring2, 1, HALF))
    total = first(0, 0) + arrived(ring, s_ring, 0, HALF) + arrived(ring, s_ring, 2, HALF)
    finish(0, HALF, total + arrived(last, s_last, 0, HALF))
    for i in range(8):
        rows = rows_of(other, i * OWN, OWN)
        out.copy(rows, rows, s_over.at[i], s_cross.at[i], me.sib).wait_send()


def gelu_parts(h):
    cdf = 0.5 * (1.0 + lax.erf(h * (2.0**-0.5)))
    return cdf


def lane_roll(a, shift):
    return pltpu.roll(a, shift % 128, 1)


def normalized(x):
    mean = jnp.mean(x, axis=1, keepdims=True)
    centered = x - mean
    scale = lax.rsqrt(jnp.mean(centered * centered, axis=1, keepdims=True) + EPS)
    return centered * scale, scale


class Loads:
    def __init__(self, sems):
        self.sems = sems
        self.count = 0

    def start(self, src, dst):
        copy = pltpu.make_async_copy(src, dst, self.sems.at[self.count])
        self.count += 1
        copy.start()
        return copy


def rotary_tables(lens, tabs, first_row, first, angles):
    token = lax.broadcasted_iota(jnp.int32, (8, T), 1)
    begin = jnp.zeros((8, T), jnp.int32)
    end = 0
    for i in range(3):
        end = end + lens[0, i]
        begin = jnp.where(token >= end, end, begin)
    first_row[...] = begin
    step = lax.broadcasted_iota(jnp.int32, (8, T), 0).astype(F32)
    angle = (token - begin).astype(F32) * jnp.exp(step * (-2.0 * math.log(10000.0) / ROT))
    angles[0:8, :] = jnp.cos(angle)
    angles[8:16, :] = jnp.sin(angle)

    def turn(i, _):
        at = pl.ds(pl.multiple_of(i * BLK, BLK), BLK)
        cos, sin = angles[0:8, at], angles[8:16, at]
        none = jnp.zeros((HD - ROT, BLK), F32)
        for k, head in enumerate(((cos, cos, none + 1.0), (-sin, sin, none))):
            tabs[k, at, :] = jnp.concatenate(head + head, axis=0).T
        first[at, :] = jnp.broadcast_to(first_row[0:1, at].astype(F32), (128, BLK)).T.astype(jnp.int32)
        return 0

    lax.fori_loop(0, NB, turn, 0)


def forward_kernel(layer, lens, x_ref, gains_ref, shifts_ref, b_qkv, b_in, b_out, b_down,
                   wqkv_h, aqkv_h, uqkv_h, win_h, ain_h, uin_h, wout_h, aout_h, uout_h, wdown_h, adown_h, udown_h, *refs):
    (o_x, o_xh, o_qkv, o_ho, o_out, o_lse, o_kt, o_wint, o_wout, o_tabs, o_first,
     xh, qkv, ho, ou, out_t, kt, scores, probs, win, wint, bias, wout, tabs, first, angles,
     wqkv, aqkv, uqkv, w_in, ain, uin, w_out, aout, uout, wdown, adown, udown,
     load_sems, send_sems, g_direct, g_cross, *scat) = refs
    gains, shifts = gains_ref.at[layer], shifts_ref.at[layer]
    me = Place()
    meet = me.arrive()
    loads = Loads(load_sems)
    ins = [
        loads.start(src.at[layer], dst)
        for src, dst in (
            (wqkv_h, wqkv), (aqkv_h, aqkv), (uqkv_h, uqkv), (win_h, w_in), (ain_h, ain), (uin_h, uin),
            (wout_h, w_out), (aout_h, aout), (uout_h, uout), (wdown_h, wdown), (adown_h, adown), (udown_h, udown),
        )
    ]
    out = Sender(send_sems, me.sib)
    rows_of(xh, me.shard(0, 0, 0) * OWN, OWN)[...] = (
        normalized(x_ref[...])[0] * gains[0:1, :] + shifts[0:1, :]
    ).astype(BF16)
    meet()
    outs = []

    def before():
        rotary_tables(lens, tabs, o_first, first, angles)
        for copy in ins[:3]:
            copy.wait()
        for j in range(3):
            here = pl.ds(j * HD, HD)
            wint[here, :] = (wqkv[here, :].astype(F32) + mm3(uqkv[j], aqkv[j], NT)).astype(BF16)
            bias[:, here] = b_qkv[j, layer:layer + 1, :]
        wint[3 * HD:NQ, :] = jnp.zeros((NQ - 3 * HD, D), BF16)
        bias[:, 3 * HD:NQ] = jnp.zeros((1, NQ - 3 * HD), F32)
        win[:, 0:NQ] = wint[0:NQ, :].astype(F32).T.astype(BF16)

    def amid():
        for copy in ins[3:]:
            copy.wait()
        ratio = gains[1:2, :] / gains[0:1, :]
        merged = w_in[...].astype(F32) + mm3(ain[...], uin[...])
        low = merged.astype(BF16)
        b_high, b_low = split_bf16(jnp.broadcast_to(shifts[1:2, :] - shifts[0:1, :] * ratio, (8, D)))
        bias[:, NQ:NIN] = b_in[layer:layer + 1, :] + (mm(b_high, low) + mm(b_low, low))[0:1]
        turned = merged.T * ratio
        wint[NQ:NIN, :] = turned.astype(BF16)
        win[:, NQ:NIN] = turned.T.astype(BF16)
        wout[0:64, :] = (w_out[...].astype(F32) + mm3(aout[...], uout[...])).astype(BF16)
        wout[64:128, :] = jnp.zeros((64, D), BF16)
        wout[128:NOUT, :] = (wdown[...].astype(F32) + mm3(adown[...], udown[...])).astype(BF16)
        outs.append(loads.start(wint, o_wint))
        outs.append(loads.start(wout, o_wout))
        if layer == 0:
            outs.append(loads.start(tabs, o_tabs))

    def project(dz, dh):
        at = pl.ds(pl.multiple_of(me.block(dz, dh) * BLK, BLK), BLK)
        rows = xh[at, :]
        pq = mm(rows, win[:, 0:NQ]) + bias[:, 0:NQ]
        qk = pq[:, 0:128]
        lane = lax.broadcasted_iota(jnp.int32, (BLK, 128), 1)
        other = jnp.where(lax.rem(lane, HD) < ROT // 2, lane_roll(qk, -8), lane_roll(qk, 8))
        turned = qk * tabs[0, at, :] + other * tabs[1, at, :]
        qkv[at, 0:128] = jnp.where(lane < HD, turned * HD**-0.5, 0.0).astype(BF16)
        keys = jnp.where(lane < HD, lane_roll(turned, HD), 0.0)
        qkv[at, 128:256] = keys.astype(BF16)
        kt[:, at] = keys.T.astype(BF16)
        qkv[at, 256:384] = pq[:, 128:256].astype(BF16)
        h = mm(rows, win[:, NQ:NIN]) + bias[:, NQ:NIN]
        ho[at, 128:NOUT] = h
        ou[at, 128:NOUT] = (h * gelu_parts(h)).astype(BF16)

    gather(me, out, xh, g_direct, g_cross, project, before, amid)
    outs.extend([loads.start(xh, o_xh), loads.start(qkv, o_qkv), loads.start(kt, o_kt)])

    def attend(dz, dh, put):
        b = me.block(dz, dh)
        at = pl.ds(pl.multiple_of(b * BLK, BLK), BLK)

        def over_keys(tiles):
            key_at = (b - 4) * BLK if tiles == 5 else 0
            width = tiles * BLK
            q = qkv[at, 0:128]
            row = b * BLK + lax.broadcasted_iota(jnp.int32, (BLK, BLK), 0)
            start = jnp.concatenate([first[at, :], first[at, :]], axis=1)
            peak = None
            for j in range(tiles):
                keys = pl.ds(pl.multiple_of(key_at + j * BLK, BLK), BLK)
                s = mm(q, qkv[keys, 128:256], NT)
                col = key_at + j * BLK + lax.broadcasted_iota(jnp.int32, (BLK, BLK), 1)
                s = jnp.where((col >= start) & (col <= row), s, FILL)
                scores[:, j * BLK:(j + 1) * BLK] = s
                peak = s if peak is None else jnp.maximum(peak, s)
            peak = jnp.max(peak, axis=1, keepdims=True)
            summed = None
            for j in range(tiles):
                p = jnp.exp(scores[:, j * BLK:(j + 1) * BLK] - peak)
                probs[:, j * BLK:(j + 1) * BLK] = p.astype(BF16)
                summed = p if summed is None else summed + p
            summed = jnp.sum(summed, axis=1, keepdims=True)
            values = qkv[pl.ds(pl.multiple_of(key_at, BLK), width), 256:384]
            o = mm(probs[:, 0:width], values) * (1.0 / summed)
            ho[at, 0:128] = o
            ou[at, 0:128] = o.astype(BF16)
            lse = jnp.broadcast_to(peak + jnp.log(summed), (BLK, 128)).T
            o_lse[:, at] = lse[0:8, :]

        pl.when(b < 2)(lambda: over_keys(2))
        pl.when((b >= 2) & (b < 4))(lambda: over_keys(4))
        pl.when(b >= 4)(lambda: over_keys(5))
        out_t[:, at] = ou[at, :].astype(F32).T.astype(BF16)
        for dc in range(2):
            put(dc, mm(rows_of(ou, me.shard(dz, dh, dc) * OWN, OWN)[...], wout[...]))

    def store():
        outs.append(loads.start(ho, o_ho))
        outs.append(loads.start(out_t, o_out))

    def nothing():
        pass

    def finish(at, rows, total):
        here = pl.ds(at, rows)
        o_x[here, :] = x_ref[here, :] + total + (b_out[layer:layer + 1, :] + b_down[layer:layer + 1, :])

    scatter(me, out, scat, attend, (store, nothing, nothing), finish)
    for copy in outs:
        copy.wait()
    out.finish()


VM = pl.BlockSpec(memory_space=pltpu.VMEM)
HBM = pl.BlockSpec(memory_space=pl.ANY)


SMEM = pl.BlockSpec(memory_space=pltpu.SMEM)


def forward(layer, lens, x, gains, shifts, biases, weights):
    vmem = pltpu.VMEM
    shapes = [
        jax.ShapeDtypeStruct((OWN, D), F32),
        jax.ShapeDtypeStruct((T, D), BF16),
        jax.ShapeDtypeStruct((T, 384), BF16),
        jax.ShapeDtypeStruct((T, NOUT), F32),
        jax.ShapeDtypeStruct((NOUT, T), BF16),
        jax.ShapeDtypeStruct((8, T), F32),
        jax.ShapeDtypeStruct((128, T), BF16),
        jax.ShapeDtypeStruct((NIN, D), BF16),
        jax.ShapeDtypeStruct((NOUT, D), BF16),
        jax.ShapeDtypeStruct((2, T, 128), F32),
        jax.ShapeDtypeStruct((8, T), jnp.int32),
    ]
    return pl.pallas_call(
        functools.partial(forward_kernel, layer),
        out_shape=shapes,
        in_specs=[SMEM] + [VM] * 7 + [HBM] * 12,
        out_specs=[VM, HBM, HBM, HBM, HBM, VM, HBM, HBM, HBM, HBM, VM],
        scratch_shapes=[
            vmem((T, D), BF16),
            vmem((T, 384), BF16),
            vmem((T, NOUT), F32),
            vmem((T, NOUT), BF16),
            vmem((NOUT, T), BF16),
            vmem((128, T), BF16),
            vmem((BLK, WIN), F32),
            vmem((BLK, WIN), BF16),
            vmem((D, NIN), BF16),
            vmem((NIN, D), BF16),
            vmem((1, NIN), F32),
            vmem((NOUT, D), BF16),
            vmem((2, T, 128), F32),
            vmem((T, 128), jnp.int32),
            vmem((16, T), F32),
            vmem((192, D), BF16),
            vmem((3, D, R), F32),
            vmem((3, HD, R), F32),
            vmem((D, FF), BF16),
            vmem((D, R), F32),
            vmem((R, FF), F32),
            vmem((64, D), BF16),
            vmem((64, R), F32),
            vmem((R, D), F32),
            vmem((FF, D), BF16),
            vmem((FF, R), F32),
            vmem((R, D), F32),
            pltpu.SemaphoreType.DMA((24,)),
            pltpu.SemaphoreType.DMA((GATHER_SENDS + SCATTER_SENDS,)),
            *GATHER_SEMS,
            *SCATTER_SCRATCH,
        ],
        compiler_params=pltpu.CompilerParams(
            collective_id=layer, has_side_effects=True, vmem_limit_bytes=60 << 20
        ),
        name=f"forward_layer{layer}",
    )(lens, x, gains, shifts, *biases, *weights)


def backward_kernel(layer, last, dy_ref, x_ref, xh_h, qkv_h, ho_h, out_h, lse_ref, kt_h, wint_h, wout_h, gains_ref, shifts_ref,
                    tabs_h, first_ref, aqkv_h, uqkv_h, ain_h, bin_h, aout_h, bout_h, adown_h, bdown_h, *refs):
    refs = list(refs)
    take = lambda count: [refs.pop(0) for _ in range(count)]
    if last:
        earlier_h, earlier_norm, earlier_group, earlier_sums = take(4)
        o_dx, o_total, o_norm_total, o_group_total = take(4)
    else:
        o_dx, o_spread, o_norm, o_group, o_sums = take(5)
    (dy, xh, qkv, ho, out_t, kt, dph, low, dph_t, acc, wint, wout, tabs, aqkv, uqkv, ain, bin_, aout, bout, adown, bdown,
     load_sems, send_sems, g_direct, g_cross) = take(25)
    scat = take(len(SCATTER_SCRATCH))
    if last:
        o_spread, o_norm, o_group, o_sums, earlier, total = take(6)
    gains, shifts = gains_ref.at[layer], shifts_ref.at[layer]
    me = Place()
    meet = me.arrive(last)
    loads = Loads(load_sems)
    early = [
        loads.start(wout_h, wout),
        loads.start(ho_h, ho),
        loads.start(qkv_h, qkv),
        loads.start(kt_h, kt),
    ]
    late = [
        loads.start(tabs_h, tabs),
        loads.start(wint_h, wint),
        loads.start(xh_h, xh),
        loads.start(out_h, out_t),
        loads.start(aqkv_h.at[layer], aqkv),
        loads.start(uqkv_h.at[layer], uqkv),
        loads.start(ain_h.at[layer], ain),
        loads.start(bin_h.at[layer], bin_),
        loads.start(aout_h.at[layer], aout),
        loads.start(bout_h.at[layer], bout),
        loads.start(adown_h.at[layer], adown),
        loads.start(bdown_h.at[layer], bdown),
    ]
    out = Sender(send_sems, me.sib)
    rows_of(dy, me.shard(0, 0, 0) * OWN, OWN)[...] = dy_ref[...].astype(BF16)
    meet()

    stages, ends = [], []
    if last:
        at_chip = Chips()
        half = pl.ds(pl.multiple_of(at_chip.c * (D // 2), D // 2), D // 2)
        copy_in = loads.start(earlier_h.at[:, half], earlier)
        n = len(path_scratch(128))
        stages = spread_stages(
            at_chip, out, earlier_h, total.at[pl.ds(768, 768)], (0, 512), "x", "z", take(n), earlier
        )
        for begin, axes in ((0, ("x", "z")), (256, ("z", "x"))):
            ends.append(spread_stages(at_chip, out, o_spread, total.at[pl.ds(0, 768)], (begin, 256), *axes, take(n)))
        ends.append(norm_group_stages(
            at_chip, out, (o_norm, earlier_norm), (o_group, earlier_group), (o_sums, earlier_sums),
            o_norm_total, o_group_total, refs,
        ))

    def stage(i):
        if stages:
            stages[i]()

    def end(i):
        for kind in ends:
            kind[i]()

    def extra(at, i):
        return {at: lambda: stage(i)} if last else None

    def before():
        if last:
            copy_in.wait()
        stage(0)
        acc[...] = jnp.zeros(acc.shape, F32)
        stage(1)

    def amid():
        for copy in early:
            copy.wait()

    def pull(dz, dh):
        b = me.block(dz, dh)
        at = pl.ds(pl.multiple_of(b * BLK, BLK), BLK)
        rows = dy[at, :]
        du = mm(rows, wout[128:NOUT, :], NT)
        h = ho[at, 128:NOUT]
        slope = gelu_parts(h) + h * (jnp.exp(-0.5 * h * h) * (2.0 * math.pi) ** -0.5)
        ho[at, 128:NOUT] = slope * du
        do = mm(rows, wout[0:128, :], NT).astype(BF16)
        drop = jnp.sum((do.astype(F32) * ho[at, 0:128]).T, axis=0, keepdims=True)
        lse = lse_ref[0:1, at]
        start = first_ref[0:1, at]
        q = qkv[at, 0:128]
        key_at = jnp.maximum(b - 5, 0)
        wide = 3 * BLK
        col = b * BLK + lax.broadcasted_iota(jnp.int32, (wide, BLK), 1)

        def step(j, dq):
            key = (key_at + 3 * j) * BLK
            keys = pl.ds(pl.multiple_of(key, BLK), wide)
            s = mm(qkv[keys, 128:256], q, NT)
            row = key + lax.broadcasted_iota(jnp.int32, (wide, BLK), 0)
            p = jnp.where((row >= start) & (row <= col), jnp.exp(s - lse), 0.0)
            dp = mm(qkv[keys, 256:384], do, NT)
            ds = (p * (dp - drop)).astype(BF16)
            acc[keys, 128:256] += mm(p.astype(BF16), do)
            acc[keys, 0:128] += mm(ds, q)
            return dq + mm(kt[:, keys], ds)

        dq = lax.fori_loop(0, (jnp.minimum(b, 5) + 3) // 3, step, jnp.zeros((128, BLK), F32))
        ho[at, 0:128] = dq.T * HD**-0.5

    gather(me, out, dy, g_direct, g_cross, pull, before, amid, extra(4, 2))
    stage(3)
    for copy in late:
        copy.wait()

    def send_back(dz, dh, put):
        b = me.block(dz, dh)
        at = pl.ds(pl.multiple_of(b * BLK, BLK), BLK)
        g = ho[at, 0:128] + lane_roll(acc[at, 0:128], HD)
        side = g * tabs[1, at, :]
        lane = lax.rem(lax.broadcasted_iota(jnp.int32, (BLK, 128), 1), HD)
        side = jnp.where(lane < ROT // 2, lane_roll(side, -8), jnp.where(lane < ROT, lane_roll(side, 8), 0.0))
        turned = g * tabs[0, at, :] + side
        dph[:, 0:128] = turned.astype(BF16)
        dph[:, 128:256] = acc[at, 128:256].astype(BF16)
        dph[:, NQ:NIN] = ho[at, 128:NOUT].astype(BF16)
        rows = dph[...]
        for dc in range(2):
            put(dc, mm(rows_of(dph, lax.rem(me.c + dc, 2) * OWN, OWN)[...], wint[...]))
        dph_t[:, at] = rows.astype(F32).T.astype(BF16)

    def by_columns(piece):
        def visit(i, _):
            piece(pl.ds(pl.multiple_of(i * 256, 256), 256))
            return 0

        lax.fori_loop(0, D // 256, visit, 0)

    def weight_grad(row, at, width):
        here = pl.ds(at, width)
        total = jnp.sum(dph_t[here, :].astype(F32), axis=1, keepdims=True)
        o_sums[:, here] = jnp.broadcast_to(total, (width, 128)).T[0:8, :]

        def piece(cols):
            grad = mm(dph_t[here, :], xh[:, cols])
            weight = wint[here, cols].astype(F32)
            by_gain = jnp.sum(grad * weight, axis=0, keepdims=True)
            by_shift = jnp.sum(total * weight, axis=0, keepdims=True)
            g, b = gains[0:1, cols], shifts[0:1, cols]
            if row == 1:
                ratio = gains[1:2, cols] / g
                by_gain, by_shift = by_gain / ratio, by_shift / ratio
                grad = grad * ratio + total * (shifts[1:2, cols] - b * ratio)
            o_norm[row:row + 1, cols] = (by_gain - b * by_shift) / g
            o_norm[2 + row:3 + row, cols] = by_shift
            low[here, cols] = grad.astype(BF16)

        by_columns(piece)

    def factors_qkv():
        stage(5)
        weight_grad(0, 0, NQ)
        for j in range(3):
            o_spread[j * R:(j + 1) * R, :] = mm(uqkv[j].astype(BF16), low[j * HD:(j + 1) * HD, :], TN).astype(BF16)
            o_group[j * HD:(j + 1) * HD, :] = mm(low[j * HD:(j + 1) * HD, :], aqkv[j].astype(BF16))

    def factors_in():
        weight_grad(1, NQ, FF)
        o_spread[3 * R:4 * R, :] = mm(bin_[...].astype(BF16), low[NQ:NIN, :]).astype(BF16)
        o_group[256:512, :] = mm(low[NQ:NIN, :], ain[...].astype(BF16))

    def factors_out():
        def piece(cols):
            low[0:64, cols] = mm(out_t[0:64, :], dy[:, cols]).astype(BF16)
            low[NQ:NIN, cols] = mm(out_t[128:NOUT, :], dy[:, cols]).astype(BF16)

        by_columns(piece)
        o_spread[4 * R:5 * R, :] = mm(aout[...].astype(BF16), low[0:64, :], TN).astype(BF16)
        o_group[192:256, :] = mm(low[0:64, :], bout[...].astype(BF16), NT)
        o_spread[5 * R:6 * R, :] = mm(adown[...].astype(BF16), low[NQ:NIN, :], TN).astype(BF16)
        o_group[512:768, :] = mm(low[NQ:NIN, :], bdown[...].astype(BF16), NT)
        o_norm[4:5, :] = jnp.sum(dy_ref[...], axis=0, keepdims=True)
        o_norm[5:8, :] = jnp.zeros((3, D), F32)
        stage(6)
        end(0)
        end(1)

    def finish(at, rows, total):
        here = pl.ds(at, rows)
        hat, rstd = normalized(x_ref[here, :])
        total = total * gains[0:1, :]
        mean = jnp.mean(total, axis=1, keepdims=True)
        along = jnp.mean(total * hat, axis=1, keepdims=True)
        o_dx[here, :] = dy_ref[here, :] + rstd * (total - mean - hat * along)

    ends_between = [lambda: None, lambda: None, lambda: end(2)]
    scatter(me, out, scat, send_back, (factors_qkv, factors_in, factors_out), finish, extra(4, 4), True, ends_between if last else None)
    if last:
        stage(7)
        for i in range(3, 8):
            end(i)
        store = loads.start(total, o_total)
        out.finish()
        store.wait()
    else:
        out.finish()


def backward(layer, dy, x, saved, gains, shifts, tabs, first, factors, earlier=None):
    last = earlier is not None
    grads = [((6 * R, D), BF16), ((8, D), F32), ((768, R), F32), ((8, NIN), F32)]
    totals = [((LAYERS * 6 * R, D), BF16), ((8 * LAYERS, D), F32), ((4 * GROUP, R), BF16)]
    shapes = [jax.ShapeDtypeStruct(*kind) for kind in [((OWN, D), F32), *(totals if last else grads)]]
    sums = [pltpu.VMEM(*kind) for kind in grads] + [pltpu.VMEM((6 * R, D // 2), BF16), pltpu.VMEM(*totals[0])]
    sums += path_scratch(512) + path_scratch(256) * 2 + NORM_GROUP_SCRATCH
    sends = GATHER_SENDS + SCATTER_SENDS + (3 * PATH_SENDS + NORM_GROUP_SENDS if last else 0)
    return pl.pallas_call(
        functools.partial(backward_kernel, layer, last),
        out_shape=shapes,
        in_specs=[VM, VM, HBM, HBM, HBM, HBM, VM, HBM, HBM, HBM, VM, VM, HBM, VM] + [HBM] * 8 + ([HBM, VM, VM, VM] if last else []),
        out_specs=[VM, HBM, VM, VM] if last else [VM] * 5,
        scratch_shapes=[
            pltpu.VMEM((T, D), BF16),
            pltpu.VMEM((T, D), BF16),
            pltpu.VMEM((T, 384), BF16),
            pltpu.VMEM((T, NOUT), F32),
            pltpu.VMEM((NOUT, T), BF16),
            pltpu.VMEM((128, T), BF16),
            pltpu.VMEM((BLK, NIN), BF16),
            pltpu.VMEM((NIN, D), BF16),
            pltpu.VMEM((NIN, T), BF16),
            pltpu.VMEM((T, 256), F32),
            pltpu.VMEM((NIN, D), BF16),
            pltpu.VMEM((NOUT, D), BF16),
            pltpu.VMEM((2, T, 128), F32),
            pltpu.VMEM((3, D, R), F32),
            pltpu.VMEM((3, HD, R), F32),
            pltpu.VMEM((D, R), F32),
            pltpu.VMEM((R, FF), F32),
            pltpu.VMEM((64, R), F32),
            pltpu.VMEM((R, D), F32),
            pltpu.VMEM((FF, R), F32),
            pltpu.VMEM((R, D), F32),
            pltpu.SemaphoreType.DMA((24,)),
            pltpu.SemaphoreType.DMA((sends,)),
            *GATHER_SEMS,
            *SCATTER_SCRATCH,
            *(sums if last else []),
        ],
        compiler_params=pltpu.CompilerParams(
            collective_id=LAYERS + layer, has_side_effects=True, vmem_limit_bytes=60 << 20
        ),
        name=f"backward_layer{layer}",
    )(dy, x, *saved, gains, shifts, tabs, first, *factors, *(earlier or ()))


QUARTER = 768 // 4
PATH_SENDS = 23


def path_scratch(width):
    dma = pltpu.SemaphoreType.DMA
    return [
        pltpu.VMEM((768, width), BF16),
        pltpu.VMEM((768, width), BF16),
        pltpu.VMEM((3, QUARTER, width), BF16),
        pltpu.VMEM((QUARTER, width), F32),
        pltpu.VMEM((QUARTER, width), BF16),
        pltpu.VMEM((3, 48, width), BF16),
        pltpu.VMEM((4, 48, width), BF16),
        pltpu.VMEM((QUARTER, width), BF16),
        dma((4,)),
        dma((3,)),
        dma((3,)),
        dma((3,)),
        dma((3,)),
        dma((3,)),
        dma((4,)),
    ]


class Chips:
    def __init__(self):
        self.yl, self.x, self.z, self.yh, self.c = (lax.axis_index(a) for a in ALL)
        self.y = self.yh * 2 + self.yl
        self.sib = {"c": 1 - self.c}

    def here(self, axis):
        return {"x": self.x, "z": self.z}[axis]

    def along(self, axis, d):
        return {axis: lax.rem(self.here(axis) + d, 4)}

    def y_peer(self, d):
        there = lax.rem(self.y + d, 4)
        return {"yh": lax.div(there, 2), "yl": lax.rem(there, 2)}

    def quarter(self, axis, d, size):
        return pl.multiple_of(lax.rem(self.here(axis) + d, 4) * size, size)


def spread_stages(at, out, src, dst, lanes, first, second, bufs, own_half=None):
    cross, low, slots1, acc, low2, slots2, along_y, totals, s_cross, s_one, s_two, s_y, s_back2, s_back1, s_backc = bufs
    begin, width = lanes
    mine = pl.ds(pl.multiple_of(at.c * 512 + begin, 128), width)
    theirs = pl.ds(pl.multiple_of((1 - at.c) * 512 + begin, 128), width)

    def rows(d):
        return pl.ds(at.quarter(first, d, QUARTER), QUARTER)

    def part(d):
        return pl.ds(at.quarter(second, d, 48), 48)

    big = dst.at[pl.ds(0, QUARTER), pl.ds(0, width)]
    small = low2.at[pl.ds(0, 48)]

    def over_core():
        for d in (2, 1, 3, 0):
            out.send(src.at[rows(d), theirs], cross.at[rows(d)], at.sib, s_cross.at[d], big)

    def along_first():
        for d in (2, 1, 3, 0):
            out.got(cross.at[rows(d)], s_cross.at[d])
            both = (src[rows(d), mine] if own_half is None else own_half[rows(d), :]).astype(F32)
            both = both + cross[rows(d), :].astype(F32)
            if d == 0:
                acc[...] = both
            else:
                low[rows(d), :] = both.astype(BF16)
                out.send(low.at[rows(d)], slots1.at[d - 1], at.along(first, d), s_one.at[d - 1], low.at[pl.ds(0, QUARTER)])

    def along_second():
        total = acc[...]
        for d in (1, 2, 3):
            out.got(slots1.at[d - 1], s_one.at[d - 1])
            total = total + slots1[d - 1].astype(F32)
        acc[...] = total
        low2[...] = total.astype(BF16)
        for d in (2, 1, 3):
            out.send(low2.at[part(d)], slots2.at[d - 1], at.along(second, d), s_two.at[d - 1], small)

    def along_third():
        total = acc[part(0), :]
        for d in (1, 2, 3):
            out.got(slots2.at[d - 1], s_two.at[d - 1])
            total = total + slots2[d - 1].astype(F32)
        own = along_y.at[at.y]
        own[...] = total.astype(BF16)
        for d in (2, 1, 3):
            out.send(own, own, at.y_peer(d), s_y.at[d - 1], along_y.at[0])

    def back_second():
        for d in (1, 2, 3):
            out.got(along_y.at[lax.rem(at.y + 4 - d, 4)], s_y.at[d - 1])
        term = [along_y[i].astype(F32) for i in range(4)]
        own = totals.at[part(0)]
        own[...] = ((term[0] + term[1]) + (term[2] + term[3])).astype(BF16)
        for d in (2, 1, 3):
            out.send(own, own, at.along(second, d), s_back2.at[d - 1], small)

    def back_first():
        for d in (1, 2, 3):
            out.got(totals.at[part(4 - d)], s_back2.at[d - 1])
        own = dst.at[rows(0), mine]
        own[...] = totals[...]
        for d in (2, 1, 3):
            out.send(own, own, at.along(first, d), s_back1.at[d - 1], big)
        out.send(own, own, at.sib, s_backc.at[0], big)

    def back_core():
        for d in (1, 3, 2):
            own = dst.at[rows(4 - d), mine]
            out.got(own, s_back1.at[d - 1])
            out.send(own, own, at.sib, s_backc.at[d], big)

    def arrive():
        for d in range(4):
            out.got(dst.at[rows(4 - d), theirs], s_backc.at[d])

    return [over_core, along_first, along_second, along_third, back_second, back_first, back_core, arrive]


GROUP = 400


NORM_GROUP_SENDS = 1 + 3 + 3 + 3 + 1 + 3 + 3 + 1
NORM_GROUP_SCRATCH = [
    pltpu.VMEM((2, 16, 512), F32),
    pltpu.VMEM((12, 16, 512), F32),
    pltpu.VMEM((4 * GROUP, R), F32),
    pltpu.VMEM((4 * GROUP, R), BF16),
    pltpu.VMEM((3, GROUP, R), BF16),
    pltpu.VMEM((2, GROUP, R), BF16),
    pltpu.SemaphoreType.DMA((11,)),
    pltpu.SemaphoreType.DMA((7,)),
]


def norm_group_stages(at, out, norms, groups, sums, o_norm, o_group, bufs):
    n_first, n_slots, g_own, g_low, g_slots, g_pair, s_norm, s_group = bufs
    mine = pl.ds(pl.multiple_of(at.c * 512, 512), 512)
    theirs = pl.ds(pl.multiple_of((1 - at.c) * 512, 512), 512)

    def n_stage(stage, value, index, peer_of, base):
        own = n_slots.at[stage * 4 + index]
        own[...] = value
        for d in (1, 2, 3):
            out.send(own, own, peer_of(d), s_norm.at[base + d - 1])

    def n_sum(stage, index, base):
        for d in (1, 2, 3):
            out.got(n_slots.at[stage * 4 + lax.rem(index + 4 - d, 4)], s_norm.at[base + d - 1])
        return (n_slots[stage * 4] + n_slots[stage * 4 + 1]) + (n_slots[stage * 4 + 2] + n_slots[stage * 4 + 3])

    def g_rows(d):
        return pl.ds(at.quarter("x", d, GROUP), GROUP)

    def begin():
        for i, norm in enumerate(norms):
            n_first[0, i * 8:i * 8 + 8, :] = norm[:, theirs]
        out.send(n_first.at[0], n_first.at[1], at.sib, s_norm.at[0])
        for i in range(4):
            group, total, half = groups[i // 2], sums[i // 2], i % 2
            g_own[i * GROUP:i * GROUP + 384, :] = group[half * 384:half * 384 + 384, :]
            for k in range(2):
                rows = pl.ds(i * GROUP + 384 + 8 * k, 8)
                g_own[rows, :] = total[:, half * 256 + 128 * k:half * 256 + 128 * k + 128]
        g_low[...] = g_own[...].astype(BF16)
        for d in (2, 1, 3):
            out.send(g_low.at[g_rows(d)], g_slots.at[d - 1], at.along("x", d), s_group.at[d - 1])

    def along_x():
        out.got(n_first.at[1], s_norm.at[0])
        first = jnp.concatenate([norm[:, mine] for norm in norms], axis=0) + n_first[1]
        n_stage(0, first, at.x, lambda d: at.along("x", d), 1)

    def along_z():
        total = g_own[g_rows(0), :]
        for d in (1, 2, 3):
            out.got(g_slots.at[d - 1], s_group.at[d - 1])
            total = total + g_slots[d - 1].astype(F32)
        g_pair[0] = total.astype(BF16)
        out.send(g_pair.at[0], g_pair.at[1], {"yl": 1 - at.yl}, s_group.at[3])
        n_stage(1, n_sum(0, at.x, 1), at.z, lambda d: at.along("z", d), 4)

    def along_third():
        out.got(g_pair.at[1], s_group.at[3])
        own = o_group.at[g_rows(0)]
        own[...] = (g_pair[0].astype(F32) + g_pair[1].astype(F32)).astype(BF16)
        for d in (1, 2, 3):
            out.send(own, own, at.along("x", d), s_group.at[3 + d])
        n_stage(2, n_sum(1, at.z, 4), at.y, at.y_peer, 7)

    def back_core():
        o_norm[:, mine] = n_sum(2, at.y, 7)
        out.send(o_norm.at[:, mine], o_norm.at[:, mine], at.sib, s_norm.at[10])

    def nothing():
        pass

    def arrive():
        for d in (1, 2, 3):
            out.got(o_group.at[g_rows(4 - d)], s_group.at[3 + d])
        out.got(o_norm.at[:, theirs], s_norm.at[10])

    return [begin, along_x, along_z, along_third, back_core, nothing, nothing, arrive]


def unpack_kernel(spread, norm, group, stream, grad, o_stream, o_grad, o_gain, o_shift, o_bqkv, o_aqkv, o_uqkv, o_bout, o_aout, o_uout, o_bin, o_ain, o_uin,
                  o_bdown, o_adown, o_udown):
    o_stream[...] = stream[...]
    o_grad[...] = grad[...]
    for j in range(3):
        o_aqkv[j] = spread[j * R:(j + 1) * R, :].astype(F32).T
    o_ain[...] = spread[3 * R:4 * R, :].astype(F32).T
    o_uout[...] = spread[4 * R:5 * R, :].astype(F32)
    o_udown[...] = spread[5 * R:6 * R, :].astype(F32)
    o_gain[...] = norm[0:2, :]
    o_shift[...] = norm[2:4, :]
    for j in range(3):
        o_uqkv[j] = group[j * HD:(j + 1) * HD, :].astype(F32)
    o_aout[...] = group[192:256, :].astype(F32)
    o_uin[:, 0:128] = group[256:384, :].astype(F32).T
    o_uin[:, 128:256] = group[GROUP:GROUP + 128, :].astype(F32).T
    o_adown[...] = group[GROUP + 128:GROUP + 384, :].astype(F32)
    query_key, value = group[384:385, :].astype(F32), group[392:393, :].astype(F32)
    hidden = [group[GROUP + 384 + 8 * k:GROUP + 385 + 8 * k, :].astype(F32) for k in range(2)]

    def small(layer):
        row = slice(layer, layer + 1)
        o_bout[row, :] = norm[4:5, :]
        o_bdown[row, :] = norm[4:5, :]
        o_bqkv[0, row, :] = query_key[:, 0:HD]
        o_bqkv[1, row, :] = query_key[:, HD:2 * HD]
        o_bqkv[2, row, :] = value[:, 0:HD]
        o_bin[row, 0:128] = hidden[0]
        o_bin[row, 128:256] = hidden[1]

    for layer in range(LAYERS):
        pl.when(pl.program_id(0) == layer)(functools.partial(small, layer))


def unpack(spread, norm, group, stream, grad):
    by_layer = {
        "gain": (2, D), "shift": (2, D), "aqkv": (3, D, R), "uqkv": (3, HD, R), "aout": (64, R), "uout": (R, D),
        "ain": (D, R), "uin": (R, FF), "adown": (FF, R), "udown": (R, D),
    }
    whole = {"bqkv": (3, LAYERS, HD), "bout": (LAYERS, D), "bin": (LAYERS, FF), "bdown": (LAYERS, D)}
    names = ["gain", "shift", "bqkv", "aqkv", "uqkv", "bout", "aout", "uout", "bin", "ain", "uin", "bdown", "adown", "udown"]

    def pair(rows, cols):
        return pl.BlockSpec((rows, cols), lambda l: (l, 0))

    shapes, specs = [(OWN, D)] * 2, [pair(OWN // 2, D)] * 2
    for name in names:
        if name in whole:
            shape, rank = whole[name], len(whole[name])
            shapes.append(shape)
            specs.append(pl.BlockSpec(shape, lambda l, rank=rank: (0,) * rank))
        else:
            shape, rank = by_layer[name], len(by_layer[name])
            shapes.append((LAYERS, *shape))
            specs.append(pl.BlockSpec((None, *shape), lambda l, rank=rank: (l,) + (0,) * rank))
    return pl.pallas_call(
        unpack_kernel,
        grid=(LAYERS,),
        out_shape=[jax.ShapeDtypeStruct(shape, F32) for shape in shapes],
        in_specs=[pair(768, D), pair(8, D), pair(2 * GROUP, R), pair(OWN // 2, D), pair(OWN // 2, D)],
        out_specs=specs,
        compiler_params=pltpu.CompilerParams(vmem_limit_bytes=60 << 20),
        name="unpack",
    )(spread, norm, group, stream, grad)


def body(x, dy, lengths, gain, shift, w_qkv, b_qkv, a_qkv, u_qkv, w_out, b_out, a_out, u_out,
         w_in, b_in, a_in, u_in, w_down, b_down, a_down, u_down):
    w_qkv = w_qkv.transpose(0, 2, 3, 1).reshape(LAYERS, 3 * HD, D)
    u_qkv = u_qkv.swapaxes(2, 3)
    weights = (w_qkv, a_qkv, u_qkv, w_in, a_in, u_in, w_out, a_out, u_out, w_down, a_down, u_down)
    biases = (b_qkv.swapaxes(0, 1), b_in, b_out, b_down)
    kept = []
    stream = x
    for layer in range(LAYERS):
        nxt, *saved = forward(layer, lengths, stream, gain, shift, biases, weights)
        if layer == 0:
            tabs, first = saved[-2:]
        kept.append((stream, saved[:-2]))
        stream = nxt
    factors = (a_qkv, u_qkv, a_in, u_in, a_out, u_out, a_down, u_down)
    grad, *earlier = backward(1, dy, *kept[1], gain, shift, tabs, first, factors)
    grad, *totals = backward(0, grad, *kept[0], gain, shift, tabs, first, factors, earlier)
    (stream, grad, g_gain, g_shift, g_bqkv, g_aqkv, g_uqkv, g_bout, g_aout, g_uout, g_bin, g_ain, g_uin, g_bdown, g_adown, g_udown) = unpack(
        *totals, stream, grad
    )
    return (
        stream,
        grad,
        g_gain,
        g_shift,
        g_bqkv.swapaxes(0, 1),
        g_aqkv,
        g_uqkv.swapaxes(2, 3),
        g_bout,
        g_aout,
        g_uout,
        g_bin,
        g_ain,
        g_uin,
        g_bdown,
        g_adown,
        g_udown,
    )


def solution(mesh):
    torus = Mesh(mesh.devices.reshape(2, 4, 4, 2, 2), ALL)
    return jax.shard_map(
        body,
        mesh=torus,
        in_specs=(
            P(ALL, None),
            P(ALL, None),
            P(DP, None),
            P(),
            P(),
            P(None, None, None, MP),
            P(None, None, MP),
            P(),
            P(None, None, None, MP),
            P(None, MP, None),
            P(),
            P(None, MP, None),
            P(),
            P(None, None, MP),
            P(None, MP),
            P(),
            P(None, None, MP),
            P(None, MP, None),
            P(),
            P(None, MP, None),
            P(),
        ),
        out_specs=(
            P(ALL, None),
            P(ALL, None),
            P(),
            P(),
            P(None, None, MP),
            P(),
            P(None, None, None, MP),
            P(),
            P(None, MP, None),
            P(),
            P(None, MP),
            P(),
            P(None, None, MP),
            P(),
            P(None, MP, None),
            P(),
        ),
        check_vma=False,
    )
```

```python
import functools
import math

import jax
import jax.numpy as jnp
from jax import lax
from jax.experimental import pallas as pl
from jax.experimental.pallas import tpu as pltpu
from jax.sharding import Mesh
from jax.sharding import PartitionSpec as P

HD = 64
ROT = 16
LAYERS = 2
EPS = 1e-05
FILL = -1000000000.0
MP = ("z", "yh", "c")
DP = ("yl", "x")
ALL = ("yl", "x", "z", "yh", "c")
MESH = pl.DeviceIdType.MESH

D = 1024
T = 2048
OWN = 128
BLK = 256
NB = T // BLK
WIN = 5 * BLK
NQ = 256
FF = 256
NIN = NQ + FF
NOUT = 128 + FF
R = 128
F32 = jnp.float32
BF16 = jnp.bfloat16
HIGH = lax.Precision.HIGHEST

NN = (((1,), (0,)), ((), ()))
NT = (((1,), (1,)), ((), ()))
TN = (((0,), (0,)), ((), ()))


def mm(a, b, dims=NN, precision=None):
    return lax.dot_general(a, b, dims, precision=precision, preferred_element_type=F32)


def split_bf16(a):
    high = a.astype(BF16)
    return high, (a - high.astype(F32)).astype(BF16)


def mm3(a, b, dims=NN):
    ah, al = split_bf16(a)
    bh, bl = split_bf16(b)
    return mm(ah, bh, dims) + (mm(al, bh, dims) + mm(ah, bl, dims))


def rows_of(ref, start, count):
    return ref.at[pl.ds(start if isinstance(start, int) else pl.multiple_of(start, count), count)]


class Place:
    def __init__(self):
        self.z, self.h, self.c = (lax.axis_index(a) for a in MP)
        self.up = {"z": lax.rem(self.z + 1, 4)}
        self.dn = {"z": lax.rem(self.z + 3, 4)}
        self.yy = {"yh": 1 - self.h}
        self.sib = {"c": 1 - self.c}

    def block(self, dz, dh):
        return lax.rem(self.z + dz, 4) * 2 + lax.rem(self.h + dh, 2)

    def shard(self, dz, dh, dc):
        return self.block(dz, dh) * 2 + lax.rem(self.c + dc, 2)

    def arrive(self, wide=False):
        peers = [self.up, self.dn, self.yy, self.sib]
        if wide:
            at = Chips()
            peers = [at.sib] + [at.along(a, d) for a in ("x", "z") for d in (1, 2, 3)] + [at.y_peer(d) for d in (1, 2, 3)]
        barrier = pltpu.get_barrier_semaphore()
        for peer in peers:
            pl.semaphore_signal(barrier, inc=1, device_id=peer, device_id_type=MESH)
        return lambda: pl.semaphore_wait(barrier, len(peers))


def entry(values, i):
    total = values[0]
    for k in range(1, len(values)):
        if values[k] != values[k - 1]:
            total = total + (values[k] - values[k - 1]) * lax.div(i + (len(values) - k), len(values))
    return total


class Sender:
    def __init__(self, sems, partner):
        self.sems = sems
        self.partner = partner
        self.live = []

    def copy(self, src, dst, send_sem, recv_sem, peer):
        return pltpu.make_async_remote_copy(
            src_ref=src, dst_ref=dst, send_sem=send_sem, recv_sem=recv_sem, device_id=peer, device_id_type=MESH
        )

    def send(self, src, dst, peer, recv_sem, like=None):
        self.copy(src, dst, self.sems.at[len(self.live)], recv_sem, peer).start()
        self.live.append(src if like is None else like)

    def got(self, ref, sem):
        self.copy(ref, ref, self.sems.at[0], sem, self.partner).wait_recv()

    def finish(self):
        for k, like in enumerate(self.live):
            self.copy(like, like, self.sems.at[k], self.sems.at[k], self.partner).wait_send()


HALF = OWN // 2
QUART = OWN // 4
GATHER_SENDS = 32
GATHER_SEMS = [pltpu.SemaphoreType.DMA((17,)), pltpu.SemaphoreType.DMA((16,))]


def gather(me, out, buf, direct, cross, compute, before, amid, extra=None):
    def part(dz, dh, dc, k):
        return rows_of(buf, me.shard(dz, dh, dc) * OWN + k * HALF, HALF)

    def sem(sems, dz, dh, k):
        return sems.at[(dz * 2 + dh) * 2 + k]

    half, fourth = rows_of(buf, 0, HALF), rows_of(buf, 0, QUART)

    def send(dz, dh, k, peer, tz, th):
        ref = part(dz, dh, 0, k)
        out.send(ref, ref, peer, sem(direct, tz, th, k), half)

    def over(dz, dh, k):
        ref = part(dz, dh, 0, k)
        out.send(ref, ref, me.sib, sem(cross, dz, dh, k), half)

    def got(dz, dh, k):
        out.got(part(dz, dh, 0, k), sem(direct, dz, dh, k))

    def quarter(dz, k):
        return rows_of(buf, me.shard(dz, 0, 0) * OWN + HALF + k * QUART, QUART)

    send(0, 0, 0, me.yy, 0, 1)
    send(0, 0, 1, me.up, 3, 0)
    send(0, 0, 1, me.dn, 1, 0)
    send(0, 0, 0, me.up, 3, 0)
    send(0, 0, 0, me.dn, 1, 0)
    send(0, 0, 1, me.yy, 0, 1)
    over(0, 0, 0)
    over(0, 0, 1)
    before()
    got(3, 0, 1)
    out.send(quarter(3, 0), quarter(3, 0), me.up, sem(direct, 2, 0, 1), fourth)
    got(1, 0, 1)
    out.send(quarter(1, 1), quarter(1, 1), me.dn, direct.at[16], fourth)
    got(0, 1, 0)
    send(0, 1, 0, me.dn, 1, 1)
    send(0, 1, 0, me.up, 3, 1)
    send(3, 0, 1, me.yy, 3, 1)
    send(1, 0, 1, me.yy, 1, 1)
    over(3, 0, 1)
    over(1, 0, 1)
    over(0, 1, 0)
    got(3, 0, 0)
    send(3, 0, 0, me.up, 2, 0)
    over(3, 0, 0)
    got(1, 0, 0)
    over(1, 0, 0)
    out.got(quarter(2, 0), sem(direct, 2, 0, 1))
    out.got(quarter(2, 1), direct.at[16])
    send(2, 0, 1, me.yy, 2, 1)
    over(2, 0, 1)
    got(0, 1, 1)
    over(0, 1, 1)
    amid()

    def onward():
        got(1, 1, 0)
        send(1, 1, 0, me.dn, 2, 1)
        over(1, 1, 0)

    def late(pairs):
        for dz, dh, k in pairs:
            got(dz, dh, k)
            over(dz, dh, k)

    order = ((0, 0), (3, 0), (1, 0), (0, 1), (2, 0), (3, 1), (1, 1), (2, 1))
    steps = {
        1: onward,
        3: lambda: late(((3, 1, 0), (2, 0, 0))),
        4: lambda: late(((3, 1, 1), (1, 1, 1))),
        7: lambda: late(((2, 1, 0), (2, 1, 1))),
    }

    def visit(i, _):
        for at, step in [*steps.items(), *(extra or {}).items()]:
            pl.when(i == at)(step)
        dz, dh = (entry([pair[j] for pair in order], i) for j in range(2))
        for k in range(2):
            out.got(part(dz, dh, 1, k), sem(cross, dz, dh, k))
        compute(dz, dh)
        return 0

    lax.fori_loop(0, 8, visit, 0)


SCATTER_SENDS = 16
SCATTER_SCRATCH = [
    pltpu.VMEM((8 * OWN, D), F32),
    pltpu.VMEM((8 * OWN, D), BF16),
    pltpu.VMEM((8 * OWN, D), BF16),
    pltpu.VMEM((8 * OWN, D), BF16),
    pltpu.VMEM((2 * HALF, D), BF16),
    pltpu.VMEM((4 * HALF, D), BF16),
    pltpu.VMEM((HALF, D), BF16),
    pltpu.VMEM((4 * HALF, D), BF16),
    pltpu.VMEM((2 * QUART, D), BF16),
    pltpu.VMEM((2 * HALF, D), BF16),
    pltpu.SemaphoreType.DMA((8,)),
    pltpu.SemaphoreType.DMA((8,)),
    pltpu.SemaphoreType.DMA((2,)),
    pltpu.SemaphoreType.DMA((4,)),
    pltpu.SemaphoreType.DMA((1,)),
    pltpu.SemaphoreType.DMA((4,)),
    pltpu.SemaphoreType.DMA((2,)),
    pltpu.SemaphoreType.DMA((2,)),
]


def scatter(me, out, bufs, compute, between, finish, extra=None, quick=False):
    (own, other, cross, sums, via, ring, last, pair, via2, ring2,
     s_over, s_cross, s_via, s_ring, s_last, s_pair, s_via2, s_ring2) = bufs

    def give(dz, dh):
        i = dz * 2 + dh

        at = pl.ds(pl.multiple_of(i * OWN, OWN), OWN)

        def put(dc, terms):
            if dc == 0:
                own[at, :] = terms
            else:
                other[at, :] = terms.astype(BF16)

        compute(dz, dh, put)
        rows = rows_of(other, i * OWN, OWN)
        out.copy(rows, rows_of(cross, i * OWN, OWN), s_over.at[i], s_cross.at[i], me.sib).start()

    def wait_cross(dz, dh):
        i = dz * 2 + dh
        out.got(rows_of(cross, i * OWN, OWN), s_cross.at[i])

    def both(dz, dh, start, rows):
        here = pl.ds((dz * 2 + dh) * OWN + start, rows)
        return own[here, :] + cross[here, :].astype(F32)

    def arrived(buf, sems, i, rows):
        ref = rows_of(buf, i * rows, rows)
        out.got(ref, sems.at[i])
        return ref[...].astype(F32)

    def pass_to(dz, dh, start, rows, value, buf, sems, i, peer):
        at = (dz * 2 + dh) * OWN + start
        sums[pl.ds(at, rows), :] = value.astype(BF16)
        out.send(rows_of(sums, at, rows), rows_of(buf, i * rows, rows), peer, sems.at[i], rows_of(sums, 0, rows))

    def first(dz, dh):
        return both(dz, dh, 0, HALF)

    def to_partner(dz):
        pass_to(dz, 1, HALF, HALF, both(dz, 1, HALF, HALF), pair, s_pair, dz, me.yy)

    def second(dz):
        return both(dz, 0, HALF, HALF) + arrived(pair, s_pair, dz, HALF)

    def start_far():
        wait_cross(2, 1)
        pass_to(2, 1, 0, HALF, first(2, 1), via, s_via, 1, me.dn)
        to_partner(2)
        wait_cross(2, 0)
        pass_to(2, 0, 0, HALF, first(2, 0), via, s_via, 0, me.up)

    def near_others():
        wait_cross(1, 1)
        pass_to(1, 1, 0, HALF, first(1, 1), ring, s_ring, 1, me.up)
        to_partner(1)

    def partner_three():
        wait_cross(3, 1)
        to_partner(3)

    def near_own():
        wait_cross(3, 0)
        pass_to(3, 0, 0, HALF, first(3, 0), ring, s_ring, 2, me.dn)

    def far_seconds():
        own[pl.ds(4 * OWN + HALF, HALF), :] = second(2)
        for k, peer in ((0, me.up), (1, me.dn)):
            value = own[pl.ds(4 * OWN + HALF + k * QUART, QUART), :]
            pass_to(2, 0, HALF + k * QUART, QUART, value, via2, s_via2, k, peer)

    def onward():
        wait_cross(1, 0)
        pass_to(3, 1, 0, HALF, first(3, 1) + arrived(via, s_via, 1, HALF), ring, s_ring, 3, me.dn)
        pass_to(1, 0, 0, HALF, first(1, 0) + arrived(via, s_via, 0, HALF), ring, s_ring, 0, me.up)

    def partner_own():
        wait_cross(0, 1)
        to_partner(0)

    if quick:
        order = ((2, 1), (2, 0), (1, 1), (3, 0), (3, 1), (1, 0), (0, 1), (0, 0))
        steps = [(1, start_far), (3, near_others), (3, near_own), (4, partner_three), (5, far_seconds), (6, partner_own), (6, onward)]
    else:
        order = ((2, 1), (2, 0), (1, 1), (3, 1), (1, 0), (3, 0), (0, 1), (0, 0))
        steps = [(1, start_far), (2, near_others), (3, partner_three), (4, onward), (4, far_seconds), (5, near_own), (6, partner_own)]

    def visit(i, _):
        give(*(entry([pair[j] for pair in order], i) for j in range(2)))
        for at, step in [*steps, *(extra or {}).items()]:
            pl.when(i == at)(step)
        return 0

    lax.fori_loop(0, 8, visit, 0)
    between[0]()
    for dz, k, peer in ((1, 0, me.up), (3, 1, me.dn)):
        mine = pl.ds(dz * 2 * OWN + HALF, HALF)
        own[mine, :] = second(dz)
        own[pl.ds(dz * 2 * OWN + HALF + k * QUART, QUART), :] += arrived(via2, s_via2, k, QUART)
        pass_to(dz, 0, HALF, HALF, own[mine, :], ring2, s_ring2, k, peer)
    between[1]()
    total = first(0, 1) + arrived(ring, s_ring, 1, HALF) + arrived(ring, s_ring, 3, HALF)
    pass_to(0, 1, 0, HALF, total, last, s_last, 0, me.yy)
    wait_cross(0, 0)
    between[2]()
    finish(HALF, HALF, second(0) + arrived(ring2, s_ring2, 0, HALF) + arrived(ring2, s_ring2, 1, HALF))
    total = first(0, 0) + arrived(ring, s_ring, 0, HALF) + arrived(ring, s_ring, 2, HALF)
    finish(0, HALF, total + arrived(last, s_last, 0, HALF))
    for i in range(8):
        rows = rows_of(other, i * OWN, OWN)
        out.copy(rows, rows, s_over.at[i], s_cross.at[i], me.sib).wait_send()


def gelu_parts(h):
    cdf = 0.5 * (1.0 + lax.erf(h * (2.0**-0.5)))
    return cdf


def lane_roll(a, shift):
    return pltpu.roll(a, shift % 128, 1)


def normalized(x):
    mean = jnp.mean(x, axis=1, keepdims=True)
    centered = x - mean
    scale = lax.rsqrt(jnp.mean(centered * centered, axis=1, keepdims=True) + EPS)
    return centered * scale, scale


class Loads:
    def __init__(self, sems):
        self.sems = sems
        self.count = 0

    def start(self, src, dst):
        copy = pltpu.make_async_copy(src, dst, self.sems.at[self.count])
        self.count += 1
        copy.start()
        return copy


def rotary_tables(lens, tabs, first_row, first, angles):
    token = lax.broadcasted_iota(jnp.int32, (8, T), 1)
    begin = jnp.zeros((8, T), jnp.int32)
    end = 0
    for i in range(3):
        end = end + lens[0, i]
        begin = jnp.where(token >= end, end, begin)
    first_row[...] = begin
    step = lax.broadcasted_iota(jnp.int32, (8, T), 0).astype(F32)
    angle = (token - begin).astype(F32) * jnp.exp(step * (-2.0 * math.log(10000.0) / ROT))
    angles[0:8, :] = jnp.cos(angle)
    angles[8:16, :] = jnp.sin(angle)

    def turn(i, _):
        at = pl.ds(pl.multiple_of(i * BLK, BLK), BLK)
        cos, sin = angles[0:8, at], angles[8:16, at]
        none = jnp.zeros((HD - ROT, BLK), F32)
        for k, head in enumerate(((cos, cos, none + 1.0), (-sin, sin, none))):
            tabs[k, at, :] = jnp.concatenate(head + head, axis=0).T
        first[at, :] = jnp.broadcast_to(first_row[0:1, at].astype(F32), (128, BLK)).T.astype(jnp.int32)
        return 0

    lax.fori_loop(0, NB, turn, 0)


def forward_kernel(layer, lens, x_ref, gains_ref, shifts_ref, b_qkv, b_in, b_out, b_down,
                   wqkv_h, aqkv_h, uqkv_h, win_h, ain_h, uin_h, wout_h, aout_h, uout_h, wdown_h, adown_h, udown_h, *refs):
    (o_x, o_xh, o_qkv, o_ho, o_out, o_lse, o_kt, o_wint, o_wout, o_tabs, o_first,
     xh, qkv, ho, ou, out_t, kt, scores, probs, win, wint, bias, wout, tabs, first, angles,
     wqkv, aqkv, uqkv, w_in, ain, uin, w_out, aout, uout, wdown, adown, udown,
     load_sems, send_sems, g_direct, g_cross, *scat) = refs
    gains, shifts = gains_ref.at[layer], shifts_ref.at[layer]
    me = Place()
    meet = me.arrive()
    loads = Loads(load_sems)
    ins = [
        loads.start(src.at[layer], dst)
        for src, dst in (
            (wqkv_h, wqkv), (aqkv_h, aqkv), (uqkv_h, uqkv), (win_h, w_in), (ain_h, ain), (uin_h, uin),
            (wout_h, w_out), (aout_h, aout), (uout_h, uout), (wdown_h, wdown), (adown_h, adown), (udown_h, udown),
        )
    ]
    out = Sender(send_sems, me.sib)
    rows_of(xh, me.shard(0, 0, 0) * OWN, OWN)[...] = (
        normalized(x_ref[...])[0] * gains[0:1, :] + shifts[0:1, :]
    ).astype(BF16)
    meet()
    outs = []

    def before():
        rotary_tables(lens, tabs, o_first, first, angles)
        for copy in ins[:3]:
            copy.wait()
        for j in range(3):
            here = pl.ds(j * HD, HD)
            wint[here, :] = (wqkv[here, :].astype(F32) + mm3(uqkv[j], aqkv[j], NT)).astype(BF16)
            bias[:, here] = b_qkv[j, layer:layer + 1, :]
        wint[3 * HD:NQ, :] = jnp.zeros((NQ - 3 * HD, D), BF16)
        bias[:, 3 * HD:NQ] = jnp.zeros((1, NQ - 3 * HD), F32)
        win[:, 0:NQ] = wint[0:NQ, :].astype(F32).T.astype(BF16)

    def amid():
        for copy in ins[3:]:
            copy.wait()
        ratio = gains[1:2, :] / gains[0:1, :]
        merged = w_in[...].astype(F32) + mm3(ain[...], uin[...])
        low = merged.astype(BF16)
        b_high, b_low = split_bf16(jnp.broadcast_to(shifts[1:2, :] - shifts[0:1, :] * ratio, (8, D)))
        bias[:, NQ:NIN] = b_in[layer:layer + 1, :] + (mm(b_high, low) + mm(b_low, low))[0:1]
        turned = merged.T * ratio
        wint[NQ:NIN, :] = turned.astype(BF16)
        win[:, NQ:NIN] = turned.T.astype(BF16)
        wout[0:64, :] = (w_out[...].astype(F32) + mm3(aout[...], uout[...])).astype(BF16)
        wout[64:128, :] = jnp.zeros((64, D), BF16)
        wout[128:NOUT, :] = (wdown[...].astype(F32) + mm3(adown[...], udown[...])).astype(BF16)
        outs.append(loads.start(wint, o_wint))
        outs.append(loads.start(wout, o_wout))
        if layer == 0:
            outs.append(loads.start(tabs, o_tabs))

    def project(dz, dh):
        at = pl.ds(pl.multiple_of(me.block(dz, dh) * BLK, BLK), BLK)
        rows = xh[at, :]
        pq = mm(rows, win[:, 0:NQ]) + bias[:, 0:NQ]
        qk = pq[:, 0:128]
        lane = lax.broadcasted_iota(jnp.int32, (BLK, 128), 1)
        other = jnp.where(lax.rem(lane, HD) < ROT // 2, lane_roll(qk, -8), lane_roll(qk, 8))
        turned = qk * tabs[0, at, :] + other * tabs[1, at, :]
        qkv[at, 0:128] = jnp.where(lane < HD, turned * HD**-0.5, 0.0).astype(BF16)
        keys = jnp.where(lane < HD, lane_roll(turned, HD), 0.0)
        qkv[at, 128:256] = keys.astype(BF16)
        kt[:, at] = keys.T.astype(BF16)
        qkv[at, 256:384] = pq[:, 128:256].astype(BF16)
        h = mm(rows, win[:, NQ:NIN]) + bias[:, NQ:NIN]
        ho[at, 128:NOUT] = h
        ou[at, 128:NOUT] = (h * gelu_parts(h)).astype(BF16)

    gather(me, out, xh, g_direct, g_cross, project, before, amid)
    outs.extend([loads.start(xh, o_xh), loads.start(qkv, o_qkv), loads.start(kt, o_kt)])

    def attend(dz, dh, put):
        b = me.block(dz, dh)
        at = pl.ds(pl.multiple_of(b * BLK, BLK), BLK)

        def over_keys(tiles):
            key_at = (b - 4) * BLK if tiles == 5 else 0
            width = tiles * BLK
            q = qkv[at, 0:128]
            row = b * BLK + lax.broadcasted_iota(jnp.int32, (BLK, BLK), 0)
            start = jnp.concatenate([first[at, :], first[at, :]], axis=1)
            peak = None
            for j in range(tiles):
                keys = pl.ds(pl.multiple_of(key_at + j * BLK, BLK), BLK)
                s = mm(q, qkv[keys, 128:256], NT)
                col = key_at + j * BLK + lax.broadcasted_iota(jnp.int32, (BLK, BLK), 1)
                allowed = col >= start
                if tiles < 5 or j == 4:
                    allowed = allowed & (col <= row)
                s = jnp.where(allowed, s, FILL)
                scores[:, j * BLK:(j + 1) * BLK] = s
                peak = s if peak is None else jnp.maximum(peak, s)
            peak = jnp.max(peak, axis=1, keepdims=True)
            summed = None
            for j in range(tiles):
                p = jnp.exp(scores[:, j * BLK:(j + 1) * BLK] - peak)
                probs[:, j * BLK:(j + 1) * BLK] = p.astype(BF16)
                summed = p if summed is None else summed + p
            summed = jnp.sum(summed, axis=1, keepdims=True)
            values = qkv[pl.ds(pl.multiple_of(key_at, BLK), width), 256:384]
            o = mm(probs[:, 0:width], values) * (1.0 / summed)
            ho[at, 0:128] = o
            ou[at, 0:128] = o.astype(BF16)
            lse = jnp.broadcast_to(peak + jnp.log(summed), (BLK, 128)).T
            o_lse[:, at] = lse[0:8, :]

        pl.when(b < 2)(lambda: over_keys(2))
        pl.when((b >= 2) & (b < 4))(lambda: over_keys(4))
        pl.when(b >= 4)(lambda: over_keys(5))
        out_t[:, at] = ou[at, :].astype(F32).T.astype(BF16)
        for dc in range(2):
            put(dc, mm(rows_of(ou, me.shard(dz, dh, dc) * OWN, OWN)[...], wout[...]))

    def store():
        outs.append(loads.start(ho, o_ho))
        outs.append(loads.start(out_t, o_out))

    def nothing():
        pass

    def finish(at, rows, total):
        here = pl.ds(at, rows)
        o_x[here, :] = x_ref[here, :] + total + (b_out[layer:layer + 1, :] + b_down[layer:layer + 1, :])

    scatter(me, out, scat, attend, (store, nothing, nothing), finish)
    for copy in outs:
        copy.wait()
    out.finish()


VM = pl.BlockSpec(memory_space=pltpu.VMEM)
HBM = pl.BlockSpec(memory_space=pl.ANY)


SMEM = pl.BlockSpec(memory_space=pltpu.SMEM)


def forward(layer, lens, x, gains, shifts, biases, weights):
    vmem = pltpu.VMEM
    shapes = [
        jax.ShapeDtypeStruct((OWN, D), F32),
        jax.ShapeDtypeStruct((T, D), BF16),
        jax.ShapeDtypeStruct((T, 384), BF16),
        jax.ShapeDtypeStruct((T, NOUT), F32),
        jax.ShapeDtypeStruct((NOUT, T), BF16),
        jax.ShapeDtypeStruct((8, T), F32),
        jax.ShapeDtypeStruct((128, T), BF16),
        jax.ShapeDtypeStruct((NIN, D), BF16),
        jax.ShapeDtypeStruct((NOUT, D), BF16),
        jax.ShapeDtypeStruct((2, T, 128), F32),
        jax.ShapeDtypeStruct((8, T), jnp.int32),
    ]
    return pl.pallas_call(
        functools.partial(forward_kernel, layer),
        out_shape=shapes,
        in_specs=[SMEM] + [VM] * 7 + [HBM] * 12,
        out_specs=[VM, HBM, HBM, HBM, HBM, VM, HBM, HBM, HBM, HBM, VM],
        scratch_shapes=[
            vmem((T, D), BF16),
            vmem((T, 384), BF16),
            vmem((T, NOUT), F32),
            vmem((T, NOUT), BF16),
            vmem((NOUT, T), BF16),
            vmem((128, T), BF16),
            vmem((BLK, WIN), F32),
            vmem((BLK, WIN), BF16),
            vmem((D, NIN), BF16),
            vmem((NIN, D), BF16),
            vmem((1, NIN), F32),
            vmem((NOUT, D), BF16),
            vmem((2, T, 128), F32),
            vmem((T, 128), jnp.int32),
            vmem((16, T), F32),
            vmem((192, D), BF16),
            vmem((3, D, R), F32),
            vmem((3, HD, R), F32),
            vmem((D, FF), BF16),
            vmem((D, R), F32),
            vmem((R, FF), F32),
            vmem((64, D), BF16),
            vmem((64, R), F32),
            vmem((R, D), F32),
            vmem((FF, D), BF16),
            vmem((FF, R), F32),
            vmem((R, D), F32),
            pltpu.SemaphoreType.DMA((24,)),
            pltpu.SemaphoreType.DMA((GATHER_SENDS + SCATTER_SENDS,)),
            *GATHER_SEMS,
            *SCATTER_SCRATCH,
        ],
        compiler_params=pltpu.CompilerParams(
            collective_id=layer, has_side_effects=True, vmem_limit_bytes=60 << 20
        ),
        name=f"forward_layer{layer}",
    )(lens, x, gains, shifts, *biases, *weights)


def backward_kernel(layer, last, dy_ref, x_ref, xh_h, qkv_h, ho_h, out_h, lse_ref, kt_h, wint_h, wout_h, gains_ref, shifts_ref,
                    tabs_h, first_ref, aqkv_h, uqkv_h, ain_h, bin_h, aout_h, bout_h, adown_h, bdown_h, *refs):
    refs = list(refs)
    take = lambda count: [refs.pop(0) for _ in range(count)]
    if last:
        earlier_h, earlier_norm, earlier_group, earlier_sums = take(4)
        o_dx, o_total, o_norm_total, o_group_total = take(4)
    else:
        o_dx, o_spread, o_norm, o_group, o_sums = take(5)
    (dy, xh, qkv, ho, out_t, kt, dph, low, dph_t, acc, wint, wout, tabs, aqkv, uqkv, ain, bin_, aout, bout, adown, bdown,
     load_sems, send_sems, g_direct, g_cross) = take(25)
    scat = take(len(SCATTER_SCRATCH))
    if last:
        o_spread, o_norm, o_group, o_sums, earlier, total = take(6)
    gains, shifts = gains_ref.at[layer], shifts_ref.at[layer]
    me = Place()
    meet = me.arrive(last)
    loads = Loads(load_sems)
    early = [
        loads.start(wout_h, wout),
        loads.start(ho_h, ho),
        loads.start(qkv_h, qkv),
        loads.start(kt_h, kt),
    ]
    late = [
        loads.start(tabs_h, tabs),
        loads.start(wint_h, wint),
        loads.start(xh_h, xh),
        loads.start(out_h, out_t),
        loads.start(aqkv_h.at[layer], aqkv),
        loads.start(uqkv_h.at[layer], uqkv),
        loads.start(ain_h.at[layer], ain),
        loads.start(bin_h.at[layer], bin_),
        loads.start(aout_h.at[layer], aout),
        loads.start(bout_h.at[layer], bout),
        loads.start(adown_h.at[layer], adown),
        loads.start(bdown_h.at[layer], bdown),
    ]
    out = Sender(send_sems, me.sib)
    rows_of(dy, me.shard(0, 0, 0) * OWN, OWN)[...] = dy_ref[...].astype(BF16)
    meet()

    stages, ends = [], []
    if last:
        at_chip = Chips()
        half = pl.ds(pl.multiple_of(at_chip.c * (D // 2), D // 2), D // 2)
        copy_in = loads.start(earlier_h.at[:, half], earlier)
        n = len(path_scratch(128))
        stages = spread_stages(
            at_chip, out, earlier_h, total.at[pl.ds(768, 768)], (0, 512), "x", "z", take(n), earlier
        )
        for begin, axes in ((0, ("x", "z")), (256, ("z", "x"))):
            ends.append(spread_stages(at_chip, out, o_spread, total.at[pl.ds(0, 768)], (begin, 256), *axes, take(n)))
        ends.append(norm_group_stages(
            at_chip, out, (o_norm, earlier_norm), (o_group, earlier_group), (o_sums, earlier_sums),
            o_norm_total, o_group_total, refs,
        ))

    def stage(i):
        if stages:
            stages[i]()

    def end(i):
        for kind in ends:
            kind[i]()

    def extra(at, i):
        return {at: lambda: stage(i)} if last else None

    def before():
        if last:
            copy_in.wait()
        stage(0)
        acc[...] = jnp.zeros(acc.shape, F32)
        stage(1)

    def amid():
        for copy in early:
            copy.wait()

    def pull(dz, dh):
        b = me.block(dz, dh)
        at = pl.ds(pl.multiple_of(b * BLK, BLK), BLK)
        rows = dy[at, :]
        du = mm(rows, wout[128:NOUT, :], NT)
        h = ho[at, 128:NOUT]
        slope = gelu_parts(h) + h * (jnp.exp(-0.5 * h * h) * (2.0 * math.pi) ** -0.5)
        ho[at, 128:NOUT] = slope * du
        do = mm(rows, wout[0:128, :], NT).astype(BF16)
        drop = jnp.sum((do.astype(F32) * ho[at, 0:128]).T, axis=0, keepdims=True)
        lse = lse_ref[0:1, at]
        start = first_ref[0:1, at]
        q = qkv[at, 0:128]
        key_at = jnp.maximum(b - 5, 0)
        wide = 3 * BLK
        col = b * BLK + lax.broadcasted_iota(jnp.int32, (wide, BLK), 1)

        def step(j, dq):
            key = (key_at + 3 * j) * BLK
            keys = pl.ds(pl.multiple_of(key, BLK), wide)
            s = mm(qkv[keys, 128:256], q, NT)
            row = key + lax.broadcasted_iota(jnp.int32, (wide, BLK), 0)
            p = jnp.where((row >= start) & (row <= col), jnp.exp(s - lse), 0.0)
            dp = mm(qkv[keys, 256:384], do, NT)
            ds = (p * (dp - drop)).astype(BF16)
            acc[keys, 128:256] += mm(p.astype(BF16), do)
            acc[keys, 0:128] += mm(ds, q)
            return dq + mm(kt[:, keys], ds)

        dq = lax.fori_loop(0, (jnp.minimum(b, 5) + 3) // 3, step, jnp.zeros((128, BLK), F32))
        ho[at, 0:128] = dq.T * HD**-0.5

    gather(me, out, dy, g_direct, g_cross, pull, before, amid, extra(4, 2))
    stage(3)
    for copy in late:
        copy.wait()

    def send_back(dz, dh, put):
        b = me.block(dz, dh)
        at = pl.ds(pl.multiple_of(b * BLK, BLK), BLK)
        g = ho[at, 0:128] + lane_roll(acc[at, 0:128], HD)
        side = g * tabs[1, at, :]
        lane = lax.rem(lax.broadcasted_iota(jnp.int32, (BLK, 128), 1), HD)
        side = jnp.where(lane < ROT // 2, lane_roll(side, -8), jnp.where(lane < ROT, lane_roll(side, 8), 0.0))
        turned = g * tabs[0, at, :] + side
        dph[:, 0:128] = turned.astype(BF16)
        dph[:, 128:256] = acc[at, 128:256].astype(BF16)
        dph[:, NQ:NIN] = ho[at, 128:NOUT].astype(BF16)
        rows = dph[...]
        for dc in range(2):
            put(dc, mm(rows_of(dph, lax.rem(me.c + dc, 2) * OWN, OWN)[...], wint[...]))
        dph_t[:, at] = rows.astype(F32).T.astype(BF16)

    def by_columns(piece):
        def visit(i, _):
            piece(pl.ds(pl.multiple_of(i * 256, 256), 256))
            return 0

        lax.fori_loop(0, D // 256, visit, 0)

    def weight_grad(row, at, width):
        here = pl.ds(at, width)
        total = jnp.sum(dph_t[here, :].astype(F32), axis=1, keepdims=True)
        o_sums[:, here] = jnp.broadcast_to(total, (width, 128)).T[0:8, :]

        def piece(cols):
            grad = mm(dph_t[here, :], xh[:, cols])
            weight = wint[here, cols].astype(F32)
            by_gain = jnp.sum(grad * weight, axis=0, keepdims=True)
            by_shift = jnp.sum(total * weight, axis=0, keepdims=True)
            g, b = gains[0:1, cols], shifts[0:1, cols]
            if row == 1:
                ratio = gains[1:2, cols] / g
                by_gain, by_shift = by_gain / ratio, by_shift / ratio
                grad = grad * ratio + total * (shifts[1:2, cols] - b * ratio)
            o_norm[row:row + 1, cols] = (by_gain - b * by_shift) / g
            o_norm[2 + row:3 + row, cols] = by_shift
            low[here, cols] = grad.astype(BF16)

        by_columns(piece)

    def factors_qkv():
        stage(5)
        weight_grad(0, 0, NQ)
        for j in range(3):
            o_spread[j * R:(j + 1) * R, :] = mm(uqkv[j].astype(BF16), low[j * HD:(j + 1) * HD, :], TN).astype(BF16)
            o_group[j * HD:(j + 1) * HD, :] = mm(low[j * HD:(j + 1) * HD, :], aqkv[j].astype(BF16))

    def factors_in():
        weight_grad(1, NQ, FF)
        o_spread[3 * R:4 * R, :] = mm(bin_[...].astype(BF16), low[NQ:NIN, :]).astype(BF16)
        o_group[256:512, :] = mm(low[NQ:NIN, :], ain[...].astype(BF16))

    def factors_out():
        def piece(cols):
            low[0:64, cols] = mm(out_t[0:64, :], dy[:, cols]).astype(BF16)
            low[NQ:NIN, cols] = mm(out_t[128:NOUT, :], dy[:, cols]).astype(BF16)

        by_columns(piece)
        o_spread[4 * R:5 * R, :] = mm(aout[...].astype(BF16), low[0:64, :], TN).astype(BF16)
        o_group[192:256, :] = mm(low[0:64, :], bout[...].astype(BF16), NT)
        o_spread[5 * R:6 * R, :] = mm(adown[...].astype(BF16), low[NQ:NIN, :], TN).astype(BF16)
        o_group[512:768, :] = mm(low[NQ:NIN, :], bdown[...].astype(BF16), NT)
        o_norm[4:5, :] = jnp.sum(dy_ref[...], axis=0, keepdims=True)
        o_norm[5:8, :] = jnp.zeros((3, D), F32)
        stage(6)
        end(0)
        end(1)

    def finish(at, rows, total):
        here = pl.ds(at, rows)
        hat, rstd = normalized(x_ref[here, :])
        total = total * gains[0:1, :]
        mean = jnp.mean(total, axis=1, keepdims=True)
        along = jnp.mean(total * hat, axis=1, keepdims=True)
        o_dx[here, :] = dy_ref[here, :] + rstd * (total - mean - hat * along)

    scatter(me, out, scat, send_back, (factors_qkv, factors_in, factors_out), finish, extra(4, 4), True)
    if last:
        stage(7)
        for i in range(2, 8):
            end(i)
        store = loads.start(total, o_total)
        out.finish()
        store.wait()
    else:
        out.finish()


def backward(layer, dy, x, saved, gains, shifts, tabs, first, factors, earlier=None):
    last = earlier is not None
    grads = [((6 * R, D), BF16), ((8, D), F32), ((768, R), F32), ((8, NIN), F32)]
    totals = [((LAYERS * 6 * R, D), BF16), ((8 * LAYERS, D), F32), ((4 * GROUP, R), BF16)]
    shapes = [jax.ShapeDtypeStruct(*kind) for kind in [((OWN, D), F32), *(totals if last else grads)]]
    sums = [pltpu.VMEM(*kind) for kind in grads] + [pltpu.VMEM((6 * R, D // 2), BF16), pltpu.VMEM(*totals[0])]
    sums += path_scratch(512) + path_scratch(256) * 2 + NORM_GROUP_SCRATCH
    sends = GATHER_SENDS + SCATTER_SENDS + (3 * PATH_SENDS + NORM_GROUP_SENDS if last else 0)
    return pl.pallas_call(
        functools.partial(backward_kernel, layer, last),
        out_shape=shapes,
        in_specs=[VM, VM, HBM, HBM, HBM, HBM, VM, HBM, HBM, HBM, VM, VM, HBM, VM] + [HBM] * 8 + ([HBM, VM, VM, VM] if last else []),
        out_specs=[VM, HBM, VM, VM] if last else [VM] * 5,
        scratch_shapes=[
            pltpu.VMEM((T, D), BF16),
            pltpu.VMEM((T, D), BF16),
            pltpu.VMEM((T, 384), BF16),
            pltpu.VMEM((T, NOUT), F32),
            pltpu.VMEM((NOUT, T), BF16),
            pltpu.VMEM((128, T), BF16),
            pltpu.VMEM((BLK, NIN), BF16),
            pltpu.VMEM((NIN, D), BF16),
            pltpu.VMEM((NIN, T), BF16),
            pltpu.VMEM((T, 256), F32),
            pltpu.VMEM((NIN, D), BF16),
            pltpu.VMEM((NOUT, D), BF16),
            pltpu.VMEM((2, T, 128), F32),
            pltpu.VMEM((3, D, R), F32),
            pltpu.VMEM((3, HD, R), F32),
            pltpu.VMEM((D, R), F32),
            pltpu.VMEM((R, FF), F32),
            pltpu.VMEM((64, R), F32),
            pltpu.VMEM((R, D), F32),
            pltpu.VMEM((FF, R), F32),
            pltpu.VMEM((R, D), F32),
            pltpu.SemaphoreType.DMA((24,)),
            pltpu.SemaphoreType.DMA((sends,)),
            *GATHER_SEMS,
            *SCATTER_SCRATCH,
            *(sums if last else []),
        ],
        compiler_params=pltpu.CompilerParams(
            collective_id=LAYERS + layer, has_side_effects=True, vmem_limit_bytes=60 << 20
        ),
        name=f"backward_layer{layer}",
    )(dy, x, *saved, gains, shifts, tabs, first, *factors, *(earlier or ()))


QUARTER = 768 // 4
PATH_SENDS = 23


def path_scratch(width):
    dma = pltpu.SemaphoreType.DMA
    return [
        pltpu.VMEM((768, width), BF16),
        pltpu.VMEM((768, width), BF16),
        pltpu.VMEM((3, QUARTER, width), BF16),
        pltpu.VMEM((QUARTER, width), F32),
        pltpu.VMEM((QUARTER, width), BF16),
        pltpu.VMEM((3, 48, width), BF16),
        pltpu.VMEM((4, 48, width), BF16),
        pltpu.VMEM((QUARTER, width), BF16),
        dma((4,)),
        dma((3,)),
        dma((3,)),
        dma((3,)),
        dma((3,)),
        dma((3,)),
        dma((4,)),
    ]


class Chips:
    def __init__(self):
        self.yl, self.x, self.z, self.yh, self.c = (lax.axis_index(a) for a in ALL)
        self.y = self.yh * 2 + self.yl
        self.sib = {"c": 1 - self.c}

    def here(self, axis):
        return {"x": self.x, "z": self.z}[axis]

    def along(self, axis, d):
        return {axis: lax.rem(self.here(axis) + d, 4)}

    def y_peer(self, d):
        there = lax.rem(self.y + d, 4)
        return {"yh": lax.div(there, 2), "yl": lax.rem(there, 2)}

    def quarter(self, axis, d, size):
        return pl.multiple_of(lax.rem(self.here(axis) + d, 4) * size, size)


def spread_stages(at, out, src, dst, lanes, first, second, bufs, own_half=None):
    cross, low, slots1, acc, low2, slots2, along_y, totals, s_cross, s_one, s_two, s_y, s_back2, s_back1, s_backc = bufs
    begin, width = lanes
    mine = pl.ds(pl.multiple_of(at.c * 512 + begin, 128), width)
    theirs = pl.ds(pl.multiple_of((1 - at.c) * 512 + begin, 128), width)

    def rows(d):
        return pl.ds(at.quarter(first, d, QUARTER), QUARTER)

    def part(d):
        return pl.ds(at.quarter(second, d, 48), 48)

    big = dst.at[pl.ds(0, QUARTER), pl.ds(0, width)]
    small = low2.at[pl.ds(0, 48)]

    def over_core():
        for d in (2, 1, 3, 0):
            out.send(src.at[rows(d), theirs], cross.at[rows(d)], at.sib, s_cross.at[d], big)

    def along_first():
        for d in (2, 1, 3, 0):
            out.got(cross.at[rows(d)], s_cross.at[d])
            both = (src[rows(d), mine] if own_half is None else own_half[rows(d), :]).astype(F32)
            both = both + cross[rows(d), :].astype(F32)
            if d == 0:
                acc[...] = both
            else:
                low[rows(d), :] = both.astype(BF16)
                out.send(low.at[rows(d)], slots1.at[d - 1], at.along(first, d), s_one.at[d - 1], low.at[pl.ds(0, QUARTER)])

    def along_second():
        total = acc[...]
        for d in (1, 2, 3):
            out.got(slots1.at[d - 1], s_one.at[d - 1])
            total = total + slots1[d - 1].astype(F32)
        acc[...] = total
        low2[...] = total.astype(BF16)
        for d in (2, 1, 3):
            out.send(low2.at[part(d)], slots2.at[d - 1], at.along(second, d), s_two.at[d - 1], small)

    def along_third():
        total = acc[part(0), :]
        for d in (1, 2, 3):
            out.got(slots2.at[d - 1], s_two.at[d - 1])
            total = total + slots2[d - 1].astype(F32)
        own = along_y.at[at.y]
        own[...] = total.astype(BF16)
        for d in (2, 1, 3):
            out.send(own, own, at.y_peer(d), s_y.at[d - 1], along_y.at[0])

    def back_second():
        for d in (1, 2, 3):
            out.got(along_y.at[lax.rem(at.y + 4 - d, 4)], s_y.at[d - 1])
        term = [along_y[i].astype(F32) for i in range(4)]
        own = totals.at[part(0)]
        own[...] = ((term[0] + term[1]) + (term[2] + term[3])).astype(BF16)
        for d in (2, 1, 3):
            out.send(own, own, at.along(second, d), s_back2.at[d - 1], small)

    def back_first():
        for d in (1, 2, 3):
            out.got(totals.at[part(4 - d)], s_back2.at[d - 1])
        own = dst.at[rows(0), mine]
        own[...] = totals[...]
        for d in (2, 1, 3):
            out.send(own, own, at.along(first, d), s_back1.at[d - 1], big)
        out.send(own, own, at.sib, s_backc.at[0], big)

    def back_core():
        for d in (1, 3, 2):
            own = dst.at[rows(4 - d), mine]
            out.got(own, s_back1.at[d - 1])
            out.send(own, own, at.sib, s_backc.at[d], big)

    def arrive():
        for d in range(4):
            out.got(dst.at[rows(4 - d), theirs], s_backc.at[d])

    return [over_core, along_first, along_second, along_third, back_second, back_first, back_core, arrive]


GROUP = 400


NORM_GROUP_SENDS = 1 + 3 + 3 + 3 + 1 + 3 + 3 + 1
NORM_GROUP_SCRATCH = [
    pltpu.VMEM((2, 16, 512), F32),
    pltpu.VMEM((12, 16, 512), F32),
    pltpu.VMEM((4 * GROUP, R), F32),
    pltpu.VMEM((4 * GROUP, R), BF16),
    pltpu.VMEM((3, GROUP, R), BF16),
    pltpu.VMEM((2, GROUP, R), BF16),
    pltpu.SemaphoreType.DMA((11,)),
    pltpu.SemaphoreType.DMA((7,)),
]


def norm_group_stages(at, out, norms, groups, sums, o_norm, o_group, bufs):
    n_first, n_slots, g_own, g_low, g_slots, g_pair, s_norm, s_group = bufs
    mine = pl.ds(pl.multiple_of(at.c * 512, 512), 512)
    theirs = pl.ds(pl.multiple_of((1 - at.c) * 512, 512), 512)

    def n_stage(stage, value, index, peer_of, base):
        own = n_slots.at[stage * 4 + index]
        own[...] = value
        for d in (1, 2, 3):
            out.send(own, own, peer_of(d), s_norm.at[base + d - 1])

    def n_sum(stage, index, base):
        for d in (1, 2, 3):
            out.got(n_slots.at[stage * 4 + lax.rem(index + 4 - d, 4)], s_norm.at[base + d - 1])
        return (n_slots[stage * 4] + n_slots[stage * 4 + 1]) + (n_slots[stage * 4 + 2] + n_slots[stage * 4 + 3])

    def g_rows(d):
        return pl.ds(at.quarter("x", d, GROUP), GROUP)

    def begin():
        for i, norm in enumerate(norms):
            n_first[0, i * 8:i * 8 + 8, :] = norm[:, theirs]
        out.send(n_first.at[0], n_first.at[1], at.sib, s_norm.at[0])
        for i in range(4):
            group, total, half = groups[i // 2], sums[i // 2], i % 2
            g_own[i * GROUP:i * GROUP + 384, :] = group[half * 384:half * 384 + 384, :]
            for k in range(2):
                rows = pl.ds(i * GROUP + 384 + 8 * k, 8)
                g_own[rows, :] = total[:, half * 256 + 128 * k:half * 256 + 128 * k + 128]
        g_low[...] = g_own[...].astype(BF16)
        for d in (2, 1, 3):
            out.send(g_low.at[g_rows(d)], g_slots.at[d - 1], at.along("x", d), s_group.at[d - 1])

    def along_x():
        out.got(n_first.at[1], s_norm.at[0])
        first = jnp.concatenate([norm[:, mine] for norm in norms], axis=0) + n_first[1]
        n_stage(0, first, at.x, lambda d: at.along("x", d), 1)

    def along_z():
        total = g_own[g_rows(0), :]
        for d in (1, 2, 3):
            out.got(g_slots.at[d - 1], s_group.at[d - 1])
            total = total + g_slots[d - 1].astype(F32)
        g_pair[0] = total.astype(BF16)
        out.send(g_pair.at[0], g_pair.at[1], {"yl": 1 - at.yl}, s_group.at[3])
        n_stage(1, n_sum(0, at.x, 1), at.z, lambda d: at.along("z", d), 4)

    def along_third():
        out.got(g_pair.at[1], s_group.at[3])
        own = o_group.at[g_rows(0)]
        own[...] = (g_pair[0].astype(F32) + g_pair[1].astype(F32)).astype(BF16)
        for d in (1, 2, 3):
            out.send(own, own, at.along("x", d), s_group.at[3 + d])
        n_stage(2, n_sum(1, at.z, 4), at.y, at.y_peer, 7)

    def back_core():
        o_norm[:, mine] = n_sum(2, at.y, 7)
        out.send(o_norm.at[:, mine], o_norm.at[:, mine], at.sib, s_norm.at[10])

    def nothing():
        pass

    def arrive():
        for d in (1, 2, 3):
            out.got(o_group.at[g_rows(4 - d)], s_group.at[3 + d])
        out.got(o_norm.at[:, theirs], s_norm.at[10])

    return [begin, along_x, along_z, along_third, back_core, nothing, nothing, arrive]


def unpack_kernel(spread, norm, group, stream, grad, o_stream, o_grad, o_gain, o_shift, o_bqkv, o_aqkv, o_uqkv, o_bout, o_aout, o_uout, o_bin, o_ain, o_uin,
                  o_bdown, o_adown, o_udown):
    o_stream[...] = stream[...]
    o_grad[...] = grad[...]
    for j in range(3):
        o_aqkv[j] = spread[j * R:(j + 1) * R, :].astype(F32).T
    o_ain[...] = spread[3 * R:4 * R, :].astype(F32).T
    o_uout[...] = spread[4 * R:5 * R, :].astype(F32)
    o_udown[...] = spread[5 * R:6 * R, :].astype(F32)
    o_gain[...] = norm[0:2, :]
    o_shift[...] = norm[2:4, :]
    for j in range(3):
        o_uqkv[j] = group[j * HD:(j + 1) * HD, :].astype(F32)
    o_aout[...] = group[192:256, :].astype(F32)
    o_uin[:, 0:128] = group[256:384, :].astype(F32).T
    o_uin[:, 128:256] = group[GROUP:GROUP + 128, :].astype(F32).T
    o_adown[...] = group[GROUP + 128:GROUP + 384, :].astype(F32)
    query_key, value = group[384:385, :].astype(F32), group[392:393, :].astype(F32)
    hidden = [group[GROUP + 384 + 8 * k:GROUP + 385 + 8 * k, :].astype(F32) for k in range(2)]

    def small(layer):
        row = slice(layer, layer + 1)
        o_bout[row, :] = norm[4:5, :]
        o_bdown[row, :] = norm[4:5, :]
        o_bqkv[0, row, :] = query_key[:, 0:HD]
        o_bqkv[1, row, :] = query_key[:, HD:2 * HD]
        o_bqkv[2, row, :] = value[:, 0:HD]
        o_bin[row, 0:128] = hidden[0]
        o_bin[row, 128:256] = hidden[1]

    for layer in range(LAYERS):
        pl.when(pl.program_id(0) == layer)(functools.partial(small, layer))


def unpack(spread, norm, group, stream, grad):
    by_layer = {
        "gain": (2, D), "shift": (2, D), "aqkv": (3, D, R), "uqkv": (3, HD, R), "aout": (64, R), "uout": (R, D),
        "ain": (D, R), "uin": (R, FF), "adown": (FF, R), "udown": (R, D),
    }
    whole = {"bqkv": (3, LAYERS, HD), "bout": (LAYERS, D), "bin": (LAYERS, FF), "bdown": (LAYERS, D)}
    names = ["gain", "shift", "bqkv", "aqkv", "uqkv", "bout", "aout", "uout", "bin", "ain", "uin", "bdown", "adown", "udown"]

    def pair(rows, cols):
        return pl.BlockSpec((rows, cols), lambda l: (l, 0))

    shapes, specs = [(OWN, D)] * 2, [pair(OWN // 2, D)] * 2
    for name in names:
        if name in whole:
            shape, rank = whole[name], len(whole[name])
            shapes.append(shape)
            specs.append(pl.BlockSpec(shape, lambda l, rank=rank: (0,) * rank))
        else:
            shape, rank = by_layer[name], len(by_layer[name])
            shapes.append((LAYERS, *shape))
            specs.append(pl.BlockSpec((None, *shape), lambda l, rank=rank: (l,) + (0,) * rank))
    return pl.pallas_call(
        unpack_kernel,
        grid=(LAYERS,),
        out_shape=[jax.ShapeDtypeStruct(shape, F32) for shape in shapes],
        in_specs=[pair(768, D), pair(8, D), pair(2 * GROUP, R), pair(OWN // 2, D), pair(OWN // 2, D)],
        out_specs=specs,
        compiler_params=pltpu.CompilerParams(vmem_limit_bytes=60 << 20),
        name="unpack",
    )(spread, norm, group, stream, grad)


def body(x, dy, lengths, gain, shift, w_qkv, b_qkv, a_qkv, u_qkv, w_out, b_out, a_out, u_out,
         w_in, b_in, a_in, u_in, w_down, b_down, a_down, u_down):
    w_qkv = w_qkv.transpose(0, 2, 3, 1).reshape(LAYERS, 3 * HD, D)
    u_qkv = u_qkv.swapaxes(2, 3)
    weights = (w_qkv, a_qkv, u_qkv, w_in, a_in, u_in, w_out, a_out, u_out, w_down, a_down, u_down)
    biases = (b_qkv.swapaxes(0, 1), b_in, b_out, b_down)
    kept = []
    stream = x
    for layer in range(LAYERS):
        nxt, *saved = forward(layer, lengths, stream, gain, shift, biases, weights)
        if layer == 0:
            tabs, first = saved[-2:]
        kept.append((stream, saved[:-2]))
        stream = nxt
    factors = (a_qkv, u_qkv, a_in, u_in, a_out, u_out, a_down, u_down)
    grad, *earlier = backward(1, dy, *kept[1], gain, shift, tabs, first, factors)
    grad, *totals = backward(0, grad, *kept[0], gain, shift, tabs, first, factors, earlier)
    (stream, grad, g_gain, g_shift, g_bqkv, g_aqkv, g_uqkv, g_bout, g_aout, g_uout, g_bin, g_ain, g_uin, g_bdown, g_adown, g_udown) = unpack(
        *totals, stream, grad
    )
    return (
        stream,
        grad,
        g_gain,
        g_shift,
        g_bqkv.swapaxes(0, 1),
        g_aqkv,
        g_uqkv.swapaxes(2, 3),
        g_bout,
        g_aout,
        g_uout,
        g_bin,
        g_ain,
        g_uin,
        g_bdown,
        g_adown,
        g_udown,
    )


def solution(mesh):
    torus = Mesh(mesh.devices.reshape(2, 4, 4, 2, 2), ALL)
    return jax.shard_map(
        body,
        mesh=torus,
        in_specs=(
            P(ALL, None),
            P(ALL, None),
            P(DP, None),
            P(),
            P(),
            P(None, None, None, MP),
            P(None, None, MP),
            P(),
            P(None, None, None, MP),
            P(None, MP, None),
            P(),
            P(None, MP, None),
            P(),
            P(None, None, MP),
            P(None, MP),
            P(),
            P(None, None, MP),
            P(None, MP, None),
            P(),
            P(None, MP, None),
            P(),
        ),
        out_specs=(
            P(ALL, None),
            P(ALL, None),
            P(),
            P(),
            P(None, None, MP),
            P(),
            P(None, None, None, MP),
            P(),
            P(None, MP, None),
            P(),
            P(None, MP),
            P(),
            P(None, None, MP),
            P(),
            P(None, MP, None),
            P(),
        ),
        check_vma=False,
    )
```
